32 devices in a mesh: dp: 16 (over z, x, core), tensor: 2 (over y).
Axes of the slice: x: 2, y: 2, z: 4, core: 2. Of those that a mesh axis runs over, the one named last changes fastest.
Arguments:
- history: bfloat16 [9, 2048, 4096], P(None, 'dp'), may hold values from -6 to 6
- mix_weights: float32 [4096, 4, 9], P('dp'), may hold values from -2 to 2
- w_qkv: bfloat16 [3, 2048, 2048], P(None, 'dp', 'tensor'), may hold values from -0.125 to 0.125
- w_out: bfloat16 [2048, 2048], P('dp', 'tensor'), may hold values from -0.5 to 0.5
- w_up: bfloat16 [2048, 8192], P('dp', 'tensor'), may hold values from -0.125 to 0.125
- w_down: bfloat16 [2048, 8192], P('dp', 'tensor'), may hold values from -0.0625 to 0.0625
- norm_gain: bfloat16 [2, 2048], P(None, 'dp'), may hold values from 0.25 to 1.75
- norm_bias: bfloat16 [2, 2048], P(None, 'dp'), may hold values from -1.796875 to 1.796875
- mix_in: bfloat16 [2048, 40], P('dp'), may hold values from -0.125 to 0.125
- mix_out: bfloat16 [40, 40], replicated, may hold values from -1 to 1
- mix_static: float32 [40], replicated, may hold values from -3 to 3
- out_cot: bfloat16 [4096, 2048], P('dp'), may hold values from -6 to 6
- next_cot: float32 [4096, 4, 10], P('dp'), may hold values from -6 to 6
Outputs:
- block_out: bfloat16 [4096, 2048], P('dp')
- next_mix: float32 [4096, 4, 10], P('dp')
- history_grad: bfloat16 [9, 2048, 4096], P(None, 'dp')
- mix_grad: float32 [4096, 4, 9], P('dp')
- w_qkv_grad: float32 [3, 2048, 2048], P(None, 'dp', 'tensor')
- w_out_grad: float32 [2048, 2048], P('dp', 'tensor')
- w_up_grad: float32 [2048, 8192], P('dp', 'tensor')
- w_down_grad: float32 [2048, 8192], P('dp', 'tensor')
- gain_grad: float32 [2, 2048], P(None, 'dp')
- bias_grad: float32 [2, 2048], P(None, 'dp')
- mix_in_grad: float32 [2048, 40], P('dp')
- mix_out_grad: float32 [40, 40], replicated
- static_grad: float32 [40], replicated
The draws below stay inside these ranges and needn't reach their ends.
All inputs are finite; a program needn't handle non-finite values.
Results may differ from the reference program's by a relative error of at most 0.015.
Values may be sent and summed in bfloat16 or wider, within the bound.
A program may use at most 384 MiB of HBM per device.

```python
import math
import jax
import jax.numpy as jnp
from jax import lax

D = 2048
H = 16
HD = 128
FF = 8192
ROT = 32
MIXH = 40
HIST = 9
STREAMS = 4
NEXT = 10
SEQ = 256
TOKENS = 4096
N_DP = 16


def strengthened(entries, own_key, source, target, shards_of, factor):
    def block_of(dim):
        return (jnp.arange(entries.shape[dim]) // (entries.shape[dim] // shards_of)).reshape((-1,) + (1,) * (entries.ndim - 1 - dim))

    near = jax.random.permutation(own_key, shards_of)[block_of(target)]
    far = (block_of(target) + shards_of // 2) % shards_of
    return jnp.where((block_of(source) == near) | (block_of(source) == far), factor * entries, entries)


def block_levels(key, dims, shards, smallest, largest):
    gain, own = 1.0, jax.random.fold_in(key, 6)
    for axis_at, parts in shards:
        draws = jnp.exp(jax.random.uniform(jax.random.fold_in(own, axis_at), (parts,), jnp.float32, smallest / len(shards), largest / len(shards)))
        gain = gain * jnp.repeat(draws, dims[axis_at] // parts).reshape([-1 if axis == axis_at else 1 for axis in range(len(dims))])
    return gain


def noise(own_key, extent, scale, limit, split=(), kind=jnp.bfloat16):
    level = block_levels(own_key, extent, split, -0.22, 0.18) if split else 1.0
    result = jax.random.normal(own_key, extent, jnp.float32) * scale * level
    return jnp.minimum(jnp.maximum(result, -limit), limit).astype(kind)


def gaussian_with(stream_key, dims, scale, bound, cuts, heavy, held_as=jnp.bfloat16):
    drawn = scale * jax.random.normal(stream_key, dims, jnp.float32)
    if cuts:
        drawn = drawn * block_levels(stream_key, dims, cuts, -0.22, 0.18)
    return jnp.clip(strengthened(drawn, jax.random.fold_in(stream_key, 3), *heavy), -bound, bound).astype(held_as)


def setup_inputs(seed: int = 0) -> dict:
    arg_keys = jax.random.split(jax.random.key(seed), 14)
    history = noise(arg_keys[0], (HIST, D, TOKENS), 1.0, 6.0, ((1, 16),))
    mix_weights = noise(arg_keys[1], (TOKENS, STREAMS, HIST), 0.35, 2.0, ((0, 16),), jnp.float32)
    w_qkv = noise(arg_keys[2], (3, D, H * HD), D ** -0.5, 0.125, ((1, 16), (2, 2)))
    w_out = noise(arg_keys[3], (D, H * HD), (H * HD // 16) ** -0.5, 0.5, ((0, 16), (1, 2)))
    w_up = noise(arg_keys[4], (D, FF), D ** -0.5, 0.125, ((0, 16), (1, 2)))
    w_down = noise(arg_keys[5], (D, FF), FF ** -0.5, 0.0625, ((0, 16), (1, 2)))
    norm_gain = jnp.clip(1.0 + 0.15 * jax.random.normal(arg_keys[6], (2, D), jnp.float32), 0.25, 1.75).astype(jnp.bfloat16)
    norm_bias = noise(arg_keys[7], (2, D), 0.3, 1.796875, ((1, 16),))
    mix_in = noise(arg_keys[8], (D, MIXH), D ** -0.5, 0.125, ((0, 16),))
    mix_out = noise(arg_keys[9], (MIXH, STREAMS * NEXT), MIXH ** -0.5, 1.0)
    mix_static = noise(arg_keys[10], (STREAMS * NEXT,), 0.5, 3.0, (), jnp.float32)
    out_cot = gaussian_with(arg_keys[11], (TOKENS, D), 1.0, 6.0, ((0, 16),), (0, 1, 16, 2.0))
    next_cot = noise(arg_keys[12], (TOKENS, STREAMS, NEXT), 1.0, 6.0, ((0, 16),), jnp.float32)
    return {"history": history, "mix_weights": mix_weights, "w_qkv": w_qkv, "w_out": w_out, "w_up": w_up, "w_down": w_down, "norm_gain": norm_gain, "norm_bias": norm_bias, "mix_in": mix_in, "mix_out": mix_out, "mix_static": mix_static, "out_cot": out_cot, "next_cot": next_cot}


@jax.custom_vjp
def low(v):
    return lax.optimization_barrier(v.astype(jnp.bfloat16)).astype(jnp.float32)

@jax.custom_vjp
def low_back(v):
    return v

def low_keep(v):
    return (low(v), None)

def low_pass(kept, grad):
    return (grad,)

def back_keep(v):
    return (v, None)

def back_low(kept, grad):
    return (low(grad),)
low.defvjp(low_keep, low_pass)
low_back.defvjp(back_keep, back_low)
HIGHEST = lax.Precision.HIGHEST
NORM_EPS = 1e-05
ROOT_EPS = 1e-06
MASKED = -1e+30

def layer_norm(values, norm_weight, norm_shift):
    centre = lax.optimization_barrier(jnp.mean(values, axis=-1, keepdims=True))
    offset = values - centre
    spread = lax.optimization_barrier(jnp.mean(offset * offset, axis=-1, keepdims=True))
    return offset * lax.rsqrt(spread + NORM_EPS) * norm_weight + norm_shift

def root_norm(values):
    return values * lax.rsqrt(lax.optimization_barrier(jnp.mean(values * values, axis=-1, keepdims=True)) + ROOT_EPS)

def exact_gelu(values):
    return jax.nn.gelu(values, approximate=False)

def rotary_tables(length, rotary, float_type):
    half_rot = rotary // 2
    places = jnp.arange(length).astype(float_type)
    frequency = jnp.exp(jnp.arange(half_rot).astype(float_type) * (-2.0 * math.log(10000.0) / rotary))
    angles = places[:, None] * frequency[None, :]
    return (jnp.cos(angles), jnp.sin(angles))

def rotate(values, cos_table, sin_table):
    half_rot = cos_table.shape[-1]
    first_half = values[..., :half_rot]
    second = values[..., half_rot:2 * half_rot]
    return jnp.concatenate([first_half * cos_table - second * sin_table, second * cos_table + first_half * sin_table, values[..., 2 * half_rot:]], axis=-1)

def attend(queries, key_rows, value_rows):
    length = queries.shape[1]
    score_scale = 1.0 / math.sqrt(queries.shape[2])
    scores = jnp.einsum('hqd,hkd->hqk', queries, key_rows, precision=HIGHEST) * score_scale
    scores = low_back(scores)
    causal = jnp.arange(length)[:, None] >= jnp.arange(length)[None, :]
    scores = jnp.where(causal[None], scores, MASKED)
    row_peak = lax.optimization_barrier(jnp.max(scores, axis=-1, keepdims=True))
    raised = jnp.exp(scores - row_peak)
    attn_prob = raised / lax.optimization_barrier(jnp.sum(raised, axis=-1, keepdims=True))
    prob_low = low(attn_prob)
    context = jnp.einsum('hqk,hkd->hqd', prob_low, value_rows, precision=HIGHEST)
    return low(low_back(context))

def forward(w_qkv, w_out, w_up, w_down, norm_gain, norm_bias, mix_in, mix_out, mix_static, history, mix_weights):
    group_span = history.shape[2]
    seqs_here = group_span // SEQ
    hist_rows = jnp.transpose(history, (0, 2, 1))
    streams = jnp.einsum('jtd,tsj->std', hist_rows, mix_weights, precision=HIGHEST)
    attn_in = low(layer_norm(streams[:3], norm_gain[0], norm_bias[0]))
    projected = low_back(jnp.einsum('std,sde->ste', attn_in, w_qkv, precision=HIGHEST))
    head_rows = jnp.transpose(projected.reshape(3, seqs_here, SEQ, H, HD), (0, 1, 3, 2, 4))
    cos_table, sin_table = rotary_tables(SEQ, ROT, jnp.float32)
    queries = low(rotate(head_rows[0], cos_table, sin_table))
    key_rows = low(rotate(head_rows[1], cos_table, sin_table))
    value_rows = low(head_rows[2])
    attended = lax.map(lambda triple: jax.checkpoint(attend)(*triple), (queries, key_rows, value_rows))
    mixed_rows = jnp.transpose(attended, (0, 2, 1, 3)).reshape(group_span, H * HD)
    attn_part = jnp.einsum('te,de->td', mixed_rows, w_out, precision=HIGHEST)
    mlp_in = low(layer_norm(streams[3], norm_gain[1], norm_bias[1]))
    up_pre = low_back(jnp.dot(mlp_in, w_up, precision=HIGHEST))
    hidden = low(exact_gelu(up_pre))
    mlp_part = jnp.einsum('tf,df->td', hidden, w_down, precision=HIGHEST)
    block_wide = streams[3] + low_back(attn_part + mlp_part)
    normed = low(root_norm(block_wide))
    inner_low = low(exact_gelu(low_back(jnp.dot(normed, mix_in, precision=HIGHEST))))
    next_flat = low_back(jnp.dot(inner_low, mix_out, precision=HIGHEST)) + mix_static
    return (block_wide, next_flat.reshape(group_span, STREAMS, NEXT))

def reference(history, mix_weights, w_qkv, w_out, w_up, w_down, norm_gain, norm_bias, mix_in, mix_out, mix_static, out_cot, next_cot):
    per_group = math.gcd(N_DP, max(1, 4096 // SEQ))
    group_span = per_group * SEQ
    group_count = N_DP // per_group
    weights = (w_qkv.astype(jnp.float32), w_out.astype(jnp.float32), w_up.astype(jnp.float32), w_down.astype(jnp.float32), norm_gain.astype(jnp.float32), norm_bias.astype(jnp.float32), mix_in.astype(jnp.float32), mix_out.astype(jnp.float32), mix_static)

    def one_group(totals, group_index):
        first_row = group_index * group_span
        hist_piece = lax.dynamic_slice_in_dim(history, first_row, group_span, 2).astype(jnp.float32)
        mix_piece = lax.dynamic_slice_in_dim(mix_weights, first_row, group_span, 0)
        out_piece = lax.dynamic_slice_in_dim(out_cot, first_row, group_span, 0).astype(jnp.float32)
        next_piece = lax.dynamic_slice_in_dim(next_cot, first_row, group_span, 0)
        outputs, pullback = jax.vjp(forward, *weights, hist_piece, mix_piece)
        gradients = pullback((out_piece, next_piece))
        totals = tuple((total_sum + grad_piece for total_sum, grad_piece in zip(totals, gradients[:9])))
        return (totals, (outputs[0].astype(jnp.bfloat16), outputs[1], gradients[9].astype(jnp.bfloat16), gradients[10]))
    zeros_start = tuple((jnp.zeros_like(weight) for weight in weights))
    totals, stacked = lax.scan(one_group, zeros_start, jnp.arange(group_count, dtype=jnp.int32))
    block_parts, next_parts, hist_parts, mix_parts = stacked
    block_out = block_parts.reshape(TOKENS, D)
    next_mix = next_parts.reshape(TOKENS, STREAMS, NEXT)
    history_grad = jnp.transpose(hist_parts, (1, 2, 0, 3)).reshape(HIST, D, TOKENS)
    mix_grad = mix_parts.reshape(TOKENS, STREAMS, HIST)
    return (block_out, next_mix, history_grad, mix_grad, totals[0], totals[1], totals[2], totals[3], totals[4], totals[5], totals[6], totals[7], totals[8])
```

```python
import functools
import math

import jax
import jax.numpy as jnp
from jax import lax
from jax.experimental import pallas as pl
from jax.experimental.pallas import tpu as pltpu
from jax.sharding import PartitionSpec as P

HD = 128
ROT = 32
HIST = 9
STREAMS = 4
NEXT = 10
MIXH = 40

NORM_EPS = 1e-05
ROOT_EPS = 1e-06
MASKED = -1e30

MESH = pl.DeviceIdType.MESH
ANY = pl.BlockSpec(memory_space=pl.ANY)
VM = pl.BlockSpec(memory_space=pltpu.VMEM)
DMA = pltpu.SemaphoreType.DMA
F32, BF16 = jnp.float32, jnp.bfloat16
CORE, SIDE, NEAR, HIGH = 1, 2, 4, 8
QUARTERS = 4


def bit(place, value):
    return lax.rem(lax.div(place, value), 2)


def flip(place, value):
    return place + value - 2 * value * bit(place, value)


def at(start, size, multiple=None):
    return pl.ds(pl.multiple_of(start, size if multiple is None else multiple), size)


def remote(src, dst, send, recv, **where):
    return pltpu.make_async_remote_copy(
        src_ref=src, dst_ref=dst, send_sem=send, recv_sem=recv, device_id=where, device_id_type=MESH
    )


def loop(lower, upper, step):
    def body(index, carry):
        step(index)
        return carry

    lax.fori_loop(lower, upper, body, 0)


def greet(targets):
    barrier = pltpu.get_barrier_semaphore()
    for target in targets:
        pl.semaphore_signal(barrier, inc=1, device_id=target, device_id_type=MESH)
    pl.semaphore_wait(barrier, len(targets))


def greet_all(n_dp, me, other_tensor):
    barrier = pltpu.get_barrier_semaphore()
    loop(
        1,
        n_dp,
        lambda step: pl.semaphore_signal(
            barrier, inc=1, device_id={"dp": lax.rem(me + step, n_dp)}, device_id_type=MESH
        ),
    )
    pl.semaphore_signal(barrier, inc=1, device_id={"tensor": other_tensor}, device_id_type=MESH)
    pl.semaphore_wait(barrier, n_dp)


class Place:
    def __init__(self):
        self.me = lax.axis_index("dp")
        self.tensor = lax.axis_index("tensor")
        self.other = 1 - self.tensor
        self.core = bit(self.me, CORE)
        self.side = bit(self.me, SIDE)
        self.near = bit(self.me, NEAR)
        self.high = lax.div(self.me, HIGH)
        self.quarter = self.near * 2 + self.core
        self.peers = (
            (flip(self.me, CORE), self.near * 2 + 1 - self.core),
            (flip(self.me, NEAR), (1 - self.near) * 2 + self.core),
            (flip(flip(self.me, NEAR), CORE), (1 - self.near) * 2 + 1 - self.core),
        )


def sum_rows(ref_at, depth, chunk, of):
    def body(index, total):
        return total + jnp.sum(of(ref_at(index)), axis=0, keepdims=True)

    return lax.fori_loop(0, depth // chunk, body, jnp.zeros((1, 128), F32))


def gather_kernel(
    n_dp, hist, mix, small, w_qkv, w_up, w_down, w_out,
    o_mix, o_small, o_streams, o_act, o_qkv, o_up, o_down, o_out,
    mix_all, small_all, hist_in, mixed, streams, act,
    early_s, early_r, hist_sem, a2a_s, a2a_r, reshard_s, reshard_r, high_s, high_r, side_s, side_r,
    act_s, act_r, act_local, own_sem, out_sem,
):
    here = Place()
    me, tensor = here.me, here.tensor
    rows = small.shape[0]
    depth = rows * n_dp
    half = hist.shape[2] // n_dp // 2
    high_bits = int(math.log2(n_dp // HIGH))
    weights = ((w_qkv, o_qkv), (w_up, o_up), (w_down, o_down), (w_out, o_out))
    greet_all(n_dp, me, here.other)

    def early(which, buf, phase):
        if phase < high_bits:
            span = 1 << phase
            block = buf.at[pl.ds(lax.div(here.high, span) * span, span), here.near, here.side, here.core]
            target = flip(me, HIGH << phase)
        elif phase == high_bits:
            block, target = buf.at[:, here.near, here.side, here.core], flip(me, NEAR)
        elif phase == high_bits + 1:
            block, target = buf.at[:, :, here.side, here.core], flip(me, SIDE)
        else:
            block, target = buf.at[:, :, :, here.core], flip(me, CORE)
        return remote(block, block, early_s.at[which, phase], early_r.at[which, phase], dp=target)

    own = [
        pltpu.make_async_copy(mix, mix_all.at[here.high, here.near, here.side, here.core], own_sem.at[0]),
        pltpu.make_async_copy(small, small_all.at[here.high, here.near, here.side, here.core], own_sem.at[1]),
    ]
    for copy in own:
        copy.start()
    for copy in own:
        copy.wait()
    early_pairs = ((0, mix_all), (1, small_all))
    early(0, mix_all, 0).start()
    early(1, small_all, 0).start()

    def cut(ref, quarter):
        width = ref.shape[-1] // QUARTERS
        columns = at(quarter * width, width)
        return ref.at[:, :, columns] if len(ref.shape) == 3 else ref.at[:, columns]

    def slot(ref):
        index = (here.high, here.near, here.side, pl.ds(pl.multiple_of(here.core * rows, rows), rows))
        return ref.at[(slice(None),) + index] if len(ref.shape) == 6 else ref.at[index]

    def keep(array):
        w, o = weights[array]
        return pltpu.make_async_copy(cut(w, here.quarter), slot(o), own_sem.at[2 + array])

    def reshard(array, peer):
        w, o = weights[array]
        target, quarter = here.peers[peer]
        return remote(cut(w, quarter), slot(o), reshard_s.at[array, peer], reshard_r.at[array, peer], dp=target)

    def high_hop(array, phase):
        o = weights[array][1]
        span = 1 << phase
        index = (pl.ds(lax.div(here.high, span) * span, span), slice(None), here.side)
        block = o.at[(slice(None),) + index] if len(o.shape) == 6 else o.at[index]
        return remote(block, block, high_s.at[array, phase], high_r.at[array, phase], dp=flip(me, HIGH << phase))

    def side_hop(array):
        o = weights[array][1]
        block = o.at[:, :, :, here.side] if len(o.shape) == 6 else o.at[:, :, here.side]
        return remote(block, block, side_s.at[array], side_r.at[array], dp=flip(me, SIDE))

    for phase in range(1, high_bits + 3):
        for which, buf in early_pairs:
            early(which, buf, phase - 1).wait()
            early(which, buf, phase).start()
        if phase == 1:
            for array in range(len(weights)):
                keep(array).start()
                for peer in range(3):
                    reshard(array, peer).start()
    early(0, mix_all, high_bits + 2).wait()

    def fetch(step, buf):
        target = lax.rem(me + step, n_dp)
        return pltpu.make_async_copy(
            hist.at[:, :, at(target * 2 * half + tensor * half, half)], hist_in.at[buf], hist_sem.at[buf]
        )

    def send(step):
        target = lax.rem(me + step, n_dp)
        return remote(
            mixed.at[step], streams.at[:, at(me * rows, rows), :], a2a_s.at[step], a2a_r.at[step], dp=target
        )

    fetch(0, 0).start()

    def mix_step(step):
        buf = lax.rem(step, 2)

        @pl.when(step + 1 < n_dp)
        def _():
            fetch(step + 1, 1 - buf).start()

        fetch(step, buf).wait()
        target = lax.rem(me + step, n_dp)
        weight = mix_all[lax.div(target, HIGH), bit(target, NEAR), bit(target, SIDE), bit(target, CORE)]
        for row in range(0, rows, 32):
            part = pl.ds(row, 32)
            sources = [hist_in[buf, source, part, :].astype(F32) for source in range(HIST)]
            for stream in range(STREAMS):
                total = sum(
                    sources[source] * weight[stream * HIST + source][None, :] for source in range(HIST)
                )
                mixed[step, stream, part, :] = total.astype(BF16)

        @pl.when(step > 0)
        def _():
            send(step).start()

    loop(0, n_dp, mix_step)
    streams[:, at(me * rows, rows), :] = mixed[0]
    for array in range(len(weights)):
        keep(array).wait()
        for peer in range(3):
            reshard(array, peer).wait()
        for phase in range(high_bits):
            if phase == 0:
                high_hop(array, 0).start()
    early(1, small_all, high_bits + 2).wait()
    loop(1, n_dp, lambda step: send(step).wait())

    chunk = min(256, depth)

    def lanes(near, core, half_at, count):
        return at(near * 4 * half + core * 2 * half + half_at * half, count * half, half)

    def act_keep(stream):
        return pltpu.make_async_copy(
            act.at[stream], o_act.at[stream, :, lanes(here.near, here.core, tensor, 1)], act_local.at[stream]
        )

    def act_near(stream):
        return remote(
            act.at[stream], o_act.at[stream, :, lanes(here.near, here.core, tensor, 1)],
            act_s.at[0, stream], act_r.at[0, stream], dp=flip(me, NEAR),
        )

    def act_tensor(stream, second):
        span = lanes(1 - here.near if second else here.near, here.core, tensor, 1)
        return remote(
            o_act.at[stream, :, span] if second else act.at[stream], o_act.at[stream, :, span],
            act_s.at[1 + second, stream], act_r.at[1 + second, stream], tensor=here.other,
        )

    def act_core(stream, near):
        span = lanes(near, here.core, 0, 2)
        return remote(
            o_act.at[stream, :, span], o_act.at[stream, :, span],
            act_s.at[3 + near, stream], act_r.at[3 + near, stream], dp=flip(me, CORE),
        )

    for stream in range(STREAMS):
        block = 0 if stream < 3 else 1

        def piece(index):
            return streams[stream, at(index * chunk, chunk), :].astype(F32)

        centre = sum_rows(piece, depth, chunk, lambda v: v) / depth
        spread = sum_rows(piece, depth, chunk, lambda v: (v - centre) * (v - centre)) / depth
        root = lax.rsqrt(spread + NORM_EPS)

        def normalise(index):
            span = chunk // rows
            first = index * span
            column = jnp.concatenate(
                [
                    small_all[
                        lax.div(first + k, HIGH), bit(first + k, NEAR), bit(first + k, SIDE), bit(first + k, CORE)
                    ]
                    for k in range(span)
                ],
                axis=0,
            ).astype(F32)
            gain = column[:, MIXH + block : MIXH + block + 1]
            bias = column[:, MIXH + 2 + block : MIXH + 3 + block]
            act[stream, at(index * chunk, chunk), :] = (
                (piece(index) - centre) * root * gain + bias
            ).astype(BF16)

        loop(0, depth // chunk, normalise)
        act_near(stream).start()
        act_tensor(stream, 0).start()
        act_keep(stream).start()

    finals = [
        pltpu.make_async_copy(mix_all, o_mix, out_sem.at[0]),
        pltpu.make_async_copy(small_all, o_small, out_sem.at[1]),
        pltpu.make_async_copy(streams, o_streams, out_sem.at[2]),
    ]
    for copy in finals:
        copy.start()
    for array in range(len(weights)):
        for phase in range(high_bits):
            high_hop(array, phase).wait()
            if phase + 1 < high_bits:
                high_hop(array, phase + 1).start()
        side_hop(array).start()
    for stream in range(STREAMS):
        act_near(stream).wait()
        act_tensor(stream, 1).start()
    for stream in range(STREAMS):
        act_keep(stream).wait()
        act_tensor(stream, 0).wait()
        act_tensor(stream, 1).wait()
        for near in range(2):
            act_core(stream, near).start()
    for array in range(len(weights)):
        side_hop(array).wait()
    for stream in range(STREAMS):
        for near in range(2):
            act_core(stream, near).wait()
    for copy in finals:
        copy.wait()


def gather(n_dp, hist, mix, small, w_qkv, w_up, w_down, w_out):
    rows = small.shape[0]
    depth = rows * n_dp
    half = hist.shape[2] // n_dp // 2
    high = n_dp // HIGH
    high_bits = int(math.log2(high))
    grid = (high, 2, 2, 2)

    def cut(width):
        return (high, 2, 2, 2 * rows, width // QUARTERS)

    shapes = [
        (grid + mix.shape, F32),
        (grid + (rows, 128), BF16),
        ((STREAMS, depth, half), BF16),
        ((STREAMS, depth, 8 * half), BF16),
        ((3,) + cut(w_qkv.shape[2]), BF16),
        (cut(w_up.shape[1]), BF16),
        (cut(w_down.shape[1]), BF16),
        (cut(w_out.shape[1]), BF16),
    ]
    return pl.pallas_call(
        functools.partial(gather_kernel, n_dp),
        out_shape=[jax.ShapeDtypeStruct(*shape) for shape in shapes],
        in_specs=[ANY] * 7,
        out_specs=[ANY] * 8,
        scratch_shapes=[
            pltpu.VMEM(grid + mix.shape, F32),
            pltpu.VMEM(grid + (rows, 128), BF16),
            pltpu.VMEM((2, HIST, rows, half), BF16),
            pltpu.VMEM((n_dp, STREAMS, rows, half), BF16),
            pltpu.VMEM((STREAMS, depth, half), BF16),
            pltpu.VMEM((STREAMS, depth, half), BF16),
            DMA((2, high_bits + 3)),
            DMA((2, high_bits + 3)),
            DMA((2,)),
            DMA((n_dp,)),
            DMA((n_dp,)),
            DMA((4, 3)),
            DMA((4, 3)),
            DMA((4, high_bits)),
            DMA((4, high_bits)),
            DMA((4,)),
            DMA((4,)),
            DMA((5, STREAMS)),
            DMA((5, STREAMS)),
            DMA((STREAMS,)),
            DMA((6,)),
            DMA((3,)),
        ],
        compiler_params=pltpu.CompilerParams(
            collective_id=1, has_side_effects=True, vmem_limit_bytes=40 * 1024 * 1024
        ),
        name="gather",
    )(hist, mix, small, w_qkv, w_up, w_down, w_out)


def lane_block(half, near, core, half_at, count):
    return at(near * 4 * half + core * 2 * half + half_at * half, count * half, half)


def gelu_parts(values):
    phi = 0.5 * (1.0 + lax.erf(values * (1.0 / math.sqrt(2.0))))
    density = jnp.exp(-0.5 * values * values) * (1.0 / math.sqrt(2.0 * math.pi))
    return values * phi, phi + values * density


def reduce_group(here, half, part, theirs, own, from_core, from_tensor, from_near, sems, local, pieces, piece):
    core_s, core_r, tensor_s, tensor_r, near_s, near_r = sems

    def load(span, near, half_at):
        return pltpu.make_async_copy(
            part.at[piece(span), lane_block(half, near, here.core, half_at, 1)],
            own.at[near, half_at, piece(span)], local.at[span, near * 2 + half_at],
        )

    def to_core(span, near, half_at):
        return remote(
            part.at[piece(span), lane_block(half, near, 1 - here.core, half_at, 1)],
            from_core.at[near, half_at, piece(span)],
            core_s.at[span, near * 2 + half_at], core_r.at[span, near * 2 + half_at], dp=flip(here.me, CORE),
        )

    def to_tensor(span, near):
        return remote(
            own.at[near, here.other, piece(span)], from_tensor.at[near, piece(span)],
            tensor_s.at[span, near], tensor_r.at[span, near], tensor=here.other,
        )

    def to_near(span):
        return remote(
            from_tensor.at[1 - here.near, piece(span)], from_near.at[piece(span)],
            near_s.at[span], near_r.at[span], dp=flip(here.me, NEAR),
        )

    def start(span):
        for near in range(2):
            for half_at in range(2):
                to_core(span, near, half_at).start()
                load(span, near, half_at).start()

    def after_core(span):
        for near in range(2):
            for half_at in range(2):
                load(span, near, half_at).wait()
                to_core(span, near, half_at).wait()
            own[near, here.other, piece(span)] += from_core[near, here.other, piece(span)]
            to_tensor(span, near).start()
        for near in range(2):
            own[near, here.tensor, piece(span)] += from_core[near, here.tensor, piece(span)]

    def after_tensor(span):
        for near in range(2):
            to_tensor(span, near).wait()
        far = 1 - here.near
        from_tensor[far, piece(span)] += own[far, here.tensor, piece(span)]
        to_near(span).start()
        from_tensor[here.near, piece(span)] += own[here.near, here.tensor, piece(span)]

    def after_near(span):
        to_near(span).wait()

    return start, after_core, after_tensor, after_near


def join_kernel(
    part, streams, cot, small, mix_in, mix_out, mix_back, static, next_cot,
    o_grad, o_wide, o_block, o_next, o_mixin, o_tiny,
    own, from_core, from_tensor, from_near, residual, wide, normed, block, back, low, next_rows, mixin, tiny,
    core_s, core_r, tensor_s, tensor_r, near_s, near_r, local, share_s, share_r, own_sem,
):
    here = Place()
    me, tensor = here.me, here.tensor
    depth, half = cot.shape
    spans = core_s.shape[0]
    size = depth // spans
    chunk = 256
    greet([{"dp": flip(me, CORE)}, {"dp": flip(me, NEAR)}, {"tensor": here.other}])

    def piece(span):
        return pl.ds(span * size, size)

    start, after_core, after_tensor, after_near = reduce_group(
        here, half, part, None, own, from_core, from_tensor, from_near,
        (core_s, core_r, tensor_s, tensor_r, near_s, near_r), local, spans, piece,
    )
    fetch = pltpu.make_async_copy(streams.at[3], residual, own_sem.at[0])
    fetch.start()
    for span in range(spans):
        start(span)
    for span in range(spans):
        after_core(span)
    for span in range(spans):
        after_tensor(span)
    fetch.wait()
    squares = jnp.zeros((1, half), F32)
    for span in range(spans):
        after_near(span)

        def widen(index, total):
            rows = at(span * size + index * chunk, chunk)
            branch = from_tensor[here.near, rows, :].astype(F32) + from_near[rows, :].astype(F32)
            value = residual[rows, :].astype(F32) + branch
            wide[rows, :] = value
            block[rows, :] = value.astype(BF16)
            return total + jnp.sum(value * value, axis=0, keepdims=True)

        squares = lax.fori_loop(0, size // chunk, widen, squares)
    root = lax.rsqrt(squares / depth + ROOT_EPS)

    def share_block(which):
        lanes = at(tensor * half, half)
        if which == 0:
            return pltpu.make_async_copy(block, o_block.at[:, lanes], own_sem.at[1])
        return remote(block, o_block.at[:, lanes], share_s.at[0], share_r.at[0], tensor=here.other)

    share_block(0).start()
    share_block(1).start()

    def norm(index):
        rows = at(index * chunk, chunk)
        normed[rows, :] = (wide[rows, :] * root).astype(BF16)

    loop(0, depth // chunk, norm)
    inner, slope = gelu_parts(jnp.dot(mix_in[...], normed[...], preferred_element_type=F32))
    inner_low = inner.astype(BF16)
    next_rows[...] = (jnp.dot(mix_out[...], inner_low, preferred_element_type=F32) + static[...])[:MIXH]
    next_low = next_cot[...].astype(BF16)

    def nt(left, right):
        return lax.dot_general(left, right, (((1,), (1,)), ((), ())), preferred_element_type=F32)

    tiny[:, :128] = nt(inner_low, next_low)
    tiny[:, 128:] = jnp.broadcast_to(jnp.sum(next_cot[...], axis=1, keepdims=True), (128, 128))
    inner_grad = (jnp.dot(mix_back[...], next_low, preferred_element_type=F32) * slope).astype(BF16)

    def pull(index, total):
        rows = at(index * chunk, chunk)
        value = jnp.dot(small[rows, :], inner_grad, preferred_element_type=F32)
        back[rows, :] = value
        return total + jnp.sum(value * wide[rows, :] * root, axis=0, keepdims=True)

    along = lax.fori_loop(0, depth // chunk, pull, jnp.zeros((1, half), F32)) / depth

    def finish(index):
        rows = at(index * chunk, chunk)
        value = cot[rows, :].astype(F32) + root * (back[rows, :] - wide[rows, :] * root * along)
        back[rows, :] = value
        low[rows, :] = value.astype(BF16)

    loop(0, depth // chunk, finish)

    def share(kind, index):
        if kind == 0:
            source, lanes, where = low, lane_block(half, here.near, here.core, tensor, 1), {"dp": flip(me, NEAR)}
        elif kind == 1:
            lanes = lane_block(half, 1 - here.near if index else here.near, here.core, tensor, 1)
            source, where = (o_grad.at[:, lanes] if index else low), {"tensor": here.other}
        else:
            lanes, where = lane_block(half, index, here.core, 0, 2), {"dp": flip(me, CORE)}
            source = o_grad.at[:, lanes]
        number = 1 + 2 * kind + index
        return remote(source, o_grad.at[:, lanes], share_s.at[number], share_r.at[number], **where)

    share(0, 0).start()
    share(1, 0).start()
    keep = pltpu.make_async_copy(
        low, o_grad.at[:, lane_block(half, here.near, here.core, tensor, 1)], own_sem.at[2]
    )
    keep.start()

    def mixin_rows(index):
        rows = at(index * chunk, chunk)
        mixin[rows, :] = nt(normed[rows, :], inner_grad)

    loop(0, depth // chunk, mixin_rows)
    share(0, 0).wait()
    share(1, 1).start()
    lanes = at(tensor * half, half)
    next_share = remote(next_rows, o_next.at[:, lanes], share_s.at[7], share_r.at[7], tensor=here.other)
    next_share.start()
    finals = [
        pltpu.make_async_copy(next_rows, o_next.at[:, lanes], own_sem.at[3]),
        pltpu.make_async_copy(back, o_wide, own_sem.at[4]),
        pltpu.make_async_copy(mixin, o_mixin, own_sem.at[5]),
        pltpu.make_async_copy(tiny, o_tiny, own_sem.at[6]),
    ]
    for copy in finals:
        copy.start()
    keep.wait()
    share(1, 0).wait()
    share(1, 1).wait()
    for near in range(2):
        share(2, near).start()
    for near in range(2):
        share(2, near).wait()
    share_block(0).wait()
    share_block(1).wait()
    next_share.wait()
    for copy in finals:
        copy.wait()


def join(part, streams, cot, small, mix_in, mix_out, mix_back, static, next_cot):
    depth, half = cot.shape
    spans = 4
    shapes = [
        ((depth, 8 * half), BF16),
        ((depth, half), F32),
        ((depth, 2 * half), BF16),
        ((MIXH, 2 * half), F32),
        ((depth, 128), F32),
        ((128, 256), F32),
    ]
    return pl.pallas_call(
        join_kernel,
        out_shape=[jax.ShapeDtypeStruct(*shape) for shape in shapes],
        in_specs=[ANY, ANY] + [VM] * 7,
        out_specs=[ANY] * 6,
        scratch_shapes=[
            pltpu.VMEM((2, 2, depth, half), BF16),
            pltpu.VMEM((2, 2, depth, half), BF16),
            pltpu.VMEM((2, depth, half), BF16),
            pltpu.VMEM((depth, half), BF16),
            pltpu.VMEM((depth, half), BF16),
            pltpu.VMEM((depth, half), F32),
            pltpu.VMEM((depth, half), BF16),
            pltpu.VMEM((depth, half), BF16),
            pltpu.VMEM((depth, half), F32),
            pltpu.VMEM((depth, half), BF16),
            pltpu.VMEM((MIXH, half), F32),
            pltpu.VMEM((depth, 128), F32),
            pltpu.VMEM((128, 256), F32),
            DMA((spans, 4)),
            DMA((spans, 4)),
            DMA((spans, 2)),
            DMA((spans, 2)),
            DMA((spans,)),
            DMA((spans,)),
            DMA((spans, 4)),
            DMA((8,)),
            DMA((8,)),
            DMA((7,)),
        ],
        compiler_params=pltpu.CompilerParams(
            collective_id=2, has_side_effects=True, vmem_limit_bytes=40 * 1024 * 1024
        ),
        name="join",
    )(part, streams, cot, small, mix_in, mix_out, mix_back, static, next_cot)


def scatter_kernel(
    n_dp, attn_grad, mlp_grad, streams, small, wide_grad, mixin_part, hist, g_qkv, g_up, g_down, g_out,
    o_stream, o_mix, o_small, o_qkv, o_up, o_down, o_out,
    own, from_core, from_tensor, from_near, rows_in, wide, stream_grad, gains, biases, tiny, tiny_in, tiny_out,
    hist_in, arrived, mix_part, mix_in, mix_sum, tiny_sum,
    side_qkv, side_up, side_down, side_out, mine_qkv, mine_up, mine_down, mine_out,
    high_qkv, high_up, high_down, high_out,
    core_s, core_r, tensor_s, tensor_r, near_s, near_r, local, in_sem,
    side_s, side_r, side_local, high_s, high_r, peer_s, peer_r, peer_local,
    a2a_s, a2a_r, keep_sem, pass_s, pass_r, tiny_s, tiny_r, mix_s, mix_r, hist_sem, last_s, last_r, last_local,
):
    here = Place()
    me, tensor = here.me, here.tensor
    depth, half = wide_grad.shape
    rows = depth // n_dp
    high_bits = int(math.log2(n_dp // HIGH))
    chunk = min(256, depth)
    greet_all(n_dp, me, here.other)
    weights = (
        (g_qkv, side_qkv, mine_qkv, high_qkv, o_qkv),
        (g_up, side_up, mine_up, high_up, o_up),
        (g_down, side_down, mine_down, high_down, o_down),
        (g_out, side_out, mine_out, high_out, o_out),
    )

    def pick(ref, *index):
        return ref.at[(slice(None),) + index] if ref.shape[0] == 3 and len(ref.shape) > len(index) + 2 else ref.at[index]

    def everything(_):
        return pl.ds(0, depth)

    steps = []
    for stream in range(STREAMS):
        part = attn_grad.at[stream] if stream < 3 else mlp_grad
        steps.append(
            reduce_group(
                here, half, part, None, own.at[stream], from_core.at[stream], from_tensor.at[stream],
                from_near.at[stream],
                tuple(
                    sem.at[pl.ds(stream, 1)]
                    for sem in (core_s, core_r, tensor_s, tensor_r, near_s, near_r)
                ),
                local.at[pl.ds(stream, 1)], 1, everything,
            )
        )
    for stream in range(STREAMS):
        steps[stream][0](0)
    loads = [
        pltpu.make_async_copy(streams, rows_in, in_sem.at[0]),
        pltpu.make_async_copy(wide_grad, wide, in_sem.at[1]),
    ]
    for copy in loads:
        copy.start()

    def is_qkv(array):
        return array == 0

    def index_of(array, *index):
        return ((slice(None),) if is_qkv(array) else ()) + index

    def side_hop(array):
        g, side, _, _, _ = weights[array]
        return remote(
            g.at[index_of(array, slice(None), slice(None), 1 - here.side)], side, side_s.at[array], side_r.at[array],
            dp=flip(me, SIDE),
        )

    def side_load(array):
        g, _, mine, _, _ = weights[array]
        return pltpu.make_async_copy(
            g.at[index_of(array, slice(None), slice(None), here.side)], mine, side_local.at[array]
        )

    def high_hop(array, phase):
        _, _, mine, high, _ = weights[array]
        span = 1 << phase
        base = lax.div(here.high, span)
        theirs = base + 1 - 2 * lax.rem(base, 2)
        return remote(
            mine.at[index_of(array, pl.ds(theirs * span, span))], high.at[index_of(array, pl.ds(span - 1, span))],
            high_s.at[array, phase], high_r.at[array, phase], dp=flip(me, HIGH << phase),
        )

    def add_blocks(array, into, other, first_into, first_other, count):
        shape = into.shape
        tall, width = shape[-2:]
        outer = 3 if is_qkv(array) else 1
        step = 32

        def add(flat):
            lead = lax.div(flat, count * 2)
            rest = lax.rem(flat, count * 2)
            high, near = lax.div(rest, 2), lax.rem(rest, 2)
            prefix = (lead,) if is_qkv(array) else ()

            def tile(index):
                span = at(index * step, step)
                into[prefix + (first_into + high, near, span)] += other[prefix + (first_other + high, near, span)]

            loop(0, tall // step, tile)

        loop(0, outer * count * 2, add)

    for array in range(4):
        side_hop(array).start()
        side_load(array).start()
    for copy in loads:
        copy.wait()
    stats = []
    for stream in range(STREAMS):

        def piece(index):
            return rows_in[stream, at(index * chunk, chunk), :].astype(F32)

        centre = sum_rows(piece, depth, chunk, lambda v: v) / depth
        spread = sum_rows(piece, depth, chunk, lambda v: (v - centre) * (v - centre)) / depth
        stats.append((centre, lax.rsqrt(spread + NORM_EPS)))
    for stream in range(STREAMS):
        steps[stream][1](0)
    for array in range(4):
        side_load(array).wait()
        side_hop(array).wait()
        _, side, mine, _, _ = weights[array]
        add_blocks(array, mine, side, 0, 0, n_dp // HIGH)
        high_hop(array, high_bits - 1).start()
    for stream in range(STREAMS):
        steps[stream][2](0)

    for stream in range(STREAMS):
        steps[stream][3](0)
        group = 0 if stream < 3 else 1
        centre, root = stats[stream]

        def parts(index):
            span = at(index * chunk, chunk)
            grad = from_tensor[stream, here.near, span].astype(F32) + from_near[stream, span].astype(F32)
            hat = (rows_in[stream, span, :].astype(F32) - centre) * root
            gain = small[span, MIXH + group : MIXH + group + 1].astype(F32)
            return span, grad, hat, grad * gain

        def sums(index, carry):
            span, grad, hat, scaled = parts(index)
            if stream in (0, 3):
                gains[group, span] = grad * hat
                biases[group, span] = grad
            else:
                gains[group, span] += grad * hat
                biases[group, span] += grad
            return (
                carry[0] + jnp.sum(scaled, axis=0, keepdims=True),
                carry[1] + jnp.sum(scaled * hat, axis=0, keepdims=True),
            )

        zero = jnp.zeros((1, half), F32)
        total, along = lax.fori_loop(0, depth // chunk, sums, (zero, zero))

        def finish(index):
            span, grad, hat, scaled = parts(index)
            value = root * (scaled - total / depth - hat * (along / depth))
            if stream == 3:
                value = value + wide[span, :]
            stream_grad[stream, span] = value.astype(BF16)

        loop(0, depth // chunk, finish)

    def send(step):
        target = lax.rem(me + step, n_dp)
        return remote(
            stream_grad.at[:, at(target * rows, rows), :], arrived.at[step], a2a_s.at[step], a2a_r.at[step], dp=target
        )

    loop(1, n_dp, lambda step: send(step).start())

    def fetch(step, buf):
        source = lax.rem(me - step + n_dp, n_dp)
        return pltpu.make_async_copy(
            hist.at[:, :, at(source * 2 * half + tensor * half, half)], hist_in.at[buf], hist_sem.at[buf]
        )

    fetch(0, 0).start()
    own_block = pltpu.make_async_copy(stream_grad.at[:, at(me * rows, rows), :], arrived.at[0], last_local.at[0])
    own_block.start()

    column = lax.broadcasted_iota(jnp.int32, (chunk, 128), 1)

    def gather_tiny(index):
        span = at(index * chunk, chunk)
        value = mixin_part[span, :]
        for group in range(2):
            gain = jnp.sum(gains[group, span], axis=1, keepdims=True)
            bias = jnp.sum(biases[group, span], axis=1, keepdims=True)
            value = jnp.where(column == MIXH + group, gain, value)
            value = jnp.where(column == MIXH + 2 + group, bias, value)
        tiny[span, :] = value.astype(BF16)

    loop(0, depth // chunk, gather_tiny)

    def tiny_send(step):
        target = lax.rem(me + step, n_dp)
        return remote(tiny.at[at(target * rows, rows), :], tiny_in.at[step], tiny_s.at[step], tiny_r.at[step], dp=target)

    loop(1, n_dp, lambda step: tiny_send(step).start())

    for array in range(4):
        _, _, mine, high, _ = weights[array]
        for phase in reversed(range(high_bits)):
            high_hop(array, phase).wait()
            span = 1 << phase
            add_blocks(array, mine, high, lax.div(here.high, span) * span, span - 1, span)
            if phase:
                high_hop(array, phase - 1).start()

    def peer_hop(array, peer):
        _, _, mine, _, out = weights[array]
        width = mine.shape[-1]
        target, _ = here.peers[peer]
        core = bit(target, CORE)
        return remote(
            mine.at[index_of(array, here.high, bit(target, NEAR), at(core * rows, rows))],
            out.at[index_of(array, slice(None), at(here.quarter * width, width))],
            peer_s.at[array, peer], peer_r.at[array, peer], dp=target,
        )

    def peer_keep(array):
        _, _, mine, _, out = weights[array]
        width = mine.shape[-1]
        return pltpu.make_async_copy(
            mine.at[index_of(array, here.high, here.near, at(here.core * rows, rows))],
            out.at[index_of(array, slice(None), at(here.quarter * width, width))], peer_local.at[array],
        )

    for array in range(4):
        peer_keep(array).start()
        for peer in range(3):
            peer_hop(array, peer).start()
    own_block.wait()

    def keep_lanes(step):
        source = lax.rem(me - step + n_dp, n_dp)
        return at(source * 2 * half + tensor * half, half)

    def keep(step):
        return pltpu.make_async_copy(arrived.at[step], o_stream.at[:, :, keep_lanes(step)], keep_sem.at[step])

    def pass_on(step):
        return remote(
            arrived.at[step], o_stream.at[:, :, keep_lanes(step)], pass_s.at[step], pass_r.at[step], tensor=here.other
        )

    def mix_send(step):
        return remote(
            mix_part.at[step], mix_in.at[step], mix_s.at[step], mix_r.at[step], dp=lax.rem(me - step + n_dp, n_dp)
        )

    def receive(step):
        buf = lax.rem(step, 2)

        @pl.when(step + 1 < n_dp)
        def _():
            fetch(step + 1, 1 - buf).start()

        @pl.when(step > 0)
        def _():
            send(step).wait()

        keep(step).start()
        pass_on(step).start()
        fetch(step, buf).wait()
        for stream in range(STREAMS):
            totals = [jnp.zeros((8, half), F32) for _ in range(HIST)]
            for row in range(0, rows, 16):
                span = pl.ds(row, 16)
                grad = arrived[step, stream, span, :].astype(F32)
                for source in range(HIST):
                    product = grad * hist_in[buf, source, span, :].astype(F32)
                    totals[source] = totals[source] + product[:8] + product[8:]
            for source in range(HIST):
                mix_part[step, pl.ds(stream * HIST + source, 1), :] = jnp.sum(totals[source], axis=0, keepdims=True)

        @pl.when(step > 0)
        def _():
            mix_send(step).start()

    mix_part[0] = jnp.zeros_like(mix_part[0])
    loop(0, n_dp, receive)

    mix_sum[...] = mix_part[0]

    def add_mix(step):
        mix_send(step).wait()
        mix_sum[...] += mix_in[step]

    loop(1, n_dp, add_mix)
    lanes = at(tensor * half, half)
    mix_share = remote(mix_sum, o_mix.at[:, lanes], last_s.at[0], last_r.at[0], tensor=here.other)
    mix_keep = pltpu.make_async_copy(mix_sum, o_mix.at[:, lanes], last_local.at[1])
    mix_share.start()
    mix_keep.start()
    tiny_sum[0] = tiny[at(me * rows, rows), :].astype(F32)

    def add_tiny(step):
        tiny_send(step).wait()
        tiny_sum[0] += tiny_in[step].astype(F32)

    loop(1, n_dp, add_tiny)
    tiny_share = remote(tiny_sum.at[0], tiny_sum.at[1], last_s.at[1], last_r.at[1], tensor=here.other)
    tiny_share.start()
    tiny_share.wait()
    tiny_out[...] = tiny_sum[0] + tiny_sum[1]
    tiny_keep = pltpu.make_async_copy(tiny_out, o_small, last_local.at[2])
    tiny_keep.start()
    for array in range(4):
        peer_keep(array).wait()
        for peer in range(3):
            peer_hop(array, peer).wait()

    def settle(step):
        keep(step).wait()
        pass_on(step).wait()

    loop(0, n_dp, settle)
    mix_share.wait()
    mix_keep.wait()
    tiny_keep.wait()


def scatter(n_dp, attn_grad, mlp_grad, streams, small, wide_grad, mixin_part, hist, g_qkv, g_up, g_down, g_out):
    depth, half = wide_grad.shape
    rows = depth // n_dp
    high = n_dp // HIGH
    high_bits = int(math.log2(high))
    grads = (g_qkv, g_up, g_down, g_out)

    def lead(g):
        return (3,) if g.ndim == 6 else ()

    def halved(g, highs):
        return lead(g) + (highs, 2) + g.shape[-2:]

    outs = [
        ((STREAMS, rows, 2 * half * n_dp), BF16),
        ((MIXH, 2 * half), F32),
        ((rows, 128), F32),
    ] + [(lead(g) + (rows, QUARTERS * g.shape[-1]), BF16) for g in grads]
    return pl.pallas_call(
        functools.partial(scatter_kernel, n_dp),
        out_shape=[jax.ShapeDtypeStruct(*shape) for shape in outs],
        in_specs=[ANY, ANY, ANY, VM, ANY, VM, ANY] + [ANY] * 4,
        out_specs=[ANY] * 7,
        scratch_shapes=[
            pltpu.VMEM((STREAMS, 2, 2, depth, half), BF16),
            pltpu.VMEM((STREAMS, 2, 2, depth, half), BF16),
            pltpu.VMEM((STREAMS, 2, depth, half), BF16),
            pltpu.VMEM((STREAMS, depth, half), BF16),
            pltpu.VMEM((STREAMS, depth, half), BF16),
            pltpu.VMEM((depth, half), F32),
            pltpu.VMEM((STREAMS, depth, half), BF16),
            pltpu.VMEM((2, depth, half), F32),
            pltpu.VMEM((2, depth, half), F32),
            pltpu.VMEM((depth, 128), BF16),
            pltpu.VMEM((n_dp, rows, 128), BF16),
            pltpu.VMEM((rows, 128), F32),
            pltpu.VMEM((2, HIST, rows, half), BF16),
            pltpu.VMEM((n_dp, STREAMS, rows, half), BF16),
            pltpu.VMEM((n_dp, MIXH, half), F32),
            pltpu.VMEM((n_dp, MIXH, half), F32),
            pltpu.VMEM((MIXH, half), F32),
            pltpu.VMEM((2, rows, 128), F32),
        ]
        + [pltpu.VMEM(halved(g, high), BF16) for g in grads]
        + [pltpu.VMEM(halved(g, high), BF16) for g in grads]
        + [pltpu.VMEM(halved(g, high - 1), BF16) for g in grads]
        + [
            DMA((STREAMS, 4)),
            DMA((STREAMS, 4)),
            DMA((STREAMS, 2)),
            DMA((STREAMS, 2)),
            DMA((STREAMS,)),
            DMA((STREAMS,)),
            DMA((STREAMS, 4)),
            DMA((2,)),
            DMA((4,)),
            DMA((4,)),
            DMA((4,)),
            DMA((4, high_bits)),
            DMA((4, high_bits)),
            DMA((4, 3)),
            DMA((4, 3)),
            DMA((4,)),
            DMA((n_dp,)),
            DMA((n_dp,)),
            DMA((n_dp,)),
            DMA((n_dp,)),
            DMA((n_dp,)),
            DMA((n_dp,)),
            DMA((n_dp,)),
            DMA((n_dp,)),
            DMA((n_dp,)),
            DMA((2,)),
            DMA((2,)),
            DMA((2,)),
            DMA((3,)),
        ],
        compiler_params=pltpu.CompilerParams(
            collective_id=3, has_side_effects=True, vmem_limit_bytes=60 * 1024 * 1024
        ),
        name="scatter",
    )(attn_grad, mlp_grad, streams, small, wide_grad, mixin_part, hist, *grads)


def exact_gelu(values):
    return jax.nn.gelu(values, approximate=False)


def rotary_tables(length, rotary, float_type):
    half_rot = rotary // 2
    places = jnp.arange(length).astype(float_type)
    frequency = jnp.exp(
        jnp.arange(half_rot).astype(float_type) * (-2.0 * math.log(10000.0) / rotary)
    )
    angles = places[:, None] * frequency[None, :]
    return (jnp.cos(angles), jnp.sin(angles))


def rotate(values, cos_table, sin_table):
    half_rot = cos_table.shape[-1]
    first_half = values[..., :half_rot]
    second = values[..., half_rot : 2 * half_rot]
    return jnp.concatenate(
        [
            first_half * cos_table - second * sin_table,
            second * cos_table + first_half * sin_table,
            values[..., 2 * half_rot :],
        ],
        axis=-1,
    )


def masked_scores(queries, key_rows):
    length = queries.shape[1]
    score_scale = 1.0 / math.sqrt(queries.shape[2])
    causal = lax.broadcasted_iota(jnp.int32, (length, length), 0) >= lax.broadcasted_iota(
        jnp.int32, (length, length), 1
    )
    scores = (
        jnp.einsum("hqd,hkd->hqk", queries, key_rows, preferred_element_type=jnp.float32)
        * score_scale
    )
    return (jnp.where(causal[None], scores, MASKED), score_scale)


def attend_forward(queries, key_rows, value_rows):
    scores, score_scale = masked_scores(queries, key_rows)
    row_peak = jnp.max(scores, axis=-1, keepdims=True)
    raised = jnp.exp(scores - row_peak)
    row_total = jnp.sum(raised, axis=-1, keepdims=True)
    prob_low = (raised / row_total).astype(jnp.bfloat16)
    context = jnp.einsum("hqk,hkd->hqd", prob_low, value_rows, preferred_element_type=jnp.float32)
    return (context.astype(jnp.bfloat16), row_peak + jnp.log(row_total))


def attend_backward(queries, key_rows, value_rows, log_sum, context_grad):
    scores, score_scale = masked_scores(queries, key_rows)
    attn_prob = jnp.exp(scores - log_sum)
    prob_low = attn_prob.astype(jnp.bfloat16)
    value_grad = jnp.einsum(
        "hqk,hqd->hkd", prob_low, context_grad, preferred_element_type=jnp.float32
    )
    prob_grad = jnp.einsum(
        "hqd,hkd->hqk", context_grad, value_rows, preferred_element_type=jnp.float32
    )
    inner_sum = jnp.sum(attn_prob * prob_grad, axis=-1, keepdims=True)
    score_grad = (attn_prob * (prob_grad - inner_sum)).astype(jnp.bfloat16)
    query_grad = (
        jnp.einsum("hqk,hkd->hqd", score_grad, key_rows, preferred_element_type=jnp.float32)
        * score_scale
    )
    key_grad = (
        jnp.einsum("hqk,hqd->hkd", score_grad, queries, preferred_element_type=jnp.float32)
        * score_scale
    )
    return (query_grad, key_grad, value_grad)


def per_device(
    n_dp, history, mix_weights, w_qkv, w_out, w_up, w_down, norm_gain, norm_bias, mix_in, mix_out, mix_static,
    out_cot, next_cot,
):
    tensor = lax.axis_index("tensor")
    seq_len = mix_weights.shape[0]
    half = seq_len // 2
    depth = mix_in.shape[0] * n_dp

    def own_half(rows):
        return lax.dynamic_slice_in_dim(rows, tensor * half, half, 0)

    mix_rows = jnp.pad(own_half(mix_weights.reshape(seq_len, -1)).T, ((0, MIXH - STREAMS * HIST), (0, 0)))
    small = jnp.concatenate([mix_in, norm_gain.T, norm_bias.T], axis=1)
    small = jnp.pad(small, ((0, 0), (0, 128 - small.shape[1])))
    mix_all, small_all, streams, act, qkv, up, down, out = gather(
        n_dp, history, mix_rows, small, w_qkv, w_up, w_down, w_out
    )
    small_all = small_all.reshape(depth, 128)
    qkv, up, down, out = (
        qkv.reshape(3, depth, -1), up.reshape(depth, -1), down.reshape(depth, -1), out.reshape(depth, -1)
    )
    tokens = act.shape[2]
    seqs = tokens // seq_len
    heads = qkv.shape[2] // HD
    projected = jnp.einsum("sdt,sde->ste", act[:3], qkv, preferred_element_type=F32)
    head_rows = jnp.transpose(projected.reshape(3, seqs, seq_len, heads, HD), (0, 1, 3, 2, 4)).reshape(
        3, seqs * heads, seq_len, HD
    )
    cos_table, sin_table = rotary_tables(seq_len, ROT, F32)
    queries = rotate(head_rows[0], cos_table, sin_table).astype(BF16)
    key_rows = rotate(head_rows[1], cos_table, sin_table).astype(BF16)
    value_rows = head_rows[2].astype(BF16)
    context, log_sum = attend_forward(queries, key_rows, value_rows)

    def join_heads(rows):
        return jnp.transpose(rows.reshape(seqs, heads, seq_len, HD), (0, 2, 1, 3)).reshape(tokens, heads * HD)

    context_rows = join_heads(context)
    up_pre = jnp.einsum("dt,df->tf", act[3], up, preferred_element_type=F32)
    hidden_wide, gelu_back = jax.vjp(exact_gelu, up_pre)
    hidden = hidden_wide.astype(BF16)
    part = (
        jnp.einsum("de,te->dt", out, context_rows, preferred_element_type=F32)
        + jnp.einsum("df,tf->dt", down, hidden, preferred_element_type=F32)
    ).astype(BF16)

    def square(values):
        return jnp.pad(values, ((0, 128 - values.shape[0]), (0, 128 - values.shape[1])))

    next_rows = own_half(next_cot.reshape(seq_len, -1)).T
    next_rows = jnp.pad(next_rows, ((0, 128 - next_rows.shape[0]), (0, 0)))
    mix_in_rows = jnp.pad(small_all[:, :MIXH].T, ((0, 128 - MIXH), (0, 0)))
    static = jnp.pad(mix_static[:, None], ((0, 128 - mix_static.shape[0]), (0, 0)))
    branch_grad, wide_grad, block, next_mix, mixin_part, tiny = join(
        part, streams, own_half(out_cot).T, small_all, mix_in_rows, square(mix_out.T), square(mix_out), static,
        next_rows,
    )
    mixout_total, static_total = lax.psum(
        (tiny[:MIXH, : STREAMS * NEXT], tiny[: STREAMS * NEXT, 128]), ("dp", "tensor")
    )
    hidden_grad = jnp.einsum("dt,df->tf", branch_grad, down, preferred_element_type=F32)
    up_grad_low = gelu_back(hidden_grad)[0].astype(BF16)
    mlp_in_grad = jnp.einsum("df,tf->dt", up, up_grad_low, preferred_element_type=F32).astype(BF16)
    context_grad_rows = jnp.einsum("dt,de->te", branch_grad, out, preferred_element_type=F32).astype(BF16)
    context_grad = jnp.transpose(context_grad_rows.reshape(seqs, seq_len, heads, HD), (0, 2, 1, 3)).reshape(
        seqs * heads, seq_len, HD
    )
    query_grad, key_grad, value_grad = attend_backward(queries, key_rows, value_rows, log_sum, context_grad)
    proj_grad = jnp.stack(
        [
            join_heads(rotate(query_grad, cos_table, -sin_table).astype(BF16)),
            join_heads(rotate(key_grad, cos_table, -sin_table).astype(BF16)),
            join_heads(value_grad.astype(BF16)),
        ]
    )
    attn_in_grad = jnp.einsum("sde,ste->sdt", qkv, proj_grad, preferred_element_type=F32).astype(BF16)
    g_qkv = jnp.einsum("sdt,ste->sde", act[:3], proj_grad, preferred_element_type=F32).astype(BF16)
    g_out = jnp.einsum("dt,te->de", branch_grad, context_rows, preferred_element_type=F32).astype(BF16)
    g_up = jnp.einsum("dt,tf->df", act[3], up_grad_low, preferred_element_type=F32).astype(BF16)
    g_down = jnp.einsum("dt,tf->df", branch_grad, hidden, preferred_element_type=F32).astype(BF16)
    grid = (n_dp // HIGH, 2, 2, 2 * mix_in.shape[0])
    stream_grad, mix_grad, small_total, qkv_total, up_total, down_total, out_total = scatter(
        n_dp, attn_in_grad, mlp_in_grad, streams, small_all, wide_grad, mixin_part, history,
        g_qkv.reshape((3,) + grid + (-1,)), g_up.reshape(grid + (-1,)), g_down.reshape(grid + (-1,)),
        g_out.reshape(grid + (-1,)),
    )
    mix_rows = mix_all.reshape(n_dp, MIXH, 1, half)
    mix_rows = lax.all_gather(mix_rows, "tensor", axis=2, tiled=True)
    mix_rows = jnp.transpose(mix_rows, (1, 0, 2, 3)).reshape(MIXH, n_dp * seq_len)
    history_grad = jnp.stack(
        [
            sum(
                mix_rows[stream * HIST + source][None, :] * stream_grad[stream].astype(F32)
                for stream in range(STREAMS)
            )
            for source in range(HIST)
        ]
    ).astype(BF16)
    return (
        block.T,
        next_mix.T.reshape(seq_len, STREAMS, NEXT),
        history_grad,
        mix_grad[: STREAMS * HIST].T.reshape(seq_len, STREAMS, HIST),
        qkv_total.astype(F32),
        out_total.astype(F32),
        up_total.astype(F32),
        down_total.astype(F32),
        small_total[:, MIXH : MIXH + 2].T,
        small_total[:, MIXH + 2 : MIXH + 4].T,
        small_total[:, :MIXH],
        mixout_total,
        static_total,
    )


def solution(mesh):
    return jax.shard_map(
        functools.partial(per_device, mesh.shape["dp"]),
        mesh=mesh,
        in_specs=(
            P(None, "dp", None),
            P("dp", None, None),
            P(None, "dp", "tensor"),
            P("dp", "tensor"),
            P("dp", "tensor"),
            P("dp", "tensor"),
            P(None, "dp"),
            P(None, "dp"),
            P("dp", None),
            P(),
            P(),
            P("dp", None),
            P("dp", None, None),
        ),
        out_specs=(
            P("dp", None),
            P("dp", None, None),
            P(None, "dp", None),
            P("dp", None, None),
            P(None, "dp", "tensor"),
            P("dp", "tensor"),
            P("dp", "tensor"),
            P("dp", "tensor"),
            P(None, "dp"),
            P(None, "dp"),
            P("dp", None),
            P(),
            P(),
        ),
        check_vma=False,
    )
```

```python
import functools
import math

import jax
import jax.numpy as jnp
from jax import lax
from jax.experimental import pallas as pl
from jax.experimental.pallas import tpu as pltpu
from jax.sharding import PartitionSpec as P

HD = 128
ROT = 32
HIST = 9
STREAMS = 4
NEXT = 10
MIXH = 40

NORM_EPS = 1e-05
ROOT_EPS = 1e-06
MASKED = -1e30

MESH = pl.DeviceIdType.MESH
ANY = pl.BlockSpec(memory_space=pl.ANY)
VM = pl.BlockSpec(memory_space=pltpu.VMEM)
DMA = pltpu.SemaphoreType.DMA
F32, BF16 = jnp.float32, jnp.bfloat16
CORE, SIDE, NEAR, HIGH = 1, 2, 4, 8
QUARTERS = 4
UNIT = 256


def bit(place, value):
    return lax.rem(lax.div(place, value), 2)


def flip(place, value):
    return place + value - 2 * value * bit(place, value)


def at(start, size, multiple=None):
    return pl.ds(pl.multiple_of(start, size if multiple is None else multiple), size)


def remote(src, dst, send, recv, **where):
    return pltpu.make_async_remote_copy(
        src_ref=src, dst_ref=dst, send_sem=send, recv_sem=recv, device_id=where, device_id_type=MESH
    )


def loop(lower, upper, step):
    def body(index, carry):
        step(index)
        return carry

    lax.fori_loop(lower, upper, body, 0)


def greet(targets):
    barrier = pltpu.get_barrier_semaphore()
    for target in targets:
        pl.semaphore_signal(barrier, inc=1, device_id=target, device_id_type=MESH)
    pl.semaphore_wait(barrier, len(targets))


def greet_all(n_dp, me, other_tensor):
    barrier = pltpu.get_barrier_semaphore()
    loop(
        1,
        n_dp,
        lambda step: pl.semaphore_signal(
            barrier, inc=1, device_id={"dp": lax.rem(me + step, n_dp)}, device_id_type=MESH
        ),
    )
    pl.semaphore_signal(barrier, inc=1, device_id={"tensor": other_tensor}, device_id_type=MESH)
    pl.semaphore_wait(barrier, n_dp)


class Place:
    def __init__(self):
        self.me = lax.axis_index("dp")
        self.tensor = lax.axis_index("tensor")
        self.other = 1 - self.tensor
        self.core = bit(self.me, CORE)
        self.side = bit(self.me, SIDE)
        self.near = bit(self.me, NEAR)
        self.high = lax.div(self.me, HIGH)
        self.quarter = self.near * 2 + self.core
        self.peers = (
            (flip(self.me, CORE), self.near * 2 + 1 - self.core),
            (flip(self.me, NEAR), (1 - self.near) * 2 + self.core),
            (flip(flip(self.me, NEAR), CORE), (1 - self.near) * 2 + 1 - self.core),
        )


def sum_rows(ref_at, depth, chunk, of):
    def body(index, total):
        return total + jnp.sum(of(ref_at(index)), axis=0, keepdims=True)

    return lax.fori_loop(0, depth // chunk, body, jnp.zeros((1, 128), F32))


def gather_kernel(
    n_dp, hist, mix, small, w_qkv, w_up, w_down, w_out,
    o_mix, o_small, o_streams, o_act, o_qkv, o_up, o_down, o_out,
    mix_all, small_all, hist_in, mixed, streams, act,
    early_s, early_r, hist_sem, a2a_s, a2a_r, reshard_s, reshard_r, high_s, high_r, side_s, side_r,
    act_s, act_r, act_local, own_sem, out_sem, share_s, share_r,
):
    here = Place()
    me, tensor = here.me, here.tensor
    rows = small.shape[0]
    depth = rows * n_dp
    half = hist.shape[2] // n_dp // 2
    high_bits = int(math.log2(n_dp // HIGH))
    weights = ((w_qkv, o_qkv), (w_up, o_up), (w_down, o_down), (w_out, o_out))
    greet_all(n_dp, me, here.other)

    def early(which, buf, phase):
        if phase == 0:
            block, target = buf.at[here.high, here.near, here.side, here.core], flip(me, NEAR)
        elif phase <= high_bits:
            span = 1 << (phase - 1)
            block = buf.at[pl.ds(lax.div(here.high, span) * span, span), :, here.side, here.core]
            target = flip(me, HIGH << (phase - 1))
        elif phase == high_bits + 1:
            block, target = buf.at[:, :, here.side, here.core], flip(me, SIDE)
        else:
            block, target = buf.at[:, :, :, here.core], flip(me, CORE)
        return remote(block, block, early_s.at[which, phase], early_r.at[which, phase], dp=target)

    own = [
        pltpu.make_async_copy(mix, mix_all.at[here.high, here.near, here.side, here.core], own_sem.at[0]),
        pltpu.make_async_copy(small, small_all.at[here.high, here.near, here.side, here.core], own_sem.at[1]),
    ]
    units = []
    for w, o in weights:
        if len(w.shape) == 3:
            units += [(w.at[part], o.at[part], 0) for part in range(w.shape[0])]
        else:
            units += [(w, o, first) for first in range(0, o.shape[-1], UNIT)]

    def cut(unit, quarter):
        w, o, first = units[unit]
        return w.at[:, at(quarter * o.shape[-1] + first, UNIT)]

    def slot(unit):
        _, o, first = units[unit]
        mine = pl.ds(pl.multiple_of(here.core * rows, rows), rows)
        return o.at[here.high, here.near, here.side, mine, pl.ds(first, UNIT)]

    def keep(unit):
        return pltpu.make_async_copy(cut(unit, here.quarter), slot(unit), own_sem.at[2 + unit])

    def reshard(unit, peer):
        target, quarter = here.peers[peer]
        return remote(cut(unit, quarter), slot(unit), reshard_s.at[unit, peer], reshard_r.at[unit, peer], dp=target)

    def high_hop(unit, phase):
        _, o, first = units[unit]
        span = 1 << phase
        block = o.at[pl.ds(lax.div(here.high, span) * span, span), :, here.side, :, pl.ds(first, UNIT)]
        return remote(block, block, high_s.at[unit, phase], high_r.at[unit, phase], dp=flip(me, HIGH << phase))

    def side_hop(unit):
        _, o, first = units[unit]
        block = o.at[:, :, here.side, :, pl.ds(first, UNIT)]
        return remote(block, block, side_s.at[unit], side_r.at[unit], dp=flip(me, SIDE))

    def fetch(step, buf):
        target = lax.rem(me + step, n_dp)
        return pltpu.make_async_copy(
            hist.at[:, :, at(target * 2 * half + tensor * half, half)], hist_in.at[buf], hist_sem.at[buf]
        )

    def send(step):
        target = lax.rem(me + step, n_dp)
        return remote(
            mixed.at[step], streams.at[:, at(me * rows, rows), :], a2a_s.at[step], a2a_r.at[step], dp=target
        )

    fetch(0, 0).start()

    def mix_step(step):
        buf = lax.rem(step, 2)

        @pl.when(step + 1 < n_dp)
        def _():
            fetch(step + 1, 1 - buf).start()

        fetch(step, buf).wait()
        target = lax.rem(me + step, n_dp)
        weight = mix_all[lax.div(target, HIGH), bit(target, NEAR), bit(target, SIDE), bit(target, CORE)]
        for row in range(0, rows, 32):
            part = pl.ds(row, 32)
            sources = [hist_in[buf, source, part, :].astype(F32) for source in range(HIST)]
            for stream in range(STREAMS):
                total = sum(
                    sources[source] * weight[stream * HIST + source][None, :] for source in range(HIST)
                )
                mixed[step, stream, part, :] = total.astype(BF16)

        @pl.when(step > 0)
        def _():
            send(step).start()

    chunk = min(256, depth)

    def lanes(near, core, half_at, count):
        return at(near * 4 * half + core * 2 * half + half_at * half, count * half, half)

    def act_keep(stream):
        return pltpu.make_async_copy(
            act.at[stream], o_act.at[stream, :, lanes(here.near, here.core, tensor, 1)], act_local.at[stream]
        )

    def act_near(stream):
        return remote(
            act.at[stream], o_act.at[stream, :, lanes(here.near, here.core, tensor, 1)],
            act_s.at[0, stream], act_r.at[0, stream], dp=flip(me, NEAR),
        )

    def act_tensor(stream, second):
        span = lanes(1 - here.near if second else here.near, here.core, tensor, 1)
        return remote(
            o_act.at[stream, :, span] if second else act.at[stream], o_act.at[stream, :, span],
            act_s.at[1 + second, stream], act_r.at[1 + second, stream], tensor=here.other,
        )

    def act_core(stream, near):
        span = lanes(near, here.core, 0, 2)
        return remote(
            o_act.at[stream, :, span], o_act.at[stream, :, span],
            act_s.at[3 + near, stream], act_r.at[3 + near, stream], dp=flip(me, CORE),
        )

    def normalise_stream(stream):
        block = 0 if stream < 3 else 1

        def piece(index):
            return streams[stream, at(index * chunk, chunk), :].astype(F32)

        centre = sum_rows(piece, depth, chunk, lambda v: v) / depth
        spread = sum_rows(piece, depth, chunk, lambda v: (v - centre) * (v - centre)) / depth
        root = lax.rsqrt(spread + NORM_EPS)

        def normalise(index):
            span = chunk // rows
            first = index * span
            column = jnp.concatenate(
                [
                    small_all[
                        lax.div(first + k, HIGH), bit(first + k, NEAR), bit(first + k, SIDE), bit(first + k, CORE)
                    ]
                    for k in range(span)
                ],
                axis=0,
            ).astype(F32)
            gain = column[:, MIXH + block : MIXH + block + 1]
            bias = column[:, MIXH + 2 + block : MIXH + 3 + block]
            act[stream, at(index * chunk, chunk), :] = (
                (piece(index) - centre) * root * gain + bias
            ).astype(BF16)

        loop(0, depth // chunk, normalise)
        act_keep(stream).start()

    finals = [
        pltpu.make_async_copy(small_all, o_small, out_sem.at[1]),
        pltpu.make_async_copy(streams, o_streams, out_sem.at[2]),
    ]
    early_pairs = ((0, mix_all), (1, small_all))
    last = high_bits + 2

    def first(array):
        keep(array).start()
        for peer in range(3):
            reshard(array, peer).start()

    def second(array):
        keep(array).wait()
        for peer in range(3):
            reshard(array, peer).wait()
        high_hop(array, 0).start()

    def third(array):
        for phase in range(high_bits):
            high_hop(array, phase).wait()
            if phase + 1 < high_bits:
                high_hop(array, phase + 1).start()
        side_hop(array).start()

    def act_first(stream):
        act_near(stream).wait()
        act_tensor(stream, 1).start()
        if stream + 1 < STREAMS:
            act_near(stream + 1).start()
        if stream and stream + 1 < STREAMS:
            act_tensor(stream + 1, 0).start()

    def act_second(stream):
        act_keep(stream).wait()
        act_tensor(stream, 0).wait()
        act_tensor(stream, 1).wait()
        for near in range(2):
            act_core(stream, near).start()

    for copy in own:
        copy.start()
    for copy in own:
        copy.wait()
    for which, buf in early_pairs:
        early(which, buf, 0).start()
    total = len(units)

    def tick(unit):
        third(unit)
        if unit + 3 < total:
            first(unit + 3)
        if unit + 1 < total:
            second(unit + 1)

    for unit in range(min(3, total)):
        first(unit)
    for phase in range(1, last + 1):
        for which, buf in early_pairs:
            early(which, buf, phase - 1).wait()
            early(which, buf, phase).start()
    early(0, mix_all, last).wait()
    mix_copy = pltpu.make_async_copy(mix_all, o_mix.at[tensor], out_sem.at[0])
    mix_share = remote(mix_all, o_mix.at[tensor], share_s.at[0], share_r.at[0], tensor=here.other)
    mix_copy.start()
    mix_share.start()
    second(0)
    loop(0, n_dp, mix_step)
    streams[:, at(me * rows, rows), :] = mixed[0]
    early(1, small_all, last).wait()
    done = 0

    def ticks(count):
        nonlocal done
        for unit in range(done, min(done + count, total)):
            tick(unit)
        done = min(done + count, total)

    ticks(3)
    loop(1, n_dp, lambda step: send(step).wait())
    for stream in range(STREAMS):
        normalise_stream(stream)
        if stream == 0:
            act_near(0).start()
        if stream < 2:
            act_tensor(stream, 0).start()
    for copy in finals:
        copy.start()
    for stream in range(STREAMS):
        ticks(2)
        act_first(stream)
    for stream in range(STREAMS):
        ticks(1)
        act_second(stream)
    ticks(total)
    for unit in range(total):
        side_hop(unit).wait()
    for stream in range(STREAMS):
        for near in range(2):
            act_core(stream, near).wait()
    for copy in finals:
        copy.wait()
    mix_copy.wait()
    mix_share.wait()


def gather(n_dp, hist, mix, small, w_qkv, w_up, w_down, w_out):
    rows = small.shape[0]
    depth = rows * n_dp
    half = hist.shape[2] // n_dp // 2
    high = n_dp // HIGH
    high_bits = int(math.log2(high))
    grid = (high, 2, 2, 2)
    units = sum(w.size // w.shape[-2] for w in (w_qkv, w_up, w_down, w_out)) // QUARTERS // UNIT

    def cut(width):
        return (high, 2, 2, 2 * rows, width // QUARTERS)

    shapes = [
        ((2,) + grid + mix.shape, F32),
        (grid + (rows, 128), BF16),
        ((STREAMS, depth, half), BF16),
        ((STREAMS, depth, 8 * half), BF16),
        ((3,) + cut(w_qkv.shape[2]), BF16),
        (cut(w_up.shape[1]), BF16),
        (cut(w_down.shape[1]), BF16),
        (cut(w_out.shape[1]), BF16),
    ]
    return pl.pallas_call(
        functools.partial(gather_kernel, n_dp),
        out_shape=[jax.ShapeDtypeStruct(*shape) for shape in shapes],
        in_specs=[ANY] * 7,
        out_specs=[ANY] * 8,
        scratch_shapes=[
            pltpu.VMEM(grid + mix.shape, F32),
            pltpu.VMEM(grid + (rows, 128), BF16),
            pltpu.VMEM((2, HIST, rows, half), BF16),
            pltpu.VMEM((n_dp, STREAMS, rows, half), BF16),
            pltpu.VMEM((STREAMS, depth, half), BF16),
            pltpu.VMEM((STREAMS, depth, half), BF16),
            DMA((2, high_bits + 3)),
            DMA((2, high_bits + 3)),
            DMA((2,)),
            DMA((n_dp,)),
            DMA((n_dp,)),
            DMA((units, 3)),
            DMA((units, 3)),
            DMA((units, high_bits)),
            DMA((units, high_bits)),
            DMA((units,)),
            DMA((units,)),
            DMA((5, STREAMS)),
            DMA((5, STREAMS)),
            DMA((STREAMS,)),
            DMA((2 + units,)),
            DMA((3,)),
            DMA((1,)),
            DMA((1,)),
        ],
        compiler_params=pltpu.CompilerParams(
            collective_id=1, has_side_effects=True, vmem_limit_bytes=40 * 1024 * 1024
        ),
        name="gather",
    )(hist, mix, small, w_qkv, w_up, w_down, w_out)


def lane_block(half, near, core, half_at, count):
    return at(near * 4 * half + core * 2 * half + half_at * half, count * half, half)


def gelu_parts(values):
    phi = 0.5 * (1.0 + lax.erf(values * (1.0 / math.sqrt(2.0))))
    density = jnp.exp(-0.5 * values * values) * (1.0 / math.sqrt(2.0 * math.pi))
    return values * phi, phi + values * density


def reduce_group(here, half, part, theirs, own, from_core, from_tensor, from_near, sems, local, pieces, piece):
    core_s, core_r, tensor_s, tensor_r, near_s, near_r = sems

    def load(span, near, half_at):
        return pltpu.make_async_copy(
            part.at[piece(span), lane_block(half, near, here.core, half_at, 1)],
            own.at[near, half_at, piece(span)], local.at[span, near * 2 + half_at],
        )

    def to_core(span, near, half_at):
        return remote(
            part.at[piece(span), lane_block(half, near, 1 - here.core, half_at, 1)],
            from_core.at[near, half_at, piece(span)],
            core_s.at[span, near * 2 + half_at], core_r.at[span, near * 2 + half_at], dp=flip(here.me, CORE),
        )

    def to_tensor(span, near):
        return remote(
            own.at[near, here.other, piece(span)], from_tensor.at[near, piece(span)],
            tensor_s.at[span, near], tensor_r.at[span, near], tensor=here.other,
        )

    def to_near(span):
        return remote(
            from_tensor.at[1 - here.near, piece(span)], from_near.at[piece(span)],
            near_s.at[span], near_r.at[span], dp=flip(here.me, NEAR),
        )

    def start(span):
        for near in range(2):
            for half_at in range(2):
                to_core(span, near, half_at).start()
                load(span, near, half_at).start()

    def after_core(span):
        for near in range(2):
            for half_at in range(2):
                load(span, near, half_at).wait()
                to_core(span, near, half_at).wait()
            own[near, here.other, piece(span)] += from_core[near, here.other, piece(span)]
            to_tensor(span, near).start()
        for near in range(2):
            own[near, here.tensor, piece(span)] += from_core[near, here.tensor, piece(span)]

    def after_tensor(span):
        for near in range(2):
            to_tensor(span, near).wait()
        far = 1 - here.near
        from_tensor[far, piece(span)] += own[far, here.tensor, piece(span)]
        to_near(span).start()
        from_tensor[here.near, piece(span)] += own[here.near, here.tensor, piece(span)]

    def after_near(span):
        to_near(span).wait()

    return start, after_core, after_tensor, after_near


def join_kernel(
    part, streams, cot, small, mix_in, mix_out, mix_back, static, next_cot,
    o_grad, o_wide, o_block, o_next, o_mixin, o_tiny,
    own, from_core, from_tensor, from_near, residual, wide, normed, block, back, low, next_rows, mixin, tiny,
    core_s, core_r, tensor_s, tensor_r, near_s, near_r, local, share_s, share_r, own_sem,
):
    here = Place()
    me, tensor = here.me, here.tensor
    depth, half = cot.shape
    spans = core_s.shape[0]
    size = depth // spans
    chunk = 256
    greet([{"dp": flip(me, CORE)}, {"dp": flip(me, NEAR)}, {"tensor": here.other}])

    def piece(span):
        return pl.ds(span * size, size)

    start, after_core, after_tensor, after_near = reduce_group(
        here, half, part, None, own, from_core, from_tensor, from_near,
        (core_s, core_r, tensor_s, tensor_r, near_s, near_r), local, spans, piece,
    )
    fetch = pltpu.make_async_copy(streams.at[3], residual, own_sem.at[0])
    fetch.start()
    for span in range(spans):
        start(span)
    for span in range(spans):
        after_core(span)
    for span in range(spans):
        after_tensor(span)
    fetch.wait()
    squares = jnp.zeros((1, half), F32)
    for span in range(spans):
        after_near(span)

        def widen(index, total):
            rows = at(span * size + index * chunk, chunk)
            branch = from_tensor[here.near, rows, :].astype(F32) + from_near[rows, :].astype(F32)
            value = residual[rows, :].astype(F32) + branch
            wide[rows, :] = value
            block[rows, :] = value.astype(BF16)
            return total + jnp.sum(value * value, axis=0, keepdims=True)

        squares = lax.fori_loop(0, size // chunk, widen, squares)
    root = lax.rsqrt(squares / depth + ROOT_EPS)

    def share_block(which):
        lanes = at(tensor * half, half)
        if which == 0:
            return pltpu.make_async_copy(block, o_block.at[:, lanes], own_sem.at[1])
        return remote(block, o_block.at[:, lanes], share_s.at[0], share_r.at[0], tensor=here.other)

    share_block(0).start()
    share_block(1).start()

    def norm(index):
        rows = at(index * chunk, chunk)
        normed[rows, :] = (wide[rows, :] * root).astype(BF16)

    loop(0, depth // chunk, norm)
    inner, slope = gelu_parts(jnp.dot(mix_in[...], normed[...], preferred_element_type=F32))
    inner_low = inner.astype(BF16)
    next_rows[...] = (jnp.dot(mix_out[...], inner_low, preferred_element_type=F32) + static[...])[:MIXH]
    next_low = next_cot[...].astype(BF16)

    def nt(left, right):
        return lax.dot_general(left, right, (((1,), (1,)), ((), ())), preferred_element_type=F32)

    tiny[:, :128] = nt(inner_low, next_low)
    tiny[:, 128:] = jnp.broadcast_to(jnp.sum(next_cot[...], axis=1, keepdims=True), (128, 128))
    inner_grad = (jnp.dot(mix_back[...], next_low, preferred_element_type=F32) * slope).astype(BF16)

    def pull(index, total):
        rows = at(index * chunk, chunk)
        value = jnp.dot(small[rows, :], inner_grad, preferred_element_type=F32)
        back[rows, :] = value
        return total + jnp.sum(value * wide[rows, :] * root, axis=0, keepdims=True)

    along = lax.fori_loop(0, depth // chunk, pull, jnp.zeros((1, half), F32)) / depth

    def finish(index):
        rows = at(index * chunk, chunk)
        value = cot[rows, :].astype(F32) + root * (back[rows, :] - wide[rows, :] * root * along)
        back[rows, :] = value
        low[rows, :] = value.astype(BF16)

    loop(0, depth // chunk, finish)

    def share(kind, index):
        if kind == 0:
            source, lanes, where = low, lane_block(half, here.near, here.core, tensor, 1), {"dp": flip(me, NEAR)}
        elif kind == 1:
            lanes = lane_block(half, 1 - here.near if index else here.near, here.core, tensor, 1)
            source, where = (o_grad.at[:, lanes] if index else low), {"tensor": here.other}
        else:
            lanes, where = lane_block(half, index, here.core, 0, 2), {"dp": flip(me, CORE)}
            source = o_grad.at[:, lanes]
        number = 1 + 2 * kind + index
        return remote(source, o_grad.at[:, lanes], share_s.at[number], share_r.at[number], **where)

    share(0, 0).start()
    share(1, 0).start()
    keep = pltpu.make_async_copy(
        low, o_grad.at[:, lane_block(half, here.near, here.core, tensor, 1)], own_sem.at[2]
    )
    keep.start()

    def mixin_rows(index):
        rows = at(index * chunk, chunk)
        mixin[rows, :] = nt(normed[rows, :], inner_grad)

    loop(0, depth // chunk, mixin_rows)
    share(0, 0).wait()
    share(1, 1).start()
    lanes = at(tensor * half, half)
    next_share = remote(next_rows, o_next.at[:, lanes], share_s.at[7], share_r.at[7], tensor=here.other)
    next_share.start()
    finals = [
        pltpu.make_async_copy(next_rows, o_next.at[:, lanes], own_sem.at[3]),
        pltpu.make_async_copy(back, o_wide, own_sem.at[4]),
        pltpu.make_async_copy(mixin, o_mixin, own_sem.at[5]),
        pltpu.make_async_copy(tiny, o_tiny, own_sem.at[6]),
    ]
    for copy in finals:
        copy.start()
    keep.wait()
    share(1, 0).wait()
    share(1, 1).wait()
    for near in range(2):
        share(2, near).start()
    for near in range(2):
        share(2, near).wait()
    share_block(0).wait()
    share_block(1).wait()
    next_share.wait()
    for copy in finals:
        copy.wait()


def join(part, streams, cot, small, mix_in, mix_out, mix_back, static, next_cot):
    depth, half = cot.shape
    spans = 4
    shapes = [
        ((depth, 8 * half), BF16),
        ((depth, half), F32),
        ((depth, 2 * half), BF16),
        ((MIXH, 2 * half), F32),
        ((depth, 128), F32),
        ((128, 256), F32),
    ]
    return pl.pallas_call(
        join_kernel,
        out_shape=[jax.ShapeDtypeStruct(*shape) for shape in shapes],
        in_specs=[ANY, ANY] + [VM] * 7,
        out_specs=[ANY] * 6,
        scratch_shapes=[
            pltpu.VMEM((2, 2, depth, half), BF16),
            pltpu.VMEM((2, 2, depth, half), BF16),
            pltpu.VMEM((2, depth, half), BF16),
            pltpu.VMEM((depth, half), BF16),
            pltpu.VMEM((depth, half), BF16),
            pltpu.VMEM((depth, half), F32),
            pltpu.VMEM((depth, half), BF16),
            pltpu.VMEM((depth, half), BF16),
            pltpu.VMEM((depth, half), F32),
            pltpu.VMEM((depth, half), BF16),
            pltpu.VMEM((MIXH, half), F32),
            pltpu.VMEM((depth, 128), F32),
            pltpu.VMEM((128, 256), F32),
            DMA((spans, 4)),
            DMA((spans, 4)),
            DMA((spans, 2)),
            DMA((spans, 2)),
            DMA((spans,)),
            DMA((spans,)),
            DMA((spans, 4)),
            DMA((8,)),
            DMA((8,)),
            DMA((7,)),
        ],
        compiler_params=pltpu.CompilerParams(
            collective_id=2, has_side_effects=True, vmem_limit_bytes=40 * 1024 * 1024
        ),
        name="join",
    )(part, streams, cot, small, mix_in, mix_out, mix_back, static, next_cot)


def scatter_kernel(
    n_dp, attn_grad, mlp_grad, streams, small, wide_grad, mixin_part, hist, g_qkv, g_up, g_down, g_out,
    o_stream, o_mix, o_small, o_qkv, o_up, o_down, o_out,
    own, from_core, from_tensor, from_near, rows_in, wide, stream_grad, gains, biases, tiny, tiny_in, tiny_out,
    hist_in, arrived, mix_part, mix_in, mix_sum, tiny_sum,
    side_qkv, side_up, side_down, side_out, mine_qkv, mine_up, mine_down, mine_out,
    high_qkv, high_up, high_down, high_out,
    core_s, core_r, tensor_s, tensor_r, near_s, near_r, local, in_sem,
    side_s, side_r, side_local, high_s, high_r, peer_s, peer_r, peer_local,
    a2a_s, a2a_r, keep_sem, pass_s, pass_r, tiny_s, tiny_r, mix_s, mix_r, hist_sem, last_s, last_r, last_local,
):
    here = Place()
    me, tensor = here.me, here.tensor
    depth, half = wide_grad.shape
    rows = depth // n_dp
    high_bits = int(math.log2(n_dp // HIGH))
    chunk = min(256, depth)
    greet_all(n_dp, me, here.other)
    weights = (
        (g_qkv, side_qkv, mine_qkv, high_qkv, o_qkv),
        (g_up, side_up, mine_up, high_up, o_up),
        (g_down, side_down, mine_down, high_down, o_down),
        (g_out, side_out, mine_out, high_out, o_out),
    )

    def pick(ref, *index):
        return ref.at[(slice(None),) + index] if ref.shape[0] == 3 and len(ref.shape) > len(index) + 2 else ref.at[index]

    def everything(_):
        return pl.ds(0, depth)

    steps = []
    for stream in range(STREAMS):
        part = attn_grad.at[stream] if stream < 3 else mlp_grad
        steps.append(
            reduce_group(
                here, half, part, None, own.at[stream], from_core.at[stream], from_tensor.at[stream],
                from_near.at[stream],
                tuple(
                    sem.at[pl.ds(stream, 1)]
                    for sem in (core_s, core_r, tensor_s, tensor_r, near_s, near_r)
                ),
                local.at[pl.ds(stream, 1)], 1, everything,
            )
        )
    for stream in range(STREAMS):
        steps[stream][0](0)
    loads = [
        pltpu.make_async_copy(streams, rows_in, in_sem.at[0]),
        pltpu.make_async_copy(wide_grad, wide, in_sem.at[1]),
    ]
    for copy in loads:
        copy.start()

    def is_qkv(array):
        return array == 0

    def index_of(array, *index):
        return ((slice(None),) if is_qkv(array) else ()) + index

    def side_hop(array):
        g, side, _, _, _ = weights[array]
        return remote(
            g.at[index_of(array, slice(None), slice(None), 1 - here.side)], side, side_s.at[array], side_r.at[array],
            dp=flip(me, SIDE),
        )

    def side_load(array):
        g, _, mine, _, _ = weights[array]
        return pltpu.make_async_copy(
            g.at[index_of(array, slice(None), slice(None), here.side)], mine, side_local.at[array]
        )

    def high_hop(array, phase):
        _, _, mine, high, _ = weights[array]
        span = 1 << phase
        base = lax.div(here.high, span)
        theirs = base + 1 - 2 * lax.rem(base, 2)
        return remote(
            mine.at[index_of(array, pl.ds(theirs * span, span))], high.at[index_of(array, pl.ds(span - 1, span))],
            high_s.at[array, phase], high_r.at[array, phase], dp=flip(me, HIGH << phase),
        )

    def add_blocks(array, into, other, first_into, first_other, count):
        shape = into.shape
        tall, width = shape[-2:]
        outer = 3 if is_qkv(array) else 1
        step = 32

        def add(flat):
            lead = lax.div(flat, count * 2)
            rest = lax.rem(flat, count * 2)
            high, near = lax.div(rest, 2), lax.rem(rest, 2)
            prefix = (lead,) if is_qkv(array) else ()

            def tile(index):
                span = at(index * step, step)
                into[prefix + (first_into + high, near, span)] += other[prefix + (first_other + high, near, span)]

            loop(0, tall // step, tile)

        loop(0, outer * count * 2, add)

    for array in range(4):
        side_hop(array).start()
        side_load(array).start()
    for copy in loads:
        copy.wait()
    stats = []
    for stream in range(STREAMS):

        def piece(index):
            return rows_in[stream, at(index * chunk, chunk), :].astype(F32)

        centre = sum_rows(piece, depth, chunk, lambda v: v) / depth
        spread = sum_rows(piece, depth, chunk, lambda v: (v - centre) * (v - centre)) / depth
        stats.append((centre, lax.rsqrt(spread + NORM_EPS)))
    for stream in range(STREAMS):
        steps[stream][1](0)
    for array in range(4):
        side_load(array).wait()
        side_hop(array).wait()
        _, side, mine, _, _ = weights[array]
        add_blocks(array, mine, side, 0, 0, n_dp // HIGH)
        high_hop(array, high_bits - 1).start()
    for stream in range(STREAMS):
        steps[stream][2](0)

    for stream in range(STREAMS):
        steps[stream][3](0)
        group = 0 if stream < 3 else 1
        centre, root = stats[stream]

        def parts(index):
            span = at(index * chunk, chunk)
            grad = from_tensor[stream, here.near, span].astype(F32) + from_near[stream, span].astype(F32)
            hat = (rows_in[stream, span, :].astype(F32) - centre) * root
            gain = small[span, MIXH + group : MIXH + group + 1].astype(F32)
            return span, grad, hat, grad * gain

        def sums(index, carry):
            span, grad, hat, scaled = parts(index)
            if stream in (0, 3):
                gains[group, span] = grad * hat
                biases[group, span] = grad
            else:
                gains[group, span] += grad * hat
                biases[group, span] += grad
            return (
                carry[0] + jnp.sum(scaled, axis=0, keepdims=True),
                carry[1] + jnp.sum(scaled * hat, axis=0, keepdims=True),
            )

        zero = jnp.zeros((1, half), F32)
        total, along = lax.fori_loop(0, depth // chunk, sums, (zero, zero))

        def finish(index):
            span, grad, hat, scaled = parts(index)
            value = root * (scaled - total / depth - hat * (along / depth))
            if stream == 3:
                value = value + wide[span, :]
            stream_grad[stream, span] = value.astype(BF16)

        loop(0, depth // chunk, finish)

    def send(step):
        target = lax.rem(me + step, n_dp)
        return remote(
            stream_grad.at[:, at(target * rows, rows), :], arrived.at[step], a2a_s.at[step], a2a_r.at[step], dp=target
        )

    loop(1, n_dp, lambda step: send(step).start())

    def fetch(step, buf):
        source = lax.rem(me - step + n_dp, n_dp)
        return pltpu.make_async_copy(
            hist.at[:, :, at(source * 2 * half + tensor * half, half)], hist_in.at[buf], hist_sem.at[buf]
        )

    fetch(0, 0).start()
    own_block = pltpu.make_async_copy(stream_grad.at[:, at(me * rows, rows), :], arrived.at[0], last_local.at[0])
    own_block.start()

    column = lax.broadcasted_iota(jnp.int32, (chunk, 128), 1)

    def gather_tiny(index):
        span = at(index * chunk, chunk)
        value = mixin_part[span, :]
        for group in range(2):
            gain = jnp.sum(gains[group, span], axis=1, keepdims=True)
            bias = jnp.sum(biases[group, span], axis=1, keepdims=True)
            value = jnp.where(column == MIXH + group, gain, value)
            value = jnp.where(column == MIXH + 2 + group, bias, value)
        tiny[span, :] = value.astype(BF16)

    loop(0, depth // chunk, gather_tiny)

    def tiny_send(step):
        target = lax.rem(me + step, n_dp)
        return remote(tiny.at[at(target * rows, rows), :], tiny_in.at[step], tiny_s.at[step], tiny_r.at[step], dp=target)

    loop(1, n_dp, lambda step: tiny_send(step).start())

    for array in range(4):
        _, _, mine, high, _ = weights[array]
        for phase in reversed(range(high_bits)):
            high_hop(array, phase).wait()
            span = 1 << phase
            add_blocks(array, mine, high, lax.div(here.high, span) * span, span - 1, span)
            if phase:
                high_hop(array, phase - 1).start()

    def peer_hop(array, peer):
        _, _, mine, _, out = weights[array]
        width = mine.shape[-1]
        target, _ = here.peers[peer]
        core = bit(target, CORE)
        return remote(
            mine.at[index_of(array, here.high, bit(target, NEAR), at(core * rows, rows))],
            out.at[index_of(array, slice(None), at(here.quarter * width, width))],
            peer_s.at[array, peer], peer_r.at[array, peer], dp=target,
        )

    def peer_keep(array):
        _, _, mine, _, out = weights[array]
        width = mine.shape[-1]
        return pltpu.make_async_copy(
            mine.at[index_of(array, here.high, here.near, at(here.core * rows, rows))],
            out.at[index_of(array, slice(None), at(here.quarter * width, width))], peer_local.at[array],
        )

    for array in range(4):
        peer_keep(array).start()
        for peer in range(3):
            peer_hop(array, peer).start()
    own_block.wait()

    def keep_lanes(step):
        source = lax.rem(me - step + n_dp, n_dp)
        return at(source * 2 * half + tensor * half, half)

    def keep(step):
        return pltpu.make_async_copy(arrived.at[step], o_stream.at[:, :, keep_lanes(step)], keep_sem.at[step])

    def pass_on(step):
        return remote(
            arrived.at[step], o_stream.at[:, :, keep_lanes(step)], pass_s.at[step], pass_r.at[step], tensor=here.other
        )

    def mix_send(step):
        return remote(
            mix_part.at[step], mix_in.at[step], mix_s.at[step], mix_r.at[step], dp=lax.rem(me - step + n_dp, n_dp)
        )

    def receive(step):
        buf = lax.rem(step, 2)

        @pl.when(step + 1 < n_dp)
        def _():
            fetch(step + 1, 1 - buf).start()

        @pl.when(step > 0)
        def _():
            send(step).wait()

        keep(step).start()
        pass_on(step).start()
        fetch(step, buf).wait()
        for stream in range(STREAMS):
            totals = [jnp.zeros((8, half), F32) for _ in range(HIST)]
            for row in range(0, rows, 16):
                span = pl.ds(row, 16)
                grad = arrived[step, stream, span, :].astype(F32)
                for source in range(HIST):
                    product = grad * hist_in[buf, source, span, :].astype(F32)
                    totals[source] = totals[source] + product[:8] + product[8:]
            for source in range(HIST):
                mix_part[step, pl.ds(stream * HIST + source, 1), :] = jnp.sum(totals[source], axis=0, keepdims=True)

        @pl.when(step > 0)
        def _():
            mix_send(step).start()

    mix_part[0] = jnp.zeros_like(mix_part[0])
    loop(0, n_dp, receive)

    mix_sum[...] = mix_part[0]

    def add_mix(step):
        mix_send(step).wait()
        mix_sum[...] += mix_in[step]

    loop(1, n_dp, add_mix)
    lanes = at(tensor * half, half)
    mix_share = remote(mix_sum, o_mix.at[:, lanes], last_s.at[0], last_r.at[0], tensor=here.other)
    mix_keep = pltpu.make_async_copy(mix_sum, o_mix.at[:, lanes], last_local.at[1])
    mix_share.start()
    mix_keep.start()
    tiny_sum[0] = tiny[at(me * rows, rows), :].astype(F32)

    def add_tiny(step):
        tiny_send(step).wait()
        tiny_sum[0] += tiny_in[step].astype(F32)

    loop(1, n_dp, add_tiny)
    tiny_share = remote(tiny_sum.at[0], tiny_sum.at[1], last_s.at[1], last_r.at[1], tensor=here.other)
    tiny_share.start()
    tiny_share.wait()
    tiny_out[...] = tiny_sum[0] + tiny_sum[1]
    tiny_keep = pltpu.make_async_copy(tiny_out, o_small, last_local.at[2])
    tiny_keep.start()
    for array in range(4):
        peer_keep(array).wait()
        for peer in range(3):
            peer_hop(array, peer).wait()

    def settle(step):
        keep(step).wait()
        pass_on(step).wait()

    loop(0, n_dp, settle)
    mix_share.wait()
    mix_keep.wait()
    tiny_keep.wait()


def scatter(n_dp, attn_grad, mlp_grad, streams, small, wide_grad, mixin_part, hist, g_qkv, g_up, g_down, g_out):
    depth, half = wide_grad.shape
    rows = depth // n_dp
    high = n_dp // HIGH
    high_bits = int(math.log2(high))
    grads = (g_qkv, g_up, g_down, g_out)

    def lead(g):
        return (3,) if g.ndim == 6 else ()

    def halved(g, highs):
        return lead(g) + (highs, 2) + g.shape[-2:]

    outs = [
        ((STREAMS, rows, 2 * half * n_dp), BF16),
        ((MIXH, 2 * half), F32),
        ((rows, 128), F32),
    ] + [(lead(g) + (rows, QUARTERS * g.shape[-1]), BF16) for g in grads]
    return pl.pallas_call(
        functools.partial(scatter_kernel, n_dp),
        out_shape=[jax.ShapeDtypeStruct(*shape) for shape in outs],
        in_specs=[ANY, ANY, ANY, VM, ANY, VM, ANY] + [ANY] * 4,
        out_specs=[ANY] * 7,
        scratch_shapes=[
            pltpu.VMEM((STREAMS, 2, 2, depth, half), BF16),
            pltpu.VMEM((STREAMS, 2, 2, depth, half), BF16),
            pltpu.VMEM((STREAMS, 2, depth, half), BF16),
            pltpu.VMEM((STREAMS, depth, half), BF16),
            pltpu.VMEM((STREAMS, depth, half), BF16),
            pltpu.VMEM((depth, half), F32),
            pltpu.VMEM((STREAMS, depth, half), BF16),
            pltpu.VMEM((2, depth, half), F32),
            pltpu.VMEM((2, depth, half), F32),
            pltpu.VMEM((depth, 128), BF16),
            pltpu.VMEM((n_dp, rows, 128), BF16),
            pltpu.VMEM((rows, 128), F32),
            pltpu.VMEM((2, HIST, rows, half), BF16),
            pltpu.VMEM((n_dp, STREAMS, rows, half), BF16),
            pltpu.VMEM((n_dp, MIXH, half), F32),
            pltpu.VMEM((n_dp, MIXH, half), F32),
            pltpu.VMEM((MIXH, half), F32),
            pltpu.VMEM((2, rows, 128), F32),
        ]
        + [pltpu.VMEM(halved(g, high), BF16) for g in grads]
        + [pltpu.VMEM(halved(g, high), BF16) for g in grads]
        + [pltpu.VMEM(halved(g, high - 1), BF16) for g in grads]
        + [
            DMA((STREAMS, 4)),
            DMA((STREAMS, 4)),
            DMA((STREAMS, 2)),
            DMA((STREAMS, 2)),
            DMA((STREAMS,)),
            DMA((STREAMS,)),
            DMA((STREAMS, 4)),
            DMA((2,)),
            DMA((4,)),
            DMA((4,)),
            DMA((4,)),
            DMA((4, high_bits)),
            DMA((4, high_bits)),
            DMA((4, 3)),
            DMA((4, 3)),
            DMA((4,)),
            DMA((n_dp,)),
            DMA((n_dp,)),
            DMA((n_dp,)),
            DMA((n_dp,)),
            DMA((n_dp,)),
            DMA((n_dp,)),
            DMA((n_dp,)),
            DMA((n_dp,)),
            DMA((n_dp,)),
            DMA((2,)),
            DMA((2,)),
            DMA((2,)),
            DMA((3,)),
        ],
        compiler_params=pltpu.CompilerParams(
            collective_id=3, has_side_effects=True, vmem_limit_bytes=60 * 1024 * 1024
        ),
        name="scatter",
    )(attn_grad, mlp_grad, streams, small, wide_grad, mixin_part, hist, *grads)


def exact_gelu(values):
    return jax.nn.gelu(values, approximate=False)


def rotary_tables(length, rotary, float_type):
    half_rot = rotary // 2
    places = jnp.arange(length).astype(float_type)
    frequency = jnp.exp(
        jnp.arange(half_rot).astype(float_type) * (-2.0 * math.log(10000.0) / rotary)
    )
    angles = places[:, None] * frequency[None, :]
    return (jnp.cos(angles), jnp.sin(angles))


def rotate(values, cos_table, sin_table):
    half_rot = cos_table.shape[-1]
    first_half = values[..., :half_rot]
    second = values[..., half_rot : 2 * half_rot]
    return jnp.concatenate(
        [
            first_half * cos_table - second * sin_table,
            second * cos_table + first_half * sin_table,
            values[..., 2 * half_rot :],
        ],
        axis=-1,
    )


def masked_scores(queries, key_rows):
    length = queries.shape[1]
    score_scale = 1.0 / math.sqrt(queries.shape[2])
    causal = lax.broadcasted_iota(jnp.int32, (length, length), 0) >= lax.broadcasted_iota(
        jnp.int32, (length, length), 1
    )
    scores = (
        jnp.einsum("hqd,hkd->hqk", queries, key_rows, preferred_element_type=jnp.float32)
        * score_scale
    )
    return (jnp.where(causal[None], scores, MASKED), score_scale)


def attend_forward(queries, key_rows, value_rows):
    scores, score_scale = masked_scores(queries, key_rows)
    row_peak = jnp.max(scores, axis=-1, keepdims=True)
    raised = jnp.exp(scores - row_peak)
    row_total = jnp.sum(raised, axis=-1, keepdims=True)
    prob_low = (raised / row_total).astype(jnp.bfloat16)
    context = jnp.einsum("hqk,hkd->hqd", prob_low, value_rows, preferred_element_type=jnp.float32)
    return (context.astype(jnp.bfloat16), row_peak + jnp.log(row_total))


def attend_backward(queries, key_rows, value_rows, log_sum, context_grad):
    scores, score_scale = masked_scores(queries, key_rows)
    attn_prob = jnp.exp(scores - log_sum)
    prob_low = attn_prob.astype(jnp.bfloat16)
    value_grad = jnp.einsum(
        "hqk,hqd->hkd", prob_low, context_grad, preferred_element_type=jnp.float32
    )
    prob_grad = jnp.einsum(
        "hqd,hkd->hqk", context_grad, value_rows, preferred_element_type=jnp.float32
    )
    inner_sum = jnp.sum(attn_prob * prob_grad, axis=-1, keepdims=True)
    score_grad = (attn_prob * (prob_grad - inner_sum)).astype(jnp.bfloat16)
    query_grad = (
        jnp.einsum("hqk,hkd->hqd", score_grad, key_rows, preferred_element_type=jnp.float32)
        * score_scale
    )
    key_grad = (
        jnp.einsum("hqk,hqd->hkd", score_grad, queries, preferred_element_type=jnp.float32)
        * score_scale
    )
    return (query_grad, key_grad, value_grad)


def per_device(
    n_dp, history, mix_weights, w_qkv, w_out, w_up, w_down, norm_gain, norm_bias, mix_in, mix_out, mix_static,
    out_cot, next_cot,
):
    tensor = lax.axis_index("tensor")
    seq_len = mix_weights.shape[0]
    half = seq_len // 2
    depth = mix_in.shape[0] * n_dp

    def own_half(rows):
        return lax.dynamic_slice_in_dim(rows, tensor * half, half, 0)

    mix_rows = jnp.pad(own_half(mix_weights.reshape(seq_len, -1)).T, ((0, MIXH - STREAMS * HIST), (0, 0)))
    small = jnp.concatenate([mix_in, norm_gain.T, norm_bias.T], axis=1)
    small = jnp.pad(small, ((0, 0), (0, 128 - small.shape[1])))
    mix_all, small_all, streams, act, qkv, up, down, out = gather(
        n_dp, history, mix_rows, small, w_qkv, w_up, w_down, w_out
    )
    small_all = small_all.reshape(depth, 128)
    qkv, up, down, out = (
        qkv.reshape(3, depth, -1), up.reshape(depth, -1), down.reshape(depth, -1), out.reshape(depth, -1)
    )
    tokens = act.shape[2]
    seqs = tokens // seq_len
    heads = qkv.shape[2] // HD
    projected = jnp.einsum("sdt,sde->ste", act[:3], qkv, preferred_element_type=F32)
    head_rows = jnp.transpose(projected.reshape(3, seqs, seq_len, heads, HD), (0, 1, 3, 2, 4)).reshape(
        3, seqs * heads, seq_len, HD
    )
    cos_table, sin_table = rotary_tables(seq_len, ROT, F32)
    queries = rotate(head_rows[0], cos_table, sin_table).astype(BF16)
    key_rows = rotate(head_rows[1], cos_table, sin_table).astype(BF16)
    value_rows = head_rows[2].astype(BF16)
    context, log_sum = attend_forward(queries, key_rows, value_rows)

    def join_heads(rows):
        return jnp.transpose(rows.reshape(seqs, heads, seq_len, HD), (0, 2, 1, 3)).reshape(tokens, heads * HD)

    context_rows = join_heads(context)
    up_pre = jnp.einsum("dt,df->tf", act[3], up, preferred_element_type=F32)
    hidden_wide, gelu_back = jax.vjp(exact_gelu, up_pre)
    hidden = hidden_wide.astype(BF16)
    part = (
        jnp.einsum("de,te->dt", out, context_rows, preferred_element_type=F32)
        + jnp.einsum("df,tf->dt", down, hidden, preferred_element_type=F32)
    ).astype(BF16)

    def square(values):
        return jnp.pad(values, ((0, 128 - values.shape[0]), (0, 128 - values.shape[1])))

    next_rows = own_half(next_cot.reshape(seq_len, -1)).T
    next_rows = jnp.pad(next_rows, ((0, 128 - next_rows.shape[0]), (0, 0)))
    mix_in_rows = jnp.pad(small_all[:, :MIXH].T, ((0, 128 - MIXH), (0, 0)))
    static = jnp.pad(mix_static[:, None], ((0, 128 - mix_static.shape[0]), (0, 0)))
    branch_grad, wide_grad, block, next_mix, mixin_part, tiny = join(
        part, streams, own_half(out_cot).T, small_all, mix_in_rows, square(mix_out.T), square(mix_out), static,
        next_rows,
    )
    mixout_total, static_total = lax.psum(
        (tiny[:MIXH, : STREAMS * NEXT], tiny[: STREAMS * NEXT, 128]), ("dp", "tensor")
    )
    hidden_grad = jnp.einsum("dt,df->tf", branch_grad, down, preferred_element_type=F32)
    up_grad_low = gelu_back(hidden_grad)[0].astype(BF16)
    mlp_in_grad = jnp.einsum("df,tf->dt", up, up_grad_low, preferred_element_type=F32).astype(BF16)
    context_grad_rows = jnp.einsum("dt,de->te", branch_grad, out, preferred_element_type=F32).astype(BF16)
    context_grad = jnp.transpose(context_grad_rows.reshape(seqs, seq_len, heads, HD), (0, 2, 1, 3)).reshape(
        seqs * heads, seq_len, HD
    )
    query_grad, key_grad, value_grad = attend_backward(queries, key_rows, value_rows, log_sum, context_grad)
    proj_grad = jnp.stack(
        [
            join_heads(rotate(query_grad, cos_table, -sin_table).astype(BF16)),
            join_heads(rotate(key_grad, cos_table, -sin_table).astype(BF16)),
            join_heads(value_grad.astype(BF16)),
        ]
    )
    attn_in_grad = jnp.einsum("sde,ste->sdt", qkv, proj_grad, preferred_element_type=F32).astype(BF16)
    g_qkv = jnp.einsum("sdt,ste->sde", act[:3], proj_grad, preferred_element_type=F32).astype(BF16)
    g_out = jnp.einsum("dt,te->de", branch_grad, context_rows, preferred_element_type=F32).astype(BF16)
    g_up = jnp.einsum("dt,tf->df", act[3], up_grad_low, preferred_element_type=F32).astype(BF16)
    g_down = jnp.einsum("dt,tf->df", branch_grad, hidden, preferred_element_type=F32).astype(BF16)
    grid = (n_dp // HIGH, 2, 2, 2 * mix_in.shape[0])
    stream_grad, mix_grad, small_total, qkv_total, up_total, down_total, out_total = scatter(
        n_dp, attn_in_grad, mlp_in_grad, streams, small_all, wide_grad, mixin_part, history,
        g_qkv.reshape((3,) + grid + (-1,)), g_up.reshape(grid + (-1,)), g_down.reshape(grid + (-1,)),
        g_out.reshape(grid + (-1,)),
    )
    mix_rows = mix_all.reshape(n_dp, MIXH, 1, half)
    mix_rows = lax.all_gather(mix_rows, "tensor", axis=2, tiled=True)
    mix_rows = jnp.transpose(mix_rows, (1, 0, 2, 3)).reshape(MIXH, n_dp * seq_len)
    history_grad = jnp.stack(
        [
            sum(
                mix_rows[stream * HIST + source][None, :] * stream_grad[stream].astype(F32)
                for stream in range(STREAMS)
            )
            for source in range(HIST)
        ]
    ).astype(BF16)
    return (
        block.T,
        next_mix.T.reshape(seq_len, STREAMS, NEXT),
        history_grad,
        mix_grad[: STREAMS * HIST].T.reshape(seq_len, STREAMS, HIST),
        qkv_total.astype(F32),
        out_total.astype(F32),
        up_total.astype(F32),
        down_total.astype(F32),
        small_total[:, MIXH : MIXH + 2].T,
        small_total[:, MIXH + 2 : MIXH + 4].T,
        small_total[:, :MIXH],
        mixout_total,
        static_total,
    )


def solution(mesh):
    return jax.shard_map(
        functools.partial(per_device, mesh.shape["dp"]),
        mesh=mesh,
        in_specs=(
            P(None, "dp", None),
            P("dp", None, None),
            P(None, "dp", "tensor"),
            P("dp", "tensor"),
            P("dp", "tensor"),
            P("dp", "tensor"),
            P(None, "dp"),
            P(None, "dp"),
            P("dp", None),
            P(),
            P(),
            P("dp", None),
            P("dp", None, None),
        ),
        out_specs=(
            P("dp", None),
            P("dp", None, None),
            P(None, "dp", None),
            P("dp", None, None),
            P(None, "dp", "tensor"),
            P("dp", "tensor"),
            P("dp", "tensor"),
            P("dp", "tensor"),
            P(None, "dp"),
            P(None, "dp"),
            P("dp", None),
            P(),
            P(),
        ),
        check_vma=False,
    )


def lane_block(half, near, core, half_at, count):
    return at(near * 4 * half + core * 2 * half + half_at * half, count * half, half)


def gelu_parts(values):
    phi = 0.5 * (1.0 + lax.erf(values * (1.0 / math.sqrt(2.0))))
    density = jnp.exp(-0.5 * values * values) * (1.0 / math.sqrt(2.0 * math.pi))
    return values * phi, phi + values * density


def reduce_group(here, half, part, theirs, own, from_core, from_tensor, from_near, sems, local, pieces, piece):
    core_s, core_r, tensor_s, tensor_r, near_s, near_r = sems

    def load(span, near, half_at):
        return pltpu.make_async_copy(
            part.at[piece(span), lane_block(half, near, here.core, half_at, 1)],
            own.at[near, half_at, piece(span)], local.at[span, near * 2 + half_at],
        )

    def to_core(span, near, half_at):
        return remote(
            part.at[piece(span), lane_block(half, near, 1 - here.core, half_at, 1)],
            from_core.at[near, half_at, piece(span)],
            core_s.at[span, near * 2 + half_at], core_r.at[span, near * 2 + half_at], dp=flip(here.me, CORE),
        )

    def to_tensor(span, near):
        return remote(
            own.at[near, here.other, piece(span)], from_tensor.at[near, piece(span)],
            tensor_s.at[span, near], tensor_r.at[span, near], tensor=here.other,
        )

    def to_near(span):
        return remote(
            from_tensor.at[1 - here.near, piece(span)], from_near.at[piece(span)],
            near_s.at[span], near_r.at[span], dp=flip(here.me, NEAR),
        )

    def start(span):
        for near in range(2):
            for half_at in range(2):
                to_core(span, near, half_at).start()
                load(span, near, half_at).start()

    def after_core(span):
        for near in range(2):
            for half_at in range(2):
                load(span, near, half_at).wait()
                to_core(span, near, half_at).wait()
            own[near, here.other, piece(span)] += from_core[near, here.other, piece(span)]
            to_tensor(span, near).start()
        for near in range(2):
            own[near, here.tensor, piece(span)] += from_core[near, here.tensor, piece(span)]

    def after_tensor(span):
        for near in range(2):
            to_tensor(span, near).wait()
        far = 1 - here.near
        from_tensor[far, piece(span)] += own[far, here.tensor, piece(span)]
        to_near(span).start()
        from_tensor[here.near, piece(span)] += own[here.near, here.tensor, piece(span)]

    def after_near(span):
        to_near(span).wait()

    return start, after_core, after_tensor, after_near


def join_kernel(
    part, streams, cot, small, mix_in, mix_out, mix_back, static, next_cot,
    o_grad, o_wide, o_block, o_next, o_mixin, o_tiny,
    own, from_core, from_tensor, from_near, residual, wide, normed, block, back, low, next_rows, mixin, tiny,
    core_s, core_r, tensor_s, tensor_r, near_s, near_r, local, share_s, share_r, own_sem,
):
    here = Place()
    me, tensor = here.me, here.tensor
    depth, half = cot.shape
    spans = core_s.shape[0]
    size = depth // spans
    chunk = 256
    greet([{"dp": flip(me, CORE)}, {"dp": flip(me, NEAR)}, {"tensor": here.other}])

    def piece(span):
        return pl.ds(span * size, size)

    start, after_core, after_tensor, after_near = reduce_group(
        here, half, part, None, own, from_core, from_tensor, from_near,
        (core_s, core_r, tensor_s, tensor_r, near_s, near_r), local, spans, piece,
    )
    fetch = pltpu.make_async_copy(streams.at[3], residual, own_sem.at[0])
    fetch.start()
    for span in range(spans):
        start(span)
    for span in range(spans):
        after_core(span)
    for span in range(spans):
        after_tensor(span)
    fetch.wait()
    squares = jnp.zeros((1, half), F32)
    for span in range(spans):
        after_near(span)

        def widen(index, total):
            rows = at(span * size + index * chunk, chunk)
            branch = from_tensor[here.near, rows, :].astype(F32) + from_near[rows, :].astype(F32)
            value = residual[rows, :].astype(F32) + branch
            wide[rows, :] = value
            block[rows, :] = value.astype(BF16)
            return total + jnp.sum(value * value, axis=0, keepdims=True)

        squares = lax.fori_loop(0, size // chunk, widen, squares)
    root = lax.rsqrt(squares / depth + ROOT_EPS)

    def share_block(which):
        lanes = at(tensor * half, half)
        if which == 0:
            return pltpu.make_async_copy(block, o_block.at[:, lanes], own_sem.at[1])
        return remote(block, o_block.at[:, lanes], share_s.at[0], share_r.at[0], tensor=here.other)

    share_block(0).start()
    share_block(1).start()

    def norm(index):
        rows = at(index * chunk, chunk)
        normed[rows, :] = (wide[rows, :] * root).astype(BF16)

    loop(0, depth // chunk, norm)
    inner, slope = gelu_parts(jnp.dot(mix_in[...], normed[...], preferred_element_type=F32))
    inner_low = inner.astype(BF16)
    next_rows[...] = (jnp.dot(mix_out[...], inner_low, preferred_element_type=F32) + static[...])[:MIXH]
    next_low = next_cot[...].astype(BF16)

    def nt(left, right):
        return lax.dot_general(left, right, (((1,), (1,)), ((), ())), preferred_element_type=F32)

    column = lax.broadcasted_iota(jnp.int32, (128, 128), 1)
    static_grad = jnp.sum(next_cot[...], axis=1, keepdims=True)
    tiny[...] = jnp.where(column == MIXH, static_grad, nt(inner_low, next_low))[:MIXH]
    inner_grad = (jnp.dot(mix_back[...], next_low, preferred_element_type=F32) * slope).astype(BF16)

    def pull(index, total):
        rows = at(index * chunk, chunk)
        value = jnp.dot(small[rows, :], inner_grad, preferred_element_type=F32)
        back[rows, :] = value
        return total + jnp.sum(value * wide[rows, :] * root, axis=0, keepdims=True)

    along = lax.fori_loop(0, depth // chunk, pull, jnp.zeros((1, half), F32)) / depth

    def finish(index):
        rows = at(index * chunk, chunk)
        value = cot[rows, :].astype(F32) + root * (back[rows, :] - wide[rows, :] * root * along)
        back[rows, :] = value
        low[rows, :] = value.astype(BF16)

    loop(0, depth // chunk, finish)

    def share(kind, index):
        if kind == 0:
            source, lanes, where = low, lane_block(half, here.near, here.core, tensor, 1), {"dp": flip(me, NEAR)}
        elif kind == 1:
            lanes = lane_block(half, 1 - here.near if index else here.near, here.core, tensor, 1)
            source, where = (o_grad.at[:, lanes] if index else low), {"tensor": here.other}
        else:
            lanes, where = lane_block(half, index, here.core, 0, 2), {"dp": flip(me, CORE)}
            source = o_grad.at[:, lanes]
        number = 1 + 2 * kind + index
        return remote(source, o_grad.at[:, lanes], share_s.at[number], share_r.at[number], **where)

    share(0, 0).start()
    share(1, 0).start()
    keep = pltpu.make_async_copy(
        low, o_grad.at[:, lane_block(half, here.near, here.core, tensor, 1)], own_sem.at[2]
    )
    keep.start()

    def mixin_rows(index):
        rows = at(index * chunk, chunk)
        mixin[rows, :] = nt(normed[rows, :], inner_grad)

    loop(0, depth // chunk, mixin_rows)
    share(0, 0).wait()
    share(1, 1).start()
    lanes = at(tensor * half, half)
    next_share = remote(next_rows, o_next.at[:, lanes], share_s.at[7], share_r.at[7], tensor=here.other)
    next_share.start()
    finals = [
        pltpu.make_async_copy(next_rows, o_next.at[:, lanes], own_sem.at[3]),
        pltpu.make_async_copy(back, o_wide, own_sem.at[4]),
        pltpu.make_async_copy(mixin, o_mixin, own_sem.at[5]),
        pltpu.make_async_copy(tiny, o_tiny, own_sem.at[6]),
    ]
    for copy in finals:
        copy.start()
    keep.wait()
    share(1, 0).wait()
    share(1, 1).wait()
    for near in range(2):
        share(2, near).start()
    for near in range(2):
        share(2, near).wait()
    share_block(0).wait()
    share_block(1).wait()
    next_share.wait()
    for copy in finals:
        copy.wait()


def join(part, streams, cot, small, mix_in, mix_out, mix_back, static, next_cot):
    depth, half = cot.shape
    spans = 4
    shapes = [
        ((depth, 8 * half), BF16),
        ((depth, half), F32),
        ((depth, 2 * half), BF16),
        ((MIXH, 2 * half), F32),
        ((depth, 128), F32),
        ((MIXH, 128), F32),
    ]
    return pl.pallas_call(
        join_kernel,
        out_shape=[jax.ShapeDtypeStruct(*shape) for shape in shapes],
        in_specs=[ANY, ANY] + [VM] * 7,
        out_specs=[ANY] * 6,
        scratch_shapes=[
            pltpu.VMEM((2, 2, depth, half), BF16),
            pltpu.VMEM((2, 2, depth, half), BF16),
            pltpu.VMEM((2, depth, half), BF16),
            pltpu.VMEM((depth, half), BF16),
            pltpu.VMEM((depth, half), BF16),
            pltpu.VMEM((depth, half), F32),
            pltpu.VMEM((depth, half), BF16),
            pltpu.VMEM((depth, half), BF16),
            pltpu.VMEM((depth, half), F32),
            pltpu.VMEM((depth, half), BF16),
            pltpu.VMEM((MIXH, half), F32),
            pltpu.VMEM((depth, 128), F32),
            pltpu.VMEM((MIXH, 128), F32),
            DMA((spans, 4)),
            DMA((spans, 4)),
            DMA((spans, 2)),
            DMA((spans, 2)),
            DMA((spans,)),
            DMA((spans,)),
            DMA((spans, 4)),
            DMA((8,)),
            DMA((8,)),
            DMA((7,)),
        ],
        compiler_params=pltpu.CompilerParams(
            collective_id=2, has_side_effects=True, vmem_limit_bytes=40 * 1024 * 1024
        ),
        name="join",
    )(part, streams, cot, small, mix_in, mix_out, mix_back, static, next_cot)


def scatter_kernel(
    n_dp, attn_grad, mlp_grad, streams, small, wide_grad, mixin_part, mix_tiny, hist, g_qkv, g_up, g_down, g_out,
    o_stream, o_mix, o_small, o_tiny, o_qkv, o_up, o_down, o_out,
    own, from_core, from_tensor, from_near, rows_in, wide, stream_grad, gains, biases, tiny, tiny_in, tiny_out,
    hist_in, arrived, mix_part, mix_in, mix_sum, tiny_sum, ring, side_in, mine, high_in,
    core_s, core_r, tensor_s, tensor_r, near_s, near_r, local, in_sem,
    side_s, side_r, side_local, high_s, high_r, peer_s, peer_r, peer_local,
    a2a_s, a2a_r, a2a_own, keep_sem, pass_s, pass_r, tiny_s, tiny_r, mix_s, mix_r, hist_sem,
    ring_s, ring_r, last_s, last_r, last_local,
):
    here = Place()
    me, tensor = here.me, here.tensor
    depth, half = wide_grad.shape
    rows = depth // n_dp
    high_bits = int(math.log2(n_dp // HIGH))
    chunk = min(256, depth)
    greet_all(n_dp, me, here.other)

    units = []
    for g, o in ((g_qkv, o_qkv), (g_up, o_up), (g_down, o_down), (g_out, o_out)):
        if len(o.shape) == 3:
            units += [(g.at[part], o.at[part], 0) for part in range(o.shape[0])]
        else:
            units += [(g, o, first) for first in range(0, g.shape[-1], UNIT)]
    total = len(units)

    def side_hop(unit):
        g, _, first = units[unit]
        return remote(
            g.at[:, :, 1 - here.side, :, pl.ds(first, UNIT)], side_in.at[unit], side_s.at[unit], side_r.at[unit],
            dp=flip(me, SIDE),
        )

    def side_load(unit):
        g, _, first = units[unit]
        return pltpu.make_async_copy(
            g.at[:, :, here.side, :, pl.ds(first, UNIT)], mine.at[unit], side_local.at[unit]
        )

    def high_hop(unit, phase):
        span = 1 << phase
        base = lax.div(here.high, span)
        theirs = base + 1 - 2 * lax.rem(base, 2)
        return remote(
            mine.at[unit, pl.ds(theirs * span, span)], high_in.at[unit, pl.ds(span - 1, span)],
            high_s.at[unit, phase], high_r.at[unit, phase], dp=flip(me, HIGH << phase),
        )

    def peer_hop(unit, peer):
        _, o, first = units[unit]
        target, _ = here.peers[peer]
        return remote(
            mine.at[unit, here.high, bit(target, NEAR), at(bit(target, CORE) * rows, rows)],
            o.at[:, at(here.quarter * (o.shape[-1] // QUARTERS) + first, UNIT)],
            peer_s.at[unit, peer], peer_r.at[unit, peer], dp=target,
        )

    def peer_keep(unit):
        _, o, first = units[unit]
        return pltpu.make_async_copy(
            mine.at[unit, here.high, here.near, at(here.core * rows, rows)],
            o.at[:, at(here.quarter * (o.shape[-1] // QUARTERS) + first, UNIT)], peer_local.at[unit],
        )

    def add_blocks(unit, other, first_mine, first_other, count):
        tall = 2 * rows
        step = min(64, tall)

        def add(flat):
            high, rest = lax.div(flat, 2 * (tall // step)), lax.rem(flat, 2 * (tall // step))
            near, span = lax.div(rest, tall // step), at(lax.rem(rest, tall // step) * step, step)
            mine[unit, first_mine + high, near, span] += other[unit, first_other + high, near, span]

        loop(0, count * 2 * (tall // step), add)

    def side_start(unit):
        side_hop(unit).start()
        side_load(unit).start()

    def finish_high(unit):
        for phase in reversed(range(high_bits)):
            high_hop(unit, phase).wait()
            span = 1 << phase
            add_blocks(unit, high_in, lax.div(here.high, span) * span, span - 1, span)
            if phase:
                high_hop(unit, phase - 1).start()
        peer_keep(unit).start()
        for peer in range(3):
            peer_hop(unit, peer).start()

    def tick(unit):
        side_load(unit).wait()
        side_hop(unit).wait()
        if unit + 2 < total:
            side_start(unit + 2)
        add_blocks(unit, side_in, 0, 0, n_dp // HIGH)
        if unit:
            finish_high(unit - 1)
        high_hop(unit, high_bits - 1).start()

    done = 0

    def ticks(count):
        nonlocal done
        for unit in range(done, min(done + count, total)):
            tick(unit)
        done = min(done + count, total)

    def load(stream, near, half_at):
        part = attn_grad.at[stream] if stream < 3 else mlp_grad
        return pltpu.make_async_copy(
            part.at[:, lane_block(half, near, here.core, half_at, 1)], own.at[stream, near, half_at],
            local.at[stream, near * 2 + half_at],
        )

    def to_core(stream, near, half_at):
        part = attn_grad.at[stream] if stream < 3 else mlp_grad
        return remote(
            part.at[:, lane_block(half, near, 1 - here.core, half_at, 1)], from_core.at[stream, near, half_at],
            core_s.at[stream, near * 2 + half_at], core_r.at[stream, near * 2 + half_at], dp=flip(me, CORE),
        )

    def to_tensor(stream, near):
        return remote(
            own.at[stream, near, here.other], from_tensor.at[stream, near],
            tensor_s.at[stream, near], tensor_r.at[stream, near], tensor=here.other,
        )

    def to_near(stream):
        return remote(
            from_tensor.at[stream, 1 - here.near], from_near.at[stream], near_s.at[stream], near_r.at[stream],
            dp=flip(me, NEAR),
        )

    def after_core(stream):
        for near in range(2):
            for half_at in range(2):
                load(stream, near, half_at).wait()
                to_core(stream, near, half_at).wait()

        def add(index):
            span = at(index * chunk, chunk)
            for near in range(2):
                for half_at in range(2):
                    own[stream, near, half_at, span] += from_core[stream, near, half_at, span]

        loop(0, depth // chunk, add)

    def after_tensor(stream):
        for near in range(2):
            to_tensor(stream, near).wait()

        def add(index):
            span = at(index * chunk, chunk)
            for near in range(2):
                from_tensor[stream, near, span] += own[stream, near, tensor, span]

        loop(0, depth // chunk, add)
        to_near(stream).start()

    stats = []

    def measure(stream):
        def piece(index):
            return rows_in[stream, at(index * chunk, chunk), :].astype(F32)

        centre = sum_rows(piece, depth, chunk, lambda v: v) / depth
        spread = sum_rows(piece, depth, chunk, lambda v: (v - centre) * (v - centre)) / depth
        stats.append((centre, lax.rsqrt(spread + NORM_EPS)))

    def back_norm(stream):
        to_near(stream).wait()
        group = 0 if stream < 3 else 1
        centre, root = stats[stream]

        def parts(index):
            span = at(index * chunk, chunk)
            grad = from_tensor[stream, here.near, span].astype(F32) + from_near[stream, span].astype(F32)
            hat = (rows_in[stream, span, :].astype(F32) - centre) * root
            gain = small[span, MIXH + group : MIXH + group + 1].astype(F32)
            return span, grad, hat, grad * gain

        def sums(index, carry):
            span, grad, hat, scaled = parts(index)
            if stream in (0, 3):
                gains[group, span] = grad * hat
                biases[group, span] = grad
            else:
                gains[group, span] += grad * hat
                biases[group, span] += grad
            return (
                carry[0] + jnp.sum(scaled, axis=0, keepdims=True),
                carry[1] + jnp.sum(scaled * hat, axis=0, keepdims=True),
            )

        zero = jnp.zeros((1, half), F32)
        whole, along = lax.fori_loop(0, depth // chunk, sums, (zero, zero))

        def finish(index):
            span, _, hat, scaled = parts(index)
            value = root * (scaled - whole / depth - hat * (along / depth))
            if stream == 3:
                value = value + wide[span, :]
            stream_grad[stream, span] = value.astype(BF16)

        loop(0, depth // chunk, finish)
        loop(1, n_dp, lambda step: send(stream, step).start())
        send_own(stream).start()

    def send(stream, step):
        target = lax.rem(me + step, n_dp)
        return remote(
            stream_grad.at[stream, at(target * rows, rows), :], arrived.at[stream, step],
            a2a_s.at[stream, step], a2a_r.at[stream, step], dp=target,
        )

    def send_own(stream):
        return pltpu.make_async_copy(
            stream_grad.at[stream, at(me * rows, rows), :], arrived.at[stream, 0], a2a_own.at[stream]
        )

    def source_of(step):
        return lax.rem(me - step + n_dp, n_dp)

    def lanes_of(step):
        return at(source_of(step) * 2 * half + tensor * half, half)

    def fetch(step):
        return pltpu.make_async_copy(hist.at[:, :, lanes_of(step)], hist_in.at[step], hist_sem.at[step])

    def keep(stream, step):
        return pltpu.make_async_copy(
            arrived.at[stream, step], o_stream.at[stream, :, lanes_of(step)], keep_sem.at[stream, step]
        )

    def pass_on(stream, step):
        return remote(
            arrived.at[stream, step], o_stream.at[stream, :, lanes_of(step)],
            pass_s.at[stream, step], pass_r.at[stream, step], tensor=here.other,
        )

    def mix_send(step):
        return remote(mix_part.at[step], mix_in.at[step], mix_s.at[step], mix_r.at[step], dp=source_of(step))

    def receive(stream):
        send_own(stream).wait()

        def one(step):
            @pl.when(step > 0)
            def _():
                send(stream, step).wait()

            keep(stream, step).start()
            pass_on(stream, step).start()
            if stream == 0:
                fetch(step).wait()
            totals = [jnp.zeros((8, half), F32) for _ in range(HIST)]
            for row in range(0, rows, 16):
                span = pl.ds(row, 16)
                grad = arrived[stream, step, span, :].astype(F32)
                for source in range(HIST):
                    product = grad * hist_in[step, source, span, :].astype(F32)
                    totals[source] = totals[source] + product[:8] + product[8:]
            for source in range(HIST):
                mix_part[step, pl.ds(stream * HIST + source, 1), :] = jnp.sum(totals[source], axis=0, keepdims=True)
            if stream == STREAMS - 1:

                @pl.when(step > 0)
                def _():
                    mix_send(step).start()

        loop(0, n_dp, one)

    ring_targets = [{"dp": flip(me, value)} for value in (CORE, SIDE, NEAR)]
    ring_targets += [{"dp": flip(me, HIGH << phase)} for phase in range(high_bits)]
    ring_targets.append({"tensor": here.other})
    hops = len(ring_targets)

    def ring_hop(hop):
        return remote(ring.at[hop, 0], ring.at[hop, 1], ring_s.at[hop], ring_r.at[hop], **ring_targets[hop])

    def ring_step(hop):
        ring_hop(hop).wait()
        ring[hop + 1, 0] = ring[hop, 0] + ring[hop, 1]
        if hop + 1 < hops:
            ring_hop(hop + 1).start()

    side_start(0)
    for stream in range(STREAMS):
        for near in range(2):
            for half_at in range(2):
                to_core(stream, near, half_at).start()
                load(stream, near, half_at).start()
        if stream == 0:
            side_start(1)
    loads = [
        pltpu.make_async_copy(streams, rows_in, in_sem.at[0]),
        pltpu.make_async_copy(wide_grad, wide, in_sem.at[1]),
        pltpu.make_async_copy(mix_tiny, ring.at[0, 0], in_sem.at[2]),
    ]
    for copy in loads:
        copy.start()
    after_core(0)
    for near in range(2):
        to_tensor(0, near).start()
    for copy in loads:
        copy.wait()
    ring_hop(0).start()
    loop(0, n_dp, lambda step: fetch(step).start())
    mix_part[...] = jnp.zeros_like(mix_part)
    for stream in range(STREAMS):
        measure(stream)
    for stream in range(1, STREAMS):
        after_core(stream)
    ring_step(0)
    for stream in range(STREAMS):
        ticks(2)
        after_tensor(stream)
        if stream + 1 < STREAMS:
            for near in range(2):
                to_tensor(stream + 1, near).start()
            if stream + 1 < hops:
                ring_step(stream + 1)
        if stream > 0:
            back_norm(stream - 1)
        if stream > 1:
            receive(stream - 2)
    back_norm(STREAMS - 1)

    column = lax.broadcasted_iota(jnp.int32, (chunk, 128), 1)
    pltpu.make_async_copy(mixin_part, wide, in_sem.at[0]).start()
    pltpu.make_async_copy(mixin_part, wide, in_sem.at[0]).wait()

    def gather_tiny(index):
        span = at(index * chunk, chunk)
        value = wide[span, :]
        for group in range(2):
            gain = jnp.sum(gains[group, span], axis=1, keepdims=True)
            bias = jnp.sum(biases[group, span], axis=1, keepdims=True)
            value = jnp.where(column == MIXH + group, gain, value)
            value = jnp.where(column == MIXH + 2 + group, bias, value)
        tiny[span, :] = value.astype(BF16)

    loop(0, depth // chunk, gather_tiny)

    def tiny_send(step):
        target = lax.rem(me + step, n_dp)
        return remote(tiny.at[at(target * rows, rows), :], tiny_in.at[step], tiny_s.at[step], tiny_r.at[step], dp=target)

    loop(1, n_dp, lambda step: tiny_send(step).start())
    receive(2)
    ticks(2)
    receive(3)
    for hop in range(STREAMS, hops):
        ring_step(hop)
    tiny_final = pltpu.make_async_copy(ring.at[hops, 0], o_tiny, last_local.at[0])
    tiny_final.start()
    ticks(total)

    tiny_sum[0] = tiny[at(me * rows, rows), :].astype(F32)

    def add_tiny(step):
        tiny_send(step).wait()
        tiny_sum[0] += tiny_in[step].astype(F32)

    loop(1, n_dp, add_tiny)
    tiny_share = remote(tiny_sum.at[0], tiny_sum.at[1], last_s.at[1], last_r.at[1], tensor=here.other)
    tiny_share.start()
    mix_sum[...] = mix_part[0]

    def add_mix(step):
        mix_send(step).wait()
        mix_sum[...] += mix_in[step]

    loop(1, n_dp, add_mix)
    lanes = at(tensor * half, half)
    mix_share = remote(mix_sum, o_mix.at[:, lanes], last_s.at[0], last_r.at[0], tensor=here.other)
    mix_keep = pltpu.make_async_copy(mix_sum, o_mix.at[:, lanes], last_local.at[1])
    mix_share.start()
    mix_keep.start()
    finish_high(total - 1)
    tiny_share.wait()
    tiny_out[...] = tiny_sum[0] + tiny_sum[1]
    tiny_keep = pltpu.make_async_copy(tiny_out, o_small, last_local.at[2])
    tiny_keep.start()
    for unit in range(total):
        peer_keep(unit).wait()
        for peer in range(3):
            peer_hop(unit, peer).wait()

    def settle(step):
        for stream in range(STREAMS):
            keep(stream, step).wait()
            pass_on(stream, step).wait()

    loop(0, n_dp, settle)
    mix_share.wait()
    mix_keep.wait()
    tiny_keep.wait()
    tiny_final.wait()


def scatter(
    n_dp, attn_grad, mlp_grad, streams, small, wide_grad, mixin_part, mix_tiny, hist, g_qkv, g_up, g_down, g_out
):
    depth, half = wide_grad.shape
    rows = depth // n_dp
    high = n_dp // HIGH
    high_bits = int(math.log2(high))
    grads = (g_qkv, g_up, g_down, g_out)
    units = sum(g.size for g in grads) // depth // UNIT
    hops = high_bits + 4

    outs = [
        ((STREAMS, rows, 2 * half * n_dp), BF16),
        ((MIXH, 2 * half), F32),
        ((rows, 128), F32),
        (mix_tiny.shape, F32),
    ] + [((3,) * (g.ndim == 6) + (rows, QUARTERS * g.shape[-1]), BF16) for g in grads]
    return pl.pallas_call(
        functools.partial(scatter_kernel, n_dp),
        out_shape=[jax.ShapeDtypeStruct(*shape) for shape in outs],
        in_specs=[ANY, ANY, ANY, VM, ANY, ANY, ANY, ANY] + [ANY] * 4,
        out_specs=[ANY] * 8,
        scratch_shapes=[
            pltpu.VMEM((STREAMS, 2, 2, depth, half), BF16),
            pltpu.VMEM((STREAMS, 2, 2, depth, half), BF16),
            pltpu.VMEM((STREAMS, 2, depth, half), BF16),
            pltpu.VMEM((STREAMS, depth, half), BF16),
            pltpu.VMEM((STREAMS, depth, half), BF16),
            pltpu.VMEM((depth, half), F32),
            pltpu.VMEM((STREAMS, depth, half), BF16),
            pltpu.VMEM((2, depth, half), F32),
            pltpu.VMEM((2, depth, half), F32),
            pltpu.VMEM((depth, 128), BF16),
            pltpu.VMEM((n_dp, rows, 128), BF16),
            pltpu.VMEM((rows, 128), F32),
            pltpu.VMEM((n_dp, HIST, rows, half), BF16),
            pltpu.VMEM((STREAMS, n_dp, rows, half), BF16),
            pltpu.VMEM((n_dp, MIXH, half), F32),
            pltpu.VMEM((n_dp, MIXH, half), F32),
            pltpu.VMEM((MIXH, half), F32),
            pltpu.VMEM((2, rows, 128), F32),
            pltpu.VMEM((hops + 1, 2) + mix_tiny.shape, F32),
            pltpu.VMEM((units, high, 2, 2 * rows, UNIT), BF16),
            pltpu.VMEM((units, high, 2, 2 * rows, UNIT), BF16),
            pltpu.VMEM((units, high - 1, 2, 2 * rows, UNIT), BF16),
            DMA((STREAMS, 4)),
            DMA((STREAMS, 4)),
            DMA((STREAMS, 2)),
            DMA((STREAMS, 2)),
            DMA((STREAMS,)),
            DMA((STREAMS,)),
            DMA((STREAMS, 4)),
            DMA((3,)),
            DMA((units,)),
            DMA((units,)),
            DMA((units,)),
            DMA((units, high_bits)),
            DMA((units, high_bits)),
            DMA((units, 3)),
            DMA((units, 3)),
            DMA((units,)),
            DMA((STREAMS, n_dp)),
            DMA((STREAMS, n_dp)),
            DMA((STREAMS,)),
            DMA((STREAMS, n_dp)),
            DMA((STREAMS, n_dp)),
            DMA((STREAMS, n_dp)),
            DMA((n_dp,)),
            DMA((n_dp,)),
            DMA((n_dp,)),
            DMA((n_dp,)),
            DMA((n_dp,)),
            DMA((hops,)),
            DMA((hops,)),
            DMA((2,)),
            DMA((2,)),
            DMA((3,)),
        ],
        compiler_params=pltpu.CompilerParams(
            collective_id=3, has_side_effects=True, vmem_limit_bytes=62 * 1024 * 1024
        ),
        name="scatter",
    )(attn_grad, mlp_grad, streams, small, wide_grad, mixin_part, mix_tiny, hist, *grads)


def exact_gelu(values):
    return jax.nn.gelu(values, approximate=False)


def rotary_tables(length, rotary, float_type):
    half_rot = rotary // 2
    places = jnp.arange(length).astype(float_type)
    frequency = jnp.exp(
        jnp.arange(half_rot).astype(float_type) * (-2.0 * math.log(10000.0) / rotary)
    )
    angles = places[:, None] * frequency[None, :]
    return (jnp.cos(angles), jnp.sin(angles))


def rotate(values, cos_table, sin_table):
    half_rot = cos_table.shape[-1]
    first_half = values[..., :half_rot]
    second = values[..., half_rot : 2 * half_rot]
    return jnp.concatenate(
        [
            first_half * cos_table - second * sin_table,
            second * cos_table + first_half * sin_table,
            values[..., 2 * half_rot :],
        ],
        axis=-1,
    )


def masked_scores(queries, key_rows):
    length = queries.shape[1]
    score_scale = 1.0 / math.sqrt(queries.shape[2])
    causal = lax.broadcasted_iota(jnp.int32, (length, length), 0) >= lax.broadcasted_iota(
        jnp.int32, (length, length), 1
    )
    scores = (
        jnp.einsum("hqd,hkd->hqk", queries, key_rows, preferred_element_type=jnp.float32)
        * score_scale
    )
    return (jnp.where(causal[None], scores, MASKED), score_scale)


def attend_forward(queries, key_rows, value_rows):
    scores, score_scale = masked_scores(queries, key_rows)
    row_peak = jnp.max(scores, axis=-1, keepdims=True)
    raised = jnp.exp(scores - row_peak)
    row_total = jnp.sum(raised, axis=-1, keepdims=True)
    prob_low = (raised / row_total).astype(jnp.bfloat16)
    context = jnp.einsum("hqk,hkd->hqd", prob_low, value_rows, preferred_element_type=jnp.float32)
    return (context.astype(jnp.bfloat16), row_peak + jnp.log(row_total))


def attend_backward(queries, key_rows, value_rows, log_sum, context_grad):
    scores, score_scale = masked_scores(queries, key_rows)
    attn_prob = jnp.exp(scores - log_sum)
    prob_low = attn_prob.astype(jnp.bfloat16)
    value_grad = jnp.einsum(
        "hqk,hqd->hkd", prob_low, context_grad, preferred_element_type=jnp.float32
    )
    prob_grad = jnp.einsum(
        "hqd,hkd->hqk", context_grad, value_rows, preferred_element_type=jnp.float32
    )
    inner_sum = jnp.sum(attn_prob * prob_grad, axis=-1, keepdims=True)
    score_grad = (attn_prob * (prob_grad - inner_sum)).astype(jnp.bfloat16)
    query_grad = (
        jnp.einsum("hqk,hkd->hqd", score_grad, key_rows, preferred_element_type=jnp.float32)
        * score_scale
    )
    key_grad = (
        jnp.einsum("hqk,hqd->hkd", score_grad, queries, preferred_element_type=jnp.float32)
        * score_scale
    )
    return (query_grad, key_grad, value_grad)


def per_device(
    n_dp, history, mix_weights, w_qkv, w_out, w_up, w_down, norm_gain, norm_bias, mix_in, mix_out, mix_static,
    out_cot, next_cot,
):
    tensor = lax.axis_index("tensor")
    seq_len = mix_weights.shape[0]
    half = seq_len // 2
    depth = mix_in.shape[0] * n_dp

    def own_half(rows):
        return lax.dynamic_slice_in_dim(rows, tensor * half, half, 0)

    mix_rows = jnp.pad(own_half(mix_weights.reshape(seq_len, -1)).T, ((0, MIXH - STREAMS * HIST), (0, 0)))
    small = jnp.concatenate([mix_in, norm_gain.T, norm_bias.T], axis=1)
    small = jnp.pad(small, ((0, 0), (0, 128 - small.shape[1])))
    mix_all, small_all, streams, act, qkv, up, down, out = gather(
        n_dp, history, mix_rows, small, w_qkv, w_up, w_down, w_out
    )
    small_all = small_all.reshape(depth, 128)
    qkv, up, down, out = (
        qkv.reshape(3, depth, -1), up.reshape(depth, -1), down.reshape(depth, -1), out.reshape(depth, -1)
    )
    tokens = act.shape[2]
    seqs = tokens // seq_len
    heads = qkv.shape[2] // HD
    projected = jnp.einsum("sdt,sde->ste", act[:3], qkv, preferred_element_type=F32)
    head_rows = jnp.transpose(projected.reshape(3, seqs, seq_len, heads, HD), (0, 1, 3, 2, 4)).reshape(
        3, seqs * heads, seq_len, HD
    )
    cos_table, sin_table = rotary_tables(seq_len, ROT, F32)
    queries = rotate(head_rows[0], cos_table, sin_table).astype(BF16)
    key_rows = rotate(head_rows[1], cos_table, sin_table).astype(BF16)
    value_rows = head_rows[2].astype(BF16)
    context, log_sum = attend_forward(queries, key_rows, value_rows)

    def join_heads(rows):
        return jnp.transpose(rows.reshape(seqs, heads, seq_len, HD), (0, 2, 1, 3)).reshape(tokens, heads * HD)

    context_rows = join_heads(context)
    up_pre = jnp.einsum("dt,df->tf", act[3], up, preferred_element_type=F32)
    hidden_wide, gelu_back = jax.vjp(exact_gelu, up_pre)
    hidden = hidden_wide.astype(BF16)
    part = (
        jnp.einsum("de,te->dt", out, context_rows, preferred_element_type=F32)
        + jnp.einsum("df,tf->dt", down, hidden, preferred_element_type=F32)
    ).astype(BF16)

    def square(values):
        return jnp.pad(values, ((0, 128 - values.shape[0]), (0, 128 - values.shape[1])))

    next_rows = own_half(next_cot.reshape(seq_len, -1)).T
    next_rows = jnp.pad(next_rows, ((0, 128 - next_rows.shape[0]), (0, 0)))
    mix_in_rows = jnp.pad(small_all[:, :MIXH].T, ((0, 128 - MIXH), (0, 0)))
    static = jnp.pad(mix_static[:, None], ((0, 128 - mix_static.shape[0]), (0, 0)))
    branch_grad, wide_grad, block, next_mix, mixin_part, tiny = join(
        part, streams, own_half(out_cot).T, small_all, mix_in_rows, square(mix_out.T), square(mix_out), static,
        next_rows,
    )
    hidden_grad = jnp.einsum("dt,df->tf", branch_grad, down, preferred_element_type=F32)
    up_grad_low = gelu_back(hidden_grad)[0].astype(BF16)
    mlp_in_grad = jnp.einsum("df,tf->dt", up, up_grad_low, preferred_element_type=F32).astype(BF16)
    context_grad_rows = jnp.einsum("dt,de->te", branch_grad, out, preferred_element_type=F32).astype(BF16)
    context_grad = jnp.transpose(context_grad_rows.reshape(seqs, seq_len, heads, HD), (0, 2, 1, 3)).reshape(
        seqs * heads, seq_len, HD
    )
    query_grad, key_grad, value_grad = attend_backward(queries, key_rows, value_rows, log_sum, context_grad)
    proj_grad = jnp.stack(
        [
            join_heads(rotate(query_grad, cos_table, -sin_table).astype(BF16)),
            join_heads(rotate(key_grad, cos_table, -sin_table).astype(BF16)),
            join_heads(value_grad.astype(BF16)),
        ]
    )
    attn_in_grad = jnp.einsum("sde,ste->sdt", qkv, proj_grad, preferred_element_type=F32).astype(BF16)
    g_qkv = jnp.einsum("sdt,ste->sde", act[:3], proj_grad, preferred_element_type=F32).astype(BF16)
    g_out = jnp.einsum("dt,te->de", branch_grad, context_rows, preferred_element_type=F32).astype(BF16)
    g_up = jnp.einsum("dt,tf->df", act[3], up_grad_low, preferred_element_type=F32).astype(BF16)
    g_down = jnp.einsum("dt,tf->df", branch_grad, hidden, preferred_element_type=F32).astype(BF16)
    grid = (n_dp // HIGH, 2, 2, 2 * mix_in.shape[0])
    stream_grad, mix_grad, small_total, tiny, qkv_total, up_total, down_total, out_total = scatter(
        n_dp, attn_in_grad, mlp_in_grad, streams, small_all, wide_grad, mixin_part, tiny, history,
        g_qkv.reshape((3,) + grid + (-1,)), g_up.reshape(grid + (-1,)), g_down.reshape(grid + (-1,)),
        g_out.reshape(grid + (-1,)),
    )
    mix_rows = jnp.transpose(mix_all.reshape(2, n_dp, MIXH, half), (2, 1, 0, 3)).reshape(MIXH, n_dp * seq_len)
    history_grad = jnp.stack(
        [
            sum(
                mix_rows[stream * HIST + source][None, :] * stream_grad[stream].astype(F32)
                for stream in range(STREAMS)
            )
            for source in range(HIST)
        ]
    ).astype(BF16)
    return (
        block.T,
        next_mix.T.reshape(seq_len, STREAMS, NEXT),
        history_grad,
        mix_grad[: STREAMS * HIST].T.reshape(seq_len, STREAMS, HIST),
        qkv_total.astype(F32),
        out_total.astype(F32),
        up_total.astype(F32),
        down_total.astype(F32),
        small_total[:, MIXH : MIXH + 2].T,
        small_total[:, MIXH + 2 : MIXH + 4].T,
        small_total[:, :MIXH],
        tiny[:, : STREAMS * NEXT],
        tiny[: STREAMS * NEXT, MIXH],
    )


def solution(mesh):
    return jax.shard_map(
        functools.partial(per_device, mesh.shape["dp"]),
        mesh=mesh,
        in_specs=(
            P(None, "dp", None),
            P("dp", None, None),
            P(None, "dp", "tensor"),
            P("dp", "tensor"),
            P("dp", "tensor"),
            P("dp", "tensor"),
            P(None, "dp"),
            P(None, "dp"),
            P("dp", None),
            P(),
            P(),
            P("dp", None),
            P("dp", None, None),
        ),
        out_specs=(
            P("dp", None),
            P("dp", None, None),
            P(None, "dp", None),
            P("dp", None, None),
            P(None, "dp", "tensor"),
            P("dp", "tensor"),
            P("dp", "tensor"),
            P("dp", "tensor"),
            P(None, "dp"),
            P(None, "dp"),
            P("dp", None),
            P(),
            P(),
        ),
        check_vma=False,
    )
```

```python
import functools
import math

import jax
import jax.numpy as jnp
from jax import lax
from jax.experimental import pallas as pl
from jax.experimental.pallas import tpu as pltpu
from jax.sharding import PartitionSpec as P

HD = 128
ROT = 32
HIST = 9
STREAMS = 4
NEXT = 10
MIXH = 40

NORM_EPS = 1e-05
ROOT_EPS = 1e-06
MASKED = -1e30

MESH = pl.DeviceIdType.MESH
ANY = pl.BlockSpec(memory_space=pltpu.HBM)
VM = pl.BlockSpec(memory_space=pltpu.VMEM)
DMA = pltpu.SemaphoreType.DMA
F32, BF16 = jnp.float32, jnp.bfloat16
CORE, SIDE, NEAR, HIGH = 1, 2, 4, 8
QUARTERS = 4
UNIT = 256
PLAN = (
    "T", "T", "n0", "T", "T", "n1", "T", "T", "n2", "s0", "T", "n3", "t0", "s1", "w0", "p0", "T", "t1", "s2", "p1",
    "T", "t2", "s3", "p2", "t3", "a0", "u0",
)


def bit(place, value):
    return lax.rem(lax.div(place, value), 2)


def flip(place, value):
    return place + value - 2 * value * bit(place, value)


def at(start, size, multiple=None):
    return pl.ds(pl.multiple_of(start, size if multiple is None else multiple), size)


def remote(src, dst, send, recv, **where):
    return pltpu.make_async_remote_copy(
        src_ref=src, dst_ref=dst, send_sem=send, recv_sem=recv, device_id=where, device_id_type=MESH
    )


def loop(lower, upper, step):
    def body(index, carry):
        step(index)
        return carry

    lax.fori_loop(lower, upper, body, 0)


def greet(targets):
    barrier = pltpu.get_barrier_semaphore()
    for target in targets:
        pl.semaphore_signal(barrier, inc=1, device_id=target, device_id_type=MESH)
    pl.semaphore_wait(barrier, len(targets))


def greet_all(n_dp, me, other_tensor):
    barrier = pltpu.get_barrier_semaphore()
    loop(
        1,
        n_dp,
        lambda step: pl.semaphore_signal(
            barrier, inc=1, device_id={"dp": lax.rem(me + step, n_dp)}, device_id_type=MESH
        ),
    )
    pl.semaphore_signal(barrier, inc=1, device_id={"tensor": other_tensor}, device_id_type=MESH)
    pl.semaphore_wait(barrier, n_dp)


class Place:
    def __init__(self):
        self.me = lax.axis_index("dp")
        self.tensor = lax.axis_index("tensor")
        self.other = 1 - self.tensor
        self.core = bit(self.me, CORE)
        self.side = bit(self.me, SIDE)
        self.near = bit(self.me, NEAR)
        self.high = lax.div(self.me, HIGH)
        self.quarter = self.near * 2 + self.core
        self.peers = (
            (flip(self.me, CORE), self.near * 2 + 1 - self.core),
            (flip(self.me, NEAR), (1 - self.near) * 2 + self.core),
            (flip(flip(self.me, NEAR), CORE), (1 - self.near) * 2 + 1 - self.core),
        )


def sum_rows(ref_at, depth, chunk, of):
    def body(index, total):
        return total + jnp.sum(of(ref_at(index)), axis=0, keepdims=True)

    return lax.fori_loop(0, depth // chunk, body, jnp.zeros((1, 128), F32))


def gelu_parts(values):
    phi = 0.5 * (1.0 + lax.erf(values * (1.0 / math.sqrt(2.0))))
    density = jnp.exp(-0.5 * values * values) * (1.0 / math.sqrt(2.0 * math.pi))
    return values * phi, phi + values * density


def tn(left, right):
    return lax.dot_general(left, right, (((0,), (0,)), ((), ())), preferred_element_type=F32)


def nt(left, right):
    return lax.dot_general(left, right, (((1,), (1,)), ((), ())), preferred_element_type=F32)


def nn(left, right):
    return jnp.dot(left, right, preferred_element_type=F32)


def turned(values, cos, sin):
    pieces = []
    half_rot = ROT // 2
    repeats = values.shape[1] // cos.shape[1]
    cos, sin = (jnp.concatenate([table] * repeats, axis=1) for table in (cos, sin))
    for head in range(values.shape[0] // HD):
        rows = values[head * HD : (head + 1) * HD]
        first, second = rows[:half_rot], rows[half_rot:ROT]
        pieces += [first * cos - second * sin, second * cos + first * sin, rows[ROT:]]
    return jnp.concatenate(pieces, axis=0)


def causal_scores(keys, queries):
    scores = tn(keys, queries) * (1.0 / math.sqrt(HD))
    length = scores.shape[0]
    key = lax.broadcasted_iota(jnp.int32, (length, length), 0)
    query = lax.broadcasted_iota(jnp.int32, (length, length), 1)
    return jnp.where(query >= key, scores, MASKED)


def gather_kernel(
    n_dp, hist, mix, small, w_qkv, w_out, w_up, w_down, cos, sin,
    o_mix, o_small, o_streams, o_act, o_qkv, o_out, o_up, o_down,
    o_rows, o_context, o_sums, o_hidden, o_slope, o_part,
    mix_all, small_all, hist_in, mixed, streams, act,
    early_s, early_r, hist_sem, a2a_s, a2a_r, reshard_s, reshard_r, high_s, high_r, side_s, side_r,
    act_s, act_r, act_local, own_sem, out_sem, share_s, share_r, share_l,
    act_in, qkv_in, out_in, up_in, down_in, rows_out, context, sums, hidden, slope, part, load_sem, save_sem,
):
    here = Place()
    me, tensor = here.me, here.tensor
    rows = small.shape[0]
    depth = rows * n_dp
    half = hist.shape[2] // n_dp // 2
    high_bits = int(math.log2(n_dp // HIGH))
    weights = ((w_qkv, o_qkv), (w_out, o_out), (w_up, o_up), (w_down, o_down))
    greet_all(n_dp, me, here.other)

    def early(which, buf, phase):
        if phase == 0:
            block, target = buf.at[here.high, here.near, here.side, here.core], flip(me, NEAR)
        elif phase <= high_bits:
            span = 1 << (phase - 1)
            block = buf.at[pl.ds(lax.div(here.high, span) * span, span), :, here.side, here.core]
            target = flip(me, HIGH << (phase - 1))
        elif phase == high_bits + 1:
            block, target = buf.at[:, :, here.side, here.core], flip(me, SIDE)
        else:
            block, target = buf.at[:, :, :, here.core], flip(me, CORE)
        return remote(block, block, early_s.at[which, phase], early_r.at[which, phase], dp=target)

    own = [
        pltpu.make_async_copy(mix, mix_all.at[here.high, here.near, here.side, here.core], own_sem.at[0]),
        pltpu.make_async_copy(small, small_all.at[here.high, here.near, here.side, here.core], own_sem.at[1]),
    ]
    units = []
    for w, o in weights:
        if len(w.shape) == 3:
            units += [(w.at[part], o.at[part], 0) for part in range(w.shape[0])]
        else:
            units += [(w, o, first) for first in range(0, o.shape[-1], UNIT)]

    def cut(unit, quarter):
        w, o, first = units[unit]
        return w.at[:, at(quarter * o.shape[-1] + first, UNIT)]

    def slot(unit):
        _, o, first = units[unit]
        mine = pl.ds(pl.multiple_of(here.core * rows, rows), rows)
        return o.at[here.high, here.near, here.side, mine, pl.ds(first, UNIT)]

    def keep(unit):
        return pltpu.make_async_copy(cut(unit, here.quarter), slot(unit), own_sem.at[2 + unit])

    def reshard(unit, peer):
        target, quarter = here.peers[peer]
        return remote(cut(unit, quarter), slot(unit), reshard_s.at[unit, peer], reshard_r.at[unit, peer], dp=target)

    def high_hop(unit, phase):
        _, o, first = units[unit]
        span = 1 << phase
        block = o.at[pl.ds(lax.div(here.high, span) * span, span), :, here.side, :, pl.ds(first, UNIT)]
        return remote(block, block, high_s.at[unit, phase], high_r.at[unit, phase], dp=flip(me, HIGH << phase))

    def side_hop(unit):
        _, o, first = units[unit]
        block = o.at[:, :, here.side, :, pl.ds(first, UNIT)]
        return remote(block, block, side_s.at[unit], side_r.at[unit], dp=flip(me, SIDE))

    def fetch(step, buf):
        target = lax.rem(me + step, n_dp)
        return pltpu.make_async_copy(
            hist.at[:, :, at(target * 2 * half + tensor * half, half)], hist_in.at[buf], hist_sem.at[buf]
        )

    def send(step):
        target = lax.rem(me + step, n_dp)
        return remote(
            mixed.at[step], streams.at[:, at(me * rows, rows), :], a2a_s.at[step], a2a_r.at[step], dp=target
        )

    fetch(0, 0).start()

    def mix_step(step):
        buf = lax.rem(step, 2)

        @pl.when(step + 1 < n_dp)
        def _():
            fetch(step + 1, 1 - buf).start()

        fetch(step, buf).wait()
        target = lax.rem(me + step, n_dp)
        weight = mix_all[lax.div(target, HIGH), bit(target, NEAR), bit(target, SIDE), bit(target, CORE)]
        for row in range(0, rows, 32):
            part = pl.ds(row, 32)
            sources = [hist_in[buf, source, part, :].astype(F32) for source in range(HIST)]
            for stream in range(STREAMS):
                total = sum(
                    sources[source] * weight[stream * HIST + source][None, :] for source in range(HIST)
                )
                mixed[step, stream, part, :] = total.astype(BF16)

        @pl.when(step > 0)
        def _():
            send(step).start()

    chunk = min(256, depth)

    def lanes(near, core, half_at, count):
        return at(near * 4 * half + core * 2 * half + half_at * half, count * half, half)

    def act_keep(stream):
        return pltpu.make_async_copy(
            act.at[stream], o_act.at[stream, :, lanes(here.near, here.core, tensor, 1)], act_local.at[stream]
        )

    def act_near(stream):
        return remote(
            act.at[stream], o_act.at[stream, :, lanes(here.near, here.core, tensor, 1)],
            act_s.at[0, stream], act_r.at[0, stream], dp=flip(me, NEAR),
        )

    def act_tensor(stream, second):
        span = lanes(1 - here.near if second else here.near, here.core, tensor, 1)
        return remote(
            o_act.at[stream, :, span] if second else act.at[stream], o_act.at[stream, :, span],
            act_s.at[1 + second, stream], act_r.at[1 + second, stream], tensor=here.other,
        )

    def act_core(stream, near):
        span = lanes(near, here.core, 0, 2)
        return remote(
            o_act.at[stream, :, span], o_act.at[stream, :, span],
            act_s.at[3 + near, stream], act_r.at[3 + near, stream], dp=flip(me, CORE),
        )

    def normalise_stream(stream):
        block = 0 if stream < 3 else 1

        def piece(index):
            return streams[stream, at(index * chunk, chunk), :].astype(F32)

        centre = sum_rows(piece, depth, chunk, lambda v: v) / depth
        spread = sum_rows(piece, depth, chunk, lambda v: (v - centre) * (v - centre)) / depth
        root = lax.rsqrt(spread + NORM_EPS)

        def normalise(index):
            span = chunk // rows
            first = index * span
            column = jnp.concatenate(
                [
                    small_all[
                        lax.div(first + k, HIGH), bit(first + k, NEAR), bit(first + k, SIDE), bit(first + k, CORE)
                    ]
                    for k in range(span)
                ],
                axis=0,
            ).astype(F32)
            gain = column[:, MIXH + block : MIXH + block + 1]
            bias = column[:, MIXH + 2 + block : MIXH + 3 + block]
            act[stream, at(index * chunk, chunk), :] = (
                (piece(index) - centre) * root * gain + bias
            ).astype(BF16)

        loop(0, depth // chunk, normalise)
        act_keep(stream).start()

    finals = [
        pltpu.make_async_copy(small_all, o_small, out_sem.at[1]),
        pltpu.make_async_copy(streams, o_streams, out_sem.at[2]),
    ]
    early_pairs = ((0, mix_all), (1, small_all))
    last = high_bits + 2

    def first(array):
        keep(array).start()
        for peer in range(3):
            reshard(array, peer).start()

    def second(array):
        keep(array).wait()
        for peer in range(3):
            reshard(array, peer).wait()
        high_hop(array, 0).start()

    def third(array):
        for phase in range(high_bits):
            high_hop(array, phase).wait()
            if phase + 1 < high_bits:
                high_hop(array, phase + 1).start()
        side_hop(array).start()

    def act_first(stream):
        act_near(stream).wait()
        act_tensor(stream, 1).start()
        if stream + 1 < STREAMS:
            act_near(stream + 1).start()
        if stream and stream + 1 < STREAMS:
            act_tensor(stream + 1, 0).start()

    def act_second(stream):
        act_keep(stream).wait()
        act_tensor(stream, 0).wait()
        act_tensor(stream, 1).wait()
        for near in range(2):
            act_core(stream, near).start()

    for copy in own:
        copy.start()
    for copy in own:
        copy.wait()
    for which, buf in early_pairs:
        early(which, buf, 0).start()
    total = len(units)

    def tick(unit):
        third(unit)
        if unit + 3 < total:
            first(unit + 3)
        if unit + 1 < total:
            second(unit + 1)

    for unit in range(min(3, total)):
        first(unit)
    for phase in range(1, last + 1):
        for which, buf in early_pairs:
            early(which, buf, phase - 1).wait()
            early(which, buf, phase).start()
        if phase == 2:
            second(0)
    early(0, mix_all, last).wait()
    def mix_lanes(index):
        return mix_all.at[lax.div(index, HIGH), bit(index, NEAR), bit(index, SIDE), bit(index, CORE)], o_mix.at[
            :, at(index * 2 * half + tensor * half, half)
        ]

    def mix_copy(index):
        source, target = mix_lanes(index)
        return pltpu.make_async_copy(source, target, share_l.at[index])

    def mix_share(index):
        source, target = mix_lanes(index)
        return remote(source, target, share_s.at[index], share_r.at[index], tensor=here.other)

    def mix_out(index):
        mix_copy(index).start()
        mix_share(index).start()

    loop(0, n_dp, mix_out)
    loop(0, n_dp, mix_step)
    streams[:, at(me * rows, rows), :] = mixed[0]
    early(1, small_all, last).wait()
    done = 0

    def ticks(count):
        nonlocal done
        for unit in range(done, min(done + count, total)):
            tick(unit)
        done = min(done + count, total)

    ticks(3)
    loop(1, n_dp, lambda step: send(step).wait())
    for stream in range(STREAMS):
        normalise_stream(stream)
        if stream == 0:
            act_near(0).start()
        if stream < 2:
            act_tensor(stream, 0).start()
    for copy in finals:
        copy.start()
    depth, tokens = act_in.shape[1:]
    seq_len = 2 * half
    heads = context.shape[0] // HD
    tile = 256

    def act_load(stream):
        return pltpu.make_async_copy(o_act.at[stream], act_in.at[stream], load_sem.at[stream])

    def act_third(stream):
        for near in range(2):
            act_core(stream, near).wait()
        act_load(stream).start()

    loads = {
        "qkv": pltpu.make_async_copy(o_qkv.reshape(3, depth, qkv_in.shape[2]), qkv_in, load_sem.at[4]),
        "out": pltpu.make_async_copy(o_out.reshape(depth, out_in.shape[1]), out_in, load_sem.at[5]),
        "up": pltpu.make_async_copy(o_up.reshape(depth, up_in.shape[1]), up_in, load_sem.at[6]),
        "down": pltpu.make_async_copy(o_down.reshape(depth, down_in.shape[1]), down_in, load_sem.at[7]),
    }
    held = 0

    def arrive(count):
        nonlocal held
        ticks(max(held + count - done, 0))
        for unit in range(held, held + count):
            side_hop(unit).wait()
        held += count

    def project(stream):
        act_load(stream).wait()
        values = tn(qkv_in[stream], act_in[stream])
        if stream < 2:
            values = turned(values, cos[...], sin[...])
        rows_out[stream] = values.astype(BF16)

    def attend(seq):
        span = at(seq * seq_len, seq_len)
        for head in range(heads):
            lane = pl.ds(head * HD, HD)
            scores = causal_scores(rows_out[1, lane, span], rows_out[0, lane, span])
            peak = jnp.max(scores, axis=0, keepdims=True)
            raised = jnp.exp(scores - peak)
            total_weight = jnp.sum(raised, axis=0, keepdims=True)
            prob = (raised / total_weight).astype(BF16)
            context[lane, span] = nn(rows_out[2, lane, span], prob).astype(BF16)
            sums[pl.ds(seq * heads + head, 1), :] = peak + jnp.log(total_weight)

    def raise_up(index):
        span = at(index * tile, tile)
        value, derivative = gelu_parts(tn(up_in[:, span], act_in[3]))
        hidden[span, :] = value.astype(BF16)
        slope[span, :] = derivative

    def lower(index):
        span = at(index * tile, tile)
        part[span, :] = (nn(out_in[span, :], context[...]) + nn(down_in[span, :], hidden[...])).astype(BF16)

    saves = []

    def save(*pairs):
        for source, target in pairs:
            copy = pltpu.make_async_copy(source, target, save_sem.at[len(saves)])
            copy.start()
            saves.append(copy)

    def rows_arrive(_):
        arrive(4)
        loads["qkv"].start()
        loads["out"].start()
        loads["qkv"].wait()

    def attend_all(_):
        loop(0, tokens // seq_len, attend)
        save((rows_out, o_rows), (context, o_context), (sums, o_sums))

    def raise_all(_):
        arrive(up_in.shape[1] // UNIT)
        loads["up"].start()
        act_load(3).wait()
        loads["up"].wait()
        loop(0, hidden.shape[0] // tile, raise_up)
        save((hidden, o_hidden), (slope, o_slope))

    actions = {
        "n": act_first, "s": act_second, "t": act_third, "w": rows_arrive, "p": project, "a": attend_all, "u": raise_all
    }
    for action in PLAN:
        if action == "T":
            ticks(1)
        else:
            actions[action[0]](int(action[1]))
    arrive(total - held)
    loads["down"].start()
    loads["out"].wait()
    loads["down"].wait()
    loop(0, depth // tile, lower)
    save((part, o_part))
    for copy in finals + saves:
        copy.wait()

    def settle(index):
        mix_copy(index).wait()
        mix_share(index).wait()

    loop(0, n_dp, settle)


def gather(n_dp, hist, mix, small, w_qkv, w_out, w_up, w_down, cos, sin):
    rows = small.shape[0]
    depth = rows * n_dp
    half = hist.shape[2] // n_dp // 2
    high = n_dp // HIGH
    high_bits = int(math.log2(high))
    grid = (high, 2, 2, 2)
    units = sum(w.size // w.shape[-2] for w in (w_qkv, w_out, w_up, w_down)) // QUARTERS // UNIT

    def cut(width):
        return (high, 2, 2, 2 * rows, width // QUARTERS)

    tokens = 8 * half
    narrow, width = w_qkv.shape[2] // QUARTERS, w_up.shape[1] // QUARTERS
    results = [
        ((3, narrow, tokens), BF16),
        ((narrow, tokens), BF16),
        ((tokens // (2 * half) * (narrow // HD), 2 * half), F32),
        ((width, tokens), BF16),
        ((width, tokens), F32),
        ((depth, tokens), BF16),
    ]
    shapes = [
        ((mix.shape[0], n_dp * 2 * half), F32),
        (grid + (rows, 128), BF16),
        ((STREAMS, depth, half), BF16),
        ((STREAMS, depth, tokens), BF16),
        ((3,) + cut(w_qkv.shape[2]), BF16),
        (cut(w_out.shape[1]), BF16),
        (cut(w_up.shape[1]), BF16),
        (cut(w_down.shape[1]), BF16),
    ] + results
    return pl.pallas_call(
        functools.partial(gather_kernel, n_dp),
        out_shape=[jax.ShapeDtypeStruct(*shape) for shape in shapes],
        in_specs=[ANY] * 7 + [VM] * 2,
        out_specs=[ANY] * 14,
        scratch_shapes=[
            pltpu.VMEM(grid + mix.shape, F32),
            pltpu.VMEM(grid + (rows, 128), BF16),
            pltpu.VMEM((2, HIST, rows, half), BF16),
            pltpu.VMEM((n_dp, STREAMS, rows, half), BF16),
            pltpu.VMEM((STREAMS, depth, half), BF16),
            pltpu.VMEM((STREAMS, depth, half), BF16),
            DMA((2, high_bits + 3)),
            DMA((2, high_bits + 3)),
            DMA((2,)),
            DMA((n_dp,)),
            DMA((n_dp,)),
            DMA((units, 3)),
            DMA((units, 3)),
            DMA((units, high_bits)),
            DMA((units, high_bits)),
            DMA((units,)),
            DMA((units,)),
            DMA((5, STREAMS)),
            DMA((5, STREAMS)),
            DMA((STREAMS,)),
            DMA((2 + units,)),
            DMA((3,)),
            DMA((n_dp,)),
            DMA((n_dp,)),
            DMA((n_dp,)),
            pltpu.VMEM((STREAMS, depth, tokens), BF16),
            pltpu.VMEM((3, depth, narrow), BF16),
            pltpu.VMEM((depth, narrow), BF16),
            pltpu.VMEM((depth, width), BF16),
            pltpu.VMEM((depth, width), BF16),
        ]
        + [pltpu.VMEM(*shape) for shape in results]
        + [DMA((8,)), DMA((6,))],
        compiler_params=pltpu.CompilerParams(
            collective_id=1, has_side_effects=True, vmem_limit_bytes=61 * 1024 * 1024
        ),
        name="gather",
    )(hist, mix, small, w_qkv, w_out, w_up, w_down, cos, sin)


def lane_block(half, near, core, half_at, count):
    return at(near * 4 * half + core * 2 * half + half_at * half, count * half, half)


def gelu_parts(values):
    phi = 0.5 * (1.0 + lax.erf(values * (1.0 / math.sqrt(2.0))))
    density = jnp.exp(-0.5 * values * values) * (1.0 / math.sqrt(2.0 * math.pi))
    return values * phi, phi + values * density


def reduce_group(here, half, part, theirs, own, from_core, from_tensor, from_near, sems, local, pieces, piece):
    core_s, core_r, tensor_s, tensor_r, near_s, near_r = sems

    def load(span, near, half_at):
        return pltpu.make_async_copy(
            part.at[piece(span), lane_block(half, near, here.core, half_at, 1)],
            own.at[near, half_at, piece(span)], local.at[span, near * 2 + half_at],
        )

    def to_core(span, near, half_at):
        return remote(
            part.at[piece(span), lane_block(half, near, 1 - here.core, half_at, 1)],
            from_core.at[near, half_at, piece(span)],
            core_s.at[span, near * 2 + half_at], core_r.at[span, near * 2 + half_at], dp=flip(here.me, CORE),
        )

    def to_tensor(span, near):
        return remote(
            own.at[near, here.other, piece(span)], from_tensor.at[near, piece(span)],
            tensor_s.at[span, near], tensor_r.at[span, near], tensor=here.other,
        )

    def to_near(span):
        return remote(
            from_tensor.at[1 - here.near, piece(span)], from_near.at[piece(span)],
            near_s.at[span], near_r.at[span], dp=flip(here.me, NEAR),
        )

    def start(span):
        for near in range(2):
            for half_at in range(2):
                to_core(span, near, half_at).start()
                load(span, near, half_at).start()

    def after_core(span):
        for near in range(2):
            for half_at in range(2):
                load(span, near, half_at).wait()
                to_core(span, near, half_at).wait()
            own[near, here.other, piece(span)] += from_core[near, here.other, piece(span)]
            to_tensor(span, near).start()
        for near in range(2):
            own[near, here.tensor, piece(span)] += from_core[near, here.tensor, piece(span)]

    def after_tensor(span):
        for near in range(2):
            to_tensor(span, near).wait()
        far = 1 - here.near
        from_tensor[far, piece(span)] += own[far, here.tensor, piece(span)]
        to_near(span).start()
        from_tensor[here.near, piece(span)] += own[here.near, here.tensor, piece(span)]

    def after_near(span):
        to_near(span).wait()

    return start, after_core, after_tensor, after_near


def join_kernel(
    part, streams, cot, small, mix_in, mix_out, mix_back, static, next_cot,
    o_grad, o_wide, o_block, o_next, o_mixin, o_tiny,
    own, from_core, from_tensor, from_near, residual, wide, normed, block, back, low, next_rows, mixin, tiny,
    core_s, core_r, tensor_s, tensor_r, near_s, near_r, local, share_s, share_r, own_sem,
):
    here = Place()
    me, tensor = here.me, here.tensor
    depth, half = cot.shape
    spans = core_s.shape[0]
    size = depth // spans
    chunk = 256
    greet([{"dp": flip(me, CORE)}, {"dp": flip(me, NEAR)}, {"tensor": here.other}])

    def piece(span):
        return pl.ds(span * size, size)

    start, after_core, after_tensor, after_near = reduce_group(
        here, half, part, None, own, from_core, from_tensor, from_near,
        (core_s, core_r, tensor_s, tensor_r, near_s, near_r), local, spans, piece,
    )
    fetch = pltpu.make_async_copy(streams.at[3], residual, own_sem.at[0])
    fetch.start()
    for span in range(spans):
        start(span)
    for span in range(spans):
        after_core(span)
    for span in range(spans):
        after_tensor(span)
    fetch.wait()
    squares = jnp.zeros((1, half), F32)
    for span in range(spans):
        after_near(span)

        def widen(index, total):
            rows = at(span * size + index * chunk, chunk)
            branch = from_tensor[here.near, rows, :].astype(F32) + from_near[rows, :].astype(F32)
            value = residual[rows, :].astype(F32) + branch
            wide[rows, :] = value
            block[rows, :] = value.astype(BF16)
            return total + jnp.sum(value * value, axis=0, keepdims=True)

        squares = lax.fori_loop(0, size // chunk, widen, squares)
    root = lax.rsqrt(squares / depth + ROOT_EPS)

    def share_block(which):
        lanes = at(tensor * half, half)
        if which == 0:
            return pltpu.make_async_copy(block, o_block.at[:, lanes], own_sem.at[1])
        return remote(block, o_block.at[:, lanes], share_s.at[0], share_r.at[0], tensor=here.other)

    share_block(0).start()
    share_block(1).start()

    def norm(index):
        rows = at(index * chunk, chunk)
        normed[rows, :] = (wide[rows, :] * root).astype(BF16)

    loop(0, depth // chunk, norm)
    inner, slope = gelu_parts(jnp.dot(mix_in[...], normed[...], preferred_element_type=F32))
    inner_low = inner.astype(BF16)
    next_rows[...] = (jnp.dot(mix_out[...], inner_low, preferred_element_type=F32) + static[...])[:MIXH]
    next_low = next_cot[...].astype(BF16)

    def nt(left, right):
        return lax.dot_general(left, right, (((1,), (1,)), ((), ())), preferred_element_type=F32)

    tiny[:, :128] = nt(inner_low, next_low)
    tiny[:, 128:] = jnp.broadcast_to(jnp.sum(next_cot[...], axis=1, keepdims=True), (128, 128))
    inner_grad = (jnp.dot(mix_back[...], next_low, preferred_element_type=F32) * slope).astype(BF16)

    def pull(index, total):
        rows = at(index * chunk, chunk)
        value = jnp.dot(small[rows, :], inner_grad, preferred_element_type=F32)
        back[rows, :] = value
        return total + jnp.sum(value * wide[rows, :] * root, axis=0, keepdims=True)

    along = lax.fori_loop(0, depth // chunk, pull, jnp.zeros((1, half), F32)) / depth

    def finish(index):
        rows = at(index * chunk, chunk)
        value = cot[rows, :].astype(F32) + root * (back[rows, :] - wide[rows, :] * root * along)
        back[rows, :] = value
        low[rows, :] = value.astype(BF16)

    loop(0, depth // chunk, finish)

    def share(kind, index):
        if kind == 0:
            source, lanes, where = low, lane_block(half, here.near, here.core, tensor, 1), {"dp": flip(me, NEAR)}
        elif kind == 1:
            lanes = lane_block(half, 1 - here.near if index else here.near, here.core, tensor, 1)
            source, where = (o_grad.at[:, lanes] if index else low), {"tensor": here.other}
        else:
            lanes, where = lane_block(half, index, here.core, 0, 2), {"dp": flip(me, CORE)}
            source = o_grad.at[:, lanes]
        number = 1 + 2 * kind + index
        return remote(source, o_grad.at[:, lanes], share_s.at[number], share_r.at[number], **where)

    share(0, 0).start()
    share(1, 0).start()
    keep = pltpu.make_async_copy(
        low, o_grad.at[:, lane_block(half, here.near, here.core, tensor, 1)], own_sem.at[2]
    )
    keep.start()

    def mixin_rows(index):
        rows = at(index * chunk, chunk)
        mixin[rows, :] = nt(normed[rows, :], inner_grad)

    loop(0, depth // chunk, mixin_rows)
    share(0, 0).wait()
    share(1, 1).start()
    lanes = at(tensor * half, half)
    next_share = remote(next_rows, o_next.at[:, lanes], share_s.at[7], share_r.at[7], tensor=here.other)
    next_share.start()
    finals = [
        pltpu.make_async_copy(next_rows, o_next.at[:, lanes], own_sem.at[3]),
        pltpu.make_async_copy(back, o_wide, own_sem.at[4]),
        pltpu.make_async_copy(mixin, o_mixin, own_sem.at[5]),
        pltpu.make_async_copy(tiny, o_tiny, own_sem.at[6]),
    ]
    for copy in finals:
        copy.start()
    keep.wait()
    share(1, 0).wait()
    share(1, 1).wait()
    for near in range(2):
        share(2, near).start()
    for near in range(2):
        share(2, near).wait()
    share_block(0).wait()
    share_block(1).wait()
    next_share.wait()
    for copy in finals:
        copy.wait()


def join(part, streams, cot, small, mix_in, mix_out, mix_back, static, next_cot):
    depth, half = cot.shape
    spans = 4
    shapes = [
        ((depth, 8 * half), BF16),
        ((depth, half), F32),
        ((depth, 2 * half), BF16),
        ((MIXH, 2 * half), F32),
        ((depth, 128), F32),
        ((128, 256), F32),
    ]
    return pl.pallas_call(
        join_kernel,
        out_shape=[jax.ShapeDtypeStruct(*shape) for shape in shapes],
        in_specs=[ANY, ANY] + [VM] * 7,
        out_specs=[ANY] * 6,
        scratch_shapes=[
            pltpu.VMEM((2, 2, depth, half), BF16),
            pltpu.VMEM((2, 2, depth, half), BF16),
            pltpu.VMEM((2, depth, half), BF16),
            pltpu.VMEM((depth, half), BF16),
            pltpu.VMEM((depth, half), BF16),
            pltpu.VMEM((depth, half), F32),
            pltpu.VMEM((depth, half), BF16),
            pltpu.VMEM((depth, half), BF16),
            pltpu.VMEM((depth, half), F32),
            pltpu.VMEM((depth, half), BF16),
            pltpu.VMEM((MIXH, half), F32),
            pltpu.VMEM((depth, 128), F32),
            pltpu.VMEM((128, 256), F32),
            DMA((spans, 4)),
            DMA((spans, 4)),
            DMA((spans, 2)),
            DMA((spans, 2)),
            DMA((spans,)),
            DMA((spans,)),
            DMA((spans, 4)),
            DMA((8,)),
            DMA((8,)),
            DMA((7,)),
        ],
        compiler_params=pltpu.CompilerParams(
            collective_id=2, has_side_effects=True, vmem_limit_bytes=40 * 1024 * 1024
        ),
        name="join",
    )(part, streams, cot, small, mix_in, mix_out, mix_back, static, next_cot)


def scatter_kernel(
    n_dp, attn_grad, mlp_grad, streams, small, wide_grad, mixin_part, hist, g_qkv, g_up, g_down, g_out,
    o_stream, o_mix, o_small, o_qkv, o_up, o_down, o_out,
    own, from_core, from_tensor, from_near, rows_in, wide, stream_grad, gains, biases, tiny, tiny_in, tiny_out,
    hist_in, arrived, mix_part, mix_in, mix_sum, tiny_sum,
    side_qkv, side_up, side_down, side_out, mine_qkv, mine_up, mine_down, mine_out,
    high_qkv, high_up, high_down, high_out,
    core_s, core_r, tensor_s, tensor_r, near_s, near_r, local, in_sem,
    side_s, side_r, side_local, high_s, high_r, peer_s, peer_r, peer_local,
    a2a_s, a2a_r, keep_sem, pass_s, pass_r, tiny_s, tiny_r, mix_s, mix_r, hist_sem, last_s, last_r, last_local,
):
    here = Place()
    me, tensor = here.me, here.tensor
    depth, half = wide_grad.shape
    rows = depth // n_dp
    high_bits = int(math.log2(n_dp // HIGH))
    chunk = min(256, depth)
    greet_all(n_dp, me, here.other)
    weights = (
        (g_qkv, side_qkv, mine_qkv, high_qkv, o_qkv),
        (g_up, side_up, mine_up, high_up, o_up),
        (g_down, side_down, mine_down, high_down, o_down),
        (g_out, side_out, mine_out, high_out, o_out),
    )

    def pick(ref, *index):
        return ref.at[(slice(None),) + index] if ref.shape[0] == 3 and len(ref.shape) > len(index) + 2 else ref.at[index]

    def everything(_):
        return pl.ds(0, depth)

    steps = []
    for stream in range(STREAMS):
        part = attn_grad.at[stream] if stream < 3 else mlp_grad
        steps.append(
            reduce_group(
                here, half, part, None, own.at[stream], from_core.at[stream], from_tensor.at[stream],
                from_near.at[stream],
                tuple(
                    sem.at[pl.ds(stream, 1)]
                    for sem in (core_s, core_r, tensor_s, tensor_r, near_s, near_r)
                ),
                local.at[pl.ds(stream, 1)], 1, everything,
            )
        )
    for stream in range(STREAMS):
        steps[stream][0](0)
    loads = [
        pltpu.make_async_copy(streams, rows_in, in_sem.at[0]),
        pltpu.make_async_copy(wide_grad, wide, in_sem.at[1]),
    ]
    for copy in loads:
        copy.start()

    def is_qkv(array):
        return array == 0

    def index_of(array, *index):
        return ((slice(None),) if is_qkv(array) else ()) + index

    def side_hop(array):
        g, side, _, _, _ = weights[array]
        return remote(
            g.at[index_of(array, slice(None), slice(None), 1 - here.side)], side, side_s.at[array], side_r.at[array],
            dp=flip(me, SIDE),
        )

    def side_load(array):
        g, _, mine, _, _ = weights[array]
        return pltpu.make_async_copy(
            g.at[index_of(array, slice(None), slice(None), here.side)], mine, side_local.at[array]
        )

    def high_hop(array, phase):
        _, _, mine, high, _ = weights[array]
        span = 1 << phase
        base = lax.div(here.high, span)
        theirs = base + 1 - 2 * lax.rem(base, 2)
        return remote(
            mine.at[index_of(array, pl.ds(theirs * span, span))], high.at[index_of(array, pl.ds(span - 1, span))],
            high_s.at[array, phase], high_r.at[array, phase], dp=flip(me, HIGH << phase),
        )

    def add_blocks(array, into, other, first_into, first_other, count):
        shape = into.shape
        tall, width = shape[-2:]
        outer = 3 if is_qkv(array) else 1
        step = 32

        def add(flat):
            lead = lax.div(flat, count * 2)
            rest = lax.rem(flat, count * 2)
            high, near = lax.div(rest, 2), lax.rem(rest, 2)
            prefix = (lead,) if is_qkv(array) else ()

            def tile(index):
                span = at(index * step, step)
                into[prefix + (first_into + high, near, span)] += other[prefix + (first_other + high, near, span)]

            loop(0, tall // step, tile)

        loop(0, outer * count * 2, add)

    for array in range(4):
        side_hop(array).start()
        side_load(array).start()
    for copy in loads:
        copy.wait()
    stats = []
    for stream in range(STREAMS):

        def piece(index):
            return rows_in[stream, at(index * chunk, chunk), :].astype(F32)

        centre = sum_rows(piece, depth, chunk, lambda v: v) / depth
        spread = sum_rows(piece, depth, chunk, lambda v: (v - centre) * (v - centre)) / depth
        stats.append((centre, lax.rsqrt(spread + NORM_EPS)))
    for stream in range(STREAMS):
        steps[stream][1](0)
    for array in range(4):
        side_load(array).wait()
        side_hop(array).wait()
        _, side, mine, _, _ = weights[array]
        add_blocks(array, mine, side, 0, 0, n_dp // HIGH)
        high_hop(array, high_bits - 1).start()
    for stream in range(STREAMS):
        steps[stream][2](0)

    for stream in range(STREAMS):
        steps[stream][3](0)
        group = 0 if stream < 3 else 1
        centre, root = stats[stream]

        def parts(index):
            span = at(index * chunk, chunk)
            grad = from_tensor[stream, here.near, span].astype(F32) + from_near[stream, span].astype(F32)
            hat = (rows_in[stream, span, :].astype(F32) - centre) * root
            gain = small[span, MIXH + group : MIXH + group + 1].astype(F32)
            return span, grad, hat, grad * gain

        def sums(index, carry):
            span, grad, hat, scaled = parts(index)
            if stream in (0, 3):
                gains[group, span] = grad * hat
                biases[group, span] = grad
            else:
                gains[group, span] += grad * hat
                biases[group, span] += grad
            return (
                carry[0] + jnp.sum(scaled, axis=0, keepdims=True),
                carry[1] + jnp.sum(scaled * hat, axis=0, keepdims=True),
            )

        zero = jnp.zeros((1, half), F32)
        total, along = lax.fori_loop(0, depth // chunk, sums, (zero, zero))

        def finish(index):
            span, grad, hat, scaled = parts(index)
            value = root * (scaled - total / depth - hat * (along / depth))
            if stream == 3:
                value = value + wide[span, :]
            stream_grad[stream, span] = value.astype(BF16)

        loop(0, depth // chunk, finish)

    def send(step):
        target = lax.rem(me + step, n_dp)
        return remote(
            stream_grad.at[:, at(target * rows, rows), :], arrived.at[step], a2a_s.at[step], a2a_r.at[step], dp=target
        )

    loop(1, n_dp, lambda step: send(step).start())

    def fetch(step, buf):
        source = lax.rem(me - step + n_dp, n_dp)
        return pltpu.make_async_copy(
            hist.at[:, :, at(source * 2 * half + tensor * half, half)], hist_in.at[buf], hist_sem.at[buf]
        )

    fetch(0, 0).start()
    own_block = pltpu.make_async_copy(stream_grad.at[:, at(me * rows, rows), :], arrived.at[0], last_local.at[0])
    own_block.start()

    column = lax.broadcasted_iota(jnp.int32, (chunk, 128), 1)

    def gather_tiny(index):
        span = at(index * chunk, chunk)
        value = mixin_part[span, :]
        for group in range(2):
            gain = jnp.sum(gains[group, span], axis=1, keepdims=True)
            bias = jnp.sum(biases[group, span], axis=1, keepdims=True)
            value = jnp.where(column == MIXH + group, gain, value)
            value = jnp.where(column == MIXH + 2 + group, bias, value)
        tiny[span, :] = value.astype(BF16)

    loop(0, depth // chunk, gather_tiny)

    def tiny_send(step):
        target = lax.rem(me + step, n_dp)
        return remote(tiny.at[at(target * rows, rows), :], tiny_in.at[step], tiny_s.at[step], tiny_r.at[step], dp=target)

    loop(1, n_dp, lambda step: tiny_send(step).start())

    for array in range(4):
        _, _, mine, high, _ = weights[array]
        for phase in reversed(range(high_bits)):
            high_hop(array, phase).wait()
            span = 1 << phase
            add_blocks(array, mine, high, lax.div(here.high, span) * span, span - 1, span)
            if phase:
                high_hop(array, phase - 1).start()

    def peer_hop(array, peer):
        _, _, mine, _, out = weights[array]
        width = mine.shape[-1]
        target, _ = here.peers[peer]
        core = bit(target, CORE)
        return remote(
            mine.at[index_of(array, here.high, bit(target, NEAR), at(core * rows, rows))],
            out.at[index_of(array, slice(None), at(here.quarter * width, width))],
            peer_s.at[array, peer], peer_r.at[array, peer], dp=target,
        )

    def peer_keep(array):
        _, _, mine, _, out = weights[array]
        width = mine.shape[-1]
        return pltpu.make_async_copy(
            mine.at[index_of(array, here.high, here.near, at(here.core * rows, rows))],
            out.at[index_of(array, slice(None), at(here.quarter * width, width))], peer_local.at[array],
        )

    for array in range(4):
        peer_keep(array).start()
        for peer in range(3):
            peer_hop(array, peer).start()
    own_block.wait()

    def keep_lanes(step):
        source = lax.rem(me - step + n_dp, n_dp)
        return at(source * 2 * half + tensor * half, half)

    def keep(step):
        return pltpu.make_async_copy(arrived.at[step], o_stream.at[:, :, keep_lanes(step)], keep_sem.at[step])

    def pass_on(step):
        return remote(
            arrived.at[step], o_stream.at[:, :, keep_lanes(step)], pass_s.at[step], pass_r.at[step], tensor=here.other
        )

    def mix_send(step):
        return remote(
            mix_part.at[step], mix_in.at[step], mix_s.at[step], mix_r.at[step], dp=lax.rem(me - step + n_dp, n_dp)
        )

    def receive(step):
        buf = lax.rem(step, 2)

        @pl.when(step + 1 < n_dp)
        def _():
            fetch(step + 1, 1 - buf).start()

        @pl.when(step > 0)
        def _():
            send(step).wait()

        keep(step).start()
        pass_on(step).start()
        fetch(step, buf).wait()
        for stream in range(STREAMS):
            totals = [jnp.zeros((8, half), F32) for _ in range(HIST)]
            for row in range(0, rows, 16):
                span = pl.ds(row, 16)
                grad = arrived[step, stream, span, :].astype(F32)
                for source in range(HIST):
                    product = grad * hist_in[buf, source, span, :].astype(F32)
                    totals[source] = totals[source] + product[:8] + product[8:]
            for source in range(HIST):
                mix_part[step, pl.ds(stream * HIST + source, 1), :] = jnp.sum(totals[source], axis=0, keepdims=True)

        @pl.when(step > 0)
        def _():
            mix_send(step).start()

    mix_part[0] = jnp.zeros_like(mix_part[0])
    loop(0, n_dp, receive)

    mix_sum[...] = mix_part[0]

    def add_mix(step):
        mix_send(step).wait()
        mix_sum[...] += mix_in[step]

    loop(1, n_dp, add_mix)
    lanes = at(tensor * half, half)
    mix_share = remote(mix_sum, o_mix.at[:, lanes], last_s.at[0], last_r.at[0], tensor=here.other)
    mix_keep = pltpu.make_async_copy(mix_sum, o_mix.at[:, lanes], last_local.at[1])
    mix_share.start()
    mix_keep.start()
    tiny_sum[0] = tiny[at(me * rows, rows), :].astype(F32)

    def add_tiny(step):
        tiny_send(step).wait()
        tiny_sum[0] += tiny_in[step].astype(F32)

    loop(1, n_dp, add_tiny)
    tiny_share = remote(tiny_sum.at[0], tiny_sum.at[1], last_s.at[1], last_r.at[1], tensor=here.other)
    tiny_share.start()
    tiny_share.wait()
    tiny_out[...] = tiny_sum[0] + tiny_sum[1]
    tiny_keep = pltpu.make_async_copy(tiny_out, o_small, last_local.at[2])
    tiny_keep.start()
    for array in range(4):
        peer_keep(array).wait()
        for peer in range(3):
            peer_hop(array, peer).wait()

    def settle(step):
        keep(step).wait()
        pass_on(step).wait()

    loop(0, n_dp, settle)
    mix_share.wait()
    mix_keep.wait()
    tiny_keep.wait()


def scatter(n_dp, attn_grad, mlp_grad, streams, small, wide_grad, mixin_part, hist, g_qkv, g_up, g_down, g_out):
    depth, half = wide_grad.shape
    rows = depth // n_dp
    high = n_dp // HIGH
    high_bits = int(math.log2(high))
    grads = (g_qkv, g_up, g_down, g_out)

    def lead(g):
        return (3,) if g.ndim == 6 else ()

    def halved(g, highs):
        return lead(g) + (highs, 2) + g.shape[-2:]

    outs = [
        ((STREAMS, rows, 2 * half * n_dp), BF16),
        ((MIXH, 2 * half), F32),
        ((rows, 128), F32),
    ] + [(lead(g) + (rows, QUARTERS * g.shape[-1]), BF16) for g in grads]
    return pl.pallas_call(
        functools.partial(scatter_kernel, n_dp),
        out_shape=[jax.ShapeDtypeStruct(*shape) for shape in outs],
        in_specs=[ANY, ANY, ANY, VM, ANY, VM, ANY] + [ANY] * 4,
        out_specs=[ANY] * 7,
        scratch_shapes=[
            pltpu.VMEM((STREAMS, 2, 2, depth, half), BF16),
            pltpu.VMEM((STREAMS, 2, 2, depth, half), BF16),
            pltpu.VMEM((STREAMS, 2, depth, half), BF16),
            pltpu.VMEM((STREAMS, depth, half), BF16),
            pltpu.VMEM((STREAMS, depth, half), BF16),
            pltpu.VMEM((depth, half), F32),
            pltpu.VMEM((STREAMS, depth, half), BF16),
            pltpu.VMEM((2, depth, half), F32),
            pltpu.VMEM((2, depth, half), F32),
            pltpu.VMEM((depth, 128), BF16),
            pltpu.VMEM((n_dp, rows, 128), BF16),
            pltpu.VMEM((rows, 128), F32),
            pltpu.VMEM((2, HIST, rows, half), BF16),
            pltpu.VMEM((n_dp, STREAMS, rows, half), BF16),
            pltpu.VMEM((n_dp, MIXH, half), F32),
            pltpu.VMEM((n_dp, MIXH, half), F32),
            pltpu.VMEM((MIXH, half), F32),
            pltpu.VMEM((2, rows, 128), F32),
        ]
        + [pltpu.VMEM(halved(g, high), BF16) for g in grads]
        + [pltpu.VMEM(halved(g, high), BF16) for g in grads]
        + [pltpu.VMEM(halved(g, high - 1), BF16) for g in grads]
        + [
            DMA((STREAMS, 4)),
            DMA((STREAMS, 4)),
            DMA((STREAMS, 2)),
            DMA((STREAMS, 2)),
            DMA((STREAMS,)),
            DMA((STREAMS,)),
            DMA((STREAMS, 4)),
            DMA((2,)),
            DMA((4,)),
            DMA((4,)),
            DMA((4,)),
            DMA((4, high_bits)),
            DMA((4, high_bits)),
            DMA((4, 3)),
            DMA((4, 3)),
            DMA((4,)),
            DMA((n_dp,)),
            DMA((n_dp,)),
            DMA((n_dp,)),
            DMA((n_dp,)),
            DMA((n_dp,)),
            DMA((n_dp,)),
            DMA((n_dp,)),
            DMA((n_dp,)),
            DMA((n_dp,)),
            DMA((2,)),
            DMA((2,)),
            DMA((2,)),
            DMA((3,)),
        ],
        compiler_params=pltpu.CompilerParams(
            collective_id=3, has_side_effects=True, vmem_limit_bytes=60 * 1024 * 1024
        ),
        name="scatter",
    )(attn_grad, mlp_grad, streams, small, wide_grad, mixin_part, hist, *grads)


def exact_gelu(values):
    return jax.nn.gelu(values, approximate=False)


def rotary_tables(length, rotary, float_type):
    half_rot = rotary // 2
    places = jnp.arange(length).astype(float_type)
    frequency = jnp.exp(
        jnp.arange(half_rot).astype(float_type) * (-2.0 * math.log(10000.0) / rotary)
    )
    angles = places[:, None] * frequency[None, :]
    return (jnp.cos(angles), jnp.sin(angles))


def rotate(values, cos_table, sin_table):
    half_rot = cos_table.shape[-1]
    first_half = values[..., :half_rot]
    second = values[..., half_rot : 2 * half_rot]
    return jnp.concatenate(
        [
            first_half * cos_table - second * sin_table,
            second * cos_table + first_half * sin_table,
            values[..., 2 * half_rot :],
        ],
        axis=-1,
    )


def masked_scores(queries, key_rows):
    length = queries.shape[1]
    score_scale = 1.0 / math.sqrt(queries.shape[2])
    causal = lax.broadcasted_iota(jnp.int32, (length, length), 0) >= lax.broadcasted_iota(
        jnp.int32, (length, length), 1
    )
    scores = (
        jnp.einsum("hqd,hkd->hqk", queries, key_rows, preferred_element_type=jnp.float32)
        * score_scale
    )
    return (jnp.where(causal[None], scores, MASKED), score_scale)


def attend_forward(queries, key_rows, value_rows):
    scores, score_scale = masked_scores(queries, key_rows)
    row_peak = jnp.max(scores, axis=-1, keepdims=True)
    raised = jnp.exp(scores - row_peak)
    row_total = jnp.sum(raised, axis=-1, keepdims=True)
    prob_low = (raised / row_total).astype(jnp.bfloat16)
    context = jnp.einsum("hqk,hkd->hqd", prob_low, value_rows, preferred_element_type=jnp.float32)
    return (context.astype(jnp.bfloat16), row_peak + jnp.log(row_total))


def attend_backward(queries, key_rows, value_rows, log_sum, context_grad):
    scores, score_scale = masked_scores(queries, key_rows)
    attn_prob = jnp.exp(scores - log_sum)
    prob_low = attn_prob.astype(jnp.bfloat16)
    value_grad = jnp.einsum(
        "hqk,hqd->hkd", prob_low, context_grad, preferred_element_type=jnp.float32
    )
    prob_grad = jnp.einsum(
        "hqd,hkd->hqk", context_grad, value_rows, preferred_element_type=jnp.float32
    )
    inner_sum = jnp.sum(attn_prob * prob_grad, axis=-1, keepdims=True)
    score_grad = (attn_prob * (prob_grad - inner_sum)).astype(jnp.bfloat16)
    query_grad = (
        jnp.einsum("hqk,hkd->hqd", score_grad, key_rows, preferred_element_type=jnp.float32)
        * score_scale
    )
    key_grad = (
        jnp.einsum("hqk,hqd->hkd", score_grad, queries, preferred_element_type=jnp.float32)
        * score_scale
    )
    return (query_grad, key_grad, value_grad)


def per_device(
    n_dp, history, mix_weights, w_qkv, w_out, w_up, w_down, norm_gain, norm_bias, mix_in, mix_out, mix_static,
    out_cot, next_cot,
):
    tensor = lax.axis_index("tensor")
    seq_len = mix_weights.shape[0]
    half = seq_len // 2
    depth = mix_in.shape[0] * n_dp

    def own_half(rows):
        return lax.dynamic_slice_in_dim(rows, tensor * half, half, 0)

    mix_rows = jnp.pad(own_half(mix_weights.reshape(seq_len, -1)).T, ((0, MIXH - STREAMS * HIST), (0, 0)))
    small = jnp.concatenate([mix_in, norm_gain.T, norm_bias.T], axis=1)
    small = jnp.pad(small, ((0, 0), (0, 128 - small.shape[1])))
    mix_all, small_all, streams, act, qkv, up, down, out = gather(
        n_dp, history, mix_rows, small, w_qkv, w_up, w_down, w_out
    )
    small_all = small_all.reshape(depth, 128)
    qkv, up, down, out = (
        qkv.reshape(3, depth, -1), up.reshape(depth, -1), down.reshape(depth, -1), out.reshape(depth, -1)
    )
    tokens = act.shape[2]
    seqs = tokens // seq_len
    heads = qkv.shape[2] // HD
    projected = jnp.einsum("sdt,sde->ste", act[:3], qkv, preferred_element_type=F32)
    head_rows = jnp.transpose(projected.reshape(3, seqs, seq_len, heads, HD), (0, 1, 3, 2, 4)).reshape(
        3, seqs * heads, seq_len, HD
    )
    cos_table, sin_table = rotary_tables(seq_len, ROT, F32)
    queries = rotate(head_rows[0], cos_table, sin_table).astype(BF16)
    key_rows = rotate(head_rows[1], cos_table, sin_table).astype(BF16)
    value_rows = head_rows[2].astype(BF16)
    context, log_sum = attend_forward(queries, key_rows, value_rows)

    def join_heads(rows):
        return jnp.transpose(rows.reshape(seqs, heads, seq_len, HD), (0, 2, 1, 3)).reshape(tokens, heads * HD)

    context_rows = join_heads(context)
    up_pre = jnp.einsum("dt,df->tf", act[3], up, preferred_element_type=F32)
    hidden_wide, gelu_back = jax.vjp(exact_gelu, up_pre)
    hidden = hidden_wide.astype(BF16)
    part = (
        jnp.einsum("de,te->dt", out, context_rows, preferred_element_type=F32)
        + jnp.einsum("df,tf->dt", down, hidden, preferred_element_type=F32)
    ).astype(BF16)

    def square(values):
        return jnp.pad(values, ((0, 128 - values.shape[0]), (0, 128 - values.shape[1])))

    next_rows = own_half(next_cot.reshape(seq_len, -1)).T
    next_rows = jnp.pad(next_rows, ((0, 128 - next_rows.shape[0]), (0, 0)))
    mix_in_rows = jnp.pad(small_all[:, :MIXH].T, ((0, 128 - MIXH), (0, 0)))
    static = jnp.pad(mix_static[:, None], ((0, 128 - mix_static.shape[0]), (0, 0)))
    branch_grad, wide_grad, block, next_mix, mixin_part, tiny = join(
        part, streams, own_half(out_cot).T, small_all, mix_in_rows, square(mix_out.T), square(mix_out), static,
        next_rows,
    )
    mixout_total, static_total = lax.psum(
        (tiny[:MIXH, : STREAMS * NEXT], tiny[: STREAMS * NEXT, 128]), ("dp", "tensor")
    )
    hidden_grad = jnp.einsum("dt,df->tf", branch_grad, down, preferred_element_type=F32)
    up_grad_low = gelu_back(hidden_grad)[0].astype(BF16)
    mlp_in_grad = jnp.einsum("df,tf->dt", up, up_grad_low, preferred_element_type=F32).astype(BF16)
    context_grad_rows = jnp.einsum("dt,de->te", branch_grad, out, preferred_element_type=F32).astype(BF16)
    context_grad = jnp.transpose(context_grad_rows.reshape(seqs, seq_len, heads, HD), (0, 2, 1, 3)).reshape(
        seqs * heads, seq_len, HD
    )
    query_grad, key_grad, value_grad = attend_backward(queries, key_rows, value_rows, log_sum, context_grad)
    proj_grad = jnp.stack(
        [
            join_heads(rotate(query_grad, cos_table, -sin_table).astype(BF16)),
            join_heads(rotate(key_grad, cos_table, -sin_table).astype(BF16)),
            join_heads(value_grad.astype(BF16)),
        ]
    )
    attn_in_grad = jnp.einsum("sde,ste->sdt", qkv, proj_grad, preferred_element_type=F32).astype(BF16)
    g_qkv = jnp.einsum("sdt,ste->sde", act[:3], proj_grad, preferred_element_type=F32).astype(BF16)
    g_out = jnp.einsum("dt,te->de", branch_grad, context_rows, preferred_element_type=F32).astype(BF16)
    g_up = jnp.einsum("dt,tf->df", act[3], up_grad_low, preferred_element_type=F32).astype(BF16)
    g_down = jnp.einsum("dt,tf->df", branch_grad, hidden, preferred_element_type=F32).astype(BF16)
    grid = (n_dp // HIGH, 2, 2, 2 * mix_in.shape[0])
    stream_grad, mix_grad, small_total, qkv_total, up_total, down_total, out_total = scatter(
        n_dp, attn_in_grad, mlp_in_grad, streams, small_all, wide_grad, mixin_part, history,
        g_qkv.reshape((3,) + grid + (-1,)), g_up.reshape(grid + (-1,)), g_down.reshape(grid + (-1,)),
        g_out.reshape(grid + (-1,)),
    )
    mix_rows = mix_all.reshape(n_dp, MIXH, 1, half)
    mix_rows = lax.all_gather(mix_rows, "tensor", axis=2, tiled=True)
    mix_rows = jnp.transpose(mix_rows, (1, 0, 2, 3)).reshape(MIXH, n_dp * seq_len)
    history_grad = jnp.stack(
        [
            sum(
                mix_rows[stream * HIST + source][None, :] * stream_grad[stream].astype(F32)
                for stream in range(STREAMS)
            )
            for source in range(HIST)
        ]
    ).astype(BF16)
    return (
        block.T,
        next_mix.T.reshape(seq_len, STREAMS, NEXT),
        history_grad,
        mix_grad[: STREAMS * HIST].T.reshape(seq_len, STREAMS, HIST),
        qkv_total.astype(F32),
        out_total.astype(F32),
        up_total.astype(F32),
        down_total.astype(F32),
        small_total[:, MIXH : MIXH + 2].T,
        small_total[:, MIXH + 2 : MIXH + 4].T,
        small_total[:, :MIXH],
        mixout_total,
        static_total,
    )


def solution(mesh):
    return jax.shard_map(
        functools.partial(per_device, mesh.shape["dp"]),
        mesh=mesh,
        in_specs=(
            P(None, "dp", None),
            P("dp", None, None),
            P(None, "dp", "tensor"),
            P("dp", "tensor"),
            P("dp", "tensor"),
            P("dp", "tensor"),
            P(None, "dp"),
            P(None, "dp"),
            P("dp", None),
            P(),
            P(),
            P("dp", None),
            P("dp", None, None),
        ),
        out_specs=(
            P("dp", None),
            P("dp", None, None),
            P(None, "dp", None),
            P("dp", None, None),
            P(None, "dp", "tensor"),
            P("dp", "tensor"),
            P("dp", "tensor"),
            P("dp", "tensor"),
            P(None, "dp"),
            P(None, "dp"),
            P("dp", None),
            P(),
            P(),
        ),
        check_vma=False,
    )


def lane_block(half, near, core, half_at, count):
    return at(near * 4 * half + core * 2 * half + half_at * half, count * half, half)


def reduce_group(here, half, part, theirs, own, from_core, from_tensor, from_near, sems, local, pieces, piece):
    core_s, core_r, tensor_s, tensor_r, near_s, near_r = sems

    def load(span, near, half_at):
        return pltpu.make_async_copy(
            part.at[piece(span), lane_block(half, near, here.core, half_at, 1)],
            own.at[near, half_at, piece(span)], local.at[span, near * 2 + half_at],
        )

    def to_core(span, near, half_at):
        return remote(
            part.at[piece(span), lane_block(half, near, 1 - here.core, half_at, 1)],
            from_core.at[near, half_at, piece(span)],
            core_s.at[span, near * 2 + half_at], core_r.at[span, near * 2 + half_at], dp=flip(here.me, CORE),
        )

    def to_tensor(span, near):
        return remote(
            own.at[near, here.other, piece(span)], from_tensor.at[near, piece(span)],
            tensor_s.at[span, near], tensor_r.at[span, near], tensor=here.other,
        )

    def to_near(span):
        return remote(
            from_tensor.at[1 - here.near, piece(span)], from_near.at[piece(span)],
            near_s.at[span], near_r.at[span], dp=flip(here.me, NEAR),
        )

    def start(span):
        for near in range(2):
            for half_at in range(2):
                to_core(span, near, half_at).start()
                load(span, near, half_at).start()

    def after_core(span):
        for near in range(2):
            for half_at in range(2):
                load(span, near, half_at).wait()
                to_core(span, near, half_at).wait()
            own[near, here.other, piece(span)] += from_core[near, here.other, piece(span)]
            to_tensor(span, near).start()
        for near in range(2):
            own[near, here.tensor, piece(span)] += from_core[near, here.tensor, piece(span)]

    def after_tensor(span):
        for near in range(2):
            to_tensor(span, near).wait()
        far = 1 - here.near
        from_tensor[far, piece(span)] += own[far, here.tensor, piece(span)]
        to_near(span).start()
        from_tensor[here.near, piece(span)] += own[here.near, here.tensor, piece(span)]

    def after_near(span):
        to_near(span).wait()

    return start, after_core, after_tensor, after_near


def join_kernel(
    part, streams, out_cot, small, mix_out, next_cot,
    o_grad, o_wide, o_block, o_next, o_mixin, o_tiny,
    own, from_core, from_tensor, from_near, residual, wide, normed, block, cot, cot_in, back, low, next_rows, mixin, tiny,
    core_s, core_r, tensor_s, tensor_r, near_s, near_r, local, share_s, share_r, own_sem,
):
    here = Place()
    me, tensor = here.me, here.tensor
    depth, half = cot.shape
    spans = core_s.shape[0]
    size = depth // spans
    chunk = 256
    greet([{"dp": flip(me, CORE)}, {"dp": flip(me, NEAR)}, {"tensor": here.other}])

    def piece(span):
        return pl.ds(span * size, size)

    start, after_core, after_tensor, after_near = reduce_group(
        here, half, part, None, own, from_core, from_tensor, from_near,
        (core_s, core_r, tensor_s, tensor_r, near_s, near_r), local, spans, piece,
    )
    fetch = pltpu.make_async_copy(streams.at[3], residual, own_sem.at[0])
    fetch.start()
    cot_fetch = pltpu.make_async_copy(out_cot.at[at(tensor * half, half), :], cot_in, own_sem.at[7])
    cot_fetch.start()
    for span in range(spans):
        start(span)
    for span in range(spans):
        after_core(span)
    for span in range(spans):
        after_tensor(span)
    fetch.wait()
    cot_fetch.wait()

    def turn(index):
        rows = at(index * chunk, chunk)
        cot[rows, :] = cot_in[:, rows].T

    loop(0, depth // chunk, turn)
    squares = jnp.zeros((1, half), F32)
    for span in range(spans):
        after_near(span)

        def widen(index, total):
            rows = at(span * size + index * chunk, chunk)
            branch = from_tensor[here.near, rows, :].astype(F32) + from_near[rows, :].astype(F32)
            value = residual[rows, :].astype(F32) + branch
            wide[rows, :] = value
            block[:, rows] = value.T.astype(BF16)
            return total + jnp.sum(value * value, axis=0, keepdims=True)

        squares = lax.fori_loop(0, size // chunk, widen, squares)
    root = lax.rsqrt(squares / depth + ROOT_EPS)

    def share_block(which):
        mine = o_block.at[at(tensor * half, half), :]
        if which == 0:
            return pltpu.make_async_copy(block, mine, own_sem.at[1])
        return remote(block, mine, share_s.at[0], share_r.at[0], tensor=here.other)

    share_block(0).start()
    share_block(1).start()

    def norm(index):
        rows = at(index * chunk, chunk)
        normed[rows, :] = (wide[rows, :] * root).astype(BF16)

    loop(0, depth // chunk, norm)
    inner, slope = gelu_parts(tn(small[...], normed[...]))
    inner_low = inner.astype(BF16)
    next_rows[...] = tn(mix_out[...], inner_low)[:MIXH]
    next_low = next_cot[...].astype(BF16)

    column = lax.broadcasted_iota(jnp.int32, (128, 128), 1)
    static_grad = jnp.sum(next_cot[...], axis=1, keepdims=True)
    tiny[...] = jnp.where(column == MIXH, static_grad, nt(inner_low, next_low))[:MIXH]
    inner_grad = (nn(mix_out[...], next_low) * slope).astype(BF16)

    def pull(index, total):
        rows = at(index * chunk, chunk)
        value = jnp.dot(small[rows, :], inner_grad, preferred_element_type=F32)
        back[rows, :] = value
        return total + jnp.sum(value * wide[rows, :] * root, axis=0, keepdims=True)

    along = lax.fori_loop(0, depth // chunk, pull, jnp.zeros((1, half), F32)) / depth

    def finish(index):
        rows = at(index * chunk, chunk)
        value = cot[rows, :].astype(F32) + root * (back[rows, :] - wide[rows, :] * root * along)
        back[rows, :] = value
        low[rows, :] = value.astype(BF16)

    loop(0, depth // chunk, finish)

    def share(kind, index):
        if kind == 0:
            source, lanes, where = low, lane_block(half, here.near, here.core, tensor, 1), {"dp": flip(me, NEAR)}
        elif kind == 1:
            lanes = lane_block(half, 1 - here.near if index else here.near, here.core, tensor, 1)
            source, where = (o_grad.at[:, lanes] if index else low), {"tensor": here.other}
        else:
            lanes, where = lane_block(half, index, here.core, 0, 2), {"dp": flip(me, CORE)}
            source = o_grad.at[:, lanes]
        number = 1 + 2 * kind + index
        return remote(source, o_grad.at[:, lanes], share_s.at[number], share_r.at[number], **where)

    share(0, 0).start()
    share(1, 0).start()
    keep = pltpu.make_async_copy(
        low, o_grad.at[:, lane_block(half, here.near, here.core, tensor, 1)], own_sem.at[2]
    )
    keep.start()

    def mixin_rows(index):
        rows = at(index * chunk, chunk)
        mixin[rows, :] = nt(normed[rows, :], inner_grad)

    loop(0, depth // chunk, mixin_rows)
    share(0, 0).wait()
    share(1, 1).start()
    lanes = at(tensor * half, half)
    next_share = remote(next_rows, o_next.at[:, lanes], share_s.at[7], share_r.at[7], tensor=here.other)
    next_share.start()
    finals = [
        pltpu.make_async_copy(next_rows, o_next.at[:, lanes], own_sem.at[3]),
        pltpu.make_async_copy(back, o_wide, own_sem.at[4]),
        pltpu.make_async_copy(mixin, o_mixin, own_sem.at[5]),
        pltpu.make_async_copy(tiny, o_tiny, own_sem.at[6]),
    ]
    for copy in finals:
        copy.start()
    keep.wait()
    share(1, 0).wait()
    share(1, 1).wait()
    for near in range(2):
        share(2, near).start()
    for near in range(2):
        share(2, near).wait()
    share_block(0).wait()
    share_block(1).wait()
    next_share.wait()
    for copy in finals:
        copy.wait()


def join(part, streams, out_cot, small, mix_out, next_cot):
    depth, half = streams.shape[1:]
    spans = 4
    shapes = [
        ((depth, 8 * half), BF16),
        ((depth, half), F32),
        ((2 * half, depth), BF16),
        ((MIXH, 2 * half), F32),
        ((depth, 128), F32),
        ((MIXH, 128), F32),
    ]
    return pl.pallas_call(
        join_kernel,
        out_shape=[jax.ShapeDtypeStruct(*shape) for shape in shapes],
        in_specs=[ANY] * 3 + [VM] * 3,
        out_specs=[ANY] * 6,
        scratch_shapes=[
            pltpu.VMEM((2, 2, depth, half), BF16),
            pltpu.VMEM((2, 2, depth, half), BF16),
            pltpu.VMEM((2, depth, half), BF16),
            pltpu.VMEM((depth, half), BF16),
            pltpu.VMEM((depth, half), BF16),
            pltpu.VMEM((depth, half), F32),
            pltpu.VMEM((depth, half), BF16),
            pltpu.VMEM((half, depth), BF16),
            pltpu.VMEM((depth, half), BF16),
            pltpu.VMEM((half, depth), BF16),
            pltpu.VMEM((depth, half), F32),
            pltpu.VMEM((depth, half), BF16),
            pltpu.VMEM((MIXH, half), F32),
            pltpu.VMEM((depth, 128), F32),
            pltpu.VMEM((MIXH, 128), F32),
            DMA((spans, 4)),
            DMA((spans, 4)),
            DMA((spans, 2)),
            DMA((spans, 2)),
            DMA((spans,)),
            DMA((spans,)),
            DMA((spans, 4)),
            DMA((8,)),
            DMA((8,)),
            DMA((8,)),
        ],
        compiler_params=pltpu.CompilerParams(
            collective_id=2, has_side_effects=True, vmem_limit_bytes=56 * 1024 * 1024
        ),
        name="join",
    )(part, streams, out_cot, small, mix_out, next_cot)


def back_kernel(
    grad, act, w_qkv, w_out, w_up, w_down, rows, context, sums, hidden, slope, cos, sin,
    o_attn, o_mlp, o_qkv, o_out, o_up, o_down,
    grad_in, act_in, qkv_in, out_in, up_in, down_in, rows_in, context_in, sums_in, hidden_in, slope_in,
    up_grad, context_grad, row_grad, tall, wide, load_sem, tall_sem, wide_sem,
):
    depth, tokens = grad.shape
    seq_len = sums.shape[1]
    heads = context.shape[0] // HD
    tile = 256
    loads = {}
    pairs = (
        ("grad", grad, grad_in), ("down", w_down, down_in), ("slope", slope, slope_in), ("hidden", hidden, hidden_in),
        ("up", w_up, up_in), ("out", w_out, out_in), ("rows", rows, rows_in), ("sums", sums, sums_in),
        ("context", context, context_in), ("qkv", w_qkv, qkv_in), ("act3", act.at[3], act_in.at[0]),
    )
    for number, (name, source, target) in enumerate(pairs):
        loads[name] = pltpu.make_async_copy(source, target, load_sem.at[number])
        loads[name].start()

    def act_load(stream):
        slot = (stream + 1) % 2
        return pltpu.make_async_copy(act.at[stream], act_in.at[slot], load_sem.at[len(pairs) + slot])

    act_load(0).start()

    pending = {}

    def write(kind, turn, out, width, compute):
        buf, sem = (tall, tall_sem) if kind == "tall" else (wide, wide_sem)
        slots = buf.shape[1]
        if (kind, turn) in pending:
            pending.pop((kind, turn))()

        def copy(index):
            slot = lax.rem(index, slots)
            target = out.at[at(index * tile, tile), :]
            return pltpu.make_async_copy(buf.at[turn, slot, :, pl.ds(0, width)], target, sem.at[turn, slot])

        def body(index):
            @pl.when(index >= slots)
            def _():
                copy(index - slots).wait()

            buf[turn, lax.rem(index, slots), :, :width] = compute(at(index * tile, tile)).astype(BF16)
            copy(index).start()

        steps = depth // tile
        loop(0, steps, body)
        pending[kind, turn] = lambda: loop(steps - slots, steps, lambda index: copy(index).wait())

    for name in ("grad", "down", "slope"):
        loads[name].wait()

    def lift(index):
        span = at(index * tile, tile)
        up_grad[span, :] = (tn(down_in[:, span], grad_in[...]) * slope_in[span, :]).astype(BF16)

    loop(0, hidden.shape[0] // tile, lift)
    loads["up"].wait()
    write("tall", 1, o_mlp, tokens, lambda span: nn(up_in[span, :], up_grad[...]))
    for name in ("out", "rows", "sums", "context"):
        loads[name].wait()
    context_grad[...] = tn(out_in[...], grad_in[...]).astype(BF16)

    def attend(seq):
        span = at(seq * seq_len, seq_len)
        for head in range(heads):
            lane = pl.ds(head * HD, HD)
            queries, keys, values = (rows_in[s, lane, span] for s in range(3))
            prob = jnp.exp(causal_scores(keys, queries) - sums_in[pl.ds(seq * heads + head, 1), :])
            outer = context_grad[lane, span]
            value_grad = nt(outer, prob.astype(BF16))
            prob_grad = tn(values, outer)
            inner = jnp.sum(prob * prob_grad, axis=0, keepdims=True)
            score_grad = (prob * (prob_grad - inner)).astype(BF16)
            query_grad = nn(keys, score_grad) * (1.0 / math.sqrt(HD))
            key_grad = nt(queries, score_grad) * (1.0 / math.sqrt(HD))
            row_grad[0, lane, span] = turned(query_grad, cos[...], -sin[...]).astype(BF16)
            row_grad[1, lane, span] = turned(key_grad, cos[...], -sin[...]).astype(BF16)
            row_grad[2, lane, span] = value_grad.astype(BF16)

    loop(0, tokens // seq_len, attend)
    loads["qkv"].wait()
    for stream in range(3):
        write("tall", stream % 2, o_attn.at[stream], tokens, lambda span: nn(qkv_in[stream, span, :], row_grad[stream]))
    loads["hidden"].wait()
    width, narrow = hidden.shape[0], context.shape[0]
    write("wide", 0, o_down, width, lambda span: nt(grad_in[span, :], hidden_in[...]))
    write("wide", 1, o_out, narrow, lambda span: nt(grad_in[span, :], context_in[...]))
    loads["act3"].wait()
    write("wide", 0, o_up, width, lambda span: nt(act_in[0, span, :], up_grad[...]))
    for stream in range(3):
        slot = (stream + 1) % 2
        act_load(stream).wait()
        if stream < 2:
            act_load(stream + 1).start()
        write(
            "wide", (stream + 1) % 2, o_qkv.at[stream], narrow,
            lambda span: nt(act_in[slot, span, :], row_grad[stream]),
        )
    for drain in pending.values():
        drain()


def back(grad, act, w_qkv, w_out, w_up, w_down, rows, context, sums, hidden, slope, cos, sin):
    depth, tokens = grad.shape
    weights = (w_qkv, w_out, w_up, w_down)
    shapes = [(3, depth, tokens), (depth, tokens)] + [w.shape for w in weights]
    return pl.pallas_call(
        back_kernel,
        out_shape=[jax.ShapeDtypeStruct(shape, BF16) for shape in shapes],
        in_specs=[ANY] * 11 + [VM] * 2,
        out_specs=[ANY] * 6,
        scratch_shapes=[pltpu.VMEM((depth, tokens), BF16), pltpu.VMEM((2, depth, tokens), BF16)]
        + [pltpu.VMEM(v.shape, v.dtype) for v in weights + (rows, context, sums, hidden, slope)]
        + [
            pltpu.VMEM(hidden.shape, BF16),
            pltpu.VMEM(context.shape, BF16),
            pltpu.VMEM(rows.shape, BF16),
            pltpu.VMEM((2, 4, 256, tokens), BF16),
            pltpu.VMEM((2, 4, 256, hidden.shape[0]), BF16),
            DMA((13,)),
            DMA((2, 4)),
            DMA((2, 4)),
        ],
        compiler_params=pltpu.CompilerParams(vmem_limit_bytes=56 * 1024 * 1024),
        name="back",
    )(grad, act, w_qkv, w_out, w_up, w_down, rows, context, sums, hidden, slope, cos, sin)


def scatter_kernel(
    n_dp, attn_grad, mlp_grad, streams, small, wide_grad, mixin_part, mix_tiny, hist, g_qkv, g_up, g_down, g_out,
    o_stream, o_mix, o_small, o_tiny, o_qkv, o_up, o_down, o_out,
    own, from_core, from_tensor, from_near, rows_in, wide, stream_grad, gains, biases, tiny, tiny_in, tiny_out,
    hist_in, arrived, mix_part, mix_in, mix_sum, tiny_sum, ring, side_in, mine, high_in,
    core_s, core_r, tensor_s, tensor_r, near_s, near_r, local, in_sem,
    side_s, side_r, side_local, high_s, high_r, peer_s, peer_r, peer_local,
    a2a_s, a2a_r, a2a_own, keep_sem, pass_s, pass_r, tiny_s, tiny_r, mix_s, mix_r, hist_sem,
    ring_s, ring_r, last_s, last_r, last_local,
):
    here = Place()
    me, tensor = here.me, here.tensor
    depth, half = wide_grad.shape
    rows = depth // n_dp
    high_bits = int(math.log2(n_dp // HIGH))
    chunk = min(256, depth)
    greet_all(n_dp, me, here.other)

    units = []
    for g, o in ((g_qkv, o_qkv), (g_up, o_up), (g_down, o_down), (g_out, o_out)):
        if len(o.shape) == 3:
            units += [(g.at[part], o.at[part], 0) for part in range(o.shape[0])]
        else:
            units += [(g, o, first) for first in range(0, g.shape[-1], UNIT)]
    total = len(units)

    def side_hop(unit):
        g, _, first = units[unit]
        return remote(
            g.at[:, :, 1 - here.side, :, pl.ds(first, UNIT)], side_in.at[unit], side_s.at[unit], side_r.at[unit],
            dp=flip(me, SIDE),
        )

    def side_load(unit):
        g, _, first = units[unit]
        return pltpu.make_async_copy(
            g.at[:, :, here.side, :, pl.ds(first, UNIT)], mine.at[unit], side_local.at[unit]
        )

    def high_hop(unit, phase):
        span = 1 << phase
        base = lax.div(here.high, span)
        theirs = base + 1 - 2 * lax.rem(base, 2)
        return remote(
            mine.at[unit, pl.ds(theirs * span, span)], high_in.at[unit, pl.ds(span - 1, span)],
            high_s.at[unit, phase], high_r.at[unit, phase], dp=flip(me, HIGH << phase),
        )

    def peer_hop(unit, peer):
        _, o, first = units[unit]
        target, _ = here.peers[peer]
        return remote(
            mine.at[unit, here.high, bit(target, NEAR), at(bit(target, CORE) * rows, rows)],
            o.at[:, at(here.quarter * (o.shape[-1] // QUARTERS) + first, UNIT)],
            peer_s.at[unit, peer], peer_r.at[unit, peer], dp=target,
        )

    def peer_keep(unit):
        _, o, first = units[unit]
        return pltpu.make_async_copy(
            mine.at[unit, here.high, here.near, at(here.core * rows, rows)],
            o.at[:, at(here.quarter * (o.shape[-1] // QUARTERS) + first, UNIT)], peer_local.at[unit],
        )

    def add_blocks(unit, other, first_mine, first_other, count):
        tall = 2 * rows
        step = min(64, tall)

        def add(flat):
            high, rest = lax.div(flat, 2 * (tall // step)), lax.rem(flat, 2 * (tall // step))
            near, span = lax.div(rest, tall // step), at(lax.rem(rest, tall // step) * step, step)
            mine[unit, first_mine + high, near, span] += other[unit, first_other + high, near, span]

        loop(0, count * 2 * (tall // step), add)

    def side_start(unit):
        side_hop(unit).start()
        side_load(unit).start()

    def finish_high(unit):
        for phase in reversed(range(high_bits)):
            high_hop(unit, phase).wait()
            span = 1 << phase
            add_blocks(unit, high_in, lax.div(here.high, span) * span, span - 1, span)
            if phase:
                high_hop(unit, phase - 1).start()
        peer_keep(unit).start()
        for peer in range(3):
            peer_hop(unit, peer).start()

    def tick(unit):
        side_load(unit).wait()
        side_hop(unit).wait()
        if unit + 2 < total:
            side_start(unit + 2)
        add_blocks(unit, side_in, 0, 0, n_dp // HIGH)
        if unit:
            finish_high(unit - 1)
        high_hop(unit, high_bits - 1).start()

    done = 0

    def ticks(count):
        nonlocal done
        for unit in range(done, min(done + count, total)):
            tick(unit)
        done = min(done + count, total)

    def load(stream, near, half_at):
        part = attn_grad.at[stream] if stream < 3 else mlp_grad
        return pltpu.make_async_copy(
            part.at[:, lane_block(half, near, here.core, half_at, 1)], own.at[stream, near, half_at],
            local.at[stream, near * 2 + half_at],
        )

    def to_core(stream, near, half_at):
        part = attn_grad.at[stream] if stream < 3 else mlp_grad
        return remote(
            part.at[:, lane_block(half, near, 1 - here.core, half_at, 1)], from_core.at[stream, near, half_at],
            core_s.at[stream, near * 2 + half_at], core_r.at[stream, near * 2 + half_at], dp=flip(me, CORE),
        )

    def to_tensor(stream, near):
        return remote(
            own.at[stream, near, here.other], from_tensor.at[stream, near],
            tensor_s.at[stream, near], tensor_r.at[stream, near], tensor=here.other,
        )

    def to_near(stream):
        return remote(
            from_tensor.at[stream, 1 - here.near], from_near.at[stream], near_s.at[stream], near_r.at[stream],
            dp=flip(me, NEAR),
        )

    def after_core(stream):
        for near in range(2):
            for half_at in range(2):
                load(stream, near, half_at).wait()
                to_core(stream, near, half_at).wait()

        def add(index):
            span = at(index * chunk, chunk)
            for near in range(2):
                for half_at in range(2):
                    own[stream, near, half_at, span] += from_core[stream, near, half_at, span]

        loop(0, depth // chunk, add)

    def after_tensor(stream):
        for near in range(2):
            to_tensor(stream, near).wait()

        def add(index):
            span = at(index * chunk, chunk)
            for near in range(2):
                from_tensor[stream, near, span] += own[stream, near, tensor, span]

        loop(0, depth // chunk, add)
        to_near(stream).start()

    stats = []

    def measure(stream):
        def piece(index):
            return rows_in[stream, at(index * chunk, chunk), :].astype(F32)

        centre = sum_rows(piece, depth, chunk, lambda v: v) / depth
        spread = sum_rows(piece, depth, chunk, lambda v: (v - centre) * (v - centre)) / depth
        stats.append((centre, lax.rsqrt(spread + NORM_EPS)))

    def back_norm(stream):
        to_near(stream).wait()
        group = 0 if stream < 3 else 1
        centre, root = stats[stream]

        def parts(index):
            span = at(index * chunk, chunk)
            grad = from_tensor[stream, here.near, span].astype(F32) + from_near[stream, span].astype(F32)
            hat = (rows_in[stream, span, :].astype(F32) - centre) * root
            gain = small[span, MIXH + group : MIXH + group + 1].astype(F32)
            return span, grad, hat, grad * gain

        def sums(index, carry):
            span, grad, hat, scaled = parts(index)
            if stream in (0, 3):
                gains[group, span] = grad * hat
                biases[group, span] = grad
            else:
                gains[group, span] += grad * hat
                biases[group, span] += grad
            return (
                carry[0] + jnp.sum(scaled, axis=0, keepdims=True),
                carry[1] + jnp.sum(scaled * hat, axis=0, keepdims=True),
            )

        zero = jnp.zeros((1, half), F32)
        whole, along = lax.fori_loop(0, depth // chunk, sums, (zero, zero))

        def finish(index):
            span, _, hat, scaled = parts(index)
            value = root * (scaled - whole / depth - hat * (along / depth))
            if stream == 3:
                value = value + wide[span, :]
            stream_grad[stream, span] = value.astype(BF16)

        loop(0, depth // chunk, finish)
        loop(1, n_dp, lambda step: send(stream, step).start())
        send_own(stream).start()

    def send(stream, step):
        target = lax.rem(me + step, n_dp)
        return remote(
            stream_grad.at[stream, at(target * rows, rows), :], arrived.at[stream, step],
            a2a_s.at[stream, step], a2a_r.at[stream, step], dp=target,
        )

    def send_own(stream):
        return pltpu.make_async_copy(
            stream_grad.at[stream, at(me * rows, rows), :], arrived.at[stream, 0], a2a_own.at[stream]
        )

    def source_of(step):
        return lax.rem(me - step + n_dp, n_dp)

    def lanes_of(step):
        return at(source_of(step) * 2 * half + tensor * half, half)

    def fetch(step):
        return pltpu.make_async_copy(hist.at[:, :, lanes_of(step)], hist_in.at[step], hist_sem.at[step])

    def keep(stream, step):
        return pltpu.make_async_copy(
            arrived.at[stream, step], o_stream.at[stream, :, lanes_of(step)], keep_sem.at[stream, step]
        )

    def pass_on(stream, step):
        return remote(
            arrived.at[stream, step], o_stream.at[stream, :, lanes_of(step)],
            pass_s.at[stream, step], pass_r.at[stream, step], tensor=here.other,
        )

    def mix_send(step):
        return remote(mix_part.at[step], mix_in.at[step], mix_s.at[step], mix_r.at[step], dp=source_of(step))

    def receive(stream):
        send_own(stream).wait()

        def one(step):
            @pl.when(step > 0)
            def _():
                send(stream, step).wait()

            keep(stream, step).start()
            pass_on(stream, step).start()
            if stream == 0:
                fetch(step).wait()
            totals = [jnp.zeros((8, half), F32) for _ in range(HIST)]
            for row in range(0, rows, 16):
                span = pl.ds(row, 16)
                grad = arrived[stream, step, span, :].astype(F32)
                for source in range(HIST):
                    product = grad * hist_in[step, source, span, :].astype(F32)
                    totals[source] = totals[source] + product[:8] + product[8:]
            for source in range(HIST):
                mix_part[step, pl.ds(stream * HIST + source, 1), :] = jnp.sum(totals[source], axis=0, keepdims=True)
            if stream == STREAMS - 1:

                @pl.when(step > 0)
                def _():
                    mix_send(step).start()

        loop(0, n_dp, one)

    ring_targets = [{"dp": flip(me, value)} for value in (CORE, SIDE, NEAR)]
    ring_targets += [{"dp": flip(me, HIGH << phase)} for phase in range(high_bits)]
    ring_targets.append({"tensor": here.other})
    hops = len(ring_targets)

    def ring_hop(hop):
        return remote(ring.at[hop, 0], ring.at[hop, 1], ring_s.at[hop], ring_r.at[hop], **ring_targets[hop])

    def ring_step(hop):
        ring_hop(hop).wait()
        ring[hop + 1, 0] = ring[hop, 0] + ring[hop, 1]
        if hop + 1 < hops:
            ring_hop(hop + 1).start()

    side_start(0)
    for stream in range(STREAMS):
        for near in range(2):
            for half_at in range(2):
                to_core(stream, near, half_at).start()
                load(stream, near, half_at).start()
        if stream == 0:
            side_start(1)
    loads = [
        pltpu.make_async_copy(streams, rows_in, in_sem.at[0]),
        pltpu.make_async_copy(wide_grad, wide, in_sem.at[1]),
        pltpu.make_async_copy(mix_tiny, ring.at[0, 0], in_sem.at[2]),
    ]
    for copy in loads:
        copy.start()
    after_core(0)
    for near in range(2):
        to_tensor(0, near).start()
    for copy in loads:
        copy.wait()
    ring_hop(0).start()
    loop(0, n_dp, lambda step: fetch(step).start())
    mix_part[...] = jnp.zeros_like(mix_part)
    for stream in range(STREAMS):
        measure(stream)
    for stream in range(1, STREAMS):
        after_core(stream)
    ring_step(0)
    for stream in range(STREAMS):
        ticks(2)
        after_tensor(stream)
        if stream + 1 < STREAMS:
            for near in range(2):
                to_tensor(stream + 1, near).start()
            if stream + 1 < hops:
                ring_step(stream + 1)
        if stream > 0:
            back_norm(stream - 1)
        if stream > 1:
            receive(stream - 2)
    back_norm(STREAMS - 1)

    column = lax.broadcasted_iota(jnp.int32, (chunk, 128), 1)
    pltpu.make_async_copy(mixin_part, wide, in_sem.at[0]).start()
    pltpu.make_async_copy(mixin_part, wide, in_sem.at[0]).wait()

    def gather_tiny(index):
        span = at(index * chunk, chunk)
        value = wide[span, :]
        for group in range(2):
            gain = jnp.sum(gains[group, span], axis=1, keepdims=True)
            bias = jnp.sum(biases[group, span], axis=1, keepdims=True)
            value = jnp.where(column == MIXH + group, gain, value)
            value = jnp.where(column == MIXH + 2 + group, bias, value)
        tiny[span, :] = value.astype(BF16)

    loop(0, depth // chunk, gather_tiny)

    def tiny_send(step):
        target = lax.rem(me + step, n_dp)
        return remote(tiny.at[at(target * rows, rows), :], tiny_in.at[step], tiny_s.at[step], tiny_r.at[step], dp=target)

    loop(1, n_dp, lambda step: tiny_send(step).start())
    receive(2)
    ticks(2)
    receive(3)
    for hop in range(STREAMS, hops):
        ring_step(hop)
    tiny_final = pltpu.make_async_copy(ring.at[hops, 0], o_tiny, last_local.at[0])
    tiny_final.start()
    ticks(total)

    tiny_sum[0] = tiny[at(me * rows, rows), :].astype(F32)

    def add_tiny(step):
        tiny_send(step).wait()
        tiny_sum[0] += tiny_in[step].astype(F32)

    loop(1, n_dp, add_tiny)
    tiny_share = remote(tiny_sum.at[0], tiny_sum.at[1], last_s.at[1], last_r.at[1], tensor=here.other)
    tiny_share.start()
    mix_sum[...] = mix_part[0]

    def add_mix(step):
        mix_send(step).wait()
        mix_sum[...] += mix_in[step]

    loop(1, n_dp, add_mix)
    lanes = at(tensor * half, half)
    mix_share = remote(mix_sum, o_mix.at[:, lanes], last_s.at[0], last_r.at[0], tensor=here.other)
    mix_keep = pltpu.make_async_copy(mix_sum, o_mix.at[:, lanes], last_local.at[1])
    mix_share.start()
    mix_keep.start()
    finish_high(total - 1)
    tiny_share.wait()
    tiny_out[...] = tiny_sum[0] + tiny_sum[1]
    tiny_keep = pltpu.make_async_copy(tiny_out, o_small, last_local.at[2])
    tiny_keep.start()
    for unit in range(total):
        peer_keep(unit).wait()
        for peer in range(3):
            peer_hop(unit, peer).wait()

    def settle(step):
        for stream in range(STREAMS):
            keep(stream, step).wait()
            pass_on(stream, step).wait()

    loop(0, n_dp, settle)
    mix_share.wait()
    mix_keep.wait()
    tiny_keep.wait()
    tiny_final.wait()


def scatter(
    n_dp, attn_grad, mlp_grad, streams, small, wide_grad, mixin_part, mix_tiny, hist, g_qkv, g_up, g_down, g_out
):
    depth, half = wide_grad.shape
    rows = depth // n_dp
    high = n_dp // HIGH
    high_bits = int(math.log2(high))
    grads = (g_qkv, g_up, g_down, g_out)
    units = sum(g.size for g in grads) // depth // UNIT
    hops = high_bits + 4

    outs = [
        ((STREAMS, rows, 2 * half * n_dp), BF16),
        ((MIXH, 2 * half), F32),
        ((rows, 128), F32),
        (mix_tiny.shape, F32),
    ] + [((3,) * (g.ndim == 6) + (rows, QUARTERS * g.shape[-1]), BF16) for g in grads]
    return pl.pallas_call(
        functools.partial(scatter_kernel, n_dp),
        out_shape=[jax.ShapeDtypeStruct(*shape) for shape in outs],
        in_specs=[ANY, ANY, ANY, VM, ANY, ANY, ANY, ANY] + [ANY] * 4,
        out_specs=[ANY] * 8,
        scratch_shapes=[
            pltpu.VMEM((STREAMS, 2, 2, depth, half), BF16),
            pltpu.VMEM((STREAMS, 2, 2, depth, half), BF16),
            pltpu.VMEM((STREAMS, 2, depth, half), BF16),
            pltpu.VMEM((STREAMS, depth, half), BF16),
            pltpu.VMEM((STREAMS, depth, half), BF16),
            pltpu.VMEM((depth, half), F32),
            pltpu.VMEM((STREAMS, depth, half), BF16),
            pltpu.VMEM((2, depth, half), F32),
            pltpu.VMEM((2, depth, half), F32),
            pltpu.VMEM((depth, 128), BF16),
            pltpu.VMEM((n_dp, rows, 128), BF16),
            pltpu.VMEM((rows, 128), F32),
            pltpu.VMEM((n_dp, HIST, rows, half), BF16),
            pltpu.VMEM((STREAMS, n_dp, rows, half), BF16),
            pltpu.VMEM((n_dp, MIXH, half), F32),
            pltpu.VMEM((n_dp, MIXH, half), F32),
            pltpu.VMEM((MIXH, half), F32),
            pltpu.VMEM((2, rows, 128), F32),
            pltpu.VMEM((hops + 1, 2) + mix_tiny.shape, F32),
            pltpu.VMEM((units, high, 2, 2 * rows, UNIT), BF16),
            pltpu.VMEM((units, high, 2, 2 * rows, UNIT), BF16),
            pltpu.VMEM((units, high - 1, 2, 2 * rows, UNIT), BF16),
            DMA((STREAMS, 4)),
            DMA((STREAMS, 4)),
            DMA((STREAMS, 2)),
            DMA((STREAMS, 2)),
            DMA((STREAMS,)),
            DMA((STREAMS,)),
            DMA((STREAMS, 4)),
            DMA((3,)),
            DMA((units,)),
            DMA((units,)),
            DMA((units,)),
            DMA((units, high_bits)),
            DMA((units, high_bits)),
            DMA((units, 3)),
            DMA((units, 3)),
            DMA((units,)),
            DMA((STREAMS, n_dp)),
            DMA((STREAMS, n_dp)),
            DMA((STREAMS,)),
            DMA((STREAMS, n_dp)),
            DMA((STREAMS, n_dp)),
            DMA((STREAMS, n_dp)),
            DMA((n_dp,)),
            DMA((n_dp,)),
            DMA((n_dp,)),
            DMA((n_dp,)),
            DMA((n_dp,)),
            DMA((hops,)),
            DMA((hops,)),
            DMA((2,)),
            DMA((2,)),
            DMA((3,)),
        ],
        compiler_params=pltpu.CompilerParams(
            collective_id=3, has_side_effects=True, vmem_limit_bytes=62 * 1024 * 1024
        ),
        name="scatter",
    )(attn_grad, mlp_grad, streams, small, wide_grad, mixin_part, mix_tiny, hist, *grads)


def rotary_tables(length, rotary, float_type):
    half_rot = rotary // 2
    places = jnp.arange(length).astype(float_type)
    frequency = jnp.exp(
        jnp.arange(half_rot).astype(float_type) * (-2.0 * math.log(10000.0) / rotary)
    )
    angles = places[:, None] * frequency[None, :]
    return (jnp.cos(angles), jnp.sin(angles))


def per_device(
    n_dp, history, mix_weights, w_qkv, w_out, w_up, w_down, norm_gain, norm_bias, mix_in, mix_out, mix_static,
    out_cot, next_cot,
):
    tensor = lax.axis_index("tensor")
    seq_len = mix_weights.shape[0]
    half = seq_len // 2
    depth = mix_in.shape[0] * n_dp

    def own_half(rows):
        return lax.dynamic_slice_in_dim(rows, tensor * half, half, 0)

    mix_rows = own_half(mix_weights.reshape(seq_len, -1)).T
    small = jnp.concatenate(
        [mix_in, norm_gain.T, norm_bias.T, jnp.zeros((mix_in.shape[0], 128 - MIXH - 4), BF16)], axis=1
    )
    cos, sin = (table.T for table in rotary_tables(seq_len, ROT, F32))
    mix_rows, small_all, streams, act, qkv, out, up, down, rows, context, sums, hidden, slope, part = gather(
        n_dp, history, mix_rows, small, w_qkv, w_out, w_up, w_down, cos, sin
    )
    small_all = small_all.reshape(depth, 128)
    qkv, up, down, out = (
        qkv.reshape(3, depth, -1), up.reshape(depth, -1), down.reshape(depth, -1), out.reshape(depth, -1)
    )

    def square(values):
        return jnp.pad(values, ((0, 128 - values.shape[0]), (0, 128 - values.shape[1])))

    next_rows = jnp.pad(own_half(next_cot.reshape(seq_len, -1)).T, ((0, 128 - STREAMS * NEXT), (0, 0)))
    branch_grad, wide_grad, block, next_mix, mixin_part, tiny = join(
        part, streams, out_cot, small_all, square(mix_out), next_rows
    )
    attn_in_grad, mlp_in_grad, g_qkv, g_out, g_up, g_down = back(
        branch_grad, act, qkv, out, up, down, rows, context, sums, hidden, slope, cos, sin
    )
    grid = (n_dp // HIGH, 2, 2, 2 * mix_in.shape[0])
    stream_grad, mix_grad, small_total, tiny, qkv_total, up_total, down_total, out_total = scatter(
        n_dp, attn_in_grad, mlp_in_grad, streams, small_all, wide_grad, mixin_part, tiny, history,
        g_qkv.reshape((3,) + grid + (-1,)), g_up.reshape(grid + (-1,)), g_down.reshape(grid + (-1,)),
        g_out.reshape(grid + (-1,)),
    )
    history_grad = jnp.stack(
        [
            sum(
                mix_rows[stream * HIST + source][None, :] * stream_grad[stream].astype(F32)
                for stream in range(STREAMS)
            )
            for source in range(HIST)
        ]
    ).astype(BF16)
    return (
        block,
        (next_mix.T + mix_static).reshape(seq_len, STREAMS, NEXT),
        history_grad,
        mix_grad[: STREAMS * HIST].T.reshape(seq_len, STREAMS, HIST),
        qkv_total.astype(F32),
        out_total.astype(F32),
        up_total.astype(F32),
        down_total.astype(F32),
        small_total[:, MIXH : MIXH + 2].T,
        small_total[:, MIXH + 2 : MIXH + 4].T,
        small_total[:, :MIXH],
        tiny[:, : STREAMS * NEXT],
        tiny[: STREAMS * NEXT, MIXH],
    )


def solution(mesh):
    return jax.shard_map(
        functools.partial(per_device, mesh.shape["dp"]),
        mesh=mesh,
        in_specs=(
            P(None, "dp", None),
            P("dp", None, None),
            P(None, "dp", "tensor"),
            P("dp", "tensor"),
            P("dp", "tensor"),
            P("dp", "tensor"),
            P(None, "dp"),
            P(None, "dp"),
            P("dp", None),
            P(),
            P(),
            P("dp", None),
            P("dp", None, None),
        ),
        out_specs=(
            P("dp", None),
            P("dp", None, None),
            P(None, "dp", None),
            P("dp", None, None),
            P(None, "dp", "tensor"),
            P("dp", "tensor"),
            P("dp", "tensor"),
            P("dp", "tensor"),
            P(None, "dp"),
            P(None, "dp"),
            P("dp", None),
            P(),
            P(),
        ),
        check_vma=False,
    )
```

```python
import functools
import math

import jax
import jax.numpy as jnp
from jax import lax
from jax.experimental import pallas as pl
from jax.experimental.pallas import tpu as pltpu
from jax.sharding import PartitionSpec as P

HD = 128
ROT = 32
HIST = 9
STREAMS = 4
NEXT = 10
MIXH = 40

NORM_EPS = 1e-05
ROOT_EPS = 1e-06
MASKED = -1e30

MESH = pl.DeviceIdType.MESH
ANY = pl.BlockSpec(memory_space=pltpu.HBM)
VM = pl.BlockSpec(memory_space=pltpu.VMEM)
DMA = pltpu.SemaphoreType.DMA
F32, BF16 = jnp.float32, jnp.bfloat16
CORE, SIDE, NEAR, HIGH = 1, 2, 4, 8
QUARTERS = 4
UNIT = 256
PLAN = (
    "T", "T", "n0", "T", "T", "n1", "T", "T", "n2", "s0", "T", "n3", "t0", "s1", "w0", "p0", "T", "t1", "s2", "p1",
    "T", "t2", "s3", "p2", "t3", "a0", "u0",
)


def bit(place, value):
    return lax.rem(lax.div(place, value), 2)


def flip(place, value):
    return place + value - 2 * value * bit(place, value)


def at(start, size, multiple=None):
    return pl.ds(pl.multiple_of(start, size if multiple is None else multiple), size)


def remote(src, dst, send, recv, **where):
    return pltpu.make_async_remote_copy(
        src_ref=src, dst_ref=dst, send_sem=send, recv_sem=recv, device_id=where, device_id_type=MESH
    )


def loop(lower, upper, step):
    def body(index, carry):
        step(index)
        return carry

    lax.fori_loop(lower, upper, body, 0)


def greet(targets):
    barrier = pltpu.get_barrier_semaphore()
    for target in targets:
        pl.semaphore_signal(barrier, inc=1, device_id=target, device_id_type=MESH)
    pl.semaphore_wait(barrier, len(targets))


def greet_all(n_dp, me, other_tensor):
    barrier = pltpu.get_barrier_semaphore()
    loop(
        1,
        n_dp,
        lambda step: pl.semaphore_signal(
            barrier, inc=1, device_id={"dp": lax.rem(me + step, n_dp)}, device_id_type=MESH
        ),
    )
    pl.semaphore_signal(barrier, inc=1, device_id={"tensor": other_tensor}, device_id_type=MESH)
    pl.semaphore_wait(barrier, n_dp)


class Place:
    def __init__(self):
        self.me = lax.axis_index("dp")
        self.tensor = lax.axis_index("tensor")
        self.other = 1 - self.tensor
        self.core = bit(self.me, CORE)
        self.side = bit(self.me, SIDE)
        self.near = bit(self.me, NEAR)
        self.high = lax.div(self.me, HIGH)
        self.quarter = self.near * 2 + self.core
        self.peers = (
            (flip(self.me, CORE), self.near * 2 + 1 - self.core),
            (flip(self.me, NEAR), (1 - self.near) * 2 + self.core),
            (flip(flip(self.me, NEAR), CORE), (1 - self.near) * 2 + 1 - self.core),
        )


def sum_rows(ref_at, depth, chunk, of):
    def body(index, total):
        return total + jnp.sum(of(ref_at(index)), axis=0, keepdims=True)

    return lax.fori_loop(0, depth // chunk, body, jnp.zeros((1, 128), F32))


def gelu_parts(values):
    phi = 0.5 * (1.0 + lax.erf(values * (1.0 / math.sqrt(2.0))))
    density = jnp.exp(-0.5 * values * values) * (1.0 / math.sqrt(2.0 * math.pi))
    return values * phi, phi + values * density


def tn(left, right):
    return lax.dot_general(left, right, (((0,), (0,)), ((), ())), preferred_element_type=F32)


def nt(left, right):
    return lax.dot_general(left, right, (((1,), (1,)), ((), ())), preferred_element_type=F32)


def nn(left, right):
    return jnp.dot(left, right, preferred_element_type=F32)


def turned(values, cos, sin):
    pieces = []
    half_rot = ROT // 2
    repeats = values.shape[1] // cos.shape[1]
    cos, sin = (jnp.concatenate([table] * repeats, axis=1) for table in (cos, sin))
    for head in range(values.shape[0] // HD):
        rows = values[head * HD : (head + 1) * HD]
        first, second = rows[:half_rot], rows[half_rot:ROT]
        pieces += [first * cos - second * sin, second * cos + first * sin, rows[ROT:]]
    return jnp.concatenate(pieces, axis=0)


def causal_scores(keys, queries):
    scores = tn(keys, queries) * (1.0 / math.sqrt(HD))
    length = scores.shape[0]
    key = lax.broadcasted_iota(jnp.int32, (length, length), 0)
    query = lax.broadcasted_iota(jnp.int32, (length, length), 1)
    return jnp.where(query >= key, scores, MASKED)


def gather_kernel(
    n_dp, hist, mix, small, w_qkv, w_out, w_up, w_down, cos, sin,
    o_mix, o_small, o_streams, o_act, o_qkv, o_out, o_up, o_down,
    o_rows, o_context, o_sums, o_hidden, o_slope, o_part,
    mix_all, small_all, hist_in, mixed, streams, act,
    early_s, early_r, hist_sem, a2a_s, a2a_r, reshard_s, reshard_r, high_s, high_r, side_s, side_r,
    act_s, act_r, act_local, own_sem, out_sem, share_s, share_r, share_l,
    act_in, qkv_in, out_in, up_in, down_in, rows_out, context, sums, hidden, slope, part, load_sem, save_sem,
):
    here = Place()
    me, tensor = here.me, here.tensor
    rows = small.shape[1]
    depth = rows * n_dp
    half = hist.shape[2] // n_dp // 2
    high_bits = int(math.log2(n_dp // HIGH))
    weights = ((w_qkv, o_qkv), (w_out, o_out), (w_up, o_up), (w_down, o_down))
    greet_all(n_dp, me, here.other)

    def early(which, buf, phase):
        if phase == 0:
            block, target = buf.at[here.high, here.near, here.side, here.core], flip(me, NEAR)
        elif phase <= high_bits:
            span = 1 << (phase - 1)
            block = buf.at[pl.ds(lax.div(here.high, span) * span, span), :, here.side, here.core]
            target = flip(me, HIGH << (phase - 1))
        elif phase == high_bits + 1:
            block, target = buf.at[:, :, here.side, here.core], flip(me, SIDE)
        else:
            block, target = buf.at[:, :, :, here.core], flip(me, CORE)
        return remote(block, block, early_s.at[which, phase], early_r.at[which, phase], dp=target)

    own_mix = pltpu.make_async_copy(mix, mix_all.at[here.high, here.near, here.side, here.core], own_sem.at[0])
    units = []
    for w, o in weights:
        if len(w.shape) == 3:
            units += [(w.at[part], o.at[part], 0) for part in range(w.shape[0])]
        else:
            units += [(w, o, first) for first in range(0, o.shape[-1], UNIT)]

    def cut(unit, quarter):
        w, o, first = units[unit]
        return w.at[:, at(quarter * o.shape[-1] + first, UNIT)]

    def slot(unit):
        _, o, first = units[unit]
        mine = pl.ds(pl.multiple_of(here.core * rows, rows), rows)
        return o.at[here.high, here.near, here.side, mine, pl.ds(first, UNIT)]

    def keep(unit):
        return pltpu.make_async_copy(cut(unit, here.quarter), slot(unit), own_sem.at[2 + unit])

    def reshard(unit, peer):
        target, quarter = here.peers[peer]
        return remote(cut(unit, quarter), slot(unit), reshard_s.at[unit, peer], reshard_r.at[unit, peer], dp=target)

    def high_hop(unit, phase):
        _, o, first = units[unit]
        span = 1 << phase
        block = o.at[pl.ds(lax.div(here.high, span) * span, span), :, here.side, :, pl.ds(first, UNIT)]
        return remote(block, block, high_s.at[unit, phase], high_r.at[unit, phase], dp=flip(me, HIGH << phase))

    def side_hop(unit):
        _, o, first = units[unit]
        block = o.at[:, :, here.side, :, pl.ds(first, UNIT)]
        return remote(block, block, side_s.at[unit], side_r.at[unit], dp=flip(me, SIDE))

    def fetch(step, buf):
        target = lax.rem(me + step, n_dp)
        return pltpu.make_async_copy(
            hist.at[:, :, at(target * 2 * half + tensor * half, half)], hist_in.at[buf], hist_sem.at[buf]
        )

    def send(step):
        target = lax.rem(me + step, n_dp)
        return remote(
            mixed.at[step], streams.at[:, at(me * rows, rows), :], a2a_s.at[step], a2a_r.at[step], dp=target
        )

    fetch(0, 0).start()

    def mix_step(step):
        buf = lax.rem(step, 2)

        @pl.when(step + 1 < n_dp)
        def _():
            fetch(step + 1, 1 - buf).start()

        fetch(step, buf).wait()
        target = lax.rem(me + step, n_dp)
        weight = mix_all[lax.div(target, HIGH), bit(target, NEAR), bit(target, SIDE), bit(target, CORE)]
        for row in range(0, rows, 32):
            part = pl.ds(row, 32)
            sources = [hist_in[buf, source, part, :].astype(F32) for source in range(HIST)]
            for stream in range(STREAMS):
                total = sum(
                    sources[source] * weight[stream * HIST + source][None, :] for source in range(HIST)
                )
                mixed[step, stream, part, :] = total.astype(BF16)

        @pl.when(step > 0)
        def _():
            send(step).start()

    chunk = min(256, depth)

    def lanes(near, core, half_at, count):
        return at(near * 4 * half + core * 2 * half + half_at * half, count * half, half)

    def act_keep(stream):
        return pltpu.make_async_copy(
            act.at[stream], o_act.at[stream, :, lanes(here.near, here.core, tensor, 1)], act_local.at[stream]
        )

    def act_near(stream):
        return remote(
            act.at[stream], o_act.at[stream, :, lanes(here.near, here.core, tensor, 1)],
            act_s.at[0, stream], act_r.at[0, stream], dp=flip(me, NEAR),
        )

    def act_tensor(stream, second):
        span = lanes(1 - here.near if second else here.near, here.core, tensor, 1)
        return remote(
            o_act.at[stream, :, span] if second else act.at[stream], o_act.at[stream, :, span],
            act_s.at[1 + second, stream], act_r.at[1 + second, stream], tensor=here.other,
        )

    def act_core(stream, near):
        span = lanes(near, here.core, 0, 2)
        return remote(
            o_act.at[stream, :, span], o_act.at[stream, :, span],
            act_s.at[3 + near, stream], act_r.at[3 + near, stream], dp=flip(me, CORE),
        )

    def normalise_stream(stream):
        block = 0 if stream < 3 else 1

        def piece(index):
            return streams[stream, at(index * chunk, chunk), :].astype(F32)

        centre = sum_rows(piece, depth, chunk, lambda v: v) / depth
        spread = sum_rows(piece, depth, chunk, lambda v: (v - centre) * (v - centre)) / depth
        root = lax.rsqrt(spread + NORM_EPS)

        def normalise(index):
            span = chunk // rows
            first = index * span
            column = jnp.concatenate(
                [
                    small_all[
                        lax.div(first + k, HIGH), bit(first + k, NEAR), bit(first + k, SIDE), bit(first + k, CORE)
                    ]
                    for k in range(span)
                ],
                axis=0,
            ).astype(F32)
            gain = column[:, MIXH + block : MIXH + block + 1]
            bias = column[:, MIXH + 2 + block : MIXH + 3 + block]
            act[stream, at(index * chunk, chunk), :] = (
                (piece(index) - centre) * root * gain + bias
            ).astype(BF16)

        loop(0, depth // chunk, normalise)
        act_keep(stream).start()

    finals = [
        pltpu.make_async_copy(small_all, o_small, out_sem.at[1]),
        pltpu.make_async_copy(streams, o_streams, out_sem.at[2]),
    ]
    early_pairs = ((0, mix_all), (1, small_all))
    last = high_bits + 2

    def first(array):
        keep(array).start()
        for peer in range(3):
            reshard(array, peer).start()

    def second(array):
        keep(array).wait()
        for peer in range(3):
            reshard(array, peer).wait()
        high_hop(array, 0).start()

    def third(array):
        for phase in range(high_bits):
            high_hop(array, phase).wait()
            if phase + 1 < high_bits:
                high_hop(array, phase + 1).start()
        side_hop(array).start()

    def act_first(stream):
        act_near(stream).wait()
        act_tensor(stream, 1).start()
        if stream + 1 < STREAMS:
            act_near(stream + 1).start()
        if stream and stream + 1 < STREAMS:
            act_tensor(stream + 1, 0).start()

    def act_second(stream):
        act_keep(stream).wait()
        act_tensor(stream, 0).wait()
        act_tensor(stream, 1).wait()
        for near in range(2):
            act_core(stream, near).start()

    own_mix.start()
    small_all[here.high, here.near, here.side, here.core] = small[...].T
    own_mix.wait()
    for which, buf in early_pairs:
        early(which, buf, 0).start()
    total = len(units)

    def tick(unit):
        third(unit)
        if unit + 3 < total:
            first(unit + 3)
        if unit + 1 < total:
            second(unit + 1)

    for unit in range(min(3, total)):
        first(unit)
    for phase in range(1, last + 1):
        for which, buf in early_pairs:
            early(which, buf, phase - 1).wait()
            early(which, buf, phase).start()
        if phase == 2:
            second(0)
    early(0, mix_all, last).wait()
    def mix_lanes(index):
        return mix_all.at[lax.div(index, HIGH), bit(index, NEAR), bit(index, SIDE), bit(index, CORE)], o_mix.at[
            :, at(index * 2 * half + tensor * half, half)
        ]

    def mix_copy(index):
        source, target = mix_lanes(index)
        return pltpu.make_async_copy(source, target, share_l.at[index])

    def mix_share(index):
        source, target = mix_lanes(index)
        return remote(source, target, share_s.at[index], share_r.at[index], tensor=here.other)

    def mix_out(index):
        mix_copy(index).start()
        mix_share(index).start()

    loop(0, n_dp, mix_out)
    loop(0, n_dp, mix_step)
    streams[:, at(me * rows, rows), :] = mixed[0]
    early(1, small_all, last).wait()
    done = 0

    def ticks(count):
        nonlocal done
        for unit in range(done, min(done + count, total)):
            tick(unit)
        done = min(done + count, total)

    ticks(3)
    loop(1, n_dp, lambda step: send(step).wait())
    for stream in range(STREAMS):
        normalise_stream(stream)
        if stream == 0:
            act_near(0).start()
        if stream < 2:
            act_tensor(stream, 0).start()
    for copy in finals:
        copy.start()
    depth, tokens = act_in.shape[1:]
    seq_len = 2 * half
    heads = context.shape[0] // HD
    tile = 256

    def act_load(stream):
        return pltpu.make_async_copy(o_act.at[stream], act_in.at[stream], load_sem.at[stream])

    def act_third(stream):
        for near in range(2):
            act_core(stream, near).wait()
        act_load(stream).start()

    loads = {
        "qkv": pltpu.make_async_copy(o_qkv.reshape(3, depth, qkv_in.shape[2]), qkv_in, load_sem.at[4]),
        "out": pltpu.make_async_copy(o_out.reshape(depth, out_in.shape[1]), out_in, load_sem.at[5]),
        "up": pltpu.make_async_copy(o_up.reshape(depth, up_in.shape[1]), up_in, load_sem.at[6]),
        "down": pltpu.make_async_copy(o_down.reshape(depth, down_in.shape[1]), down_in, load_sem.at[7]),
    }
    held = 0

    def arrive(count):
        nonlocal held
        ticks(max(held + count - done, 0))
        for unit in range(held, held + count):
            side_hop(unit).wait()
        held += count

    def project(stream):
        act_load(stream).wait()
        values = tn(qkv_in[stream], act_in[stream])
        if stream < 2:
            values = turned(values, cos[...], sin[...])
        rows_out[stream] = values.astype(BF16)

    def attend(seq):
        span = at(seq * seq_len, seq_len)
        for head in range(heads):
            lane = pl.ds(head * HD, HD)
            scores = causal_scores(rows_out[1, lane, span], rows_out[0, lane, span])
            peak = jnp.max(scores, axis=0, keepdims=True)
            raised = jnp.exp(scores - peak)
            total_weight = jnp.sum(raised, axis=0, keepdims=True)
            prob = (raised / total_weight).astype(BF16)
            context[lane, span] = nn(rows_out[2, lane, span], prob).astype(BF16)
            sums[pl.ds(seq * heads + head, 1), :] = peak + jnp.log(total_weight)

    def raise_up(index):
        span = at(index * tile, tile)
        value, derivative = gelu_parts(tn(up_in[:, span], act_in[3]))
        hidden[span, :] = value.astype(BF16)
        slope[span, :] = derivative

    def lower(index):
        span = at(index * tile, tile)
        part[span, :] = (nn(out_in[span, :], context[...]) + nn(down_in[span, :], hidden[...])).astype(BF16)

    saves = []

    def save(*pairs):
        for source, target in pairs:
            copy = pltpu.make_async_copy(source, target, save_sem.at[len(saves)])
            copy.start()
            saves.append(copy)

    def rows_arrive(_):
        arrive(4)
        loads["qkv"].start()
        loads["out"].start()
        loads["qkv"].wait()

    def attend_all(_):
        loop(0, tokens // seq_len, attend)
        save((rows_out, o_rows), (context, o_context), (sums, o_sums))

    def raise_all(_):
        arrive(up_in.shape[1] // UNIT)
        loads["up"].start()
        act_load(3).wait()
        loads["up"].wait()
        loop(0, hidden.shape[0] // tile, raise_up)
        save((hidden, o_hidden), (slope, o_slope))

    actions = {
        "n": act_first, "s": act_second, "t": act_third, "w": rows_arrive, "p": project, "a": attend_all, "u": raise_all
    }
    for action in PLAN:
        if action == "T":
            ticks(1)
        else:
            actions[action[0]](int(action[1]))
    arrive(total - held)
    loads["down"].start()
    loads["out"].wait()
    loads["down"].wait()
    loop(0, depth // tile, lower)
    save((part, o_part))
    for copy in finals + saves:
        copy.wait()

    def settle(index):
        mix_copy(index).wait()
        mix_share(index).wait()

    loop(0, n_dp, settle)


def gather(n_dp, hist, mix, small, w_qkv, w_out, w_up, w_down, cos, sin):
    rows = small.shape[1]
    depth = rows * n_dp
    half = hist.shape[2] // n_dp // 2
    high = n_dp // HIGH
    high_bits = int(math.log2(high))
    grid = (high, 2, 2, 2)
    units = sum(w.size // w.shape[-2] for w in (w_qkv, w_out, w_up, w_down)) // QUARTERS // UNIT

    def cut(width):
        return (high, 2, 2, 2 * rows, width // QUARTERS)

    tokens = 8 * half
    narrow, width = w_qkv.shape[2] // QUARTERS, w_up.shape[1] // QUARTERS
    results = [
        ((3, narrow, tokens), BF16),
        ((narrow, tokens), BF16),
        ((tokens // (2 * half) * (narrow // HD), 2 * half), F32),
        ((width, tokens), BF16),
        ((width, tokens), F32),
        ((depth, tokens), BF16),
    ]
    shapes = [
        ((mix.shape[0], n_dp * 2 * half), F32),
        (grid + (rows, 128), BF16),
        ((STREAMS, depth, half), BF16),
        ((STREAMS, depth, tokens), BF16),
        ((3,) + cut(w_qkv.shape[2]), BF16),
        (cut(w_out.shape[1]), BF16),
        (cut(w_up.shape[1]), BF16),
        (cut(w_down.shape[1]), BF16),
    ] + results
    return pl.pallas_call(
        functools.partial(gather_kernel, n_dp),
        out_shape=[jax.ShapeDtypeStruct(*shape) for shape in shapes],
        in_specs=[ANY, ANY, VM] + [ANY] * 4 + [VM] * 2,
        out_specs=[ANY] * 14,
        scratch_shapes=[
            pltpu.VMEM(grid + mix.shape, F32),
            pltpu.VMEM(grid + (rows, 128), BF16),
            pltpu.VMEM((2, HIST, rows, half), BF16),
            pltpu.VMEM((n_dp, STREAMS, rows, half), BF16),
            pltpu.VMEM((STREAMS, depth, half), BF16),
            pltpu.VMEM((STREAMS, depth, half), BF16),
            DMA((2, high_bits + 3)),
            DMA((2, high_bits + 3)),
            DMA((2,)),
            DMA((n_dp,)),
            DMA((n_dp,)),
            DMA((units, 3)),
            DMA((units, 3)),
            DMA((units, high_bits)),
            DMA((units, high_bits)),
            DMA((units,)),
            DMA((units,)),
            DMA((5, STREAMS)),
            DMA((5, STREAMS)),
            DMA((STREAMS,)),
            DMA((2 + units,)),
            DMA((3,)),
            DMA((n_dp,)),
            DMA((n_dp,)),
            DMA((n_dp,)),
            pltpu.VMEM((STREAMS, depth, tokens), BF16),
            pltpu.VMEM((3, depth, narrow), BF16),
            pltpu.VMEM((depth, narrow), BF16),
            pltpu.VMEM((depth, width), BF16),
            pltpu.VMEM((depth, width), BF16),
        ]
        + [pltpu.VMEM(*shape) for shape in results]
        + [DMA((8,)), DMA((6,))],
        compiler_params=pltpu.CompilerParams(
            collective_id=1, has_side_effects=True, vmem_limit_bytes=61 * 1024 * 1024
        ),
        name="gather",
    )(hist, mix, small, w_qkv, w_out, w_up, w_down, cos, sin)


def lane_block(half, near, core, half_at, count):
    return at(near * 4 * half + core * 2 * half + half_at * half, count * half, half)


def gelu_parts(values):
    phi = 0.5 * (1.0 + lax.erf(values * (1.0 / math.sqrt(2.0))))
    density = jnp.exp(-0.5 * values * values) * (1.0 / math.sqrt(2.0 * math.pi))
    return values * phi, phi + values * density


def reduce_group(here, half, part, theirs, own, from_core, from_tensor, from_near, sems, local, pieces, piece):
    core_s, core_r, tensor_s, tensor_r, near_s, near_r = sems

    def load(span, near, half_at):
        return pltpu.make_async_copy(
            part.at[piece(span), lane_block(half, near, here.core, half_at, 1)],
            own.at[near, half_at, piece(span)], local.at[span, near * 2 + half_at],
        )

    def to_core(span, near, half_at):
        return remote(
            part.at[piece(span), lane_block(half, near, 1 - here.core, half_at, 1)],
            from_core.at[near, half_at, piece(span)],
            core_s.at[span, near * 2 + half_at], core_r.at[span, near * 2 + half_at], dp=flip(here.me, CORE),
        )

    def to_tensor(span, near):
        return remote(
            own.at[near, here.other, piece(span)], from_tensor.at[near, piece(span)],
            tensor_s.at[span, near], tensor_r.at[span, near], tensor=here.other,
        )

    def to_near(span):
        return remote(
            from_tensor.at[1 - here.near, piece(span)], from_near.at[piece(span)],
            near_s.at[span], near_r.at[span], dp=flip(here.me, NEAR),
        )

    def start(span):
        for near in range(2):
            for half_at in range(2):
                to_core(span, near, half_at).start()
                load(span, near, half_at).start()

    def after_core(span):
        for near in range(2):
            for half_at in range(2):
                load(span, near, half_at).wait()
                to_core(span, near, half_at).wait()
            own[near, here.other, piece(span)] += from_core[near, here.other, piece(span)]
            to_tensor(span, near).start()
        for near in range(2):
            own[near, here.tensor, piece(span)] += from_core[near, here.tensor, piece(span)]

    def after_tensor(span):
        for near in range(2):
            to_tensor(span, near).wait()
        far = 1 - here.near
        from_tensor[far, piece(span)] += own[far, here.tensor, piece(span)]
        to_near(span).start()
        from_tensor[here.near, piece(span)] += own[here.near, here.tensor, piece(span)]

    def after_near(span):
        to_near(span).wait()

    return start, after_core, after_tensor, after_near


def join_kernel(
    part, streams, cot, small, mix_in, mix_out, mix_back, static, next_cot,
    o_grad, o_wide, o_block, o_next, o_mixin, o_tiny,
    own, from_core, from_tensor, from_near, residual, wide, normed, block, back, low, next_rows, mixin, tiny,
    core_s, core_r, tensor_s, tensor_r, near_s, near_r, local, share_s, share_r, own_sem,
):
    here = Place()
    me, tensor = here.me, here.tensor
    depth, half = cot.shape
    spans = core_s.shape[0]
    size = depth // spans
    chunk = 256
    greet([{"dp": flip(me, CORE)}, {"dp": flip(me, NEAR)}, {"tensor": here.other}])

    def piece(span):
        return pl.ds(span * size, size)

    start, after_core, after_tensor, after_near = reduce_group(
        here, half, part, None, own, from_core, from_tensor, from_near,
        (core_s, core_r, tensor_s, tensor_r, near_s, near_r), local, spans, piece,
    )
    fetch = pltpu.make_async_copy(streams.at[3], residual, own_sem.at[0])
    fetch.start()
    for span in range(spans):
        start(span)
    for span in range(spans):
        after_core(span)
    for span in range(spans):
        after_tensor(span)
    fetch.wait()
    squares = jnp.zeros((1, half), F32)
    for span in range(spans):
        after_near(span)

        def widen(index, total):
            rows = at(span * size + index * chunk, chunk)
            branch = from_tensor[here.near, rows, :].astype(F32) + from_near[rows, :].astype(F32)
            value = residual[rows, :].astype(F32) + branch
            wide[rows, :] = value
            block[rows, :] = value.astype(BF16)
            return total + jnp.sum(value * value, axis=0, keepdims=True)

        squares = lax.fori_loop(0, size // chunk, widen, squares)
    root = lax.rsqrt(squares / depth + ROOT_EPS)

    def share_block(which):
        lanes = at(tensor * half, half)
        if which == 0:
            return pltpu.make_async_copy(block, o_block.at[:, lanes], own_sem.at[1])
        return remote(block, o_block.at[:, lanes], share_s.at[0], share_r.at[0], tensor=here.other)

    share_block(0).start()
    share_block(1).start()

    def norm(index):
        rows = at(index * chunk, chunk)
        normed[rows, :] = (wide[rows, :] * root).astype(BF16)

    loop(0, depth // chunk, norm)
    inner, slope = gelu_parts(jnp.dot(mix_in[...], normed[...], preferred_element_type=F32))
    inner_low = inner.astype(BF16)
    next_rows[...] = (jnp.dot(mix_out[...], inner_low, preferred_element_type=F32) + static[...])[:MIXH]
    next_low = next_cot[...].astype(BF16)

    def nt(left, right):
        return lax.dot_general(left, right, (((1,), (1,)), ((), ())), preferred_element_type=F32)

    tiny[:, :128] = nt(inner_low, next_low)
    tiny[:, 128:] = jnp.broadcast_to(jnp.sum(next_cot[...], axis=1, keepdims=True), (128, 128))
    inner_grad = (jnp.dot(mix_back[...], next_low, preferred_element_type=F32) * slope).astype(BF16)

    def pull(index, total):
        rows = at(index * chunk, chunk)
        value = jnp.dot(small[rows, :], inner_grad, preferred_element_type=F32)
        back[rows, :] = value
        return total + jnp.sum(value * wide[rows, :] * root, axis=0, keepdims=True)

    along = lax.fori_loop(0, depth // chunk, pull, jnp.zeros((1, half), F32)) / depth

    def finish(index):
        rows = at(index * chunk, chunk)
        value = cot[rows, :].astype(F32) + root * (back[rows, :] - wide[rows, :] * root * along)
        back[rows, :] = value
        low[rows, :] = value.astype(BF16)

    loop(0, depth // chunk, finish)

    def share(kind, index):
        if kind == 0:
            source, lanes, where = low, lane_block(half, here.near, here.core, tensor, 1), {"dp": flip(me, NEAR)}
        elif kind == 1:
            lanes = lane_block(half, 1 - here.near if index else here.near, here.core, tensor, 1)
            source, where = (o_grad.at[:, lanes] if index else low), {"tensor": here.other}
        else:
            lanes, where = lane_block(half, index, here.core, 0, 2), {"dp": flip(me, CORE)}
            source = o_grad.at[:, lanes]
        number = 1 + 2 * kind + index
        return remote(source, o_grad.at[:, lanes], share_s.at[number], share_r.at[number], **where)

    share(0, 0).start()
    share(1, 0).start()
    keep = pltpu.make_async_copy(
        low, o_grad.at[:, lane_block(half, here.near, here.core, tensor, 1)], own_sem.at[2]
    )
    keep.start()

    def mixin_rows(index):
        rows = at(index * chunk, chunk)
        mixin[rows, :] = nt(normed[rows, :], inner_grad)

    loop(0, depth // chunk, mixin_rows)
    share(0, 0).wait()
    share(1, 1).start()
    lanes = at(tensor * half, half)
    next_share = remote(next_rows, o_next.at[:, lanes], share_s.at[7], share_r.at[7], tensor=here.other)
    next_share.start()
    finals = [
        pltpu.make_async_copy(next_rows, o_next.at[:, lanes], own_sem.at[3]),
        pltpu.make_async_copy(back, o_wide, own_sem.at[4]),
        pltpu.make_async_copy(mixin, o_mixin, own_sem.at[5]),
        pltpu.make_async_copy(tiny, o_tiny, own_sem.at[6]),
    ]
    for copy in finals:
        copy.start()
    keep.wait()
    share(1, 0).wait()
    share(1, 1).wait()
    for near in range(2):
        share(2, near).start()
    for near in range(2):
        share(2, near).wait()
    share_block(0).wait()
    share_block(1).wait()
    next_share.wait()
    for copy in finals:
        copy.wait()


def join(part, streams, cot, small, mix_in, mix_out, mix_back, static, next_cot):
    depth, half = cot.shape
    spans = 4
    shapes = [
        ((depth, 8 * half), BF16),
        ((depth, half), F32),
        ((depth, 2 * half), BF16),
        ((MIXH, 2 * half), F32),
        ((depth, 128), F32),
        ((128, 256), F32),
    ]
    return pl.pallas_call(
        join_kernel,
        out_shape=[jax.ShapeDtypeStruct(*shape) for shape in shapes],
        in_specs=[ANY, ANY] + [VM] * 7,
        out_specs=[ANY] * 6,
        scratch_shapes=[
            pltpu.VMEM((2, 2, depth, half), BF16),
            pltpu.VMEM((2, 2, depth, half), BF16),
            pltpu.VMEM((2, depth, half), BF16),
            pltpu.VMEM((depth, half), BF16),
            pltpu.VMEM((depth, half), BF16),
            pltpu.VMEM((depth, half), F32),
            pltpu.VMEM((depth, half), BF16),
            pltpu.VMEM((depth, half), BF16),
            pltpu.VMEM((depth, half), F32),
            pltpu.VMEM((depth, half), BF16),
            pltpu.VMEM((MIXH, half), F32),
            pltpu.VMEM((depth, 128), F32),
            pltpu.VMEM((128, 256), F32),
            DMA((spans, 4)),
            DMA((spans, 4)),
            DMA((spans, 2)),
            DMA((spans, 2)),
            DMA((spans,)),
            DMA((spans,)),
            DMA((spans, 4)),
            DMA((8,)),
            DMA((8,)),
            DMA((7,)),
        ],
        compiler_params=pltpu.CompilerParams(
            collective_id=2, has_side_effects=True, vmem_limit_bytes=40 * 1024 * 1024
        ),
        name="join",
    )(part, streams, cot, small, mix_in, mix_out, mix_back, static, next_cot)


def scatter_kernel(
    n_dp, attn_grad, mlp_grad, streams, small, wide_grad, mixin_part, hist, g_qkv, g_up, g_down, g_out,
    o_stream, o_mix, o_small, o_qkv, o_up, o_down, o_out,
    own, from_core, from_tensor, from_near, rows_in, wide, stream_grad, gains, biases, tiny, tiny_in, tiny_out,
    hist_in, arrived, mix_part, mix_in, mix_sum, tiny_sum,
    side_qkv, side_up, side_down, side_out, mine_qkv, mine_up, mine_down, mine_out,
    high_qkv, high_up, high_down, high_out,
    core_s, core_r, tensor_s, tensor_r, near_s, near_r, local, in_sem,
    side_s, side_r, side_local, high_s, high_r, peer_s, peer_r, peer_local,
    a2a_s, a2a_r, keep_sem, pass_s, pass_r, tiny_s, tiny_r, mix_s, mix_r, hist_sem, last_s, last_r, last_local,
):
    here = Place()
    me, tensor = here.me, here.tensor
    depth, half = wide_grad.shape
    rows = depth // n_dp
    high_bits = int(math.log2(n_dp // HIGH))
    chunk = min(256, depth)
    greet_all(n_dp, me, here.other)
    weights = (
        (g_qkv, side_qkv, mine_qkv, high_qkv, o_qkv),
        (g_up, side_up, mine_up, high_up, o_up),
        (g_down, side_down, mine_down, high_down, o_down),
        (g_out, side_out, mine_out, high_out, o_out),
    )

    def pick(ref, *index):
        return ref.at[(slice(None),) + index] if ref.shape[0] == 3 and len(ref.shape) > len(index) + 2 else ref.at[index]

    def everything(_):
        return pl.ds(0, depth)

    steps = []
    for stream in range(STREAMS):
        part = attn_grad.at[stream] if stream < 3 else mlp_grad
        steps.append(
            reduce_group(
                here, half, part, None, own.at[stream], from_core.at[stream], from_tensor.at[stream],
                from_near.at[stream],
                tuple(
                    sem.at[pl.ds(stream, 1)]
                    for sem in (core_s, core_r, tensor_s, tensor_r, near_s, near_r)
                ),
                local.at[pl.ds(stream, 1)], 1, everything,
            )
        )
    for stream in range(STREAMS):
        steps[stream][0](0)
    loads = [
        pltpu.make_async_copy(streams, rows_in, in_sem.at[0]),
        pltpu.make_async_copy(wide_grad, wide, in_sem.at[1]),
    ]
    for copy in loads:
        copy.start()

    def is_qkv(array):
        return array == 0

    def index_of(array, *index):
        return ((slice(None),) if is_qkv(array) else ()) + index

    def side_hop(array):
        g, side, _, _, _ = weights[array]
        return remote(
            g.at[index_of(array, slice(None), slice(None), 1 - here.side)], side, side_s.at[array], side_r.at[array],
            dp=flip(me, SIDE),
        )

    def side_load(array):
        g, _, mine, _, _ = weights[array]
        return pltpu.make_async_copy(
            g.at[index_of(array, slice(None), slice(None), here.side)], mine, side_local.at[array]
        )

    def high_hop(array, phase):
        _, _, mine, high, _ = weights[array]
        span = 1 << phase
        base = lax.div(here.high, span)
        theirs = base + 1 - 2 * lax.rem(base, 2)
        return remote(
            mine.at[index_of(array, pl.ds(theirs * span, span))], high.at[index_of(array, pl.ds(span - 1, span))],
            high_s.at[array, phase], high_r.at[array, phase], dp=flip(me, HIGH << phase),
        )

    def add_blocks(array, into, other, first_into, first_other, count):
        shape = into.shape
        tall, width = shape[-2:]
        outer = 3 if is_qkv(array) else 1
        step = 32

        def add(flat):
            lead = lax.div(flat, count * 2)
            rest = lax.rem(flat, count * 2)
            high, near = lax.div(rest, 2), lax.rem(rest, 2)
            prefix = (lead,) if is_qkv(array) else ()

            def tile(index):
                span = at(index * step, step)
                into[prefix + (first_into + high, near, span)] += other[prefix + (first_other + high, near, span)]

            loop(0, tall // step, tile)

        loop(0, outer * count * 2, add)

    for array in range(4):
        side_hop(array).start()
        side_load(array).start()
    for copy in loads:
        copy.wait()
    stats = []
    for stream in range(STREAMS):

        def piece(index):
            return rows_in[stream, at(index * chunk, chunk), :].astype(F32)

        centre = sum_rows(piece, depth, chunk, lambda v: v) / depth
        spread = sum_rows(piece, depth, chunk, lambda v: (v - centre) * (v - centre)) / depth
        stats.append((centre, lax.rsqrt(spread + NORM_EPS)))
    for stream in range(STREAMS):
        steps[stream][1](0)
    for array in range(4):
        side_load(array).wait()
        side_hop(array).wait()
        _, side, mine, _, _ = weights[array]
        add_blocks(array, mine, side, 0, 0, n_dp // HIGH)
        high_hop(array, high_bits - 1).start()
    for stream in range(STREAMS):
        steps[stream][2](0)

    for stream in range(STREAMS):
        steps[stream][3](0)
        group = 0 if stream < 3 else 1
        centre, root = stats[stream]

        def parts(index):
            span = at(index * chunk, chunk)
            grad = from_tensor[stream, here.near, span].astype(F32) + from_near[stream, span].astype(F32)
            hat = (rows_in[stream, span, :].astype(F32) - centre) * root
            gain = small[span, MIXH + group : MIXH + group + 1].astype(F32)
            return span, grad, hat, grad * gain

        def sums(index, carry):
            span, grad, hat, scaled = parts(index)
            if stream in (0, 3):
                gains[group, span] = grad * hat
                biases[group, span] = grad
            else:
                gains[group, span] += grad * hat
                biases[group, span] += grad
            return (
                carry[0] + jnp.sum(scaled, axis=0, keepdims=True),
                carry[1] + jnp.sum(scaled * hat, axis=0, keepdims=True),
            )

        zero = jnp.zeros((1, half), F32)
        total, along = lax.fori_loop(0, depth // chunk, sums, (zero, zero))

        def finish(index):
            span, grad, hat, scaled = parts(index)
            value = root * (scaled - total / depth - hat * (along / depth))
            if stream == 3:
                value = value + wide[span, :]
            stream_grad[stream, span] = value.astype(BF16)

        loop(0, depth // chunk, finish)

    def send(step):
        target = lax.rem(me + step, n_dp)
        return remote(
            stream_grad.at[:, at(target * rows, rows), :], arrived.at[step], a2a_s.at[step], a2a_r.at[step], dp=target
        )

    loop(1, n_dp, lambda step: send(step).start())

    def fetch(step, buf):
        source = lax.rem(me - step + n_dp, n_dp)
        return pltpu.make_async_copy(
            hist.at[:, :, at(source * 2 * half + tensor * half, half)], hist_in.at[buf], hist_sem.at[buf]
        )

    fetch(0, 0).start()
    own_block = pltpu.make_async_copy(stream_grad.at[:, at(me * rows, rows), :], arrived.at[0], last_local.at[0])
    own_block.start()

    column = lax.broadcasted_iota(jnp.int32, (chunk, 128), 1)

    def gather_tiny(index):
        span = at(index * chunk, chunk)
        value = mixin_part[span, :]
        for group in range(2):
            gain = jnp.sum(gains[group, span], axis=1, keepdims=True)
            bias = jnp.sum(biases[group, span], axis=1, keepdims=True)
            value = jnp.where(column == MIXH + group, gain, value)
            value = jnp.where(column == MIXH + 2 + group, bias, value)
        tiny[span, :] = value.astype(BF16)

    loop(0, depth // chunk, gather_tiny)

    def tiny_send(step):
        target = lax.rem(me + step, n_dp)
        return remote(tiny.at[at(target * rows, rows), :], tiny_in.at[step], tiny_s.at[step], tiny_r.at[step], dp=target)

    loop(1, n_dp, lambda step: tiny_send(step).start())

    for array in range(4):
        _, _, mine, high, _ = weights[array]
        for phase in reversed(range(high_bits)):
            high_hop(array, phase).wait()
            span = 1 << phase
            add_blocks(array, mine, high, lax.div(here.high, span) * span, span - 1, span)
            if phase:
                high_hop(array, phase - 1).start()

    def peer_hop(array, peer):
        _, _, mine, _, out = weights[array]
        width = mine.shape[-1]
        target, _ = here.peers[peer]
        core = bit(target, CORE)
        return remote(
            mine.at[index_of(array, here.high, bit(target, NEAR), at(core * rows, rows))],
            out.at[index_of(array, slice(None), at(here.quarter * width, width))],
            peer_s.at[array, peer], peer_r.at[array, peer], dp=target,
        )

    def peer_keep(array):
        _, _, mine, _, out = weights[array]
        width = mine.shape[-1]
        return pltpu.make_async_copy(
            mine.at[index_of(array, here.high, here.near, at(here.core * rows, rows))],
            out.at[index_of(array, slice(None), at(here.quarter * width, width))], peer_local.at[array],
        )

    for array in range(4):
        peer_keep(array).start()
        for peer in range(3):
            peer_hop(array, peer).start()
    own_block.wait()

    def keep_lanes(step):
        source = lax.rem(me - step + n_dp, n_dp)
        return at(source * 2 * half + tensor * half, half)

    def keep(step):
        return pltpu.make_async_copy(arrived.at[step], o_stream.at[:, :, keep_lanes(step)], keep_sem.at[step])

    def pass_on(step):
        return remote(
            arrived.at[step], o_stream.at[:, :, keep_lanes(step)], pass_s.at[step], pass_r.at[step], tensor=here.other
        )

    def mix_send(step):
        return remote(
            mix_part.at[step], mix_in.at[step], mix_s.at[step], mix_r.at[step], dp=lax.rem(me - step + n_dp, n_dp)
        )

    def receive(step):
        buf = lax.rem(step, 2)

        @pl.when(step + 1 < n_dp)
        def _():
            fetch(step + 1, 1 - buf).start()

        @pl.when(step > 0)
        def _():
            send(step).wait()

        keep(step).start()
        pass_on(step).start()
        fetch(step, buf).wait()
        for stream in range(STREAMS):
            totals = [jnp.zeros((8, half), F32) for _ in range(HIST)]
            for row in range(0, rows, 16):
                span = pl.ds(row, 16)
                grad = arrived[step, stream, span, :].astype(F32)
                for source in range(HIST):
                    product = grad * hist_in[buf, source, span, :].astype(F32)
                    totals[source] = totals[source] + product[:8] + product[8:]
            for source in range(HIST):
                mix_part[step, pl.ds(stream * HIST + source, 1), :] = jnp.sum(totals[source], axis=0, keepdims=True)

        @pl.when(step > 0)
        def _():
            mix_send(step).start()

    mix_part[0] = jnp.zeros_like(mix_part[0])
    loop(0, n_dp, receive)

    mix_sum[...] = mix_part[0]

    def add_mix(step):
        mix_send(step).wait()
        mix_sum[...] += mix_in[step]

    loop(1, n_dp, add_mix)
    lanes = at(tensor * half, half)
    mix_share = remote(mix_sum, o_mix.at[:, lanes], last_s.at[0], last_r.at[0], tensor=here.other)
    mix_keep = pltpu.make_async_copy(mix_sum, o_mix.at[:, lanes], last_local.at[1])
    mix_share.start()
    mix_keep.start()
    tiny_sum[0] = tiny[at(me * rows, rows), :].astype(F32)

    def add_tiny(step):
        tiny_send(step).wait()
        tiny_sum[0] += tiny_in[step].astype(F32)

    loop(1, n_dp, add_tiny)
    tiny_share = remote(tiny_sum.at[0], tiny_sum.at[1], last_s.at[1], last_r.at[1], tensor=here.other)
    tiny_share.start()
    tiny_share.wait()
    tiny_out[...] = tiny_sum[0] + tiny_sum[1]
    tiny_keep = pltpu.make_async_copy(tiny_out, o_small, last_local.at[2])
    tiny_keep.start()
    for array in range(4):
        peer_keep(array).wait()
        for peer in range(3):
            peer_hop(array, peer).wait()

    def settle(step):
        keep(step).wait()
        pass_on(step).wait()

    loop(0, n_dp, settle)
    mix_share.wait()
    mix_keep.wait()
    tiny_keep.wait()


def scatter(n_dp, attn_grad, mlp_grad, streams, small, wide_grad, mixin_part, hist, g_qkv, g_up, g_down, g_out):
    depth, half = wide_grad.shape
    rows = depth // n_dp
    high = n_dp // HIGH
    high_bits = int(math.log2(high))
    grads = (g_qkv, g_up, g_down, g_out)

    def lead(g):
        return (3,) if g.ndim == 6 else ()

    def halved(g, highs):
        return lead(g) + (highs, 2) + g.shape[-2:]

    outs = [
        ((STREAMS, rows, 2 * half * n_dp), BF16),
        ((MIXH, 2 * half), F32),
        ((rows, 128), F32),
    ] + [(lead(g) + (rows, QUARTERS * g.shape[-1]), BF16) for g in grads]
    return pl.pallas_call(
        functools.partial(scatter_kernel, n_dp),
        out_shape=[jax.ShapeDtypeStruct(*shape) for shape in outs],
        in_specs=[ANY, ANY, ANY, VM, ANY, VM, ANY] + [ANY] * 4,
        out_specs=[ANY] * 7,
        scratch_shapes=[
            pltpu.VMEM((STREAMS, 2, 2, depth, half), BF16),
            pltpu.VMEM((STREAMS, 2, 2, depth, half), BF16),
            pltpu.VMEM((STREAMS, 2, depth, half), BF16),
            pltpu.VMEM((STREAMS, depth, half), BF16),
            pltpu.VMEM((STREAMS, depth, half), BF16),
            pltpu.VMEM((depth, half), F32),
            pltpu.VMEM((STREAMS, depth, half), BF16),
            pltpu.VMEM((2, depth, half), F32),
            pltpu.VMEM((2, depth, half), F32),
            pltpu.VMEM((depth, 128), BF16),
            pltpu.VMEM((n_dp, rows, 128), BF16),
            pltpu.VMEM((rows, 128), F32),
            pltpu.VMEM((2, HIST, rows, half), BF16),
            pltpu.VMEM((n_dp, STREAMS, rows, half), BF16),
            pltpu.VMEM((n_dp, MIXH, half), F32),
            pltpu.VMEM((n_dp, MIXH, half), F32),
            pltpu.VMEM((MIXH, half), F32),
            pltpu.VMEM((2, rows, 128), F32),
        ]
        + [pltpu.VMEM(halved(g, high), BF16) for g in grads]
        + [pltpu.VMEM(halved(g, high), BF16) for g in grads]
        + [pltpu.VMEM(halved(g, high - 1), BF16) for g in grads]
        + [
            DMA((STREAMS, 4)),
            DMA((STREAMS, 4)),
            DMA((STREAMS, 2)),
            DMA((STREAMS, 2)),
            DMA((STREAMS,)),
            DMA((STREAMS,)),
            DMA((STREAMS, 4)),
            DMA((2,)),
            DMA((4,)),
            DMA((4,)),
            DMA((4,)),
            DMA((4, high_bits)),
            DMA((4, high_bits)),
            DMA((4, 3)),
            DMA((4, 3)),
            DMA((4,)),
            DMA((n_dp,)),
            DMA((n_dp,)),
            DMA((n_dp,)),
            DMA((n_dp,)),
            DMA((n_dp,)),
            DMA((n_dp,)),
            DMA((n_dp,)),
            DMA((n_dp,)),
            DMA((n_dp,)),
            DMA((2,)),
            DMA((2,)),
            DMA((2,)),
            DMA((3,)),
        ],
        compiler_params=pltpu.CompilerParams(
            collective_id=3, has_side_effects=True, vmem_limit_bytes=60 * 1024 * 1024
        ),
        name="scatter",
    )(attn_grad, mlp_grad, streams, small, wide_grad, mixin_part, hist, *grads)


def exact_gelu(values):
    return jax.nn.gelu(values, approximate=False)


def rotary_tables(length, rotary, float_type):
    half_rot = rotary // 2
    places = jnp.arange(length).astype(float_type)
    frequency = jnp.exp(
        jnp.arange(half_rot).astype(float_type) * (-2.0 * math.log(10000.0) / rotary)
    )
    angles = places[:, None] * frequency[None, :]
    return (jnp.cos(angles), jnp.sin(angles))


def rotate(values, cos_table, sin_table):
    half_rot = cos_table.shape[-1]
    first_half = values[..., :half_rot]
    second = values[..., half_rot : 2 * half_rot]
    return jnp.concatenate(
        [
            first_half * cos_table - second * sin_table,
            second * cos_table + first_half * sin_table,
            values[..., 2 * half_rot :],
        ],
        axis=-1,
    )


def masked_scores(queries, key_rows):
    length = queries.shape[1]
    score_scale = 1.0 / math.sqrt(queries.shape[2])
    causal = lax.broadcasted_iota(jnp.int32, (length, length), 0) >= lax.broadcasted_iota(
        jnp.int32, (length, length), 1
    )
    scores = (
        jnp.einsum("hqd,hkd->hqk", queries, key_rows, preferred_element_type=jnp.float32)
        * score_scale
    )
    return (jnp.where(causal[None], scores, MASKED), score_scale)


def attend_forward(queries, key_rows, value_rows):
    scores, score_scale = masked_scores(queries, key_rows)
    row_peak = jnp.max(scores, axis=-1, keepdims=True)
    raised = jnp.exp(scores - row_peak)
    row_total = jnp.sum(raised, axis=-1, keepdims=True)
    prob_low = (raised / row_total).astype(jnp.bfloat16)
    context = jnp.einsum("hqk,hkd->hqd", prob_low, value_rows, preferred_element_type=jnp.float32)
    return (context.astype(jnp.bfloat16), row_peak + jnp.log(row_total))


def attend_backward(queries, key_rows, value_rows, log_sum, context_grad):
    scores, score_scale = masked_scores(queries, key_rows)
    attn_prob = jnp.exp(scores - log_sum)
    prob_low = attn_prob.astype(jnp.bfloat16)
    value_grad = jnp.einsum(
        "hqk,hqd->hkd", prob_low, context_grad, preferred_element_type=jnp.float32
    )
    prob_grad = jnp.einsum(
        "hqd,hkd->hqk", context_grad, value_rows, preferred_element_type=jnp.float32
    )
    inner_sum = jnp.sum(attn_prob * prob_grad, axis=-1, keepdims=True)
    score_grad = (attn_prob * (prob_grad - inner_sum)).astype(jnp.bfloat16)
    query_grad = (
        jnp.einsum("hqk,hkd->hqd", score_grad, key_rows, preferred_element_type=jnp.float32)
        * score_scale
    )
    key_grad = (
        jnp.einsum("hqk,hqd->hkd", score_grad, queries, preferred_element_type=jnp.float32)
        * score_scale
    )
    return (query_grad, key_grad, value_grad)


def per_device(
    n_dp, history, mix_weights, w_qkv, w_out, w_up, w_down, norm_gain, norm_bias, mix_in, mix_out, mix_static,
    out_cot, next_cot,
):
    tensor = lax.axis_index("tensor")
    seq_len = mix_weights.shape[0]
    half = seq_len // 2
    depth = mix_in.shape[0] * n_dp

    def own_half(rows):
        return lax.dynamic_slice_in_dim(rows, tensor * half, half, 0)

    mix_rows = jnp.pad(own_half(mix_weights.reshape(seq_len, -1)).T, ((0, MIXH - STREAMS * HIST), (0, 0)))
    small = jnp.concatenate([mix_in, norm_gain.T, norm_bias.T], axis=1)
    small = jnp.pad(small, ((0, 0), (0, 128 - small.shape[1])))
    mix_all, small_all, streams, act, qkv, up, down, out = gather(
        n_dp, history, mix_rows, small, w_qkv, w_up, w_down, w_out
    )
    small_all = small_all.reshape(depth, 128)
    qkv, up, down, out = (
        qkv.reshape(3, depth, -1), up.reshape(depth, -1), down.reshape(depth, -1), out.reshape(depth, -1)
    )
    tokens = act.shape[2]
    seqs = tokens // seq_len
    heads = qkv.shape[2] // HD
    projected = jnp.einsum("sdt,sde->ste", act[:3], qkv, preferred_element_type=F32)
    head_rows = jnp.transpose(projected.reshape(3, seqs, seq_len, heads, HD), (0, 1, 3, 2, 4)).reshape(
        3, seqs * heads, seq_len, HD
    )
    cos_table, sin_table = rotary_tables(seq_len, ROT, F32)
    queries = rotate(head_rows[0], cos_table, sin_table).astype(BF16)
    key_rows = rotate(head_rows[1], cos_table, sin_table).astype(BF16)
    value_rows = head_rows[2].astype(BF16)
    context, log_sum = attend_forward(queries, key_rows, value_rows)

    def join_heads(rows):
        return jnp.transpose(rows.reshape(seqs, heads, seq_len, HD), (0, 2, 1, 3)).reshape(tokens, heads * HD)

    context_rows = join_heads(context)
    up_pre = jnp.einsum("dt,df->tf", act[3], up, preferred_element_type=F32)
    hidden_wide, gelu_back = jax.vjp(exact_gelu, up_pre)
    hidden = hidden_wide.astype(BF16)
    part = (
        jnp.einsum("de,te->dt", out, context_rows, preferred_element_type=F32)
        + jnp.einsum("df,tf->dt", down, hidden, preferred_element_type=F32)
    ).astype(BF16)

    def square(values):
        return jnp.pad(values, ((0, 128 - values.shape[0]), (0, 128 - values.shape[1])))

    next_rows = own_half(next_cot.reshape(seq_len, -1)).T
    next_rows = jnp.pad(next_rows, ((0, 128 - next_rows.shape[0]), (0, 0)))
    mix_in_rows = jnp.pad(small_all[:, :MIXH].T, ((0, 128 - MIXH), (0, 0)))
    static = jnp.pad(mix_static[:, None], ((0, 128 - mix_static.shape[0]), (0, 0)))
    branch_grad, wide_grad, block, next_mix, mixin_part, tiny = join(
        part, streams, own_half(out_cot).T, small_all, mix_in_rows, square(mix_out.T), square(mix_out), static,
        next_rows,
    )
    mixout_total, static_total = lax.psum(
        (tiny[:MIXH, : STREAMS * NEXT], tiny[: STREAMS * NEXT, 128]), ("dp", "tensor")
    )
    hidden_grad = jnp.einsum("dt,df->tf", branch_grad, down, preferred_element_type=F32)
    up_grad_low = gelu_back(hidden_grad)[0].astype(BF16)
    mlp_in_grad = jnp.einsum("df,tf->dt", up, up_grad_low, preferred_element_type=F32).astype(BF16)
    context_grad_rows = jnp.einsum("dt,de->te", branch_grad, out, preferred_element_type=F32).astype(BF16)
    context_grad = jnp.transpose(context_grad_rows.reshape(seqs, seq_len, heads, HD), (0, 2, 1, 3)).reshape(
        seqs * heads, seq_len, HD
    )
    query_grad, key_grad, value_grad = attend_backward(queries, key_rows, value_rows, log_sum, context_grad)
    proj_grad = jnp.stack(
        [
            join_heads(rotate(query_grad, cos_table, -sin_table).astype(BF16)),
            join_heads(rotate(key_grad, cos_table, -sin_table).astype(BF16)),
            join_heads(value_grad.astype(BF16)),
        ]
    )
    attn_in_grad = jnp.einsum("sde,ste->sdt", qkv, proj_grad, preferred_element_type=F32).astype(BF16)
    g_qkv = jnp.einsum("sdt,ste->sde", act[:3], proj_grad, preferred_element_type=F32).astype(BF16)
    g_out = jnp.einsum("dt,te->de", branch_grad, context_rows, preferred_element_type=F32).astype(BF16)
    g_up = jnp.einsum("dt,tf->df", act[3], up_grad_low, preferred_element_type=F32).astype(BF16)
    g_down = jnp.einsum("dt,tf->df", branch_grad, hidden, preferred_element_type=F32).astype(BF16)
    grid = (n_dp // HIGH, 2, 2, 2 * mix_in.shape[0])
    stream_grad, mix_grad, small_total, qkv_total, up_total, down_total, out_total = scatter(
        n_dp, attn_in_grad, mlp_in_grad, streams, small_all, wide_grad, mixin_part, history,
        g_qkv.reshape((3,) + grid + (-1,)), g_up.reshape(grid + (-1,)), g_down.reshape(grid + (-1,)),
        g_out.reshape(grid + (-1,)),
    )
    mix_rows = mix_all.reshape(n_dp, MIXH, 1, half)
    mix_rows = lax.all_gather(mix_rows, "tensor", axis=2, tiled=True)
    mix_rows = jnp.transpose(mix_rows, (1, 0, 2, 3)).reshape(MIXH, n_dp * seq_len)
    history_grad = jnp.stack(
        [
            sum(
                mix_rows[stream * HIST + source][None, :] * stream_grad[stream].astype(F32)
                for stream in range(STREAMS)
            )
            for source in range(HIST)
        ]
    ).astype(BF16)
    return (
        block.T,
        next_mix.T.reshape(seq_len, STREAMS, NEXT),
        history_grad,
        mix_grad[: STREAMS * HIST].T.reshape(seq_len, STREAMS, HIST),
        qkv_total.astype(F32),
        out_total.astype(F32),
        up_total.astype(F32),
        down_total.astype(F32),
        small_total[:, MIXH : MIXH + 2].T,
        small_total[:, MIXH + 2 : MIXH + 4].T,
        small_total[:, :MIXH],
        mixout_total,
        static_total,
    )


def solution(mesh):
    return jax.shard_map(
        functools.partial(per_device, mesh.shape["dp"]),
        mesh=mesh,
        in_specs=(
            P(None, "dp", None),
            P("dp", None, None),
            P(None, "dp", "tensor"),
            P("dp", "tensor"),
            P("dp", "tensor"),
            P("dp", "tensor"),
            P(None, "dp"),
            P(None, "dp"),
            P("dp", None),
            P(),
            P(),
            P("dp", None),
            P("dp", None, None),
        ),
        out_specs=(
            P("dp", None),
            P("dp", None, None),
            P(None, "dp", None),
            P("dp", None, None),
            P(None, "dp", "tensor"),
            P("dp", "tensor"),
            P("dp", "tensor"),
            P("dp", "tensor"),
            P(None, "dp"),
            P(None, "dp"),
            P("dp", None),
            P(),
            P(),
        ),
        check_vma=False,
    )


def lane_block(half, near, core, half_at, count):
    return at(near * 4 * half + core * 2 * half + half_at * half, count * half, half)


def join_kernel(
    part, streams, out_cot, small, mix_raw, next_raw,
    o_grad, o_wide, o_block, o_next, o_mixin, o_tiny,
    mix_out, next_cot, own, from_core, from_first, from_second, residual, wide, normed, block, cot, cot_in, back, low, next_rows, mixin, tiny,
    core_s, core_r, first_s, first_r, second_s, second_r, local, share_s, share_r, own_sem,
):
    here = Place()
    me, tensor = here.me, here.tensor
    depth, half = cot.shape
    spans = core_s.shape[0]
    size = depth // spans
    chunk = 256
    greet([{"dp": flip(me, CORE)}, {"dp": flip(me, NEAR)}, {"tensor": here.other}])

    def piece(span):
        return pl.ds(span * size, size)

    def tensor_first(span):
        return span < spans // 2

    def load(span, near, half_at):
        return pltpu.make_async_copy(
            part.at[piece(span), lane_block(half, near, here.core, half_at, 1)],
            own.at[near, half_at, piece(span)], local.at[span, near * 2 + half_at],
        )

    def to_core(span, near, half_at):
        return remote(
            part.at[piece(span), lane_block(half, near, 1 - here.core, half_at, 1)],
            from_core.at[near, half_at, piece(span)],
            core_s.at[span, near * 2 + half_at], core_r.at[span, near * 2 + half_at], dp=flip(me, CORE),
        )

    across = {"tensor": here.other}
    beside = {"dp": flip(me, NEAR)}

    def first_hop(span, block):
        source = own.at[block, here.other, piece(span)] if tensor_first(span) else own.at[1 - here.near, block, piece(span)]
        return remote(
            source, from_first.at[block, piece(span)], first_s.at[span, block], first_r.at[span, block],
            **(across if tensor_first(span) else beside),
        )

    def kept(span):
        return here.near if tensor_first(span) else tensor

    def second_hop(span):
        return remote(
            from_first.at[1 - kept(span), piece(span)], from_second.at[piece(span)], second_s.at[span], second_r.at[span],
            **(beside if tensor_first(span) else across),
        )

    def start(span):
        for near in range(2):
            for half_at in range(2):
                to_core(span, near, half_at).start()
                load(span, near, half_at).start()

    def after_core(span):
        for near in range(2):
            for half_at in range(2):
                load(span, near, half_at).wait()
                to_core(span, near, half_at).wait()
                own[near, half_at, piece(span)] += from_core[near, half_at, piece(span)]
        for block in range(2):
            first_hop(span, block).start()

    def after_first(span):
        for block in range(2):
            first_hop(span, block).wait()

        def add(block):
            mine = own[block, tensor, piece(span)] if tensor_first(span) else own[here.near, block, piece(span)]
            from_first[block, piece(span)] += mine

        add(1 - kept(span))
        second_hop(span).start()
        add(kept(span))

    mix_out[...] = jnp.zeros_like(mix_out)
    next_cot[...] = jnp.zeros_like(next_cot)
    mix_out[:MIXH, : STREAMS * NEXT] = mix_raw[...]
    next_cot[: STREAMS * NEXT, :] = next_raw[...]
    fetch = pltpu.make_async_copy(streams.at[3], residual, own_sem.at[0])
    fetch.start()
    cot_fetch = pltpu.make_async_copy(out_cot.at[at(tensor * half, half), :], cot_in, own_sem.at[7])
    cot_fetch.start()
    order = [span for pair in zip(range(spans // 2), range(spans // 2, spans)) for span in pair]
    for span in order:
        start(span)
    for span in order:
        after_core(span)
    for span in order:
        after_first(span)
    fetch.wait()
    cot_fetch.wait()

    def turn(index):
        rows = at(index * chunk, chunk)
        cot[rows, :] = cot_in[:, rows].T

    loop(0, depth // chunk, turn)
    squares = jnp.zeros((1, half), F32)
    for span in order:
        second_hop(span).wait()

        def widen(index, total):
            rows = at(span * size + index * chunk, chunk)
            branch = from_first[kept(span), rows, :].astype(F32) + from_second[rows, :].astype(F32)
            value = residual[rows, :].astype(F32) + branch
            wide[rows, :] = value
            block[:, rows] = value.T.astype(BF16)
            return total + jnp.sum(value * value, axis=0, keepdims=True)

        squares = lax.fori_loop(0, size // chunk, widen, squares)
    root = lax.rsqrt(squares / depth + ROOT_EPS)

    def share_block(which):
        mine = o_block.at[at(tensor * half, half), :]
        if which == 0:
            return pltpu.make_async_copy(block, mine, own_sem.at[1])
        return remote(block, mine, share_s.at[0], share_r.at[0], tensor=here.other)

    share_block(0).start()
    share_block(1).start()

    def norm(index):
        rows = at(index * chunk, chunk)
        normed[rows, :] = (wide[rows, :] * root).astype(BF16)

    loop(0, depth // chunk, norm)
    inner, slope = gelu_parts(tn(small[...], normed[...]))
    inner_low = inner.astype(BF16)
    next_rows[...] = tn(mix_out[...], inner_low)[:MIXH]
    next_low = next_cot[...].astype(BF16)

    column = lax.broadcasted_iota(jnp.int32, (128, 128), 1)
    static_grad = jnp.sum(next_cot[...], axis=1, keepdims=True)
    tiny[...] = jnp.where(column == MIXH, static_grad, nt(inner_low, next_low))[:MIXH]
    inner_grad = (nn(mix_out[...], next_low) * slope).astype(BF16)

    def pull(index, total):
        rows = at(index * chunk, chunk)
        value = jnp.dot(small[rows, :], inner_grad, preferred_element_type=F32)
        back[rows, :] = value
        return total + jnp.sum(value * wide[rows, :] * root, axis=0, keepdims=True)

    along = lax.fori_loop(0, depth // chunk, pull, jnp.zeros((1, half), F32)) / depth

    def finish(index):
        rows = at(index * chunk, chunk)
        value = cot[rows, :].astype(F32) + root * (back[rows, :] - wide[rows, :] * root * along)
        back[rows, :] = value
        low[rows, :] = value.astype(BF16)

    loop(0, depth // chunk, finish)

    def share(part_at, kind, index=0):
        rows = pl.ds(part_at * (depth // 2), depth // 2)
        number = 2 + part_at * 5 + kind + index
        if kind < 2:
            source, lanes, where = low.at[rows], lane_block(half, here.near, here.core, tensor, 1), (beside, across)[kind]
        elif kind == 2:
            far, where = (1 - here.near, across) if part_at == 0 else (here.near, beside)
            lanes = lane_block(half, far, here.core, tensor if part_at == 0 else here.other, 1)
            source = o_grad.at[rows, lanes]
        else:
            lanes, where = lane_block(half, index, here.core, 0, 2), {"dp": flip(me, CORE)}
            source = o_grad.at[rows, lanes]
        return remote(source, o_grad.at[rows, lanes], share_s.at[number], share_r.at[number], **where)

    for part_at in range(2):
        share(part_at, 0).start()
        share(part_at, 1).start()
    keep = pltpu.make_async_copy(
        low, o_grad.at[:, lane_block(half, here.near, here.core, tensor, 1)], own_sem.at[2]
    )
    keep.start()

    def mixin_rows(index):
        rows = at(index * chunk, chunk)
        mixin[rows, :] = nt(normed[rows, :], inner_grad)

    loop(0, depth // chunk, mixin_rows)
    for part_at in range(2):
        share(part_at, part_at).wait()
        share(part_at, 2).start()
    lanes = at(tensor * half, half)
    next_share = remote(next_rows, o_next.at[:, lanes], share_s.at[1], share_r.at[1], tensor=here.other)
    next_share.start()
    finals = [
        pltpu.make_async_copy(next_rows, o_next.at[:, lanes], own_sem.at[3]),
        pltpu.make_async_copy(back, o_wide, own_sem.at[4]),
        pltpu.make_async_copy(mixin, o_mixin, own_sem.at[5]),
        pltpu.make_async_copy(tiny, o_tiny, own_sem.at[6]),
    ]
    for copy in finals:
        copy.start()
    keep.wait()
    for part_at in range(2):
        share(part_at, 1 - part_at).wait()
        share(part_at, 2).wait()
        for near in range(2):
            share(part_at, 3, near).start()
    for part_at in range(2):
        for near in range(2):
            share(part_at, 3, near).wait()
    share_block(0).wait()
    share_block(1).wait()
    next_share.wait()
    for copy in finals:
        copy.wait()


def join(part, streams, out_cot, small, mix_out, next_cot):
    depth, half = streams.shape[1:]
    spans = 4
    shapes = [
        ((depth, 8 * half), BF16),
        ((depth, half), F32),
        ((2 * half, depth), BF16),
        ((MIXH, 2 * half), F32),
        ((depth, 128), F32),
        ((MIXH, 128), F32),
    ]
    return pl.pallas_call(
        join_kernel,
        out_shape=[jax.ShapeDtypeStruct(*shape) for shape in shapes],
        in_specs=[ANY] * 3 + [VM] * 3,
        out_specs=[ANY] * 6,
        scratch_shapes=[
            pltpu.VMEM((128, 128), BF16),
            pltpu.VMEM((128, half), F32),
            pltpu.VMEM((2, 2, depth, half), BF16),
            pltpu.VMEM((2, 2, depth, half), BF16),
            pltpu.VMEM((2, depth, half), BF16),
            pltpu.VMEM((depth, half), BF16),
            pltpu.VMEM((depth, half), BF16),
            pltpu.VMEM((depth, half), F32),
            pltpu.VMEM((depth, half), BF16),
            pltpu.VMEM((half, depth), BF16),
            pltpu.VMEM((depth, half), BF16),
            pltpu.VMEM((half, depth), BF16),
            pltpu.VMEM((depth, half), F32),
            pltpu.VMEM((depth, half), BF16),
            pltpu.VMEM((MIXH, half), F32),
            pltpu.VMEM((depth, 128), F32),
            pltpu.VMEM((MIXH, 128), F32),
            DMA((spans, 4)),
            DMA((spans, 4)),
            DMA((spans, 2)),
            DMA((spans, 2)),
            DMA((spans,)),
            DMA((spans,)),
            DMA((spans, 4)),
            DMA((12,)),
            DMA((12,)),
            DMA((8,)),
        ],
        compiler_params=pltpu.CompilerParams(
            collective_id=2, has_side_effects=True, vmem_limit_bytes=56 * 1024 * 1024
        ),
        name="join",
    )(part, streams, out_cot, small, mix_out, next_cot)


def back_kernel(
    grad, w_qkv, w_out, w_up, w_down, rows, sums, slope, cos, sin,
    o_attn, o_mlp, o_up_grad, o_row_grad,
    grad_in, qkv_in, out_in, up_in, down_in, rows_in, sums_in, slope_in,
    up_grad, context_grad, row_grad, tall, load_sem, tall_sem, save_sem,
):
    depth, tokens = grad.shape
    seq_len = sums.shape[1]
    heads = rows.shape[1] // HD
    tile = 256
    loads = {}
    pairs = (
        ("grad", grad, grad_in), ("down", w_down, down_in), ("slope", slope, slope_in), ("up", w_up, up_in),
        ("out", w_out, out_in), ("rows", rows, rows_in), ("sums", sums, sums_in), ("qkv", w_qkv, qkv_in),
    )
    for number, (name, source, target) in enumerate(pairs):
        loads[name] = pltpu.make_async_copy(source, target, load_sem.at[number])
        loads[name].start()

    pending = {}

    def write(turn, out, compute):
        slots = tall.shape[1]
        if turn in pending:
            pending.pop(turn)()

        def copy(index):
            slot = lax.rem(index, slots)
            target = out.at[at(index * tile, tile), :]
            return pltpu.make_async_copy(tall.at[turn, slot], target, tall_sem.at[turn, slot])

        def body(index):
            @pl.when(index >= slots)
            def _():
                copy(index - slots).wait()

            tall[turn, lax.rem(index, slots)] = compute(at(index * tile, tile)).astype(BF16)
            copy(index).start()

        steps = depth // tile
        loop(0, steps, body)
        pending[turn] = lambda: loop(steps - slots, steps, lambda index: copy(index).wait())

    for name in ("grad", "down", "slope"):
        loads[name].wait()

    def lift(index):
        span = at(index * tile, tile)
        up_grad[span, :] = (tn(down_in[:, span], grad_in[...]) * slope_in[span, :]).astype(BF16)

    loop(0, up_grad.shape[0] // tile, lift)
    loads["up"].wait()
    save_up = pltpu.make_async_copy(up_grad, o_up_grad, save_sem.at[0])
    save_up.start()
    write(1, o_mlp, lambda span: nn(up_in[span, :], up_grad[...]))
    for name in ("out", "rows", "sums"):
        loads[name].wait()
    context_grad[...] = tn(out_in[...], grad_in[...]).astype(BF16)

    def attend(seq):
        span = at(seq * seq_len, seq_len)
        for head in range(heads):
            lane = pl.ds(head * HD, HD)
            queries, keys, values = (rows_in[s, lane, span] for s in range(3))
            prob = jnp.exp(causal_scores(keys, queries) - sums_in[pl.ds(seq * heads + head, 1), :])
            outer = context_grad[lane, span]
            value_grad = nt(outer, prob.astype(BF16))
            prob_grad = tn(values, outer)
            inner = jnp.sum(prob * prob_grad, axis=0, keepdims=True)
            score_grad = (prob * (prob_grad - inner)).astype(BF16)
            query_grad = nn(keys, score_grad) * (1.0 / math.sqrt(HD))
            key_grad = nt(queries, score_grad) * (1.0 / math.sqrt(HD))
            row_grad[0, lane, span] = turned(query_grad, cos[...], -sin[...]).astype(BF16)
            row_grad[1, lane, span] = turned(key_grad, cos[...], -sin[...]).astype(BF16)
            row_grad[2, lane, span] = value_grad.astype(BF16)

    loop(0, tokens // seq_len, attend)
    save_rows = pltpu.make_async_copy(row_grad, o_row_grad, save_sem.at[1])
    save_rows.start()
    loads["qkv"].wait()
    for stream in range(3):
        write(stream % 2, o_attn.at[stream], lambda span: nn(qkv_in[stream, span, :], row_grad[stream]))
    for drain in pending.values():
        drain()
    save_up.wait()
    save_rows.wait()


def back(grad, w_qkv, w_out, w_up, w_down, rows, sums, slope, cos, sin):
    depth, tokens = grad.shape
    operands = (grad, w_qkv, w_out, w_up, w_down, rows, sums, slope)
    shapes = [(3, depth, tokens), (depth, tokens), slope.shape, rows.shape]
    return pl.pallas_call(
        back_kernel,
        out_shape=[jax.ShapeDtypeStruct(shape, BF16) for shape in shapes],
        in_specs=[ANY] * 8 + [VM] * 2,
        out_specs=[ANY] * 4,
        scratch_shapes=[pltpu.VMEM(v.shape, v.dtype) for v in operands]
        + [
            pltpu.VMEM(slope.shape, BF16),
            pltpu.VMEM(rows.shape[1:], BF16),
            pltpu.VMEM(rows.shape, BF16),
            pltpu.VMEM((2, 4, 256, tokens), BF16),
            DMA((8,)),
            DMA((2, 4)),
            DMA((2,)),
        ],
        compiler_params=pltpu.CompilerParams(vmem_limit_bytes=56 * 1024 * 1024),
        name="back",
    )(*operands, cos, sin)


def scatter_kernel(
    n_dp, attn_grad, mlp_grad, streams, small, wide_grad, mixin_part, mix_tiny, hist,
    branch_grad, act, hidden, up_grad, context, row_grad,
    o_stream, o_mix, o_small, o_tiny, o_qkv, o_up, o_down, o_out, sent_qkv, sent_up, sent_down, sent_out,
    own, from_core, from_tensor, from_near, rows_in, wide, stream_grad, gains, biases, tiny, tiny_in, tiny_out,
    hist_in, arrived, mix_part, mix_in, mix_sum, tiny_sum, ring, side_in, mine, high_in,
    hidden_in, up_in, context_in, rows_grad_in, tile_in, stage, tile_sem, stage_sem, right_sem,
    core_s, core_r, tensor_s, tensor_r, near_s, near_r, local, in_sem,
    side_s, side_r, high_s, high_r, peer_s, peer_r, peer_local,
    a2a_s, a2a_r, a2a_own, keep_sem, pass_s, pass_r, tiny_s, tiny_r, mix_s, mix_r, hist_sem,
    ring_s, ring_r, last_s, last_r, last_local,
):
    here = Place()
    me, tensor = here.me, here.tensor
    depth, half = wide_grad.shape
    rows = depth // n_dp
    high_bits = int(math.log2(n_dp // HIGH))
    chunk = min(256, depth)
    greet_all(n_dp, me, here.other)

    highs = n_dp // HIGH
    tall = 2 * rows
    arrays = (
        (branch_grad, hidden_in, sent_down, o_down),
        (act.at[3], up_in, sent_up, o_up),
        (branch_grad, context_in, sent_out, o_out),
    ) + tuple((act.at[s], rows_grad_in.at[s], sent_qkv.at[s], o_qkv.at[s]) for s in range(3))
    units, first_unit = [], []
    for _, right, sent, o in arrays:
        first_unit.append(len(units))
        units += [(sent, o, first) for first in range(0, right.shape[0], UNIT)]
    total = len(units)
    rights = [
        pltpu.make_async_copy(source, target, right_sem.at[number])
        for number, (source, target) in enumerate(
            ((hidden, hidden_in), (up_grad, up_in), (context, context_in), (row_grad, rows_grad_in))
        )
    ]

    def side_hop(unit):
        sent, _, first = units[unit]
        return remote(
            sent.at[:, :, :, pl.ds(first, UNIT)], side_in.at[unit], side_s.at[unit], side_r.at[unit], dp=flip(me, SIDE)
        )

    count = highs * 2

    def tile_load(array, block):
        mine_now = lax.div(block, count)
        side = here.side * mine_now + (1 - here.side) * (1 - mine_now)
        row = (lax.rem(block, count) * 2 + side) * tall
        slot = lax.rem(block, 2)
        return pltpu.make_async_copy(arrays[array][0].at[at(row, tall), :], tile_in.at[slot], tile_sem.at[slot])

    def product(array, block):
        @pl.when(block + 1 < 2 * count)
        def _():
            tile_load(array, block + 1).start()

        tile_load(array, block).wait()
        return nt(tile_in[lax.rem(block, 2)], arrays[array][1][...]).astype(BF16)

    def compute_sent(array):
        _, right, sent, _ = arrays[array]
        width = right.shape[0]

        def put(block):
            slot = lax.rem(block, 2)
            return pltpu.make_async_copy(
                stage.at[slot, :, pl.ds(0, width)], sent.at[lax.div(block, 2), slot], stage_sem.at[slot]
            )

        def body(block):
            value = product(array, block)

            @pl.when(block >= 2)
            def _():
                put(block - 2).wait()

            stage[lax.rem(block, 2), :, :width] = value
            put(block).start()

        tile_load(array, 0).start()
        loop(0, count, body)
        put(count - 2).wait()
        put(count - 1).wait()

    def compute_mine(array):
        width = arrays[array][1].shape[0]

        def body(block):
            value = product(array, block)
            flat = block - count
            for part in range(width // UNIT):
                mine[first_unit[array] + part, lax.div(flat, 2), lax.rem(flat, 2)] = value[
                    :, part * UNIT : (part + 1) * UNIT
                ]

        loop(count, 2 * count, body)

    def high_hop(unit, phase):
        span = 1 << phase
        base = lax.div(here.high, span)
        theirs = base + 1 - 2 * lax.rem(base, 2)
        return remote(
            mine.at[unit, pl.ds(theirs * span, span)], high_in.at[unit, pl.ds(span - 1, span)],
            high_s.at[unit, phase], high_r.at[unit, phase], dp=flip(me, HIGH << phase),
        )

    def peer_hop(unit, peer):
        _, o, first = units[unit]
        target, _ = here.peers[peer]
        return remote(
            mine.at[unit, here.high, bit(target, NEAR), at(bit(target, CORE) * rows, rows)],
            o.at[:, at(here.quarter * (o.shape[-1] // QUARTERS) + first, UNIT)],
            peer_s.at[unit, peer], peer_r.at[unit, peer], dp=target,
        )

    def peer_keep(unit):
        _, o, first = units[unit]
        return pltpu.make_async_copy(
            mine.at[unit, here.high, here.near, at(here.core * rows, rows)],
            o.at[:, at(here.quarter * (o.shape[-1] // QUARTERS) + first, UNIT)], peer_local.at[unit],
        )

    def add_blocks(unit, other, first_mine, first_other, count):
        step = min(64, tall)

        def add(flat):
            high, rest = lax.div(flat, 2 * (tall // step)), lax.rem(flat, 2 * (tall // step))
            near, span = lax.div(rest, tall // step), at(lax.rem(rest, tall // step) * step, step)
            mine[unit, first_mine + high, near, span] += other[unit, first_other + high, near, span]

        loop(0, count * 2 * (tall // step), add)

    def finish_high(unit):
        for phase in reversed(range(high_bits)):
            high_hop(unit, phase).wait()
            span = 1 << phase
            add_blocks(unit, high_in, lax.div(here.high, span) * span, span - 1, span)
            if phase:
                high_hop(unit, phase - 1).start()
        peer_keep(unit).start()
        for peer in range(3):
            peer_hop(unit, peer).start()

    def tick(unit):
        side_hop(unit).wait()
        if unit + 2 < total:
            side_hop(unit + 2).start()
        add_blocks(unit, side_in, 0, 0, n_dp // HIGH)
        if unit:
            finish_high(unit - 1)
        high_hop(unit, high_bits - 1).start()

    done = 0

    def ticks(count):
        nonlocal done
        for unit in range(done, min(done + count, total)):
            tick(unit)
        done = min(done + count, total)

    def load(stream, near, half_at):
        part = attn_grad.at[stream] if stream < 3 else mlp_grad
        return pltpu.make_async_copy(
            part.at[:, lane_block(half, near, here.core, half_at, 1)], own.at[stream % 2, near, half_at],
            local.at[stream, near * 2 + half_at],
        )

    def to_core(stream, near, half_at):
        part = attn_grad.at[stream] if stream < 3 else mlp_grad
        return remote(
            part.at[:, lane_block(half, near, 1 - here.core, half_at, 1)], from_core.at[stream, near, half_at],
            core_s.at[stream, near * 2 + half_at], core_r.at[stream, near * 2 + half_at], dp=flip(me, CORE),
        )

    def to_tensor(stream, near):
        return remote(
            own.at[stream % 2, near, here.other], from_tensor.at[stream, near],
            tensor_s.at[stream, near], tensor_r.at[stream, near], tensor=here.other,
        )

    def to_near(stream):
        return remote(
            from_tensor.at[stream, 1 - here.near], from_near.at[stream], near_s.at[stream], near_r.at[stream],
            dp=flip(me, NEAR),
        )

    def after_core(stream):
        for near in range(2):
            for half_at in range(2):
                load(stream, near, half_at).wait()
                to_core(stream, near, half_at).wait()

        def add(index):
            span = at(index * chunk, chunk)
            for near in range(2):
                for half_at in range(2):
                    own[stream % 2, near, half_at, span] += from_core[stream, near, half_at, span]

        loop(0, depth // chunk, add)

    def after_tensor(stream):
        for near in range(2):
            to_tensor(stream, near).wait()

        def add(index):
            span = at(index * chunk, chunk)
            for near in range(2):
                from_tensor[stream, near, span] += own[stream % 2, near, tensor, span]

        loop(0, depth // chunk, add)
        to_near(stream).start()

    stats = []

    def measure(stream):
        def piece(index):
            return rows_in[stream, at(index * chunk, chunk), :].astype(F32)

        centre = sum_rows(piece, depth, chunk, lambda v: v) / depth
        spread = sum_rows(piece, depth, chunk, lambda v: (v - centre) * (v - centre)) / depth
        stats.append((centre, lax.rsqrt(spread + NORM_EPS)))

    def back_norm(stream):
        to_near(stream).wait()
        group = 0 if stream < 3 else 1
        centre, root = stats[stream]

        def parts(index):
            span = at(index * chunk, chunk)
            grad = from_tensor[stream, here.near, span].astype(F32) + from_near[stream, span].astype(F32)
            hat = (rows_in[stream, span, :].astype(F32) - centre) * root
            gain = small[span, MIXH + group : MIXH + group + 1].astype(F32)
            return span, grad, hat, grad * gain

        def sums(index, carry):
            span, grad, hat, scaled = parts(index)
            if stream in (0, 3):
                gains[group, span] = grad * hat
                biases[group, span] = grad
            else:
                gains[group, span] += grad * hat
                biases[group, span] += grad
            return (
                carry[0] + jnp.sum(scaled, axis=0, keepdims=True),
                carry[1] + jnp.sum(scaled * hat, axis=0, keepdims=True),
            )

        zero = jnp.zeros((1, half), F32)
        whole, along = lax.fori_loop(0, depth // chunk, sums, (zero, zero))

        def finish(index):
            span, _, hat, scaled = parts(index)
            value = root * (scaled - whole / depth - hat * (along / depth))
            if stream == 3:
                value = value + wide[span, :]
            stream_grad[stream, span] = value.astype(BF16)

        loop(0, depth // chunk, finish)
        loop(1, n_dp, lambda step: send(stream, step).start())
        send_own(stream).start()

    def send(stream, step):
        target = lax.rem(me + step, n_dp)
        return remote(
            stream_grad.at[stream, at(target * rows, rows), :], arrived.at[stream, step],
            a2a_s.at[stream, step], a2a_r.at[stream, step], dp=target,
        )

    def send_own(stream):
        return pltpu.make_async_copy(
            stream_grad.at[stream, at(me * rows, rows), :], arrived.at[stream, 0], a2a_own.at[stream]
        )

    def source_of(step):
        return lax.rem(me - step + n_dp, n_dp)

    def lanes_of(step):
        return at(source_of(step) * 2 * half + tensor * half, half)

    def fetch(step):
        slot = lax.rem(step, 2)
        return pltpu.make_async_copy(hist.at[:, :, lanes_of(step)], hist_in.at[slot], hist_sem.at[slot])

    def keep(stream, step):
        return pltpu.make_async_copy(
            arrived.at[stream, step], o_stream.at[stream, :, lanes_of(step)], keep_sem.at[stream, step]
        )

    def pass_on(stream, step):
        return remote(
            arrived.at[stream, step], o_stream.at[stream, :, lanes_of(step)],
            pass_s.at[stream, step], pass_r.at[stream, step], tensor=here.other,
        )

    def mix_send(step):
        return remote(mix_part.at[step], mix_in.at[step], mix_s.at[step], mix_r.at[step], dp=source_of(step))

    def receive(stream):
        fetch(0).start()
        send_own(stream).wait()

        def one(step):
            @pl.when(step + 1 < n_dp)
            def _():
                fetch(step + 1).start()

            @pl.when(step > 0)
            def _():
                send(stream, step).wait()

            keep(stream, step).start()
            pass_on(stream, step).start()
            fetch(step).wait()
            totals = [jnp.zeros((8, half), F32) for _ in range(HIST)]
            for row in range(0, rows, 16):
                span = pl.ds(row, 16)
                grad = arrived[stream, step, span, :].astype(F32)
                for source in range(HIST):
                    product = grad * hist_in[lax.rem(step, 2), source, span, :].astype(F32)
                    totals[source] = totals[source] + product[:8] + product[8:]
            for source in range(HIST):
                mix_part[step, pl.ds(stream * HIST + source, 1), :] = jnp.sum(totals[source], axis=0, keepdims=True)
            if stream == STREAMS - 1:

                @pl.when(step > 0)
                def _():
                    mix_send(step).start()

        loop(0, n_dp, one)

    ring_targets = [{"dp": flip(me, value)} for value in (CORE, SIDE, NEAR)]
    ring_targets += [{"dp": flip(me, HIGH << phase)} for phase in range(high_bits)]
    ring_targets.append({"tensor": here.other})
    hops = len(ring_targets)

    def ring_hop(hop):
        return remote(ring.at[hop, 0], ring.at[hop, 1], ring_s.at[hop], ring_r.at[hop], **ring_targets[hop])

    def ring_step(hop):
        ring_hop(hop).wait()
        ring[hop + 1, 0] = ring[hop, 0] + ring[hop, 1]
        if hop + 1 < hops:
            ring_hop(hop + 1).start()

    rights[0].start()
    inputs = [
        pltpu.make_async_copy(streams, rows_in, in_sem.at[0]),
        pltpu.make_async_copy(wide_grad, wide, in_sem.at[1]),
        pltpu.make_async_copy(mix_tiny, ring.at[0, 0], in_sem.at[2]),
    ]

    def load_own(stream):
        for near in range(2):
            for half_at in range(2):
                load(stream, near, half_at).start()

    def tensor_start(stream):
        for near in range(2):
            to_tensor(stream, near).start()

    for stream in range(STREAMS):
        for near in range(2):
            for half_at in range(2):
                to_core(stream, near, half_at).start()
        if stream < 2:
            load_own(stream)
    for copy in rights[1:] + inputs:
        copy.start()
    rights[0].wait()
    compute_sent(0)
    side_hop(0).start()
    side_hop(1).start()
    after_core(0)
    tensor_start(0)
    compute_mine(0)
    for copy in rights[1:] + inputs:
        copy.wait()
    ring_hop(0).start()
    mix_part[...] = jnp.zeros_like(mix_part)
    for stream in range(STREAMS):
        measure(stream)
    after_core(1)
    ring_step(0)
    compute_sent(1)
    compute_mine(1)
    for stream in range(STREAMS):
        ticks(2)
        after_tensor(stream)
        if stream + 1 < STREAMS:
            tensor_start(stream + 1)
            if stream + 1 < hops:
                ring_step(stream + 1)
        if stream + 2 < STREAMS:
            load_own(stream + 2)
        if stream == 0:
            for array in range(2, len(arrays)):
                compute_sent(array)
                compute_mine(array)
        if stream + 2 < STREAMS:
            after_core(stream + 2)
        if stream > 0:
            back_norm(stream - 1)
        if stream > 1:
            receive(stream - 2)
    back_norm(STREAMS - 1)

    column = lax.broadcasted_iota(jnp.int32, (chunk, 128), 1)
    pltpu.make_async_copy(mixin_part, wide, in_sem.at[0]).start()
    pltpu.make_async_copy(mixin_part, wide, in_sem.at[0]).wait()

    def gather_tiny(index):
        span = at(index * chunk, chunk)
        value = wide[span, :]
        for group in range(2):
            gain = jnp.sum(gains[group, span], axis=1, keepdims=True)
            bias = jnp.sum(biases[group, span], axis=1, keepdims=True)
            value = jnp.where(column == MIXH + group, gain, value)
            value = jnp.where(column == MIXH + 2 + group, bias, value)
        tiny[span, :] = value.astype(BF16)

    loop(0, depth // chunk, gather_tiny)

    def tiny_send(step):
        target = lax.rem(me + step, n_dp)
        return remote(tiny.at[at(target * rows, rows), :], tiny_in.at[step], tiny_s.at[step], tiny_r.at[step], dp=target)

    loop(1, n_dp, lambda step: tiny_send(step).start())
    receive(2)
    ticks(2)
    receive(3)
    for hop in range(STREAMS, hops):
        ring_step(hop)
    tiny_final = pltpu.make_async_copy(ring.at[hops, 0], o_tiny, last_local.at[0])
    tiny_final.start()
    ticks(total)

    tiny_sum[0] = tiny[at(me * rows, rows), :].astype(F32)

    def add_tiny(step):
        tiny_send(step).wait()
        tiny_sum[0] += tiny_in[step].astype(F32)

    loop(1, n_dp, add_tiny)
    tiny_share = remote(tiny_sum.at[0], tiny_sum.at[1], last_s.at[1], last_r.at[1], tensor=here.other)
    tiny_share.start()
    mix_sum[...] = mix_part[0]

    def add_mix(step):
        mix_send(step).wait()
        mix_sum[...] += mix_in[step]

    loop(1, n_dp, add_mix)
    lanes = at(tensor * half, half)
    mix_share = remote(mix_sum, o_mix.at[:, lanes], last_s.at[0], last_r.at[0], tensor=here.other)
    mix_keep = pltpu.make_async_copy(mix_sum, o_mix.at[:, lanes], last_local.at[1])
    mix_share.start()
    mix_keep.start()
    finish_high(total - 1)
    tiny_share.wait()
    tiny_out[...] = (tiny_sum[0] + tiny_sum[1]).T
    tiny_keep = pltpu.make_async_copy(tiny_out, o_small, last_local.at[2])
    tiny_keep.start()
    for unit in range(total):
        peer_keep(unit).wait()
        for peer in range(3):
            peer_hop(unit, peer).wait()

    def settle(step):
        for stream in range(STREAMS):
            keep(stream, step).wait()
            pass_on(stream, step).wait()

    loop(0, n_dp, settle)
    mix_share.wait()
    mix_keep.wait()
    tiny_keep.wait()
    tiny_final.wait()


def scatter(
    n_dp, attn_grad, mlp_grad, streams, small, wide_grad, mixin_part, mix_tiny, hist,
    branch_grad, act, hidden, up_grad, context, row_grad,
):
    depth, half = wide_grad.shape
    rows = depth // n_dp
    high = n_dp // HIGH
    high_bits = int(math.log2(high))
    tokens = act.shape[2]
    narrow, width = context.shape[0], hidden.shape[0]
    widths = ((3,), narrow), ((), width), ((), width), ((), narrow)
    units = (4 * narrow + 2 * width) // UNIT
    hops = high_bits + 4

    outs = [
        ((STREAMS, rows, 2 * half * n_dp), BF16),
        ((MIXH, 2 * half), F32),
        ((128, rows), F32),
        (mix_tiny.shape, F32),
    ]
    outs += [(lead + (rows, QUARTERS * size), BF16) for lead, size in widths]
    outs += [(lead + (high, 2, 2 * rows, size), BF16) for lead, size in widths]
    return pl.pallas_call(
        functools.partial(scatter_kernel, n_dp),
        out_shape=[jax.ShapeDtypeStruct(*shape) for shape in outs],
        in_specs=[ANY, ANY, ANY, VM] + [ANY] * 10,
        out_specs=[ANY] * 12,
        scratch_shapes=[
            pltpu.VMEM((2, 2, 2, depth, half), BF16),
            pltpu.VMEM((STREAMS, 2, 2, depth, half), BF16),
            pltpu.VMEM((STREAMS, 2, depth, half), BF16),
            pltpu.VMEM((STREAMS, depth, half), BF16),
            pltpu.VMEM((STREAMS, depth, half), BF16),
            pltpu.VMEM((depth, half), F32),
            pltpu.VMEM((STREAMS, depth, half), BF16),
            pltpu.VMEM((2, depth, half), F32),
            pltpu.VMEM((2, depth, half), F32),
            pltpu.VMEM((depth, 128), BF16),
            pltpu.VMEM((n_dp, rows, 128), BF16),
            pltpu.VMEM((128, rows), F32),
            pltpu.VMEM((2, HIST, rows, half), BF16),
            pltpu.VMEM((STREAMS, n_dp, rows, half), BF16),
            pltpu.VMEM((n_dp, MIXH, half), F32),
            pltpu.VMEM((n_dp, MIXH, half), F32),
            pltpu.VMEM((MIXH, half), F32),
            pltpu.VMEM((2, rows, 128), F32),
            pltpu.VMEM((hops + 1, 2) + mix_tiny.shape, F32),
            pltpu.VMEM((units, high, 2, 2 * rows, UNIT), BF16),
            pltpu.VMEM((units, high, 2, 2 * rows, UNIT), BF16),
            pltpu.VMEM((units, high - 1, 2, 2 * rows, UNIT), BF16),
            pltpu.VMEM(hidden.shape, BF16),
            pltpu.VMEM(up_grad.shape, BF16),
            pltpu.VMEM(context.shape, BF16),
            pltpu.VMEM(row_grad.shape, BF16),
            pltpu.VMEM((2, 2 * rows, tokens), BF16),
            pltpu.VMEM((2, 2 * rows, width), BF16),
            DMA((2,)),
            DMA((2,)),
            DMA((4,)),
            DMA((STREAMS, 4)),
            DMA((STREAMS, 4)),
            DMA((STREAMS, 2)),
            DMA((STREAMS, 2)),
            DMA((STREAMS,)),
            DMA((STREAMS,)),
            DMA((STREAMS, 4)),
            DMA((3,)),
            DMA((units,)),
            DMA((units,)),
            DMA((units, high_bits)),
            DMA((units, high_bits)),
            DMA((units, 3)),
            DMA((units, 3)),
            DMA((units,)),
            DMA((STREAMS, n_dp)),
            DMA((STREAMS, n_dp)),
            DMA((STREAMS,)),
            DMA((STREAMS, n_dp)),
            DMA((STREAMS, n_dp)),
            DMA((STREAMS, n_dp)),
            DMA((n_dp,)),
            DMA((n_dp,)),
            DMA((n_dp,)),
            DMA((n_dp,)),
            DMA((2,)),
            DMA((hops,)),
            DMA((hops,)),
            DMA((2,)),
            DMA((2,)),
            DMA((3,)),
        ],
        compiler_params=pltpu.CompilerParams(
            collective_id=3, has_side_effects=True, vmem_limit_bytes=62 * 1024 * 1024
        ),
        name="scatter",
    )(
        attn_grad, mlp_grad, streams, small, wide_grad, mixin_part, mix_tiny, hist, branch_grad, act, hidden, up_grad,
        context, row_grad,
    )[:8]


def rotary_tables(length, rotary, float_type):
    half_rot = rotary // 2
    places = jnp.arange(length).astype(float_type)
    frequency = jnp.exp(
        jnp.arange(half_rot).astype(float_type) * (-2.0 * math.log(10000.0) / rotary)
    )
    angles = places[:, None] * frequency[None, :]
    return (jnp.cos(angles), jnp.sin(angles))


def finish_kernel(mix_rows, stream_grad, *refs):
    narrow, history_grad, wide = refs[:4], refs[4], refs[5:]
    rows = stream_grad.shape[1]
    tile, span = min(32, rows), 512

    def body(index):
        row = at(lax.rem(index, rows // tile) * tile, tile)
        lane = at(lax.div(index, rows // tile) * span, span)
        grads = [stream_grad[stream, row, lane].astype(F32) for stream in range(STREAMS)]
        for source in range(HIST):
            total = sum(
                mix_rows[pl.ds(stream * HIST + source, 1), lane] * grads[stream] for stream in range(STREAMS)
            )
            history_grad[source, row, lane] = total.astype(BF16)

    loop(0, rows // tile * (stream_grad.shape[2] // span), body)
    for low, full in zip(narrow, wide):
        full[...] = low[...].astype(F32)


def finish(mix_rows, stream_grad, *grads):
    rows, tokens = stream_grad.shape[1:]
    steps = rows // 16
    lanes = tokens // steps

    def weight(g):
        if g.ndim == 3:
            return pl.BlockSpec((g.shape[0], 16, g.shape[2]), lambda i: (0, i, 0))
        return pl.BlockSpec((16, g.shape[1]), lambda i: (i, 0))

    def along(count):
        return pl.BlockSpec((count, rows, lanes), lambda i: (0, 0, i))

    return pl.pallas_call(
        finish_kernel,
        grid=(steps,),
        out_shape=[jax.ShapeDtypeStruct((HIST, rows, tokens), BF16)]
        + [jax.ShapeDtypeStruct(g.shape, F32) for g in grads],
        in_specs=[pl.BlockSpec((mix_rows.shape[0], lanes), lambda i: (0, i)), along(STREAMS)]
        + [weight(g) for g in grads],
        out_specs=[along(HIST)] + [weight(g) for g in grads],
        compiler_params=pltpu.CompilerParams(vmem_limit_bytes=60 * 1024 * 1024),
        name="finish",
    )(mix_rows, stream_grad, *grads)


def per_device(
    n_dp, history, mix_weights, w_qkv, w_out, w_up, w_down, norm_gain, norm_bias, mix_in, mix_out, mix_static,
    out_cot, next_cot,
):
    tensor = lax.axis_index("tensor")
    seq_len = mix_weights.shape[0]
    half = seq_len // 2
    depth = mix_in.shape[0] * n_dp

    def own_half(rows):
        return lax.dynamic_slice_in_dim(rows, tensor * half, half, 0)

    mix_rows = own_half(mix_weights.reshape(seq_len, -1)).T
    small = jnp.concatenate(
        [mix_in.T, norm_gain, norm_bias, jnp.zeros((128 - MIXH - 4, mix_in.shape[0]), BF16)], axis=0
    )
    cos, sin = (table.T for table in rotary_tables(seq_len, ROT, F32))
    mix_rows, small_all, streams, act, qkv, out, up, down, rows, context, sums, hidden, slope, part = gather(
        n_dp, history, mix_rows, small, w_qkv, w_out, w_up, w_down, cos, sin
    )
    small_all = small_all.reshape(depth, 128)
    qkv, up, down, out = (
        qkv.reshape(3, depth, -1), up.reshape(depth, -1), down.reshape(depth, -1), out.reshape(depth, -1)
    )

    next_rows = own_half(next_cot.reshape(seq_len, -1)).T
    branch_grad, wide_grad, block, next_mix, mixin_part, tiny = join(
        part, streams, out_cot, small_all, mix_out, next_rows
    )
    attn_in_grad, mlp_in_grad, up_grad, row_grad = back(
        branch_grad, qkv, out, up, down, rows, sums, slope, cos, sin
    )
    stream_grad, mix_grad, small_total, tiny, qkv_total, up_total, down_total, out_total = scatter(
        n_dp, attn_in_grad, mlp_in_grad, streams, small_all, wide_grad, mixin_part, tiny, history,
        branch_grad, act, hidden, up_grad, context, row_grad,
    )
    history_grad, qkv_total, up_total, down_total, out_total = finish(
        mix_rows, stream_grad, qkv_total, up_total, down_total, out_total
    )
    return (
        block,
        (next_mix.T + mix_static).reshape(seq_len, STREAMS, NEXT),
        history_grad,
        mix_grad[: STREAMS * HIST].T.reshape(seq_len, STREAMS, HIST),
        qkv_total,
        out_total,
        up_total,
        down_total,
        small_total[MIXH : MIXH + 2],
        small_total[MIXH + 2 : MIXH + 4],
        small_total[:MIXH].T,
        tiny[:, : STREAMS * NEXT],
        tiny[: STREAMS * NEXT, MIXH],
    )


def solution(mesh):
    return jax.shard_map(
        functools.partial(per_device, mesh.shape["dp"]),
        mesh=mesh,
        in_specs=(
            P(None, "dp", None),
            P("dp", None, None),
            P(None, "dp", "tensor"),
            P("dp", "tensor"),
            P("dp", "tensor"),
            P("dp", "tensor"),
            P(None, "dp"),
            P(None, "dp"),
            P("dp", None),
            P(),
            P(),
            P("dp", None),
            P("dp", None, None),
        ),
        out_specs=(
            P("dp", None),
            P("dp", None, None),
            P(None, "dp", None),
            P("dp", None, None),
            P(None, "dp", "tensor"),
            P("dp", "tensor"),
            P("dp", "tensor"),
            P("dp", "tensor"),
            P(None, "dp"),
            P(None, "dp"),
            P("dp", None),
            P(),
            P(),
        ),
        check_vma=False,
    )
```

```python
import functools
import math

import jax
import jax.numpy as jnp
from jax import lax
from jax.experimental import pallas as pl
from jax.experimental.pallas import tpu as pltpu
from jax.sharding import PartitionSpec as P

HD = 128
ROT = 32
HIST = 9
STREAMS = 4
NEXT = 10
MIXH = 40

NORM_EPS = 1e-05
ROOT_EPS = 1e-06
MASKED = -1e30

MESH = pl.DeviceIdType.MESH
ANY = pl.BlockSpec(memory_space=pltpu.HBM)
VM = pl.BlockSpec(memory_space=pltpu.VMEM)
DMA = pltpu.SemaphoreType.DMA
F32, BF16 = jnp.float32, jnp.bfloat16
CORE, SIDE, NEAR, HIGH = 1, 2, 4, 8
QUARTERS = 4
UNIT = 256
PLAN = (
    "T", "T", "n0", "T", "T", "n1", "T", "T", "n2", "s0", "T", "n3", "t0", "s1", "w0", "p0", "T", "t1", "s2", "p1",
    "T", "t2", "s3", "p2", "t3", "a0", "u0",
)


def bit(place, value):
    return lax.rem(lax.div(place, value), 2)


def flip(place, value):
    return place + value - 2 * value * bit(place, value)


def at(start, size, multiple=None):
    return pl.ds(pl.multiple_of(start, size if multiple is None else multiple), size)


def remote(src, dst, send, recv, **where):
    return pltpu.make_async_remote_copy(
        src_ref=src, dst_ref=dst, send_sem=send, recv_sem=recv, device_id=where, device_id_type=MESH
    )


def loop(lower, upper, step):
    def body(index, carry):
        step(index)
        return carry

    lax.fori_loop(lower, upper, body, 0)


def greet(targets):
    barrier = pltpu.get_barrier_semaphore()
    for target in targets:
        pl.semaphore_signal(barrier, inc=1, device_id=target, device_id_type=MESH)
    pl.semaphore_wait(barrier, len(targets))


def greet_all(n_dp, me, other_tensor):
    barrier = pltpu.get_barrier_semaphore()
    loop(
        1,
        n_dp,
        lambda step: pl.semaphore_signal(
            barrier, inc=1, device_id={"dp": lax.rem(me + step, n_dp)}, device_id_type=MESH
        ),
    )
    pl.semaphore_signal(barrier, inc=1, device_id={"tensor": other_tensor}, device_id_type=MESH)
    pl.semaphore_wait(barrier, n_dp)


class Place:
    def __init__(self):
        self.me = lax.axis_index("dp")
        self.tensor = lax.axis_index("tensor")
        self.other = 1 - self.tensor
        self.core = bit(self.me, CORE)
        self.side = bit(self.me, SIDE)
        self.near = bit(self.me, NEAR)
        self.high = lax.div(self.me, HIGH)
        self.quarter = self.near * 2 + self.core
        self.peers = (
            (flip(self.me, CORE), self.near * 2 + 1 - self.core),
            (flip(self.me, NEAR), (1 - self.near) * 2 + self.core),
            (flip(flip(self.me, NEAR), CORE), (1 - self.near) * 2 + 1 - self.core),
        )


def sum_rows(ref_at, depth, chunk, of):
    def body(index, total):
        return total + jnp.sum(of(ref_at(index)), axis=0, keepdims=True)

    return lax.fori_loop(0, depth // chunk, body, jnp.zeros((1, 128), F32))


def gelu_parts(values):
    phi = 0.5 * (1.0 + lax.erf(values * (1.0 / math.sqrt(2.0))))
    density = jnp.exp(-0.5 * values * values) * (1.0 / math.sqrt(2.0 * math.pi))
    return values * phi, phi + values * density


def tn(left, right):
    return lax.dot_general(left, right, (((0,), (0,)), ((), ())), preferred_element_type=F32)


def nt(left, right):
    return lax.dot_general(left, right, (((1,), (1,)), ((), ())), preferred_element_type=F32)


def nn(left, right):
    return jnp.dot(left, right, preferred_element_type=F32)


def turned(values, cos, sin):
    pieces = []
    half_rot = ROT // 2
    repeats = values.shape[1] // cos.shape[1]
    cos, sin = (jnp.concatenate([table] * repeats, axis=1) for table in (cos, sin))
    for head in range(values.shape[0] // HD):
        rows = values[head * HD : (head + 1) * HD]
        first, second = rows[:half_rot], rows[half_rot:ROT]
        pieces += [first * cos - second * sin, second * cos + first * sin, rows[ROT:]]
    return jnp.concatenate(pieces, axis=0)


def causal_scores(keys, queries):
    scores = tn(keys, queries) * (1.0 / math.sqrt(HD))
    length = scores.shape[0]
    key = lax.broadcasted_iota(jnp.int32, (length, length), 0)
    query = lax.broadcasted_iota(jnp.int32, (length, length), 1)
    return jnp.where(query >= key, scores, MASKED)


def gather_kernel(
    n_dp, hist, mix, small, w_qkv, w_out, w_up, w_down, cos, sin,
    o_mix, o_small, o_streams, o_act, o_qkv, o_out, o_up, o_down,
    o_rows, o_context, o_sums, o_hidden, o_slope, o_part,
    mix_all, small_all, hist_in, mixed, streams, act,
    early_s, early_r, hist_sem, a2a_s, a2a_r, reshard_s, reshard_r, high_s, high_r, side_s, side_r,
    act_s, act_r, act_local, own_sem, out_sem, share_s, share_r, share_l,
    act_in, qkv_in, out_in, up_in, down_in, rows_out, context, sums, hidden, slope, part, load_sem, save_sem,
):
    here = Place()
    me, tensor = here.me, here.tensor
    rows = small.shape[1]
    depth = rows * n_dp
    half = hist.shape[2] // n_dp // 2
    high_bits = int(math.log2(n_dp // HIGH))
    weights = ((w_qkv, o_qkv), (w_out, o_out), (w_up, o_up), (w_down, o_down))
    greet_all(n_dp, me, here.other)

    def early(which, buf, phase):
        if phase == 0:
            block, target = buf.at[here.high, here.near, here.side, here.core], flip(me, NEAR)
        elif phase <= high_bits:
            span = 1 << (phase - 1)
            block = buf.at[pl.ds(lax.div(here.high, span) * span, span), :, here.side, here.core]
            target = flip(me, HIGH << (phase - 1))
        elif phase == high_bits + 1:
            block, target = buf.at[:, :, here.side, here.core], flip(me, SIDE)
        else:
            block, target = buf.at[:, :, :, here.core], flip(me, CORE)
        return remote(block, block, early_s.at[which, phase], early_r.at[which, phase], dp=target)

    own_mix = pltpu.make_async_copy(mix, mix_all.at[here.high, here.near, here.side, here.core], own_sem.at[0])
    units = []
    for w, o in weights:
        if len(w.shape) == 3:
            units += [(w.at[part], o.at[part], 0) for part in range(w.shape[0])]
        else:
            units += [(w, o, first) for first in range(0, o.shape[-1], UNIT)]

    def cut(unit, quarter):
        w, o, first = units[unit]
        return w.at[:, at(quarter * o.shape[-1] + first, UNIT)]

    def slot(unit):
        _, o, first = units[unit]
        mine = pl.ds(pl.multiple_of(here.core * rows, rows), rows)
        return o.at[here.high, here.near, here.side, mine, pl.ds(first, UNIT)]

    def keep(unit):
        return pltpu.make_async_copy(cut(unit, here.quarter), slot(unit), own_sem.at[2 + unit])

    def reshard(unit, peer):
        target, quarter = here.peers[peer]
        return remote(cut(unit, quarter), slot(unit), reshard_s.at[unit, peer], reshard_r.at[unit, peer], dp=target)

    def high_hop(unit, phase):
        _, o, first = units[unit]
        span = 1 << phase
        block = o.at[pl.ds(lax.div(here.high, span) * span, span), :, here.side, :, pl.ds(first, UNIT)]
        return remote(block, block, high_s.at[unit, phase], high_r.at[unit, phase], dp=flip(me, HIGH << phase))

    def side_hop(unit):
        _, o, first = units[unit]
        block = o.at[:, :, here.side, :, pl.ds(first, UNIT)]
        return remote(block, block, side_s.at[unit], side_r.at[unit], dp=flip(me, SIDE))

    def fetch(step, buf):
        target = lax.rem(me + step, n_dp)
        return pltpu.make_async_copy(
            hist.at[:, :, at(target * 2 * half + tensor * half, half)], hist_in.at[buf], hist_sem.at[buf]
        )

    def send(step):
        target = lax.rem(me + step, n_dp)
        return remote(
            mixed.at[step], streams.at[:, at(me * rows, rows), :], a2a_s.at[step], a2a_r.at[step], dp=target
        )

    fetch(0, 0).start()

    def mix_step(step):
        buf = lax.rem(step, 2)

        @pl.when(step + 1 < n_dp)
        def _():
            fetch(step + 1, 1 - buf).start()

        fetch(step, buf).wait()
        target = lax.rem(me + step, n_dp)
        weight = mix_all[lax.div(target, HIGH), bit(target, NEAR), bit(target, SIDE), bit(target, CORE)]
        for row in range(0, rows, 32):
            part = pl.ds(row, 32)
            sources = [hist_in[buf, source, part, :].astype(F32) for source in range(HIST)]
            for stream in range(STREAMS):
                total = sum(
                    sources[source] * weight[stream * HIST + source][None, :] for source in range(HIST)
                )
                mixed[step, stream, part, :] = total.astype(BF16)

        @pl.when(step > 0)
        def _():
            send(step).start()

    chunk = min(256, depth)

    def lanes(near, core, half_at, count):
        return at(near * 4 * half + core * 2 * half + half_at * half, count * half, half)

    def act_keep(stream):
        return pltpu.make_async_copy(
            act.at[stream], o_act.at[stream, :, lanes(here.near, here.core, tensor, 1)], act_local.at[stream]
        )

    def act_near(stream):
        return remote(
            act.at[stream], o_act.at[stream, :, lanes(here.near, here.core, tensor, 1)],
            act_s.at[0, stream], act_r.at[0, stream], dp=flip(me, NEAR),
        )

    def act_tensor(stream, second):
        span = lanes(1 - here.near if second else here.near, here.core, tensor, 1)
        return remote(
            o_act.at[stream, :, span] if second else act.at[stream], o_act.at[stream, :, span],
            act_s.at[1 + second, stream], act_r.at[1 + second, stream], tensor=here.other,
        )

    def act_core(stream, near):
        span = lanes(near, here.core, 0, 2)
        return remote(
            o_act.at[stream, :, span], o_act.at[stream, :, span],
            act_s.at[3 + near, stream], act_r.at[3 + near, stream], dp=flip(me, CORE),
        )

    def normalise_stream(stream):
        block = 0 if stream < 3 else 1

        def piece(index):
            return streams[stream, at(index * chunk, chunk), :].astype(F32)

        centre = sum_rows(piece, depth, chunk, lambda v: v) / depth
        spread = sum_rows(piece, depth, chunk, lambda v: (v - centre) * (v - centre)) / depth
        root = lax.rsqrt(spread + NORM_EPS)

        def normalise(index):
            span = chunk // rows
            first = index * span
            column = jnp.concatenate(
                [
                    small_all[
                        lax.div(first + k, HIGH), bit(first + k, NEAR), bit(first + k, SIDE), bit(first + k, CORE)
                    ]
                    for k in range(span)
                ],
                axis=0,
            ).astype(F32)
            gain = column[:, MIXH + block : MIXH + block + 1]
            bias = column[:, MIXH + 2 + block : MIXH + 3 + block]
            act[stream, at(index * chunk, chunk), :] = (
                (piece(index) - centre) * root * gain + bias
            ).astype(BF16)

        loop(0, depth // chunk, normalise)
        act_keep(stream).start()

    finals = [
        pltpu.make_async_copy(small_all, o_small, out_sem.at[1]),
        pltpu.make_async_copy(streams, o_streams, out_sem.at[2]),
    ]
    early_pairs = ((0, mix_all), (1, small_all))
    last = high_bits + 2

    def first(array):
        keep(array).start()
        for peer in range(3):
            reshard(array, peer).start()

    def second(array):
        keep(array).wait()
        for peer in range(3):
            reshard(array, peer).wait()
        high_hop(array, 0).start()

    def third(array):
        for phase in range(high_bits):
            high_hop(array, phase).wait()
            if phase + 1 < high_bits:
                high_hop(array, phase + 1).start()
        side_hop(array).start()

    def act_first(stream):
        act_near(stream).wait()
        act_tensor(stream, 1).start()
        if stream + 1 < STREAMS:
            act_near(stream + 1).start()
        if stream and stream + 1 < STREAMS:
            act_tensor(stream + 1, 0).start()

    def act_second(stream):
        act_keep(stream).wait()
        act_tensor(stream, 0).wait()
        act_tensor(stream, 1).wait()
        for near in range(2):
            act_core(stream, near).start()

    own_mix.start()
    small_all[here.high, here.near, here.side, here.core] = small[...].T
    own_mix.wait()
    for which, buf in early_pairs:
        early(which, buf, 0).start()
    total = len(units)

    def tick(unit):
        third(unit)
        if unit + 3 < total:
            first(unit + 3)
        if unit + 1 < total:
            second(unit + 1)

    for unit in range(min(3, total)):
        first(unit)
    for phase in range(1, last + 1):
        for which, buf in early_pairs:
            early(which, buf, phase - 1).wait()
            early(which, buf, phase).start()
        if phase == 2:
            second(0)
    early(0, mix_all, last).wait()
    def mix_lanes(index):
        return mix_all.at[lax.div(index, HIGH), bit(index, NEAR), bit(index, SIDE), bit(index, CORE)], o_mix.at[
            :, at(index * 2 * half + tensor * half, half)
        ]

    def mix_copy(index):
        source, target = mix_lanes(index)
        return pltpu.make_async_copy(source, target, share_l.at[index])

    def mix_share(index):
        source, target = mix_lanes(index)
        return remote(source, target, share_s.at[index], share_r.at[index], tensor=here.other)

    def mix_out(index):
        mix_copy(index).start()
        mix_share(index).start()

    loop(0, n_dp, mix_out)
    loop(0, n_dp, mix_step)
    streams[:, at(me * rows, rows), :] = mixed[0]
    early(1, small_all, last).wait()
    done = 0

    def ticks(count):
        nonlocal done
        for unit in range(done, min(done + count, total)):
            tick(unit)
        done = min(done + count, total)

    ticks(3)
    loop(1, n_dp, lambda step: send(step).wait())
    for stream in range(STREAMS):
        normalise_stream(stream)
        if stream == 0:
            act_near(0).start()
        if stream < 2:
            act_tensor(stream, 0).start()
    for copy in finals:
        copy.start()
    depth, tokens = act_in.shape[1:]
    seq_len = 2 * half
    heads = context.shape[0] // HD
    tile = 256

    def act_load(stream):
        return pltpu.make_async_copy(o_act.at[stream], act_in.at[stream], load_sem.at[stream])

    def act_third(stream):
        for near in range(2):
            act_core(stream, near).wait()
        act_load(stream).start()

    loads = {
        "qkv": pltpu.make_async_copy(o_qkv.reshape(3, depth, qkv_in.shape[2]), qkv_in, load_sem.at[4]),
        "out": pltpu.make_async_copy(o_out.reshape(depth, out_in.shape[1]), out_in, load_sem.at[5]),
        "up": pltpu.make_async_copy(o_up.reshape(depth, up_in.shape[1]), up_in, load_sem.at[6]),
        "down": pltpu.make_async_copy(o_down.reshape(depth, down_in.shape[1]), down_in, load_sem.at[7]),
    }
    held = 0

    def arrive(count):
        nonlocal held
        ticks(max(held + count - done, 0))
        for unit in range(held, held + count):
            side_hop(unit).wait()
        held += count

    def project(stream):
        act_load(stream).wait()
        values = tn(qkv_in[stream], act_in[stream])
        if stream < 2:
            values = turned(values, cos[...], sin[...])
        rows_out[stream] = values.astype(BF16)

    def attend(seq):
        span = at(seq * seq_len, seq_len)
        for head in range(heads):
            lane = pl.ds(head * HD, HD)
            scores = causal_scores(rows_out[1, lane, span], rows_out[0, lane, span])
            peak = jnp.max(scores, axis=0, keepdims=True)
            raised = jnp.exp(scores - peak)
            total_weight = jnp.sum(raised, axis=0, keepdims=True)
            prob = (raised / total_weight).astype(BF16)
            context[lane, span] = nn(rows_out[2, lane, span], prob).astype(BF16)
            sums[pl.ds(seq * heads + head, 1), :] = peak + jnp.log(total_weight)

    def raise_up(index):
        span = at(index * tile, tile)
        value, derivative = gelu_parts(tn(up_in[:, span], act_in[3]))
        hidden[span, :] = value.astype(BF16)
        slope[span, :] = derivative

    def lower(index):
        span = at(index * tile, tile)
        part[span, :] = (nn(out_in[span, :], context[...]) + nn(down_in[span, :], hidden[...])).astype(BF16)

    saves = []

    def save(*pairs):
        for source, target in pairs:
            copy = pltpu.make_async_copy(source, target, save_sem.at[len(saves)])
            copy.start()
            saves.append(copy)

    def rows_arrive(_):
        arrive(4)
        loads["qkv"].start()
        loads["out"].start()
        loads["qkv"].wait()

    def attend_all(_):
        loop(0, tokens // seq_len, attend)
        save((rows_out, o_rows), (context, o_context), (sums, o_sums))

    def raise_all(_):
        arrive(up_in.shape[1] // UNIT)
        loads["up"].start()
        act_load(3).wait()
        loads["up"].wait()
        loop(0, hidden.shape[0] // tile, raise_up)
        save((hidden, o_hidden), (slope, o_slope))

    actions = {
        "n": act_first, "s": act_second, "t": act_third, "w": rows_arrive, "p": project, "a": attend_all, "u": raise_all
    }
    for action in PLAN:
        if action == "T":
            ticks(1)
        else:
            actions[action[0]](int(action[1]))
    arrive(total - held)
    loads["down"].start()
    loads["out"].wait()
    loads["down"].wait()
    loop(0, depth // tile, lower)
    save((part, o_part))
    for copy in finals + saves:
        copy.wait()

    def settle(index):
        mix_copy(index).wait()
        mix_share(index).wait()

    loop(0, n_dp, settle)


def gather(n_dp, hist, mix, small, w_qkv, w_out, w_up, w_down, cos, sin):
    rows = small.shape[1]
    depth = rows * n_dp
    half = hist.shape[2] // n_dp // 2
    high = n_dp // HIGH
    high_bits = int(math.log2(high))
    grid = (high, 2, 2, 2)
    units = sum(w.size // w.shape[-2] for w in (w_qkv, w_out, w_up, w_down)) // QUARTERS // UNIT

    def cut(width):
        return (high, 2, 2, 2 * rows, width // QUARTERS)

    tokens = 8 * half
    narrow, width = w_qkv.shape[2] // QUARTERS, w_up.shape[1] // QUARTERS
    results = [
        ((3, narrow, tokens), BF16),
        ((narrow, tokens), BF16),
        ((tokens // (2 * half) * (narrow // HD), 2 * half), F32),
        ((width, tokens), BF16),
        ((width, tokens), F32),
        ((depth, tokens), BF16),
    ]
    shapes = [
        ((mix.shape[0], n_dp * 2 * half), F32),
        (grid + (rows, 128), BF16),
        ((STREAMS, depth, half), BF16),
        ((STREAMS, depth, tokens), BF16),
        ((3,) + cut(w_qkv.shape[2]), BF16),
        (cut(w_out.shape[1]), BF16),
        (cut(w_up.shape[1]), BF16),
        (cut(w_down.shape[1]), BF16),
    ] + results
    return pl.pallas_call(
        functools.partial(gather_kernel, n_dp),
        out_shape=[jax.ShapeDtypeStruct(*shape) for shape in shapes],
        in_specs=[ANY, ANY, VM] + [ANY] * 4 + [VM] * 2,
        out_specs=[ANY] * 14,
        scratch_shapes=[
            pltpu.VMEM(grid + mix.shape, F32),
            pltpu.VMEM(grid + (rows, 128), BF16),
            pltpu.VMEM((2, HIST, rows, half), BF16),
            pltpu.VMEM((n_dp, STREAMS, rows, half), BF16),
            pltpu.VMEM((STREAMS, depth, half), BF16),
            pltpu.VMEM((STREAMS, depth, half), BF16),
            DMA((2, high_bits + 3)),
            DMA((2, high_bits + 3)),
            DMA((2,)),
            DMA((n_dp,)),
            DMA((n_dp,)),
            DMA((units, 3)),
            DMA((units, 3)),
            DMA((units, high_bits)),
            DMA((units, high_bits)),
            DMA((units,)),
            DMA((units,)),
            DMA((5, STREAMS)),
            DMA((5, STREAMS)),
            DMA((STREAMS,)),
            DMA((2 + units,)),
            DMA((3,)),
            DMA((n_dp,)),
            DMA((n_dp,)),
            DMA((n_dp,)),
            pltpu.VMEM((STREAMS, depth, tokens), BF16),
            pltpu.VMEM((3, depth, narrow), BF16),
            pltpu.VMEM((depth, narrow), BF16),
            pltpu.VMEM((depth, width), BF16),
            pltpu.VMEM((depth, width), BF16),
        ]
        + [pltpu.VMEM(*shape) for shape in results]
        + [DMA((8,)), DMA((6,))],
        compiler_params=pltpu.CompilerParams(
            collective_id=1, has_side_effects=True, vmem_limit_bytes=61 * 1024 * 1024
        ),
        name="gather",
    )(hist, mix, small, w_qkv, w_out, w_up, w_down, cos, sin)


def lane_block(half, near, core, half_at, count):
    return at(near * 4 * half + core * 2 * half + half_at * half, count * half, half)


def gelu_parts(values):
    phi = 0.5 * (1.0 + lax.erf(values * (1.0 / math.sqrt(2.0))))
    density = jnp.exp(-0.5 * values * values) * (1.0 / math.sqrt(2.0 * math.pi))
    return values * phi, phi + values * density


def reduce_group(here, half, part, theirs, own, from_core, from_tensor, from_near, sems, local, pieces, piece):
    core_s, core_r, tensor_s, tensor_r, near_s, near_r = sems

    def load(span, near, half_at):
        return pltpu.make_async_copy(
            part.at[piece(span), lane_block(half, near, here.core, half_at, 1)],
            own.at[near, half_at, piece(span)], local.at[span, near * 2 + half_at],
        )

    def to_core(span, near, half_at):
        return remote(
            part.at[piece(span), lane_block(half, near, 1 - here.core, half_at, 1)],
            from_core.at[near, half_at, piece(span)],
            core_s.at[span, near * 2 + half_at], core_r.at[span, near * 2 + half_at], dp=flip(here.me, CORE),
        )

    def to_tensor(span, near):
        return remote(
            own.at[near, here.other, piece(span)], from_tensor.at[near, piece(span)],
            tensor_s.at[span, near], tensor_r.at[span, near], tensor=here.other,
        )

    def to_near(span):
        return remote(
            from_tensor.at[1 - here.near, piece(span)], from_near.at[piece(span)],
            near_s.at[span], near_r.at[span], dp=flip(here.me, NEAR),
        )

    def start(span):
        for near in range(2):
            for half_at in range(2):
                to_core(span, near, half_at).start()
                load(span, near, half_at).start()

    def after_core(span):
        for near in range(2):
            for half_at in range(2):
                load(span, near, half_at).wait()
                to_core(span, near, half_at).wait()
            own[near, here.other, piece(span)] += from_core[near, here.other, piece(span)]
            to_tensor(span, near).start()
        for near in range(2):
            own[near, here.tensor, piece(span)] += from_core[near, here.tensor, piece(span)]

    def after_tensor(span):
        for near in range(2):
            to_tensor(span, near).wait()
        far = 1 - here.near
        from_tensor[far, piece(span)] += own[far, here.tensor, piece(span)]
        to_near(span).start()
        from_tensor[here.near, piece(span)] += own[here.near, here.tensor, piece(span)]

    def after_near(span):
        to_near(span).wait()

    return start, after_core, after_tensor, after_near


def join_kernel(
    part, streams, cot, small, mix_in, mix_out, mix_back, static, next_cot,
    o_grad, o_wide, o_block, o_next, o_mixin, o_tiny,
    own, from_core, from_tensor, from_near, residual, wide, normed, block, back, low, next_rows, mixin, tiny,
    core_s, core_r, tensor_s, tensor_r, near_s, near_r, local, share_s, share_r, own_sem,
):
    here = Place()
    me, tensor = here.me, here.tensor
    depth, half = cot.shape
    spans = core_s.shape[0]
    size = depth // spans
    chunk = 256
    greet([{"dp": flip(me, CORE)}, {"dp": flip(me, NEAR)}, {"tensor": here.other}])

    def piece(span):
        return pl.ds(span * size, size)

    start, after_core, after_tensor, after_near = reduce_group(
        here, half, part, None, own, from_core, from_tensor, from_near,
        (core_s, core_r, tensor_s, tensor_r, near_s, near_r), local, spans, piece,
    )
    fetch = pltpu.make_async_copy(streams.at[3], residual, own_sem.at[0])
    fetch.start()
    for span in range(spans):
        start(span)
    for span in range(spans):
        after_core(span)
    for span in range(spans):
        after_tensor(span)
    fetch.wait()
    squares = jnp.zeros((1, half), F32)
    for span in range(spans):
        after_near(span)

        def widen(index, total):
            rows = at(span * size + index * chunk, chunk)
            branch = from_tensor[here.near, rows, :].astype(F32) + from_near[rows, :].astype(F32)
            value = residual[rows, :].astype(F32) + branch
            wide[rows, :] = value
            block[rows, :] = value.astype(BF16)
            return total + jnp.sum(value * value, axis=0, keepdims=True)

        squares = lax.fori_loop(0, size // chunk, widen, squares)
    root = lax.rsqrt(squares / depth + ROOT_EPS)

    def share_block(which):
        lanes = at(tensor * half, half)
        if which == 0:
            return pltpu.make_async_copy(block, o_block.at[:, lanes], own_sem.at[1])
        return remote(block, o_block.at[:, lanes], share_s.at[0], share_r.at[0], tensor=here.other)

    share_block(0).start()
    share_block(1).start()

    def norm(index):
        rows = at(index * chunk, chunk)
        normed[rows, :] = (wide[rows, :] * root).astype(BF16)

    loop(0, depth // chunk, norm)
    inner, slope = gelu_parts(jnp.dot(mix_in[...], normed[...], preferred_element_type=F32))
    inner_low = inner.astype(BF16)
    next_rows[...] = (jnp.dot(mix_out[...], inner_low, preferred_element_type=F32) + static[...])[:MIXH]
    next_low = next_cot[...].astype(BF16)

    def nt(left, right):
        return lax.dot_general(left, right, (((1,), (1,)), ((), ())), preferred_element_type=F32)

    tiny[:, :128] = nt(inner_low, next_low)
    tiny[:, 128:] = jnp.broadcast_to(jnp.sum(next_cot[...], axis=1, keepdims=True), (128, 128))
    inner_grad = (jnp.dot(mix_back[...], next_low, preferred_element_type=F32) * slope).astype(BF16)

    def pull(index, total):
        rows = at(index * chunk, chunk)
        value = jnp.dot(small[rows, :], inner_grad, preferred_element_type=F32)
        back[rows, :] = value
        return total + jnp.sum(value * wide[rows, :] * root, axis=0, keepdims=True)

    along = lax.fori_loop(0, depth // chunk, pull, jnp.zeros((1, half), F32)) / depth

    def finish(index):
        rows = at(index * chunk, chunk)
        value = cot[rows, :].astype(F32) + root * (back[rows, :] - wide[rows, :] * root * along)
        back[rows, :] = value
        low[rows, :] = value.astype(BF16)

    loop(0, depth // chunk, finish)

    def share(kind, index):
        if kind == 0:
            source, lanes, where = low, lane_block(half, here.near, here.core, tensor, 1), {"dp": flip(me, NEAR)}
        elif kind == 1:
            lanes = lane_block(half, 1 - here.near if index else here.near, here.core, tensor, 1)
            source, where = (o_grad.at[:, lanes] if index else low), {"tensor": here.other}
        else:
            lanes, where = lane_block(half, index, here.core, 0, 2), {"dp": flip(me, CORE)}
            source = o_grad.at[:, lanes]
        number = 1 + 2 * kind + index
        return remote(source, o_grad.at[:, lanes], share_s.at[number], share_r.at[number], **where)

    share(0, 0).start()
    share(1, 0).start()
    keep = pltpu.make_async_copy(
        low, o_grad.at[:, lane_block(half, here.near, here.core, tensor, 1)], own_sem.at[2]
    )
    keep.start()

    def mixin_rows(index):
        rows = at(index * chunk, chunk)
        mixin[rows, :] = nt(normed[rows, :], inner_grad)

    loop(0, depth // chunk, mixin_rows)
    share(0, 0).wait()
    share(1, 1).start()
    lanes = at(tensor * half, half)
    next_share = remote(next_rows, o_next.at[:, lanes], share_s.at[7], share_r.at[7], tensor=here.other)
    next_share.start()
    finals = [
        pltpu.make_async_copy(next_rows, o_next.at[:, lanes], own_sem.at[3]),
        pltpu.make_async_copy(back, o_wide, own_sem.at[4]),
        pltpu.make_async_copy(mixin, o_mixin, own_sem.at[5]),
        pltpu.make_async_copy(tiny, o_tiny, own_sem.at[6]),
    ]
    for copy in finals:
        copy.start()
    keep.wait()
    share(1, 0).wait()
    share(1, 1).wait()
    for near in range(2):
        share(2, near).start()
    for near in range(2):
        share(2, near).wait()
    share_block(0).wait()
    share_block(1).wait()
    next_share.wait()
    for copy in finals:
        copy.wait()


def join(part, streams, cot, small, mix_in, mix_out, mix_back, static, next_cot):
    depth, half = cot.shape
    spans = 4
    shapes = [
        ((depth, 8 * half), BF16),
        ((depth, half), F32),
        ((depth, 2 * half), BF16),
        ((MIXH, 2 * half), F32),
        ((depth, 128), F32),
        ((128, 256), F32),
    ]
    return pl.pallas_call(
        join_kernel,
        out_shape=[jax.ShapeDtypeStruct(*shape) for shape in shapes],
        in_specs=[ANY, ANY] + [VM] * 7,
        out_specs=[ANY] * 6,
        scratch_shapes=[
            pltpu.VMEM((2, 2, depth, half), BF16),
            pltpu.VMEM((2, 2, depth, half), BF16),
            pltpu.VMEM((2, depth, half), BF16),
            pltpu.VMEM((depth, half), BF16),
            pltpu.VMEM((depth, half), BF16),
            pltpu.VMEM((depth, half), F32),
            pltpu.VMEM((depth, half), BF16),
            pltpu.VMEM((depth, half), BF16),
            pltpu.VMEM((depth, half), F32),
            pltpu.VMEM((depth, half), BF16),
            pltpu.VMEM((MIXH, half), F32),
            pltpu.VMEM((depth, 128), F32),
            pltpu.VMEM((128, 256), F32),
            DMA((spans, 4)),
            DMA((spans, 4)),
            DMA((spans, 2)),
            DMA((spans, 2)),
            DMA((spans,)),
            DMA((spans,)),
            DMA((spans, 4)),
            DMA((8,)),
            DMA((8,)),
            DMA((7,)),
        ],
        compiler_params=pltpu.CompilerParams(
            collective_id=2, has_side_effects=True, vmem_limit_bytes=40 * 1024 * 1024
        ),
        name="join",
    )(part, streams, cot, small, mix_in, mix_out, mix_back, static, next_cot)


def scatter_kernel(
    n_dp, attn_grad, mlp_grad, streams, small, wide_grad, mixin_part, hist, g_qkv, g_up, g_down, g_out,
    o_stream, o_mix, o_small, o_qkv, o_up, o_down, o_out,
    own, from_core, from_tensor, from_near, rows_in, wide, stream_grad, gains, biases, tiny, tiny_in, tiny_out,
    hist_in, arrived, mix_part, mix_in, mix_sum, tiny_sum,
    side_qkv, side_up, side_down, side_out, mine_qkv, mine_up, mine_down, mine_out,
    high_qkv, high_up, high_down, high_out,
    core_s, core_r, tensor_s, tensor_r, near_s, near_r, local, in_sem,
    side_s, side_r, side_local, high_s, high_r, peer_s, peer_r, peer_local,
    a2a_s, a2a_r, keep_sem, pass_s, pass_r, tiny_s, tiny_r, mix_s, mix_r, hist_sem, last_s, last_r, last_local,
):
    here = Place()
    me, tensor = here.me, here.tensor
    depth, half = wide_grad.shape
    rows = depth // n_dp
    high_bits = int(math.log2(n_dp // HIGH))
    chunk = min(256, depth)
    greet_all(n_dp, me, here.other)
    weights = (
        (g_qkv, side_qkv, mine_qkv, high_qkv, o_qkv),
        (g_up, side_up, mine_up, high_up, o_up),
        (g_down, side_down, mine_down, high_down, o_down),
        (g_out, side_out, mine_out, high_out, o_out),
    )

    def pick(ref, *index):
        return ref.at[(slice(None),) + index] if ref.shape[0] == 3 and len(ref.shape) > len(index) + 2 else ref.at[index]

    def everything(_):
        return pl.ds(0, depth)

    steps = []
    for stream in range(STREAMS):
        part = attn_grad.at[stream] if stream < 3 else mlp_grad
        steps.append(
            reduce_group(
                here, half, part, None, own.at[stream], from_core.at[stream], from_tensor.at[stream],
                from_near.at[stream],
                tuple(
                    sem.at[pl.ds(stream, 1)]
                    for sem in (core_s, core_r, tensor_s, tensor_r, near_s, near_r)
                ),
                local.at[pl.ds(stream, 1)], 1, everything,
            )
        )
    for stream in range(STREAMS):
        steps[stream][0](0)
    loads = [
        pltpu.make_async_copy(streams, rows_in, in_sem.at[0]),
        pltpu.make_async_copy(wide_grad, wide, in_sem.at[1]),
    ]
    for copy in loads:
        copy.start()

    def is_qkv(array):
        return array == 0

    def index_of(array, *index):
        return ((slice(None),) if is_qkv(array) else ()) + index

    def side_hop(array):
        g, side, _, _, _ = weights[array]
        return remote(
            g.at[index_of(array, slice(None), slice(None), 1 - here.side)], side, side_s.at[array], side_r.at[array],
            dp=flip(me, SIDE),
        )

    def side_load(array):
        g, _, mine, _, _ = weights[array]
        return pltpu.make_async_copy(
            g.at[index_of(array, slice(None), slice(None), here.side)], mine, side_local.at[array]
        )

    def high_hop(array, phase):
        _, _, mine, high, _ = weights[array]
        span = 1 << phase
        base = lax.div(here.high, span)
        theirs = base + 1 - 2 * lax.rem(base, 2)
        return remote(
            mine.at[index_of(array, pl.ds(theirs * span, span))], high.at[index_of(array, pl.ds(span - 1, span))],
            high_s.at[array, phase], high_r.at[array, phase], dp=flip(me, HIGH << phase),
        )

    def add_blocks(array, into, other, first_into, first_other, count):
        shape = into.shape
        tall, width = shape[-2:]
        outer = 3 if is_qkv(array) else 1
        step = 32

        def add(flat):
            lead = lax.div(flat, count * 2)
            rest = lax.rem(flat, count * 2)
            high, near = lax.div(rest, 2), lax.rem(rest, 2)
            prefix = (lead,) if is_qkv(array) else ()

            def tile(index):
                span = at(index * step, step)
                into[prefix + (first_into + high, near, span)] += other[prefix + (first_other + high, near, span)]

            loop(0, tall // step, tile)

        loop(0, outer * count * 2, add)

    for array in range(4):
        side_hop(array).start()
        side_load(array).start()
    for copy in loads:
        copy.wait()
    stats = []
    for stream in range(STREAMS):

        def piece(index):
            return rows_in[stream, at(index * chunk, chunk), :].astype(F32)

        centre = sum_rows(piece, depth, chunk, lambda v: v) / depth
        spread = sum_rows(piece, depth, chunk, lambda v: (v - centre) * (v - centre)) / depth
        stats.append((centre, lax.rsqrt(spread + NORM_EPS)))
    for stream in range(STREAMS):
        steps[stream][1](0)
    for array in range(4):
        side_load(array).wait()
        side_hop(array).wait()
        _, side, mine, _, _ = weights[array]
        add_blocks(array, mine, side, 0, 0, n_dp // HIGH)
        high_hop(array, high_bits - 1).start()
    for stream in range(STREAMS):
        steps[stream][2](0)

    for stream in range(STREAMS):
        steps[stream][3](0)
        group = 0 if stream < 3 else 1
        centre, root = stats[stream]

        def parts(index):
            span = at(index * chunk, chunk)
            grad = from_tensor[stream, here.near, span].astype(F32) + from_near[stream, span].astype(F32)
            hat = (rows_in[stream, span, :].astype(F32) - centre) * root
            gain = small[span, MIXH + group : MIXH + group + 1].astype(F32)
            return span, grad, hat, grad * gain

        def sums(index, carry):
            span, grad, hat, scaled = parts(index)
            if stream in (0, 3):
                gains[group, span] = grad * hat
                biases[group, span] = grad
            else:
                gains[group, span] += grad * hat
                biases[group, span] += grad
            return (
                carry[0] + jnp.sum(scaled, axis=0, keepdims=True),
                carry[1] + jnp.sum(scaled * hat, axis=0, keepdims=True),
            )

        zero = jnp.zeros((1, half), F32)
        total, along = lax.fori_loop(0, depth // chunk, sums, (zero, zero))

        def finish(index):
            span, grad, hat, scaled = parts(index)
            value = root * (scaled - total / depth - hat * (along / depth))
            if stream == 3:
                value = value + wide[span, :]
            stream_grad[stream, span] = value.astype(BF16)

        loop(0, depth // chunk, finish)

    def send(step):
        target = lax.rem(me + step, n_dp)
        return remote(
            stream_grad.at[:, at(target * rows, rows), :], arrived.at[step], a2a_s.at[step], a2a_r.at[step], dp=target
        )

    loop(1, n_dp, lambda step: send(step).start())

    def fetch(step, buf):
        source = lax.rem(me - step + n_dp, n_dp)
        return pltpu.make_async_copy(
            hist.at[:, :, at(source * 2 * half + tensor * half, half)], hist_in.at[buf], hist_sem.at[buf]
        )

    fetch(0, 0).start()
    own_block = pltpu.make_async_copy(stream_grad.at[:, at(me * rows, rows), :], arrived.at[0], last_local.at[0])
    own_block.start()

    column = lax.broadcasted_iota(jnp.int32, (chunk, 128), 1)

    def gather_tiny(index):
        span = at(index * chunk, chunk)
        value = mixin_part[span, :]
        for group in range(2):
            gain = jnp.sum(gains[group, span], axis=1, keepdims=True)
            bias = jnp.sum(biases[group, span], axis=1, keepdims=True)
            value = jnp.where(column == MIXH + group, gain, value)
            value = jnp.where(column == MIXH + 2 + group, bias, value)
        tiny[span, :] = value.astype(BF16)

    loop(0, depth // chunk, gather_tiny)

    def tiny_send(step):
        target = lax.rem(me + step, n_dp)
        return remote(tiny.at[at(target * rows, rows), :], tiny_in.at[step], tiny_s.at[step], tiny_r.at[step], dp=target)

    loop(1, n_dp, lambda step: tiny_send(step).start())

    for array in range(4):
        _, _, mine, high, _ = weights[array]
        for phase in reversed(range(high_bits)):
            high_hop(array, phase).wait()
            span = 1 << phase
            add_blocks(array, mine, high, lax.div(here.high, span) * span, span - 1, span)
            if phase:
                high_hop(array, phase - 1).start()

    def peer_hop(array, peer):
        _, _, mine, _, out = weights[array]
        width = mine.shape[-1]
        target, _ = here.peers[peer]
        core = bit(target, CORE)
        return remote(
            mine.at[index_of(array, here.high, bit(target, NEAR), at(core * rows, rows))],
            out.at[index_of(array, slice(None), at(here.quarter * width, width))],
            peer_s.at[array, peer], peer_r.at[array, peer], dp=target,
        )

    def peer_keep(array):
        _, _, mine, _, out = weights[array]
        width = mine.shape[-1]
        return pltpu.make_async_copy(
            mine.at[index_of(array, here.high, here.near, at(here.core * rows, rows))],
            out.at[index_of(array, slice(None), at(here.quarter * width, width))], peer_local.at[array],
        )

    for array in range(4):
        peer_keep(array).start()
        for peer in range(3):
            peer_hop(array, peer).start()
    own_block.wait()

    def keep_lanes(step):
        source = lax.rem(me - step + n_dp, n_dp)
        return at(source * 2 * half + tensor * half, half)

    def keep(step):
        return pltpu.make_async_copy(arrived.at[step], o_stream.at[:, :, keep_lanes(step)], keep_sem.at[step])

    def pass_on(step):
        return remote(
            arrived.at[step], o_stream.at[:, :, keep_lanes(step)], pass_s.at[step], pass_r.at[step], tensor=here.other
        )

    def mix_send(step):
        return remote(
            mix_part.at[step], mix_in.at[step], mix_s.at[step], mix_r.at[step], dp=lax.rem(me - step + n_dp, n_dp)
        )

    def receive(step):
        buf = lax.rem(step, 2)

        @pl.when(step + 1 < n_dp)
        def _():
            fetch(step + 1, 1 - buf).start()

        @pl.when(step > 0)
        def _():
            send(step).wait()

        keep(step).start()
        pass_on(step).start()
        fetch(step, buf).wait()
        for stream in range(STREAMS):
            totals = [jnp.zeros((8, half), F32) for _ in range(HIST)]
            for row in range(0, rows, 16):
                span = pl.ds(row, 16)
                grad = arrived[step, stream, span, :].astype(F32)
                for source in range(HIST):
                    product = grad * hist_in[buf, source, span, :].astype(F32)
                    totals[source] = totals[source] + product[:8] + product[8:]
            for source in range(HIST):
                mix_part[step, pl.ds(stream * HIST + source, 1), :] = jnp.sum(totals[source], axis=0, keepdims=True)

        @pl.when(step > 0)
        def _():
            mix_send(step).start()

    mix_part[0] = jnp.zeros_like(mix_part[0])
    loop(0, n_dp, receive)

    mix_sum[...] = mix_part[0]

    def add_mix(step):
        mix_send(step).wait()
        mix_sum[...] += mix_in[step]

    loop(1, n_dp, add_mix)
    lanes = at(tensor * half, half)
    mix_share = remote(mix_sum, o_mix.at[:, lanes], last_s.at[0], last_r.at[0], tensor=here.other)
    mix_keep = pltpu.make_async_copy(mix_sum, o_mix.at[:, lanes], last_local.at[1])
    mix_share.start()
    mix_keep.start()
    tiny_sum[0] = tiny[at(me * rows, rows), :].astype(F32)

    def add_tiny(step):
        tiny_send(step).wait()
        tiny_sum[0] += tiny_in[step].astype(F32)

    loop(1, n_dp, add_tiny)
    tiny_share = remote(tiny_sum.at[0], tiny_sum.at[1], last_s.at[1], last_r.at[1], tensor=here.other)
    tiny_share.start()
    tiny_share.wait()
    tiny_out[...] = tiny_sum[0] + tiny_sum[1]
    tiny_keep = pltpu.make_async_copy(tiny_out, o_small, last_local.at[2])
    tiny_keep.start()
    for array in range(4):
        peer_keep(array).wait()
        for peer in range(3):
            peer_hop(array, peer).wait()

    def settle(step):
        keep(step).wait()
        pass_on(step).wait()

    loop(0, n_dp, settle)
    mix_share.wait()
    mix_keep.wait()
    tiny_keep.wait()


def scatter(n_dp, attn_grad, mlp_grad, streams, small, wide_grad, mixin_part, hist, g_qkv, g_up, g_down, g_out):
    depth, half = wide_grad.shape
    rows = depth // n_dp
    high = n_dp // HIGH
    high_bits = int(math.log2(high))
    grads = (g_qkv, g_up, g_down, g_out)

    def lead(g):
        return (3,) if g.ndim == 6 else ()

    def halved(g, highs):
        return lead(g) + (highs, 2) + g.shape[-2:]

    outs = [
        ((STREAMS, rows, 2 * half * n_dp), BF16),
        ((MIXH, 2 * half), F32),
        ((rows, 128), F32),
    ] + [(lead(g) + (rows, QUARTERS * g.shape[-1]), BF16) for g in grads]
    return pl.pallas_call(
        functools.partial(scatter_kernel, n_dp),
        out_shape=[jax.ShapeDtypeStruct(*shape) for shape in outs],
        in_specs=[ANY, ANY, ANY, VM, ANY, VM, ANY] + [ANY] * 4,
        out_specs=[ANY] * 7,
        scratch_shapes=[
            pltpu.VMEM((STREAMS, 2, 2, depth, half), BF16),
            pltpu.VMEM((STREAMS, 2, 2, depth, half), BF16),
            pltpu.VMEM((STREAMS, 2, depth, half), BF16),
            pltpu.VMEM((STREAMS, depth, half), BF16),
            pltpu.VMEM((STREAMS, depth, half), BF16),
            pltpu.VMEM((depth, half), F32),
            pltpu.VMEM((STREAMS, depth, half), BF16),
            pltpu.VMEM((2, depth, half), F32),
            pltpu.VMEM((2, depth, half), F32),
            pltpu.VMEM((depth, 128), BF16),
            pltpu.VMEM((n_dp, rows, 128), BF16),
            pltpu.VMEM((rows, 128), F32),
            pltpu.VMEM((2, HIST, rows, half), BF16),
            pltpu.VMEM((n_dp, STREAMS, rows, half), BF16),
            pltpu.VMEM((n_dp, MIXH, half), F32),
            pltpu.VMEM((n_dp, MIXH, half), F32),
            pltpu.VMEM((MIXH, half), F32),
            pltpu.VMEM((2, rows, 128), F32),
        ]
        + [pltpu.VMEM(halved(g, high), BF16) for g in grads]
        + [pltpu.VMEM(halved(g, high), BF16) for g in grads]
        + [pltpu.VMEM(halved(g, high - 1), BF16) for g in grads]
        + [
            DMA((STREAMS, 4)),
            DMA((STREAMS, 4)),
            DMA((STREAMS, 2)),
            DMA((STREAMS, 2)),
            DMA((STREAMS,)),
            DMA((STREAMS,)),
            DMA((STREAMS, 4)),
            DMA((2,)),
            DMA((4,)),
            DMA((4,)),
            DMA((4,)),
            DMA((4, high_bits)),
            DMA((4, high_bits)),
            DMA((4, 3)),
            DMA((4, 3)),
            DMA((4,)),
            DMA((n_dp,)),
            DMA((n_dp,)),
            DMA((n_dp,)),
            DMA((n_dp,)),
            DMA((n_dp,)),
            DMA((n_dp,)),
            DMA((n_dp,)),
            DMA((n_dp,)),
            DMA((n_dp,)),
            DMA((2,)),
            DMA((2,)),
            DMA((2,)),
            DMA((3,)),
        ],
        compiler_params=pltpu.CompilerParams(
            collective_id=3, has_side_effects=True, vmem_limit_bytes=60 * 1024 * 1024
        ),
        name="scatter",
    )(attn_grad, mlp_grad, streams, small, wide_grad, mixin_part, hist, *grads)


def exact_gelu(values):
    return jax.nn.gelu(values, approximate=False)


def rotary_tables(length, rotary, float_type):
    half_rot = rotary // 2
    places = jnp.arange(length).astype(float_type)
    frequency = jnp.exp(
        jnp.arange(half_rot).astype(float_type) * (-2.0 * math.log(10000.0) / rotary)
    )
    angles = places[:, None] * frequency[None, :]
    return (jnp.cos(angles), jnp.sin(angles))


def rotate(values, cos_table, sin_table):
    half_rot = cos_table.shape[-1]
    first_half = values[..., :half_rot]
    second = values[..., half_rot : 2 * half_rot]
    return jnp.concatenate(
        [
            first_half * cos_table - second * sin_table,
            second * cos_table + first_half * sin_table,
            values[..., 2 * half_rot :],
        ],
        axis=-1,
    )


def masked_scores(queries, key_rows):
    length = queries.shape[1]
    score_scale = 1.0 / math.sqrt(queries.shape[2])
    causal = lax.broadcasted_iota(jnp.int32, (length, length), 0) >= lax.broadcasted_iota(
        jnp.int32, (length, length), 1
    )
    scores = (
        jnp.einsum("hqd,hkd->hqk", queries, key_rows, preferred_element_type=jnp.float32)
        * score_scale
    )
    return (jnp.where(causal[None], scores, MASKED), score_scale)


def attend_forward(queries, key_rows, value_rows):
    scores, score_scale = masked_scores(queries, key_rows)
    row_peak = jnp.max(scores, axis=-1, keepdims=True)
    raised = jnp.exp(scores - row_peak)
    row_total = jnp.sum(raised, axis=-1, keepdims=True)
    prob_low = (raised / row_total).astype(jnp.bfloat16)
    context = jnp.einsum("hqk,hkd->hqd", prob_low, value_rows, preferred_element_type=jnp.float32)
    return (context.astype(jnp.bfloat16), row_peak + jnp.log(row_total))


def attend_backward(queries, key_rows, value_rows, log_sum, context_grad):
    scores, score_scale = masked_scores(queries, key_rows)
    attn_prob = jnp.exp(scores - log_sum)
    prob_low = attn_prob.astype(jnp.bfloat16)
    value_grad = jnp.einsum(
        "hqk,hqd->hkd", prob_low, context_grad, preferred_element_type=jnp.float32
    )
    prob_grad = jnp.einsum(
        "hqd,hkd->hqk", context_grad, value_rows, preferred_element_type=jnp.float32
    )
    inner_sum = jnp.sum(attn_prob * prob_grad, axis=-1, keepdims=True)
    score_grad = (attn_prob * (prob_grad - inner_sum)).astype(jnp.bfloat16)
    query_grad = (
        jnp.einsum("hqk,hkd->hqd", score_grad, key_rows, preferred_element_type=jnp.float32)
        * score_scale
    )
    key_grad = (
        jnp.einsum("hqk,hqd->hkd", score_grad, queries, preferred_element_type=jnp.float32)
        * score_scale
    )
    return (query_grad, key_grad, value_grad)


def per_device(
    n_dp, history, mix_weights, w_qkv, w_out, w_up, w_down, norm_gain, norm_bias, mix_in, mix_out, mix_static,
    out_cot, next_cot,
):
    tensor = lax.axis_index("tensor")
    seq_len = mix_weights.shape[0]
    half = seq_len // 2
    depth = mix_in.shape[0] * n_dp

    def own_half(rows):
        return lax.dynamic_slice_in_dim(rows, tensor * half, half, 0)

    mix_rows = jnp.pad(own_half(mix_weights.reshape(seq_len, -1)).T, ((0, MIXH - STREAMS * HIST), (0, 0)))
    small = jnp.concatenate([mix_in, norm_gain.T, norm_bias.T], axis=1)
    small = jnp.pad(small, ((0, 0), (0, 128 - small.shape[1])))
    mix_all, small_all, streams, act, qkv, up, down, out = gather(
        n_dp, history, mix_rows, small, w_qkv, w_up, w_down, w_out
    )
    small_all = small_all.reshape(depth, 128)
    qkv, up, down, out = (
        qkv.reshape(3, depth, -1), up.reshape(depth, -1), down.reshape(depth, -1), out.reshape(depth, -1)
    )
    tokens = act.shape[2]
    seqs = tokens // seq_len
    heads = qkv.shape[2] // HD
    projected = jnp.einsum("sdt,sde->ste", act[:3], qkv, preferred_element_type=F32)
    head_rows = jnp.transpose(projected.reshape(3, seqs, seq_len, heads, HD), (0, 1, 3, 2, 4)).reshape(
        3, seqs * heads, seq_len, HD
    )
    cos_table, sin_table = rotary_tables(seq_len, ROT, F32)
    queries = rotate(head_rows[0], cos_table, sin_table).astype(BF16)
    key_rows = rotate(head_rows[1], cos_table, sin_table).astype(BF16)
    value_rows = head_rows[2].astype(BF16)
    context, log_sum = attend_forward(queries, key_rows, value_rows)

    def join_heads(rows):
        return jnp.transpose(rows.reshape(seqs, heads, seq_len, HD), (0, 2, 1, 3)).reshape(tokens, heads * HD)

    context_rows = join_heads(context)
    up_pre = jnp.einsum("dt,df->tf", act[3], up, preferred_element_type=F32)
    hidden_wide, gelu_back = jax.vjp(exact_gelu, up_pre)
    hidden = hidden_wide.astype(BF16)
    part = (
        jnp.einsum("de,te->dt", out, context_rows, preferred_element_type=F32)
        + jnp.einsum("df,tf->dt", down, hidden, preferred_element_type=F32)
    ).astype(BF16)

    def square(values):
        return jnp.pad(values, ((0, 128 - values.shape[0]), (0, 128 - values.shape[1])))

    next_rows = own_half(next_cot.reshape(seq_len, -1)).T
    next_rows = jnp.pad(next_rows, ((0, 128 - next_rows.shape[0]), (0, 0)))
    mix_in_rows = jnp.pad(small_all[:, :MIXH].T, ((0, 128 - MIXH), (0, 0)))
    static = jnp.pad(mix_static[:, None], ((0, 128 - mix_static.shape[0]), (0, 0)))
    branch_grad, wide_grad, block, next_mix, mixin_part, tiny = join(
        part, streams, own_half(out_cot).T, small_all, mix_in_rows, square(mix_out.T), square(mix_out), static,
        next_rows,
    )
    mixout_total, static_total = lax.psum(
        (tiny[:MIXH, : STREAMS * NEXT], tiny[: STREAMS * NEXT, 128]), ("dp", "tensor")
    )
    hidden_grad = jnp.einsum("dt,df->tf", branch_grad, down, preferred_element_type=F32)
    up_grad_low = gelu_back(hidden_grad)[0].astype(BF16)
    mlp_in_grad = jnp.einsum("df,tf->dt", up, up_grad_low, preferred_element_type=F32).astype(BF16)
    context_grad_rows = jnp.einsum("dt,de->te", branch_grad, out, preferred_element_type=F32).astype(BF16)
    context_grad = jnp.transpose(context_grad_rows.reshape(seqs, seq_len, heads, HD), (0, 2, 1, 3)).reshape(
        seqs * heads, seq_len, HD
    )
    query_grad, key_grad, value_grad = attend_backward(queries, key_rows, value_rows, log_sum, context_grad)
    proj_grad = jnp.stack(
        [
            join_heads(rotate(query_grad, cos_table, -sin_table).astype(BF16)),
            join_heads(rotate(key_grad, cos_table, -sin_table).astype(BF16)),
            join_heads(value_grad.astype(BF16)),
        ]
    )
    attn_in_grad = jnp.einsum("sde,ste->sdt", qkv, proj_grad, preferred_element_type=F32).astype(BF16)
    g_qkv = jnp.einsum("sdt,ste->sde", act[:3], proj_grad, preferred_element_type=F32).astype(BF16)
    g_out = jnp.einsum("dt,te->de", branch_grad, context_rows, preferred_element_type=F32).astype(BF16)
    g_up = jnp.einsum("dt,tf->df", act[3], up_grad_low, preferred_element_type=F32).astype(BF16)
    g_down = jnp.einsum("dt,tf->df", branch_grad, hidden, preferred_element_type=F32).astype(BF16)
    grid = (n_dp // HIGH, 2, 2, 2 * mix_in.shape[0])
    stream_grad, mix_grad, small_total, qkv_total, up_total, down_total, out_total = scatter(
        n_dp, attn_in_grad, mlp_in_grad, streams, small_all, wide_grad, mixin_part, history,
        g_qkv.reshape((3,) + grid + (-1,)), g_up.reshape(grid + (-1,)), g_down.reshape(grid + (-1,)),
        g_out.reshape(grid + (-1,)),
    )
    mix_rows = mix_all.reshape(n_dp, MIXH, 1, half)
    mix_rows = lax.all_gather(mix_rows, "tensor", axis=2, tiled=True)
    mix_rows = jnp.transpose(mix_rows, (1, 0, 2, 3)).reshape(MIXH, n_dp * seq_len)
    history_grad = jnp.stack(
        [
            sum(
                mix_rows[stream * HIST + source][None, :] * stream_grad[stream].astype(F32)
                for stream in range(STREAMS)
            )
            for source in range(HIST)
        ]
    ).astype(BF16)
    return (
        block.T,
        next_mix.T.reshape(seq_len, STREAMS, NEXT),
        history_grad,
        mix_grad[: STREAMS * HIST].T.reshape(seq_len, STREAMS, HIST),
        qkv_total.astype(F32),
        out_total.astype(F32),
        up_total.astype(F32),
        down_total.astype(F32),
        small_total[:, MIXH : MIXH + 2].T,
        small_total[:, MIXH + 2 : MIXH + 4].T,
        small_total[:, :MIXH],
        mixout_total,
        static_total,
    )


def solution(mesh):
    return jax.shard_map(
        functools.partial(per_device, mesh.shape["dp"]),
        mesh=mesh,
        in_specs=(
            P(None, "dp", None),
            P("dp", None, None),
            P(None, "dp", "tensor"),
            P("dp", "tensor"),
            P("dp", "tensor"),
            P("dp", "tensor"),
            P(None, "dp"),
            P(None, "dp"),
            P("dp", None),
            P(),
            P(),
            P("dp", None),
            P("dp", None, None),
        ),
        out_specs=(
            P("dp", None),
            P("dp", None, None),
            P(None, "dp", None),
            P("dp", None, None),
            P(None, "dp", "tensor"),
            P("dp", "tensor"),
            P("dp", "tensor"),
            P("dp", "tensor"),
            P(None, "dp"),
            P(None, "dp"),
            P("dp", None),
            P(),
            P(),
        ),
        check_vma=False,
    )


def lane_block(half, near, core, half_at, count):
    return at(near * 4 * half + core * 2 * half + half_at * half, count * half, half)


def join_kernel(
    part, streams, out_cot, small, mix_raw, next_raw,
    o_grad, o_wide, o_block, o_next, o_mixin, o_tiny,
    mix_out, next_cot, own, from_core, from_first, from_second, residual, wide, normed, block, cot, cot_in, back, low, next_rows, mixin, tiny,
    core_s, core_r, first_s, first_r, second_s, second_r, local, share_s, share_r, own_sem,
):
    here = Place()
    me, tensor = here.me, here.tensor
    depth, half = cot.shape
    spans = core_s.shape[0]
    size = depth // spans
    chunk = 256
    greet([{"dp": flip(me, CORE)}, {"dp": flip(me, NEAR)}, {"tensor": here.other}])

    def piece(span):
        return pl.ds(span * size, size)

    def tensor_first(span):
        return span < spans // 2

    def load(span, near, half_at):
        return pltpu.make_async_copy(
            part.at[piece(span), lane_block(half, near, here.core, half_at, 1)],
            own.at[near, half_at, piece(span)], local.at[span, near * 2 + half_at],
        )

    def to_core(span, near, half_at):
        return remote(
            part.at[piece(span), lane_block(half, near, 1 - here.core, half_at, 1)],
            from_core.at[near, half_at, piece(span)],
            core_s.at[span, near * 2 + half_at], core_r.at[span, near * 2 + half_at], dp=flip(me, CORE),
        )

    across = {"tensor": here.other}
    beside = {"dp": flip(me, NEAR)}

    def first_hop(span, block):
        source = own.at[block, here.other, piece(span)] if tensor_first(span) else own.at[1 - here.near, block, piece(span)]
        return remote(
            source, from_first.at[block, piece(span)], first_s.at[span, block], first_r.at[span, block],
            **(across if tensor_first(span) else beside),
        )

    def kept(span):
        return here.near if tensor_first(span) else tensor

    def second_hop(span):
        return remote(
            from_first.at[1 - kept(span), piece(span)], from_second.at[piece(span)], second_s.at[span], second_r.at[span],
            **(beside if tensor_first(span) else across),
        )

    def start(span):
        for near in range(2):
            for half_at in range(2):
                to_core(span, near, half_at).start()
                load(span, near, half_at).start()

    def after_core(span):
        for near in range(2):
            for half_at in range(2):
                load(span, near, half_at).wait()
                to_core(span, near, half_at).wait()
                own[near, half_at, piece(span)] += from_core[near, half_at, piece(span)]
        for block in range(2):
            first_hop(span, block).start()

    def after_first(span):
        for block in range(2):
            first_hop(span, block).wait()

        def add(block):
            mine = own[block, tensor, piece(span)] if tensor_first(span) else own[here.near, block, piece(span)]
            from_first[block, piece(span)] += mine

        add(1 - kept(span))
        second_hop(span).start()
        add(kept(span))

    mix_out[...] = jnp.zeros_like(mix_out)
    next_cot[...] = jnp.zeros_like(next_cot)
    mix_out[:MIXH, : STREAMS * NEXT] = mix_raw[...]
    next_cot[: STREAMS * NEXT, :] = next_raw[...]
    fetch = pltpu.make_async_copy(streams.at[3], residual, own_sem.at[0])
    fetch.start()
    cot_fetch = pltpu.make_async_copy(out_cot.at[at(tensor * half, half), :], cot_in, own_sem.at[7])
    cot_fetch.start()
    order = [span for pair in zip(range(spans // 2), range(spans // 2, spans)) for span in pair]
    for span in order:
        start(span)
    for span in order:
        after_core(span)
    for span in order:
        after_first(span)
    fetch.wait()
    cot_fetch.wait()

    def turn(index):
        rows = at(index * chunk, chunk)
        cot[rows, :] = cot_in[:, rows].T

    loop(0, depth // chunk, turn)
    squares = jnp.zeros((1, half), F32)
    for span in order:
        second_hop(span).wait()

        def widen(index, total):
            rows = at(span * size + index * chunk, chunk)
            branch = from_first[kept(span), rows, :].astype(F32) + from_second[rows, :].astype(F32)
            value = residual[rows, :].astype(F32) + branch
            wide[rows, :] = value
            block[:, rows] = value.T.astype(BF16)
            return total + jnp.sum(value * value, axis=0, keepdims=True)

        squares = lax.fori_loop(0, size // chunk, widen, squares)
    root = lax.rsqrt(squares / depth + ROOT_EPS)

    def share_block(which):
        mine = o_block.at[at(tensor * half, half), :]
        if which == 0:
            return pltpu.make_async_copy(block, mine, own_sem.at[1])
        return remote(block, mine, share_s.at[0], share_r.at[0], tensor=here.other)

    share_block(0).start()
    share_block(1).start()

    def norm(index):
        rows = at(index * chunk, chunk)
        normed[rows, :] = (wide[rows, :] * root).astype(BF16)

    loop(0, depth // chunk, norm)
    inner, slope = gelu_parts(tn(small[...], normed[...]))
    inner_low = inner.astype(BF16)
    next_rows[...] = tn(mix_out[...], inner_low)[:MIXH]
    next_low = next_cot[...].astype(BF16)

    column = lax.broadcasted_iota(jnp.int32, (128, 128), 1)
    static_grad = jnp.sum(next_cot[...], axis=1, keepdims=True)
    tiny[...] = jnp.where(column == MIXH, static_grad, nt(inner_low, next_low))[:MIXH]
    inner_grad = (nn(mix_out[...], next_low) * slope).astype(BF16)

    def pull(index, total):
        rows = at(index * chunk, chunk)
        value = jnp.dot(small[rows, :], inner_grad, preferred_element_type=F32)
        back[rows, :] = value
        return total + jnp.sum(value * wide[rows, :] * root, axis=0, keepdims=True)

    along = lax.fori_loop(0, depth // chunk, pull, jnp.zeros((1, half), F32)) / depth

    def finish(index):
        rows = at(index * chunk, chunk)
        value = cot[rows, :].astype(F32) + root * (back[rows, :] - wide[rows, :] * root * along)
        back[rows, :] = value
        low[rows, :] = value.astype(BF16)

    loop(0, depth // chunk, finish)

    def share(part_at, kind, index=0):
        rows = pl.ds(part_at * (depth // 2), depth // 2)
        number = 2 + part_at * 5 + kind + index
        if kind < 2:
            source, lanes, where = low.at[rows], lane_block(half, here.near, here.core, tensor, 1), (beside, across)[kind]
        elif kind == 2:
            far, where = (1 - here.near, across) if part_at == 0 else (here.near, beside)
            lanes = lane_block(half, far, here.core, tensor if part_at == 0 else here.other, 1)
            source = o_grad.at[rows, lanes]
        else:
            lanes, where = lane_block(half, index, here.core, 0, 2), {"dp": flip(me, CORE)}
            source = o_grad.at[rows, lanes]
        return remote(source, o_grad.at[rows, lanes], share_s.at[number], share_r.at[number], **where)

    for part_at in range(2):
        share(part_at, 0).start()
        share(part_at, 1).start()
    keep = pltpu.make_async_copy(
        low, o_grad.at[:, lane_block(half, here.near, here.core, tensor, 1)], own_sem.at[2]
    )
    keep.start()

    def mixin_rows(index):
        rows = at(index * chunk, chunk)
        mixin[rows, :] = nt(normed[rows, :], inner_grad)

    loop(0, depth // chunk, mixin_rows)
    for part_at in range(2):
        share(part_at, part_at).wait()
        share(part_at, 2).start()
    lanes = at(tensor * half, half)
    next_share = remote(next_rows, o_next.at[:, lanes], share_s.at[1], share_r.at[1], tensor=here.other)
    next_share.start()
    finals = [
        pltpu.make_async_copy(next_rows, o_next.at[:, lanes], own_sem.at[3]),
        pltpu.make_async_copy(back, o_wide, own_sem.at[4]),
        pltpu.make_async_copy(mixin, o_mixin, own_sem.at[5]),
        pltpu.make_async_copy(tiny, o_tiny, own_sem.at[6]),
    ]
    for copy in finals:
        copy.start()
    keep.wait()
    for part_at in range(2):
        share(part_at, 1 - part_at).wait()
        share(part_at, 2).wait()
        for near in range(2):
            share(part_at, 3, near).start()
    for part_at in range(2):
        for near in range(2):
            share(part_at, 3, near).wait()
    share_block(0).wait()
    share_block(1).wait()
    next_share.wait()
    for copy in finals:
        copy.wait()


def join(part, streams, out_cot, small, mix_out, next_cot):
    depth, half = streams.shape[1:]
    spans = 4
    shapes = [
        ((depth, 8 * half), BF16),
        ((depth, half), F32),
        ((2 * half, depth), BF16),
        ((MIXH, 2 * half), F32),
        ((depth, 128), F32),
        ((MIXH, 128), F32),
    ]
    return pl.pallas_call(
        join_kernel,
        out_shape=[jax.ShapeDtypeStruct(*shape) for shape in shapes],
        in_specs=[ANY] * 3 + [VM] * 3,
        out_specs=[ANY] * 6,
        scratch_shapes=[
            pltpu.VMEM((128, 128), BF16),
            pltpu.VMEM((128, half), F32),
            pltpu.VMEM((2, 2, depth, half), BF16),
            pltpu.VMEM((2, 2, depth, half), BF16),
            pltpu.VMEM((2, depth, half), BF16),
            pltpu.VMEM((depth, half), BF16),
            pltpu.VMEM((depth, half), BF16),
            pltpu.VMEM((depth, half), F32),
            pltpu.VMEM((depth, half), BF16),
            pltpu.VMEM((half, depth), BF16),
            pltpu.VMEM((depth, half), BF16),
            pltpu.VMEM((half, depth), BF16),
            pltpu.VMEM((depth, half), F32),
            pltpu.VMEM((depth, half), BF16),
            pltpu.VMEM((MIXH, half), F32),
            pltpu.VMEM((depth, 128), F32),
            pltpu.VMEM((MIXH, 128), F32),
            DMA((spans, 4)),
            DMA((spans, 4)),
            DMA((spans, 2)),
            DMA((spans, 2)),
            DMA((spans,)),
            DMA((spans,)),
            DMA((spans, 4)),
            DMA((12,)),
            DMA((12,)),
            DMA((8,)),
        ],
        compiler_params=pltpu.CompilerParams(
            collective_id=2, has_side_effects=True, vmem_limit_bytes=56 * 1024 * 1024
        ),
        name="join",
    )(part, streams, out_cot, small, mix_out, next_cot)


def back_kernel(
    grad, w_out, w_up, w_down, slope,
    o_mlp, o_up_grad, o_context,
    grad_in, out_in, up_in, down_in, slope_in,
    up_grad, context_grad, tall, load_sem, tall_sem, save_sem,
):
    depth = grad.shape[0]
    tile = 256
    loads = {}
    pairs = (
        ("grad", grad, grad_in), ("out", w_out, out_in), ("down", w_down, down_in), ("slope", slope, slope_in),
        ("up", w_up, up_in),
    )
    for number, (name, source, target) in enumerate(pairs):
        loads[name] = pltpu.make_async_copy(source, target, load_sem.at[number])
        loads[name].start()

    pending = {}

    def write(turn, out, compute):
        slots = tall.shape[1]
        if turn in pending:
            pending.pop(turn)()

        def copy(index):
            slot = lax.rem(index, slots)
            target = out.at[at(index * tile, tile), :]
            return pltpu.make_async_copy(tall.at[turn, slot], target, tall_sem.at[turn, slot])

        def body(index):
            @pl.when(index >= slots)
            def _():
                copy(index - slots).wait()

            tall[turn, lax.rem(index, slots)] = compute(at(index * tile, tile)).astype(BF16)
            copy(index).start()

        steps = depth // tile
        loop(0, steps, body)
        pending[turn] = lambda: loop(steps - slots, steps, lambda index: copy(index).wait())

    for name in ("grad", "out"):
        loads[name].wait()
    context_grad[...] = tn(out_in[...], grad_in[...]).astype(BF16)
    save_context = pltpu.make_async_copy(context_grad, o_context, save_sem.at[1])
    save_context.start()
    for name in ("down", "slope"):
        loads[name].wait()

    def lift(index):
        span = at(index * tile, tile)
        up_grad[span, :] = (tn(down_in[:, span], grad_in[...]) * slope_in[span, :]).astype(BF16)

    loop(0, up_grad.shape[0] // tile, lift)
    loads["up"].wait()
    save_up = pltpu.make_async_copy(up_grad, o_up_grad, save_sem.at[0])
    save_up.start()
    write(1, o_mlp, lambda span: nn(up_in[span, :], up_grad[...]))
    for drain in pending.values():
        drain()
    save_up.wait()
    save_context.wait()


def back(grad, w_out, w_up, w_down, slope):
    depth, tokens = grad.shape
    operands = (grad, w_out, w_up, w_down, slope)
    shapes = [(depth, tokens), slope.shape, (w_out.shape[1], tokens)]
    return pl.pallas_call(
        back_kernel,
        out_shape=[jax.ShapeDtypeStruct(shape, BF16) for shape in shapes],
        in_specs=[ANY] * 5,
        out_specs=[ANY] * 3,
        scratch_shapes=[pltpu.VMEM(v.shape, v.dtype) for v in operands]
        + [
            pltpu.VMEM(slope.shape, BF16),
            pltpu.VMEM((w_out.shape[1], tokens), BF16),
            pltpu.VMEM((2, 4, 256, tokens), BF16),
            DMA((5,)),
            DMA((2, 4)),
            DMA((2,)),
        ],
        compiler_params=pltpu.CompilerParams(vmem_limit_bytes=56 * 1024 * 1024),
        name="back",
    )(*operands)


ORDER = (3, 0, 1, 2)
SLOT = (1, 0, 1, 0)


def scatter_kernel(
    n_dp, mlp_grad, streams, small, wide_grad, mixin_part, mix_tiny, hist,
    branch_grad, act, hidden, up_grad, context, heads_rows, sums, context_grad, w_qkv, cos, sin,
    o_stream, o_mix, o_small, o_tiny, o_qkv, o_up, o_down, o_out, sent_qkv, sent_up, sent_down, sent_out, attn_grad,
    own, from_core, from_tensor, from_near, rows_in, wide, stream_grad, gains, biases, tiny, tiny_in, tiny_out,
    hist_in, arrived, mix_part, mix_in, mix_sum, tiny_sum, ring, side_in, mine, high_in,
    hidden_in, up_in, context_in, rows_grad_in, heads_in, sums_in, outer_in, qkv_in, tile_in, stage, tile_sem, stage_sem,
    right_sem, qkv_sem,
    core_s, core_r, tensor_s, tensor_r, near_s, near_r, local, in_sem,
    side_s, side_r, high_s, high_r, peer_s, peer_r, peer_local,
    a2a_s, a2a_r, a2a_own, keep_sem, pass_s, pass_r, tiny_s, tiny_r, mix_s, mix_r, hist_sem,
    ring_s, ring_r, last_s, last_r, last_local,
):
    here = Place()
    me, tensor = here.me, here.tensor
    depth, half = wide_grad.shape
    rows = depth // n_dp
    high_bits = int(math.log2(n_dp // HIGH))
    chunk = min(256, depth)
    greet_all(n_dp, me, here.other)

    highs = n_dp // HIGH
    tall = 2 * rows
    arrays = (
        (branch_grad, hidden_in, sent_down, o_down),
        (act.at[3], up_in, sent_up, o_up),
        (branch_grad, context_in, sent_out, o_out),
    ) + tuple((act.at[s], rows_grad_in.at[s], sent_qkv.at[s], o_qkv.at[s]) for s in range(3))
    units, first_unit = [], []
    for _, right, sent, o in arrays:
        first_unit.append(len(units))
        units += [(sent, o, first) for first in range(0, right.shape[0], UNIT)]
    total = len(units)
    rights = [
        pltpu.make_async_copy(source, target, right_sem.at[number])
        for number, (source, target) in enumerate(
            (
                (hidden, hidden_in), (up_grad, up_in), (context, context_in), (heads_rows, heads_in), (sums, sums_in),
                (context_grad, outer_in),
            )
        )
    ]

    def side_hop(unit):
        sent, _, first = units[unit]
        return remote(
            sent.at[:, :, :, pl.ds(first, UNIT)], side_in.at[unit], side_s.at[unit], side_r.at[unit], dp=flip(me, SIDE)
        )

    count = highs * 2

    def tile_load(array, block):
        mine_now = lax.div(block, count)
        side = here.side * mine_now + (1 - here.side) * (1 - mine_now)
        row = (lax.rem(block, count) * 2 + side) * tall
        slot = lax.rem(block, 2)
        return pltpu.make_async_copy(arrays[array][0].at[at(row, tall), :], tile_in.at[slot], tile_sem.at[slot])

    def product(array, block):
        @pl.when(block + 1 < 2 * count)
        def _():
            tile_load(array, block + 1).start()

        tile_load(array, block).wait()
        return nt(tile_in[lax.rem(block, 2)], arrays[array][1][...]).astype(BF16)

    def compute_sent(array):
        _, right, sent, _ = arrays[array]
        width = right.shape[0]

        def put(block):
            slot = lax.rem(block, 2)
            return pltpu.make_async_copy(
                stage.at[slot, :, pl.ds(0, width)], sent.at[lax.div(block, 2), slot], stage_sem.at[slot]
            )

        def body(block):
            value = product(array, block)

            @pl.when(block >= 2)
            def _():
                put(block - 2).wait()

            stage[lax.rem(block, 2), :, :width] = value
            put(block).start()

        tile_load(array, 0).start()
        loop(0, count, body)
        put(count - 2).wait()
        put(count - 1).wait()

    def compute_mine(array):
        width = arrays[array][1].shape[0]

        def body(block):
            value = product(array, block)
            flat = block - count
            for part in range(width // UNIT):
                mine[first_unit[array] + part, lax.div(flat, 2), lax.rem(flat, 2)] = value[
                    :, part * UNIT : (part + 1) * UNIT
                ]

        loop(count, 2 * count, body)

    def high_hop(unit, phase):
        span = 1 << phase
        base = lax.div(here.high, span)
        theirs = base + 1 - 2 * lax.rem(base, 2)
        return remote(
            mine.at[unit, pl.ds(theirs * span, span)], high_in.at[unit, pl.ds(span - 1, span)],
            high_s.at[unit, phase], high_r.at[unit, phase], dp=flip(me, HIGH << phase),
        )

    def peer_hop(unit, peer):
        _, o, first = units[unit]
        target, _ = here.peers[peer]
        return remote(
            mine.at[unit, here.high, bit(target, NEAR), at(bit(target, CORE) * rows, rows)],
            o.at[:, at(here.quarter * (o.shape[-1] // QUARTERS) + first, UNIT)],
            peer_s.at[unit, peer], peer_r.at[unit, peer], dp=target,
        )

    def peer_keep(unit):
        _, o, first = units[unit]
        return pltpu.make_async_copy(
            mine.at[unit, here.high, here.near, at(here.core * rows, rows)],
            o.at[:, at(here.quarter * (o.shape[-1] // QUARTERS) + first, UNIT)], peer_local.at[unit],
        )

    def add_blocks(unit, other, first_mine, first_other, count):
        step = min(64, tall)

        def add(flat):
            high, rest = lax.div(flat, 2 * (tall // step)), lax.rem(flat, 2 * (tall // step))
            near, span = lax.div(rest, tall // step), at(lax.rem(rest, tall // step) * step, step)
            mine[unit, first_mine + high, near, span] += other[unit, first_other + high, near, span]

        loop(0, count * 2 * (tall // step), add)

    def finish_high(unit):
        for phase in reversed(range(high_bits)):
            high_hop(unit, phase).wait()
            span = 1 << phase
            add_blocks(unit, high_in, lax.div(here.high, span) * span, span - 1, span)
            if phase:
                high_hop(unit, phase - 1).start()
        peer_keep(unit).start()
        for peer in range(3):
            peer_hop(unit, peer).start()

    def tick(unit):
        side_hop(unit).wait()
        if unit + 2 < total:
            side_hop(unit + 2).start()
        add_blocks(unit, side_in, 0, 0, n_dp // HIGH)
        if unit:
            finish_high(unit - 1)
        high_hop(unit, high_bits - 1).start()

    done = 0

    def ticks(count):
        nonlocal done
        for unit in range(done, min(done + count, total)):
            tick(unit)
        done = min(done + count, total)

    def load(stream, near, half_at):
        part = attn_grad.at[stream] if stream < 3 else mlp_grad
        return pltpu.make_async_copy(
            part.at[:, lane_block(half, near, here.core, half_at, 1)], own.at[SLOT[stream], near, half_at],
            local.at[stream, near * 2 + half_at],
        )

    def to_core(stream, near, half_at):
        part = attn_grad.at[stream] if stream < 3 else mlp_grad
        return remote(
            part.at[:, lane_block(half, near, 1 - here.core, half_at, 1)], from_core.at[stream, near, half_at],
            core_s.at[stream, near * 2 + half_at], core_r.at[stream, near * 2 + half_at], dp=flip(me, CORE),
        )

    def to_tensor(stream, near):
        return remote(
            own.at[SLOT[stream], near, here.other], from_tensor.at[stream, near],
            tensor_s.at[stream, near], tensor_r.at[stream, near], tensor=here.other,
        )

    def to_near(stream):
        return remote(
            from_tensor.at[stream, 1 - here.near], from_near.at[stream], near_s.at[stream], near_r.at[stream],
            dp=flip(me, NEAR),
        )

    def after_core(stream):
        for near in range(2):
            for half_at in range(2):
                load(stream, near, half_at).wait()
                to_core(stream, near, half_at).wait()

        def add(index):
            span = at(index * chunk, chunk)
            for near in range(2):
                for half_at in range(2):
                    own[SLOT[stream], near, half_at, span] += from_core[stream, near, half_at, span]

        loop(0, depth // chunk, add)

    def after_tensor(stream):
        for near in range(2):
            to_tensor(stream, near).wait()

        def add(index):
            span = at(index * chunk, chunk)
            for near in range(2):
                from_tensor[stream, near, span] += own[SLOT[stream], near, tensor, span]

        loop(0, depth // chunk, add)
        to_near(stream).start()

    stats = []

    def measure(stream):
        def piece(index):
            return rows_in[stream, at(index * chunk, chunk), :].astype(F32)

        centre = sum_rows(piece, depth, chunk, lambda v: v) / depth
        spread = sum_rows(piece, depth, chunk, lambda v: (v - centre) * (v - centre)) / depth
        stats.append((centre, lax.rsqrt(spread + NORM_EPS)))

    def back_norm(stream):
        to_near(stream).wait()
        group = 0 if stream < 3 else 1
        centre, root = stats[stream]

        def parts(index):
            span = at(index * chunk, chunk)
            grad = from_tensor[stream, here.near, span].astype(F32) + from_near[stream, span].astype(F32)
            hat = (rows_in[stream, span, :].astype(F32) - centre) * root
            gain = small[span, MIXH + group : MIXH + group + 1].astype(F32)
            return span, grad, hat, grad * gain

        def sums(index, carry):
            span, grad, hat, scaled = parts(index)
            if stream in (0, 3):
                gains[group, span] = grad * hat
                biases[group, span] = grad
            else:
                gains[group, span] += grad * hat
                biases[group, span] += grad
            return (
                carry[0] + jnp.sum(scaled, axis=0, keepdims=True),
                carry[1] + jnp.sum(scaled * hat, axis=0, keepdims=True),
            )

        zero = jnp.zeros((1, half), F32)
        whole, along = lax.fori_loop(0, depth // chunk, sums, (zero, zero))

        def finish(index):
            span, _, hat, scaled = parts(index)
            value = root * (scaled - whole / depth - hat * (along / depth))
            if stream == 3:
                value = value + wide[span, :]
            stream_grad[stream, span] = value.astype(BF16)

        loop(0, depth // chunk, finish)
        loop(1, n_dp, lambda step: send(stream, step).start())
        send_own(stream).start()

    def send(stream, step):
        target = lax.rem(me + step, n_dp)
        return remote(
            stream_grad.at[stream, at(target * rows, rows), :], arrived.at[stream, step],
            a2a_s.at[stream, step], a2a_r.at[stream, step], dp=target,
        )

    def send_own(stream):
        return pltpu.make_async_copy(
            stream_grad.at[stream, at(me * rows, rows), :], arrived.at[stream, 0], a2a_own.at[stream]
        )

    def source_of(step):
        return lax.rem(me - step + n_dp, n_dp)

    def lanes_of(step):
        return at(source_of(step) * 2 * half + tensor * half, half)

    def fetch(step):
        slot = lax.rem(step, 2)
        return pltpu.make_async_copy(hist.at[:, :, lanes_of(step)], hist_in.at[slot], hist_sem.at[slot])

    def keep(stream, step):
        return pltpu.make_async_copy(
            arrived.at[stream, step], o_stream.at[stream, :, lanes_of(step)], keep_sem.at[stream, step]
        )

    def pass_on(stream, step):
        return remote(
            arrived.at[stream, step], o_stream.at[stream, :, lanes_of(step)],
            pass_s.at[stream, step], pass_r.at[stream, step], tensor=here.other,
        )

    def mix_send(step):
        return remote(mix_part.at[step], mix_in.at[step], mix_s.at[step], mix_r.at[step], dp=source_of(step))

    def receive(stream):
        fetch(0).start()
        send_own(stream).wait()

        def one(step):
            @pl.when(step + 1 < n_dp)
            def _():
                fetch(step + 1).start()

            @pl.when(step > 0)
            def _():
                send(stream, step).wait()

            keep(stream, step).start()
            pass_on(stream, step).start()
            fetch(step).wait()
            totals = [jnp.zeros((8, half), F32) for _ in range(HIST)]
            for row in range(0, rows, 16):
                span = pl.ds(row, 16)
                grad = arrived[stream, step, span, :].astype(F32)
                for source in range(HIST):
                    product = grad * hist_in[lax.rem(step, 2), source, span, :].astype(F32)
                    totals[source] = totals[source] + product[:8] + product[8:]
            for source in range(HIST):
                mix_part[step, pl.ds(stream * HIST + source, 1), :] = jnp.sum(totals[source], axis=0, keepdims=True)
            if stream == ORDER[-1]:

                @pl.when(step > 0)
                def _():
                    mix_send(step).start()

        loop(0, n_dp, one)

    ring_targets = [{"dp": flip(me, value)} for value in (CORE, SIDE, NEAR)]
    ring_targets += [{"dp": flip(me, HIGH << phase)} for phase in range(high_bits)]
    ring_targets.append({"tensor": here.other})
    hops = len(ring_targets)

    def ring_hop(hop):
        return remote(ring.at[hop, 0], ring.at[hop, 1], ring_s.at[hop], ring_r.at[hop], **ring_targets[hop])

    def ring_step(hop):
        ring_hop(hop).wait()
        ring[hop + 1, 0] = ring[hop, 0] + ring[hop, 1]
        if hop + 1 < hops:
            ring_hop(hop + 1).start()

    rights[0].start()
    inputs = [
        pltpu.make_async_copy(streams, rows_in, in_sem.at[0]),
        pltpu.make_async_copy(wide_grad, wide, in_sem.at[1]),
        pltpu.make_async_copy(mix_tiny, ring.at[0, 0], in_sem.at[2]),
    ]

    def load_own(stream):
        for near in range(2):
            for half_at in range(2):
                load(stream, near, half_at).start()

    def tensor_start(stream):
        for near in range(2):
            to_tensor(stream, near).start()

    def core_start(stream):
        for near in range(2):
            for half_at in range(2):
                to_core(stream, near, half_at).start()

    def qkv_load(stream):
        return pltpu.make_async_copy(w_qkv.at[stream], qkv_in.at[stream % 2], qkv_sem.at[stream % 2])

    seq_len = sums_in.shape[1]
    heads = heads_in.shape[1] // HD
    scale = 1.0 / math.sqrt(HD)

    def attend_back(seq):
        span = at(seq * seq_len, seq_len)
        for head in range(heads):
            lane = pl.ds(head * HD, HD)
            queries, keys, values = (heads_in[s, lane, span] for s in range(3))
            prob = jnp.exp(causal_scores(keys, queries) - sums_in[pl.ds(seq * heads + head, 1), :])
            outer = outer_in[lane, span]
            prob_grad = tn(values, outer)
            inner = jnp.sum(prob * prob_grad, axis=0, keepdims=True)
            score_grad = (prob * (prob_grad - inner)).astype(BF16)
            turn_back = (cos[...], -sin[...])
            rows_grad_in[0, lane, span] = turned(nn(keys, score_grad) * scale, *turn_back).astype(BF16)
            rows_grad_in[1, lane, span] = turned(nt(queries, score_grad) * scale, *turn_back).astype(BF16)
            rows_grad_in[2, lane, span] = nt(outer, prob.astype(BF16)).astype(BF16)

    def input_grad(stream):
        def put(block):
            slot = lax.rem(block, 2)
            return pltpu.make_async_copy(
                stage.at[slot, :, pl.ds(0, 8 * half)], attn_grad.at[stream, at(block * tall, tall), :], stage_sem.at[slot]
            )

        def body(block):
            value = nn(qkv_in[stream % 2, at(block * tall, tall), :], rows_grad_in[stream]).astype(BF16)

            @pl.when(block >= 2)
            def _():
                put(block - 2).wait()

            stage[lax.rem(block, 2), :, : 8 * half] = value
            put(block).start()

        qkv_load(stream).wait()
        loop(0, depth // tall, body)
        put(depth // tall - 2).wait()
        put(depth // tall - 1).wait()
        if stream + 2 < 3:
            qkv_load(stream + 2).start()
        core_start(stream)

    core_start(ORDER[0])
    load_own(ORDER[0])
    for copy in rights[1:] + inputs:
        copy.start()
    qkv_load(0).start()
    qkv_load(1).start()
    rights[0].wait()
    compute_sent(0)
    side_hop(0).start()
    side_hop(1).start()
    after_core(ORDER[0])
    tensor_start(ORDER[0])
    compute_mine(0)
    for copy in rights[1:] + inputs:
        copy.wait()
    ring_hop(0).start()
    loop(0, 8 * half // seq_len, attend_back)
    for stream in range(3):
        input_grad(stream)
        if stream == 0:
            ticks(1)
        if stream == ORDER[1]:
            load_own(stream)
    mix_part[...] = jnp.zeros_like(mix_part)
    for stream in range(STREAMS):
        measure(stream)
    after_core(ORDER[1])
    ring_step(0)
    for turn, stream in enumerate(ORDER):
        ticks((1, 3, 2, 2)[turn])
        after_tensor(stream)
        if turn + 1 < STREAMS:
            tensor_start(ORDER[turn + 1])
            if turn + 1 < hops:
                ring_step(turn + 1)
        if turn + 2 < STREAMS:
            load_own(ORDER[turn + 2])
        for array in ((1,), (2, 3), (4, 5), ())[turn]:
            compute_sent(array)
            compute_mine(array)
        if turn + 2 < STREAMS:
            after_core(ORDER[turn + 2])
        if turn > 0:
            back_norm(ORDER[turn - 1])
        if turn > 1:
            receive(ORDER[turn - 2])
    back_norm(ORDER[-1])

    column = lax.broadcasted_iota(jnp.int32, (chunk, 128), 1)
    pltpu.make_async_copy(mixin_part, wide, in_sem.at[0]).start()
    pltpu.make_async_copy(mixin_part, wide, in_sem.at[0]).wait()

    def gather_tiny(index):
        span = at(index * chunk, chunk)
        value = wide[span, :]
        for group in range(2):
            gain = jnp.sum(gains[group, span], axis=1, keepdims=True)
            bias = jnp.sum(biases[group, span], axis=1, keepdims=True)
            value = jnp.where(column == MIXH + group, gain, value)
            value = jnp.where(column == MIXH + 2 + group, bias, value)
        tiny[span, :] = value.astype(BF16)

    loop(0, depth // chunk, gather_tiny)

    def tiny_send(step):
        target = lax.rem(me + step, n_dp)
        return remote(tiny.at[at(target * rows, rows), :], tiny_in.at[step], tiny_s.at[step], tiny_r.at[step], dp=target)

    loop(1, n_dp, lambda step: tiny_send(step).start())
    receive(ORDER[2])
    ticks(2)
    receive(ORDER[3])
    for hop in range(STREAMS, hops):
        ring_step(hop)
    tiny_final = pltpu.make_async_copy(ring.at[hops, 0], o_tiny, last_local.at[0])
    tiny_final.start()
    ticks(total)

    tiny_sum[0] = tiny[at(me * rows, rows), :].astype(F32)

    def add_tiny(step):
        tiny_send(step).wait()
        tiny_sum[0] += tiny_in[step].astype(F32)

    loop(1, n_dp, add_tiny)
    tiny_share = remote(tiny_sum.at[0], tiny_sum.at[1], last_s.at[1], last_r.at[1], tensor=here.other)
    tiny_share.start()
    mix_sum[...] = mix_part[0]

    def add_mix(step):
        mix_send(step).wait()
        mix_sum[...] += mix_in[step]

    loop(1, n_dp, add_mix)
    lanes = at(tensor * half, half)
    mix_share = remote(mix_sum, o_mix.at[:, lanes], last_s.at[0], last_r.at[0], tensor=here.other)
    mix_keep = pltpu.make_async_copy(mix_sum, o_mix.at[:, lanes], last_local.at[1])
    mix_share.start()
    mix_keep.start()
    finish_high(total - 1)
    tiny_share.wait()
    tiny_out[...] = (tiny_sum[0] + tiny_sum[1]).T
    tiny_keep = pltpu.make_async_copy(tiny_out, o_small, last_local.at[2])
    tiny_keep.start()
    for unit in range(total):
        peer_keep(unit).wait()
        for peer in range(3):
            peer_hop(unit, peer).wait()

    def settle(step):
        for stream in range(STREAMS):
            keep(stream, step).wait()
            pass_on(stream, step).wait()

    loop(0, n_dp, settle)
    mix_share.wait()
    mix_keep.wait()
    tiny_keep.wait()
    tiny_final.wait()


def scatter(
    n_dp, mlp_grad, streams, small, wide_grad, mixin_part, mix_tiny, hist, branch_grad, act, hidden, up_grad, context,
    rows_all, sums, context_grad, w_qkv, cos, sin,
):
    depth, half = wide_grad.shape
    rows = depth // n_dp
    high = n_dp // HIGH
    high_bits = int(math.log2(high))
    tokens = act.shape[2]
    narrow, width = context.shape[0], hidden.shape[0]
    widths = ((3,), narrow), ((), width), ((), width), ((), narrow)
    units = (4 * narrow + 2 * width) // UNIT
    hops = high_bits + 4

    outs = [
        ((STREAMS, rows, 2 * half * n_dp), BF16),
        ((MIXH, 2 * half), F32),
        ((128, rows), F32),
        (mix_tiny.shape, F32),
    ]
    outs += [(lead + (rows, QUARTERS * size), BF16) for lead, size in widths]
    outs += [(lead + (high, 2, 2 * rows, size), BF16) for lead, size in widths]
    outs.append(((3, depth, tokens), BF16))
    return pl.pallas_call(
        functools.partial(scatter_kernel, n_dp),
        out_shape=[jax.ShapeDtypeStruct(*shape) for shape in outs],
        in_specs=[ANY, ANY, VM] + [ANY] * 13 + [VM] * 2,
        out_specs=[ANY] * 13,
        scratch_shapes=[
            pltpu.VMEM((2, 2, 2, depth, half), BF16),
            pltpu.VMEM((STREAMS, 2, 2, depth, half), BF16),
            pltpu.VMEM((STREAMS, 2, depth, half), BF16),
            pltpu.VMEM((STREAMS, depth, half), BF16),
            pltpu.VMEM((STREAMS, depth, half), BF16),
            pltpu.VMEM((depth, half), F32),
            pltpu.VMEM((STREAMS, depth, half), BF16),
            pltpu.VMEM((2, depth, half), F32),
            pltpu.VMEM((2, depth, half), F32),
            pltpu.VMEM((depth, 128), BF16),
            pltpu.VMEM((n_dp, rows, 128), BF16),
            pltpu.VMEM((128, rows), F32),
            pltpu.VMEM((2, HIST, rows, half), BF16),
            pltpu.VMEM((STREAMS, n_dp, rows, half), BF16),
            pltpu.VMEM((n_dp, MIXH, half), F32),
            pltpu.VMEM((n_dp, MIXH, half), F32),
            pltpu.VMEM((MIXH, half), F32),
            pltpu.VMEM((2, rows, 128), F32),
            pltpu.VMEM((hops + 1, 2) + mix_tiny.shape, F32),
            pltpu.VMEM((units, high, 2, 2 * rows, UNIT), BF16),
            pltpu.VMEM((units, high, 2, 2 * rows, UNIT), BF16),
            pltpu.VMEM((units, high - 1, 2, 2 * rows, UNIT), BF16),
            pltpu.VMEM(hidden.shape, BF16),
            pltpu.VMEM(up_grad.shape, BF16),
            pltpu.VMEM(context.shape, BF16),
            pltpu.VMEM(rows_all.shape, BF16),
            pltpu.VMEM(rows_all.shape, BF16),
            pltpu.VMEM(sums.shape, F32),
            pltpu.VMEM(context_grad.shape, BF16),
            pltpu.VMEM((2,) + w_qkv.shape[1:], BF16),
            pltpu.VMEM((2, 2 * rows, tokens), BF16),
            pltpu.VMEM((2, 2 * rows, max(width, tokens)), BF16),
            DMA((2,)),
            DMA((2,)),
            DMA((6,)),
            DMA((2,)),
            DMA((STREAMS, 4)),
            DMA((STREAMS, 4)),
            DMA((STREAMS, 2)),
            DMA((STREAMS, 2)),
            DMA((STREAMS,)),
            DMA((STREAMS,)),
            DMA((STREAMS, 4)),
            DMA((3,)),
            DMA((units,)),
            DMA((units,)),
            DMA((units, high_bits)),
            DMA((units, high_bits)),
            DMA((units, 3)),
            DMA((units, 3)),
            DMA((units,)),
            DMA((STREAMS, n_dp)),
            DMA((STREAMS, n_dp)),
            DMA((STREAMS,)),
            DMA((STREAMS, n_dp)),
            DMA((STREAMS, n_dp)),
            DMA((STREAMS, n_dp)),
            DMA((n_dp,)),
            DMA((n_dp,)),
            DMA((n_dp,)),
            DMA((n_dp,)),
            DMA((2,)),
            DMA((hops,)),
            DMA((hops,)),
            DMA((2,)),
            DMA((2,)),
            DMA((3,)),
        ],
        compiler_params=pltpu.CompilerParams(
            collective_id=3, has_side_effects=True, vmem_limit_bytes=62 * 1024 * 1024
        ),
        name="scatter",
    )(
        mlp_grad, streams, small, wide_grad, mixin_part, mix_tiny, hist, branch_grad, act, hidden, up_grad, context,
        rows_all, sums, context_grad, w_qkv, cos, sin,
    )[:8]


def rotary_tables(length, rotary, float_type):
    half_rot = rotary // 2
    places = jnp.arange(length).astype(float_type)
    frequency = jnp.exp(
        jnp.arange(half_rot).astype(float_type) * (-2.0 * math.log(10000.0) / rotary)
    )
    angles = places[:, None] * frequency[None, :]
    return (jnp.cos(angles), jnp.sin(angles))


def finish_kernel(mix_rows, stream_grad, small, tiny, block, *refs):
    narrow, history_grad, wide = refs[:4], refs[4], refs[5:9]
    gain, bias, mix_in_grad, mix_out_grad, block_out = refs[9:]
    rows = stream_grad.shape[1]
    tile, span = min(32, rows), 512

    def body(index):
        row = at(lax.rem(index, rows // tile) * tile, tile)
        lane = at(lax.div(index, rows // tile) * span, span)
        grads = [stream_grad[stream, row, lane].astype(F32) for stream in range(STREAMS)]
        for source in range(HIST):
            total = sum(
                mix_rows[pl.ds(stream * HIST + source, 1), lane] * grads[stream] for stream in range(STREAMS)
            )
            history_grad[source, row, lane] = total.astype(BF16)

    loop(0, rows // tile * (stream_grad.shape[2] // span), body)
    for low, full in zip(narrow, wide):
        full[...] = low[...].astype(F32)
    block_out[...] = block[...]
    gain[...] = small[MIXH : MIXH + 2]
    bias[...] = small[MIXH + 2 : MIXH + 4]
    mix_in_grad[...] = small[:MIXH]
    mix_out_grad[...] = tiny[:, : STREAMS * NEXT]


def finish(mix_rows, stream_grad, small, tiny, block, *grads):
    rows, tokens = stream_grad.shape[1:]
    steps = rows // 16
    lanes = tokens // steps

    def weight(g):
        if g.ndim == 3:
            return pl.BlockSpec((g.shape[0], 16, g.shape[2]), lambda i: (0, i, 0))
        return pl.BlockSpec((16, g.shape[1]), lambda i: (i, 0))

    def along(count):
        return pl.BlockSpec((count, rows, lanes), lambda i: (0, 0, i))

    def whole(shape):
        return pl.BlockSpec(shape, lambda i: (0, 0))

    blocks = pl.BlockSpec((block.shape[0] // steps, block.shape[1]), lambda i: (i, 0))
    smalls = [(2, rows), (2, rows), (MIXH, rows), (MIXH, STREAMS * NEXT)]
    return pl.pallas_call(
        finish_kernel,
        grid=(steps,),
        out_shape=[jax.ShapeDtypeStruct((HIST, rows, tokens), BF16)]
        + [jax.ShapeDtypeStruct(g.shape, F32) for g in grads]
        + [jax.ShapeDtypeStruct(shape, F32) for shape in smalls]
        + [jax.ShapeDtypeStruct(block.shape, BF16)],
        in_specs=[pl.BlockSpec((mix_rows.shape[0], lanes), lambda i: (0, i)), along(STREAMS)]
        + [whole(small.shape), whole(tiny.shape), blocks]
        + [weight(g) for g in grads],
        out_specs=[along(HIST)] + [weight(g) for g in grads] + [whole(shape) for shape in smalls] + [blocks],
        compiler_params=pltpu.CompilerParams(vmem_limit_bytes=60 * 1024 * 1024),
        name="finish",
    )(mix_rows, stream_grad, small, tiny, block, *grads)


def per_device(
    n_dp, history, mix_weights, w_qkv, w_out, w_up, w_down, norm_gain, norm_bias, mix_in, mix_out, mix_static,
    out_cot, next_cot,
):
    tensor = lax.axis_index("tensor")
    seq_len = mix_weights.shape[0]
    half = seq_len // 2
    depth = mix_in.shape[0] * n_dp

    def own_half(rows):
        return lax.dynamic_slice_in_dim(rows, tensor * half, half, 0)

    mix_rows = own_half(mix_weights.reshape(seq_len, -1)).T
    small = jnp.concatenate(
        [mix_in.T, norm_gain, norm_bias, jnp.zeros((128 - MIXH - 4, mix_in.shape[0]), BF16)], axis=0
    )
    cos, sin = (table.T for table in rotary_tables(seq_len, ROT, F32))
    mix_rows, small_all, streams, act, qkv, out, up, down, rows, context, sums, hidden, slope, part = gather(
        n_dp, history, mix_rows, small, w_qkv, w_out, w_up, w_down, cos, sin
    )
    small_all = small_all.reshape(depth, 128)
    qkv, up, down, out = (
        qkv.reshape(3, depth, -1), up.reshape(depth, -1), down.reshape(depth, -1), out.reshape(depth, -1)
    )

    next_rows = own_half(next_cot.reshape(seq_len, -1)).T
    branch_grad, wide_grad, block, next_mix, mixin_part, tiny = join(
        part, streams, out_cot, small_all, mix_out, next_rows
    )
    mlp_in_grad, up_grad, context_grad = back(branch_grad, out, up, down, slope)
    stream_grad, mix_grad, small_total, tiny, qkv_total, up_total, down_total, out_total = scatter(
        n_dp, mlp_in_grad, streams, small_all, wide_grad, mixin_part, tiny, history, branch_grad, act, hidden, up_grad,
        context, rows, sums, context_grad, qkv, cos, sin,
    )
    (
        history_grad, qkv_total, up_total, down_total, out_total, gain_total, bias_total, mixin_total, mixout_total, block,
    ) = finish(
        mix_rows, stream_grad, small_total, tiny, block, qkv_total, up_total, down_total, out_total
    )
    return (
        block,
        (next_mix.T + mix_static).reshape(seq_len, STREAMS, NEXT),
        history_grad,
        mix_grad[: STREAMS * HIST].T.reshape(seq_len, STREAMS, HIST),
        qkv_total,
        out_total,
        up_total,
        down_total,
        gain_total,
        bias_total,
        mixin_total.T,
        mixout_total,
        tiny[: STREAMS * NEXT, MIXH],
    )


def solution(mesh):
    return jax.shard_map(
        functools.partial(per_device, mesh.shape["dp"]),
        mesh=mesh,
        in_specs=(
            P(None, "dp", None),
            P("dp", None, None),
            P(None, "dp", "tensor"),
            P("dp", "tensor"),
            P("dp", "tensor"),
            P("dp", "tensor"),
            P(None, "dp"),
            P(None, "dp"),
            P("dp", None),
            P(),
            P(),
            P("dp", None),
            P("dp", None, None),
        ),
        out_specs=(
            P("dp", None),
            P("dp", None, None),
            P(None, "dp", None),
            P("dp", None, None),
            P(None, "dp", "tensor"),
            P("dp", "tensor"),
            P("dp", "tensor"),
            P("dp", "tensor"),
            P(None, "dp"),
            P(None, "dp"),
            P("dp", None),
            P(),
            P(),
        ),
        check_vma=False,
    )
```

```python
import functools
import math

import jax
import jax.numpy as jnp
from jax import lax
from jax.experimental import pallas as pl
from jax.experimental.pallas import tpu as pltpu
from jax.sharding import PartitionSpec as P

HD = 128
ROT = 32
HIST = 9
STREAMS = 4
NEXT = 10
MIXH = 40

NORM_EPS = 1e-05
ROOT_EPS = 1e-06
MASKED = -1e30

MESH = pl.DeviceIdType.MESH
ANY = pl.BlockSpec(memory_space=pltpu.HBM)
VM = pl.BlockSpec(memory_space=pltpu.VMEM)
DMA = pltpu.SemaphoreType.DMA
F32, BF16 = jnp.float32, jnp.bfloat16
CORE, SIDE, NEAR, HIGH = 1, 2, 4, 8
QUARTERS = 4
UNIT = 256
PLAN = (
    "T", "T", "n0", "T", "T", "n1", "T", "T", "n2", "s0", "T", "n3", "t0", "s1", "w0", "p0", "T", "t1", "s2", "p1",
    "T", "t2", "s3", "p2", "t3", "a0", "u0",
)


def bit(place, value):
    return lax.rem(lax.div(place, value), 2)


def flip(place, value):
    return place + value - 2 * value * bit(place, value)


def at(start, size, multiple=None):
    return pl.ds(pl.multiple_of(start, size if multiple is None else multiple), size)


def remote(src, dst, send, recv, **where):
    return pltpu.make_async_remote_copy(
        src_ref=src, dst_ref=dst, send_sem=send, recv_sem=recv, device_id=where, device_id_type=MESH
    )


def loop(lower, upper, step):
    def body(index, carry):
        step(index)
        return carry

    lax.fori_loop(lower, upper, body, 0)


def greet(targets):
    barrier = pltpu.get_barrier_semaphore()
    for target in targets:
        pl.semaphore_signal(barrier, inc=1, device_id=target, device_id_type=MESH)
    pl.semaphore_wait(barrier, len(targets))


def greet_all(n_dp, me, other_tensor):
    barrier = pltpu.get_barrier_semaphore()
    loop(
        1,
        n_dp,
        lambda step: pl.semaphore_signal(
            barrier, inc=1, device_id={"dp": lax.rem(me + step, n_dp)}, device_id_type=MESH
        ),
    )
    pl.semaphore_signal(barrier, inc=1, device_id={"tensor": other_tensor}, device_id_type=MESH)
    pl.semaphore_wait(barrier, n_dp)


class Place:
    def __init__(self):
        self.me = lax.axis_index("dp")
        self.tensor = lax.axis_index("tensor")
        self.other = 1 - self.tensor
        self.core = bit(self.me, CORE)
        self.side = bit(self.me, SIDE)
        self.near = bit(self.me, NEAR)
        self.high = lax.div(self.me, HIGH)
        self.quarter = self.near * 2 + self.core
        self.peers = (
            (flip(self.me, CORE), self.near * 2 + 1 - self.core),
            (flip(self.me, NEAR), (1 - self.near) * 2 + self.core),
            (flip(flip(self.me, NEAR), CORE), (1 - self.near) * 2 + 1 - self.core),
        )


def sum_rows(ref_at, depth, chunk, of):
    def body(index, total):
        return total + jnp.sum(of(ref_at(index)), axis=0, keepdims=True)

    return lax.fori_loop(0, depth // chunk, body, jnp.zeros((1, 128), F32))


def gelu_parts(values):
    phi = 0.5 * (1.0 + lax.erf(values * (1.0 / math.sqrt(2.0))))
    density = jnp.exp(-0.5 * values * values) * (1.0 / math.sqrt(2.0 * math.pi))
    return values * phi, phi + values * density


def tn(left, right):
    return lax.dot_general(left, right, (((0,), (0,)), ((), ())), preferred_element_type=F32)


def nt(left, right):
    return lax.dot_general(left, right, (((1,), (1,)), ((), ())), preferred_element_type=F32)


def nn(left, right):
    return jnp.dot(left, right, preferred_element_type=F32)


def turned(values, cos, sin):
    pieces = []
    half_rot = ROT // 2
    repeats = values.shape[1] // cos.shape[1]
    cos, sin = (jnp.concatenate([table] * repeats, axis=1) for table in (cos, sin))
    for head in range(values.shape[0] // HD):
        rows = values[head * HD : (head + 1) * HD]
        first, second = rows[:half_rot], rows[half_rot:ROT]
        pieces += [first * cos - second * sin, second * cos + first * sin, rows[ROT:]]
    return jnp.concatenate(pieces, axis=0)


def causal_scores(keys, queries):
    scores = tn(keys, queries) * (1.0 / math.sqrt(HD))
    length = scores.shape[0]
    key = lax.broadcasted_iota(jnp.int32, (length, length), 0)
    query = lax.broadcasted_iota(jnp.int32, (length, length), 1)
    return jnp.where(query >= key, scores, MASKED)


def gather_kernel(
    n_dp, hist, mix, small, w_qkv, w_out, w_up, w_down, cos, sin,
    o_mix, o_small, o_streams, o_act, o_qkv, o_out, o_up, o_down,
    o_rows, o_context, o_sums, o_hidden, o_slope, o_part,
    mix_all, small_all, hist_in, mixed, streams, act,
    early_s, early_r, hist_sem, a2a_s, a2a_r, reshard_s, reshard_r, high_s, high_r, side_s, side_r,
    act_s, act_r, act_local, own_sem, out_sem, share_s, share_r, share_l,
    act_in, qkv_in, out_in, up_in, down_in, rows_out, context, sums, hidden, slope, part, load_sem, save_sem,
):
    here = Place()
    me, tensor = here.me, here.tensor
    rows = small.shape[1]
    depth = rows * n_dp
    half = hist.shape[2] // n_dp // 2
    high_bits = int(math.log2(n_dp // HIGH))
    weights = ((w_qkv, o_qkv), (w_out, o_out), (w_up, o_up), (w_down, o_down))
    greet_all(n_dp, me, here.other)

    def early(which, buf, phase):
        if phase == 0:
            block, target = buf.at[here.high, here.near, here.side, here.core], flip(me, NEAR)
        elif phase <= high_bits:
            span = 1 << (phase - 1)
            block = buf.at[pl.ds(lax.div(here.high, span) * span, span), :, here.side, here.core]
            target = flip(me, HIGH << (phase - 1))
        elif phase == high_bits + 1:
            block, target = buf.at[:, :, here.side, here.core], flip(me, SIDE)
        else:
            block, target = buf.at[:, :, :, here.core], flip(me, CORE)
        return remote(block, block, early_s.at[which, phase], early_r.at[which, phase], dp=target)

    own_mix = pltpu.make_async_copy(mix, mix_all.at[here.high, here.near, here.side, here.core], own_sem.at[0])
    units = []
    for w, o in weights:
        if len(w.shape) == 3:
            units += [(w.at[part], o.at[part], 0) for part in range(w.shape[0])]
        else:
            units += [(w, o, first) for first in range(0, o.shape[-1], UNIT)]

    def cut(unit, quarter):
        w, o, first = units[unit]
        return w.at[:, at(quarter * o.shape[-1] + first, UNIT)]

    def slot(unit):
        _, o, first = units[unit]
        mine = pl.ds(pl.multiple_of(here.core * rows, rows), rows)
        return o.at[here.high, here.near, here.side, mine, pl.ds(first, UNIT)]

    def keep(unit):
        return pltpu.make_async_copy(cut(unit, here.quarter), slot(unit), own_sem.at[2 + unit])

    def reshard(unit, peer):
        target, quarter = here.peers[peer]
        return remote(cut(unit, quarter), slot(unit), reshard_s.at[unit, peer], reshard_r.at[unit, peer], dp=target)

    def high_hop(unit, phase):
        _, o, first = units[unit]
        span = 1 << phase
        block = o.at[pl.ds(lax.div(here.high, span) * span, span), :, here.side, :, pl.ds(first, UNIT)]
        return remote(block, block, high_s.at[unit, phase], high_r.at[unit, phase], dp=flip(me, HIGH << phase))

    def side_hop(unit):
        _, o, first = units[unit]
        block = o.at[:, :, here.side, :, pl.ds(first, UNIT)]
        return remote(block, block, side_s.at[unit], side_r.at[unit], dp=flip(me, SIDE))

    def fetch(step, buf):
        target = lax.rem(me + step, n_dp)
        return pltpu.make_async_copy(
            hist.at[:, :, at(target * 2 * half + tensor * half, half)], hist_in.at[buf], hist_sem.at[buf]
        )

    def send(step):
        target = lax.rem(me + step, n_dp)
        return remote(
            mixed.at[step], streams.at[:, at(me * rows, rows), :], a2a_s.at[step], a2a_r.at[step], dp=target
        )

    fetch(0, 0).start()

    def mix_step(step):
        buf = lax.rem(step, 2)

        @pl.when(step + 1 < n_dp)
        def _():
            fetch(step + 1, 1 - buf).start()

        fetch(step, buf).wait()
        target = lax.rem(me + step, n_dp)
        weight = mix_all[lax.div(target, HIGH), bit(target, NEAR), bit(target, SIDE), bit(target, CORE)]
        for row in range(0, rows, 32):
            part = pl.ds(row, 32)
            sources = [hist_in[buf, source, part, :].astype(F32) for source in range(HIST)]
            for stream in range(STREAMS):
                total = sum(
                    sources[source] * weight[stream * HIST + source][None, :] for source in range(HIST)
                )
                mixed[step, stream, part, :] = total.astype(BF16)

        @pl.when(step > 0)
        def _():
            send(step).start()

    chunk = min(256, depth)

    def lanes(near, core, half_at, count):
        return at(near * 4 * half + core * 2 * half + half_at * half, count * half, half)

    def act_keep(stream):
        return pltpu.make_async_copy(
            act.at[stream], o_act.at[stream, :, lanes(here.near, here.core, tensor, 1)], act_local.at[stream]
        )

    def act_near(stream):
        return remote(
            act.at[stream], o_act.at[stream, :, lanes(here.near, here.core, tensor, 1)],
            act_s.at[0, stream], act_r.at[0, stream], dp=flip(me, NEAR),
        )

    def act_tensor(stream, second):
        span = lanes(1 - here.near if second else here.near, here.core, tensor, 1)
        return remote(
            o_act.at[stream, :, span] if second else act.at[stream], o_act.at[stream, :, span],
            act_s.at[1 + second, stream], act_r.at[1 + second, stream], tensor=here.other,
        )

    def act_core(stream, near):
        span = lanes(near, here.core, 0, 2)
        return remote(
            o_act.at[stream, :, span], o_act.at[stream, :, span],
            act_s.at[3 + near, stream], act_r.at[3 + near, stream], dp=flip(me, CORE),
        )

    def normalise_stream(stream):
        block = 0 if stream < 3 else 1

        def piece(index):
            return streams[stream, at(index * chunk, chunk), :].astype(F32)

        centre = sum_rows(piece, depth, chunk, lambda v: v) / depth
        spread = sum_rows(piece, depth, chunk, lambda v: (v - centre) * (v - centre)) / depth
        root = lax.rsqrt(spread + NORM_EPS)

        def normalise(index):
            span = chunk // rows
            first = index * span
            column = jnp.concatenate(
                [
                    small_all[
                        lax.div(first + k, HIGH), bit(first + k, NEAR), bit(first + k, SIDE), bit(first + k, CORE)
                    ]
                    for k in range(span)
                ],
                axis=0,
            ).astype(F32)
            gain = column[:, MIXH + block : MIXH + block + 1]
            bias = column[:, MIXH + 2 + block : MIXH + 3 + block]
            act[stream, at(index * chunk, chunk), :] = (
                (piece(index) - centre) * root * gain + bias
            ).astype(BF16)

        loop(0, depth // chunk, normalise)
        act_keep(stream).start()

    finals = [
        pltpu.make_async_copy(small_all, o_small, out_sem.at[1]),
        pltpu.make_async_copy(streams, o_streams, out_sem.at[2]),
    ]
    early_pairs = ((0, mix_all), (1, small_all))
    last = high_bits + 2

    def first(array):
        keep(array).start()
        for peer in range(3):
            reshard(array, peer).start()

    def second(array):
        keep(array).wait()
        for peer in range(3):
            reshard(array, peer).wait()
        high_hop(array, 0).start()

    def third(array):
        for phase in range(high_bits):
            high_hop(array, phase).wait()
            if phase + 1 < high_bits:
                high_hop(array, phase + 1).start()
        side_hop(array).start()

    def act_first(stream):
        act_near(stream).wait()
        act_tensor(stream, 1).start()
        if stream + 1 < STREAMS:
            act_near(stream + 1).start()
        if stream and stream + 1 < STREAMS:
            act_tensor(stream + 1, 0).start()

    def act_second(stream):
        act_keep(stream).wait()
        act_tensor(stream, 0).wait()
        act_tensor(stream, 1).wait()
        for near in range(2):
            act_core(stream, near).start()

    own_mix.start()
    small_all[here.high, here.near, here.side, here.core] = small[...].T
    own_mix.wait()
    for which, buf in early_pairs:
        early(which, buf, 0).start()
    total = len(units)

    def tick(unit):
        third(unit)
        if unit + 3 < total:
            first(unit + 3)
        if unit + 1 < total:
            second(unit + 1)

    for unit in range(min(3, total)):
        first(unit)
    for phase in range(1, last + 1):
        for which, buf in early_pairs:
            early(which, buf, phase - 1).wait()
            early(which, buf, phase).start()
        if phase == 1:
            second(0)
    early(0, mix_all, last).wait()
    def mix_lanes(index):
        return mix_all.at[lax.div(index, HIGH), bit(index, NEAR), bit(index, SIDE), bit(index, CORE)], o_mix.at[
            :, at(index * 2 * half + tensor * half, half)
        ]

    def mix_copy(index):
        source, target = mix_lanes(index)
        return pltpu.make_async_copy(source, target, share_l.at[index])

    def mix_share(index):
        source, target = mix_lanes(index)
        return remote(source, target, share_s.at[index], share_r.at[index], tensor=here.other)

    def mix_out(index):
        mix_copy(index).start()
        mix_share(index).start()

    loop(0, n_dp, mix_out)
    loop(0, n_dp, mix_step)
    streams[:, at(me * rows, rows), :] = mixed[0]
    early(1, small_all, last).wait()
    done = 0

    def ticks(count):
        nonlocal done
        for unit in range(done, min(done + count, total)):
            tick(unit)
        done = min(done + count, total)

    ticks(3)
    loop(1, n_dp, lambda step: send(step).wait())
    for stream in range(STREAMS):
        normalise_stream(stream)
        if stream == 0:
            act_near(0).start()
        if stream < 2:
            act_tensor(stream, 0).start()
    for copy in finals:
        copy.start()
    depth, tokens = act_in.shape[1:]
    seq_len = 2 * half
    heads = context.shape[0] // HD
    tile = 256

    def act_load(stream):
        return pltpu.make_async_copy(o_act.at[stream], act_in.at[stream], load_sem.at[stream])

    def act_third(stream):
        for near in range(2):
            act_core(stream, near).wait()
        act_load(stream).start()

    loads = {
        "qkv": pltpu.make_async_copy(o_qkv.reshape(3, depth, qkv_in.shape[2]), qkv_in, load_sem.at[4]),
        "out": pltpu.make_async_copy(o_out.reshape(depth, out_in.shape[1]), out_in, load_sem.at[5]),
        "up": pltpu.make_async_copy(o_up.reshape(depth, up_in.shape[1]), up_in, load_sem.at[6]),
        "down": pltpu.make_async_copy(o_down.reshape(depth, down_in.shape[1]), down_in, load_sem.at[7]),
    }
    held = 0

    def arrive(count):
        nonlocal held
        ticks(max(held + count - done, 0))
        for unit in range(held, held + count):
            side_hop(unit).wait()
        held += count

    def project(stream):
        act_load(stream).wait()
        values = tn(qkv_in[stream], act_in[stream])
        if stream < 2:
            values = turned(values, cos[...], sin[...])
        rows_out[stream] = values.astype(BF16)

    def attend(seq):
        span = at(seq * seq_len, seq_len)
        for head in range(heads):
            lane = pl.ds(head * HD, HD)
            scores = causal_scores(rows_out[1, lane, span], rows_out[0, lane, span])
            peak = jnp.max(scores, axis=0, keepdims=True)
            raised = jnp.exp(scores - peak)
            total_weight = jnp.sum(raised, axis=0, keepdims=True)
            prob = (raised / total_weight).astype(BF16)
            context[lane, span] = nn(rows_out[2, lane, span], prob).astype(BF16)
            sums[pl.ds(seq * heads + head, 1), :] = peak + jnp.log(total_weight)

    def raise_up(index):
        span = at(index * tile, tile)
        value, derivative = gelu_parts(tn(up_in[:, span], act_in[3]))
        hidden[span, :] = value.astype(BF16)
        slope[span, :] = derivative

    def lower(index):
        span = at(index * tile, tile)
        part[span, :] = (nn(out_in[span, :], context[...]) + nn(down_in[span, :], hidden[...])).astype(BF16)

    saves = []

    def save(*pairs):
        for source, target in pairs:
            copy = pltpu.make_async_copy(source, target, save_sem.at[len(saves)])
            copy.start()
            saves.append(copy)

    def rows_arrive(_):
        arrive(4)
        loads["qkv"].start()
        loads["out"].start()
        loads["qkv"].wait()

    def attend_all(_):
        loop(0, tokens // seq_len, attend)
        save((rows_out, o_rows), (context, o_context), (sums, o_sums))

    def raise_all(_):
        arrive(up_in.shape[1] // UNIT)
        loads["up"].start()
        act_load(3).wait()
        loads["up"].wait()
        loop(0, hidden.shape[0] // tile, raise_up)
        save((hidden, o_hidden), (slope, o_slope))

    actions = {
        "n": act_first, "s": act_second, "t": act_third, "w": rows_arrive, "p": project, "a": attend_all, "u": raise_all
    }
    for action in PLAN:
        if action == "T":
            ticks(1)
        else:
            actions[action[0]](int(action[1]))
    arrive(total - held)
    loads["down"].start()
    loads["out"].wait()
    loads["down"].wait()
    loop(0, depth // tile, lower)
    save((part, o_part))
    for copy in finals + saves:
        copy.wait()

    def settle(index):
        mix_copy(index).wait()
        mix_share(index).wait()

    loop(0, n_dp, settle)


def gather(n_dp, hist, mix, small, w_qkv, w_out, w_up, w_down, cos, sin):
    rows = small.shape[1]
    depth = rows * n_dp
    half = hist.shape[2] // n_dp // 2
    high = n_dp // HIGH
    high_bits = int(math.log2(high))
    grid = (high, 2, 2, 2)
    units = sum(w.size // w.shape[-2] for w in (w_qkv, w_out, w_up, w_down)) // QUARTERS // UNIT

    def cut(width):
        return (high, 2, 2, 2 * rows, width // QUARTERS)

    tokens = 8 * half
    narrow, width = w_qkv.shape[2] // QUARTERS, w_up.shape[1] // QUARTERS
    results = [
        ((3, narrow, tokens), BF16),
        ((narrow, tokens), BF16),
        ((tokens // (2 * half) * (narrow // HD), 2 * half), F32),
        ((width, tokens), BF16),
        ((width, tokens), F32),
        ((depth, tokens), BF16),
    ]
    shapes = [
        ((mix.shape[0], n_dp * 2 * half), F32),
        (grid + (rows, 128), BF16),
        ((STREAMS, depth, half), BF16),
        ((STREAMS, depth, tokens), BF16),
        ((3,) + cut(w_qkv.shape[2]), BF16),
        (cut(w_out.shape[1]), BF16),
        (cut(w_up.shape[1]), BF16),
        (cut(w_down.shape[1]), BF16),
    ] + results
    return pl.pallas_call(
        functools.partial(gather_kernel, n_dp),
        out_shape=[jax.ShapeDtypeStruct(*shape) for shape in shapes],
        in_specs=[ANY, ANY, VM] + [ANY] * 4 + [VM] * 2,
        out_specs=[ANY] * 14,
        scratch_shapes=[
            pltpu.VMEM(grid + mix.shape, F32),
            pltpu.VMEM(grid + (rows, 128), BF16),
            pltpu.VMEM((2, HIST, rows, half), BF16),
            pltpu.VMEM((n_dp, STREAMS, rows, half), BF16),
            pltpu.VMEM((STREAMS, depth, half), BF16),
            pltpu.VMEM((STREAMS, depth, half), BF16),
            DMA((2, high_bits + 3)),
            DMA((2, high_bits + 3)),
            DMA((2,)),
            DMA((n_dp,)),
            DMA((n_dp,)),
            DMA((units, 3)),
            DMA((units, 3)),
            DMA((units, high_bits)),
            DMA((units, high_bits)),
            DMA((units,)),
            DMA((units,)),
            DMA((5, STREAMS)),
            DMA((5, STREAMS)),
            DMA((STREAMS,)),
            DMA((2 + units,)),
            DMA((3,)),
            DMA((n_dp,)),
            DMA((n_dp,)),
            DMA((n_dp,)),
            pltpu.VMEM((STREAMS, depth, tokens), BF16),
            pltpu.VMEM((3, depth, narrow), BF16),
            pltpu.VMEM((depth, narrow), BF16),
            pltpu.VMEM((depth, width), BF16),
            pltpu.VMEM((depth, width), BF16),
        ]
        + [pltpu.VMEM(*shape) for shape in results]
        + [DMA((8,)), DMA((6,))],
        compiler_params=pltpu.CompilerParams(
            collective_id=1, has_side_effects=True, vmem_limit_bytes=61 * 1024 * 1024
        ),
        name="gather",
    )(hist, mix, small, w_qkv, w_out, w_up, w_down, cos, sin)


def lane_block(half, near, core, half_at, count):
    return at(near * 4 * half + core * 2 * half + half_at * half, count * half, half)


def gelu_parts(values):
    phi = 0.5 * (1.0 + lax.erf(values * (1.0 / math.sqrt(2.0))))
    density = jnp.exp(-0.5 * values * values) * (1.0 / math.sqrt(2.0 * math.pi))
    return values * phi, phi + values * density


def reduce_group(here, half, part, theirs, own, from_core, from_tensor, from_near, sems, local, pieces, piece):
    core_s, core_r, tensor_s, tensor_r, near_s, near_r = sems

    def load(span, near, half_at):
        return pltpu.make_async_copy(
            part.at[piece(span), lane_block(half, near, here.core, half_at, 1)],
            own.at[near, half_at, piece(span)], local.at[span, near * 2 + half_at],
        )

    def to_core(span, near, half_at):
        return remote(
            part.at[piece(span), lane_block(half, near, 1 - here.core, half_at, 1)],
            from_core.at[near, half_at, piece(span)],
            core_s.at[span, near * 2 + half_at], core_r.at[span, near * 2 + half_at], dp=flip(here.me, CORE),
        )

    def to_tensor(span, near):
        return remote(
            own.at[near, here.other, piece(span)], from_tensor.at[near, piece(span)],
            tensor_s.at[span, near], tensor_r.at[span, near], tensor=here.other,
        )

    def to_near(span):
        return remote(
            from_tensor.at[1 - here.near, piece(span)], from_near.at[piece(span)],
            near_s.at[span], near_r.at[span], dp=flip(here.me, NEAR),
        )

    def start(span):
        for near in range(2):
            for half_at in range(2):
                to_core(span, near, half_at).start()
                load(span, near, half_at).start()

    def after_core(span):
        for near in range(2):
            for half_at in range(2):
                load(span, near, half_at).wait()
                to_core(span, near, half_at).wait()
            own[near, here.other, piece(span)] += from_core[near, here.other, piece(span)]
            to_tensor(span, near).start()
        for near in range(2):
            own[near, here.tensor, piece(span)] += from_core[near, here.tensor, piece(span)]

    def after_tensor(span):
        for near in range(2):
            to_tensor(span, near).wait()
        far = 1 - here.near
        from_tensor[far, piece(span)] += own[far, here.tensor, piece(span)]
        to_near(span).start()
        from_tensor[here.near, piece(span)] += own[here.near, here.tensor, piece(span)]

    def after_near(span):
        to_near(span).wait()

    return start, after_core, after_tensor, after_near


def join_kernel(
    part, streams, cot, small, mix_in, mix_out, mix_back, static, next_cot,
    o_grad, o_wide, o_block, o_next, o_mixin, o_tiny,
    own, from_core, from_tensor, from_near, residual, wide, normed, block, back, low, next_rows, mixin, tiny,
    core_s, core_r, tensor_s, tensor_r, near_s, near_r, local, share_s, share_r, own_sem,
):
    here = Place()
    me, tensor = here.me, here.tensor
    depth, half = cot.shape
    spans = core_s.shape[0]
    size = depth // spans
    chunk = 256
    greet([{"dp": flip(me, CORE)}, {"dp": flip(me, NEAR)}, {"tensor": here.other}])

    def piece(span):
        return pl.ds(span * size, size)

    start, after_core, after_tensor, after_near = reduce_group(
        here, half, part, None, own, from_core, from_tensor, from_near,
        (core_s, core_r, tensor_s, tensor_r, near_s, near_r), local, spans, piece,
    )
    fetch = pltpu.make_async_copy(streams.at[3], residual, own_sem.at[0])
    fetch.start()
    for span in range(spans):
        start(span)
    for span in range(spans):
        after_core(span)
    for span in range(spans):
        after_tensor(span)
    fetch.wait()
    squares = jnp.zeros((1, half), F32)
    for span in range(spans):
        after_near(span)

        def widen(index, total):
            rows = at(span * size + index * chunk, chunk)
            branch = from_tensor[here.near, rows, :].astype(F32) + from_near[rows, :].astype(F32)
            value = residual[rows, :].astype(F32) + branch
            wide[rows, :] = value
            block[rows, :] = value.astype(BF16)
            return total + jnp.sum(value * value, axis=0, keepdims=True)

        squares = lax.fori_loop(0, size // chunk, widen, squares)
    root = lax.rsqrt(squares / depth + ROOT_EPS)

    def share_block(which):
        lanes = at(tensor * half, half)
        if which == 0:
            return pltpu.make_async_copy(block, o_block.at[:, lanes], own_sem.at[1])
        return remote(block, o_block.at[:, lanes], share_s.at[0], share_r.at[0], tensor=here.other)

    share_block(0).start()
    share_block(1).start()

    def norm(index):
        rows = at(index * chunk, chunk)
        normed[rows, :] = (wide[rows, :] * root).astype(BF16)

    loop(0, depth // chunk, norm)
    inner, slope = gelu_parts(jnp.dot(mix_in[...], normed[...], preferred_element_type=F32))
    inner_low = inner.astype(BF16)
    next_rows[...] = (jnp.dot(mix_out[...], inner_low, preferred_element_type=F32) + static[...])[:MIXH]
    next_low = next_cot[...].astype(BF16)

    def nt(left, right):
        return lax.dot_general(left, right, (((1,), (1,)), ((), ())), preferred_element_type=F32)

    tiny[:, :128] = nt(inner_low, next_low)
    tiny[:, 128:] = jnp.broadcast_to(jnp.sum(next_cot[...], axis=1, keepdims=True), (128, 128))
    inner_grad = (jnp.dot(mix_back[...], next_low, preferred_element_type=F32) * slope).astype(BF16)

    def pull(index, total):
        rows = at(index * chunk, chunk)
        value = jnp.dot(small[rows, :], inner_grad, preferred_element_type=F32)
        back[rows, :] = value
        return total + jnp.sum(value * wide[rows, :] * root, axis=0, keepdims=True)

    along = lax.fori_loop(0, depth // chunk, pull, jnp.zeros((1, half), F32)) / depth

    def finish(index):
        rows = at(index * chunk, chunk)
        value = cot[rows, :].astype(F32) + root * (back[rows, :] - wide[rows, :] * root * along)
        back[rows, :] = value
        low[rows, :] = value.astype(BF16)

    loop(0, depth // chunk, finish)

    def share(kind, index):
        if kind == 0:
            source, lanes, where = low, lane_block(half, here.near, here.core, tensor, 1), {"dp": flip(me, NEAR)}
        elif kind == 1:
            lanes = lane_block(half, 1 - here.near if index else here.near, here.core, tensor, 1)
            source, where = (o_grad.at[:, lanes] if index else low), {"tensor": here.other}
        else:
            lanes, where = lane_block(half, index, here.core, 0, 2), {"dp": flip(me, CORE)}
            source = o_grad.at[:, lanes]
        number = 1 + 2 * kind + index
        return remote(source, o_grad.at[:, lanes], share_s.at[number], share_r.at[number], **where)

    share(0, 0).start()
    share(1, 0).start()
    keep = pltpu.make_async_copy(
        low, o_grad.at[:, lane_block(half, here.near, here.core, tensor, 1)], own_sem.at[2]
    )
    keep.start()

    def mixin_rows(index):
        rows = at(index * chunk, chunk)
        mixin[rows, :] = nt(normed[rows, :], inner_grad)

    loop(0, depth // chunk, mixin_rows)
    share(0, 0).wait()
    share(1, 1).start()
    lanes = at(tensor * half, half)
    next_share = remote(next_rows, o_next.at[:, lanes], share_s.at[7], share_r.at[7], tensor=here.other)
    next_share.start()
    finals = [
        pltpu.make_async_copy(next_rows, o_next.at[:, lanes], own_sem.at[3]),
        pltpu.make_async_copy(back, o_wide, own_sem.at[4]),
        pltpu.make_async_copy(mixin, o_mixin, own_sem.at[5]),
        pltpu.make_async_copy(tiny, o_tiny, own_sem.at[6]),
    ]
    for copy in finals:
        copy.start()
    keep.wait()
    share(1, 0).wait()
    share(1, 1).wait()
    for near in range(2):
        share(2, near).start()
    for near in range(2):
        share(2, near).wait()
    share_block(0).wait()
    share_block(1).wait()
    next_share.wait()
    for copy in finals:
        copy.wait()


def join(part, streams, cot, small, mix_in, mix_out, mix_back, static, next_cot):
    depth, half = cot.shape
    spans = 4
    shapes = [
        ((depth, 8 * half), BF16),
        ((depth, half), F32),
        ((depth, 2 * half), BF16),
        ((MIXH, 2 * half), F32),
        ((depth, 128), F32),
        ((128, 256), F32),
    ]
    return pl.pallas_call(
        join_kernel,
        out_shape=[jax.ShapeDtypeStruct(*shape) for shape in shapes],
        in_specs=[ANY, ANY] + [VM] * 7,
        out_specs=[ANY] * 6,
        scratch_shapes=[
            pltpu.VMEM((2, 2, depth, half), BF16),
            pltpu.VMEM((2, 2, depth, half), BF16),
            pltpu.VMEM((2, depth, half), BF16),
            pltpu.VMEM((depth, half), BF16),
            pltpu.VMEM((depth, half), BF16),
            pltpu.VMEM((depth, half), F32),
            pltpu.VMEM((depth, half), BF16),
            pltpu.VMEM((depth, half), BF16),
            pltpu.VMEM((depth, half), F32),
            pltpu.VMEM((depth, half), BF16),
            pltpu.VMEM((MIXH, half), F32),
            pltpu.VMEM((depth, 128), F32),
            pltpu.VMEM((128, 256), F32),
            DMA((spans, 4)),
            DMA((spans, 4)),
            DMA((spans, 2)),
            DMA((spans, 2)),
            DMA((spans,)),
            DMA((spans,)),
            DMA((spans, 4)),
            DMA((8,)),
            DMA((8,)),
            DMA((7,)),
        ],
        compiler_params=pltpu.CompilerParams(
            collective_id=2, has_side_effects=True, vmem_limit_bytes=40 * 1024 * 1024
        ),
        name="join",
    )(part, streams, cot, small, mix_in, mix_out, mix_back, static, next_cot)


def scatter_kernel(
    n_dp, attn_grad, mlp_grad, streams, small, wide_grad, mixin_part, hist, g_qkv, g_up, g_down, g_out,
    o_stream, o_mix, o_small, o_qkv, o_up, o_down, o_out,
    own, from_core, from_tensor, from_near, rows_in, wide, stream_grad, gains, biases, tiny, tiny_in, tiny_out,
    hist_in, arrived, mix_part, mix_in, mix_sum, tiny_sum,
    side_qkv, side_up, side_down, side_out, mine_qkv, mine_up, mine_down, mine_out,
    high_qkv, high_up, high_down, high_out,
    core_s, core_r, tensor_s, tensor_r, near_s, near_r, local, in_sem,
    side_s, side_r, side_local, high_s, high_r, peer_s, peer_r, peer_local,
    a2a_s, a2a_r, keep_sem, pass_s, pass_r, tiny_s, tiny_r, mix_s, mix_r, hist_sem, last_s, last_r, last_local,
):
    here = Place()
    me, tensor = here.me, here.tensor
    depth, half = wide_grad.shape
    rows = depth // n_dp
    high_bits = int(math.log2(n_dp // HIGH))
    chunk = min(256, depth)
    greet_all(n_dp, me, here.other)
    weights = (
        (g_qkv, side_qkv, mine_qkv, high_qkv, o_qkv),
        (g_up, side_up, mine_up, high_up, o_up),
        (g_down, side_down, mine_down, high_down, o_down),
        (g_out, side_out, mine_out, high_out, o_out),
    )

    def pick(ref, *index):
        return ref.at[(slice(None),) + index] if ref.shape[0] == 3 and len(ref.shape) > len(index) + 2 else ref.at[index]

    def everything(_):
        return pl.ds(0, depth)

    steps = []
    for stream in range(STREAMS):
        part = attn_grad.at[stream] if stream < 3 else mlp_grad
        steps.append(
            reduce_group(
                here, half, part, None, own.at[stream], from_core.at[stream], from_tensor.at[stream],
                from_near.at[stream],
                tuple(
                    sem.at[pl.ds(stream, 1)]
                    for sem in (core_s, core_r, tensor_s, tensor_r, near_s, near_r)
                ),
                local.at[pl.ds(stream, 1)], 1, everything,
            )
        )
    for stream in range(STREAMS):
        steps[stream][0](0)
    loads = [
        pltpu.make_async_copy(streams, rows_in, in_sem.at[0]),
        pltpu.make_async_copy(wide_grad, wide, in_sem.at[1]),
    ]
    for copy in loads:
        copy.start()

    def is_qkv(array):
        return array == 0

    def index_of(array, *index):
        return ((slice(None),) if is_qkv(array) else ()) + index

    def side_hop(array):
        g, side, _, _, _ = weights[array]
        return remote(
            g.at[index_of(array, slice(None), slice(None), 1 - here.side)], side, side_s.at[array], side_r.at[array],
            dp=flip(me, SIDE),
        )

    def side_load(array):
        g, _, mine, _, _ = weights[array]
        return pltpu.make_async_copy(
            g.at[index_of(array, slice(None), slice(None), here.side)], mine, side_local.at[array]
        )

    def high_hop(array, phase):
        _, _, mine, high, _ = weights[array]
        span = 1 << phase
        base = lax.div(here.high, span)
        theirs = base + 1 - 2 * lax.rem(base, 2)
        return remote(
            mine.at[index_of(array, pl.ds(theirs * span, span))], high.at[index_of(array, pl.ds(span - 1, span))],
            high_s.at[array, phase], high_r.at[array, phase], dp=flip(me, HIGH << phase),
        )

    def add_blocks(array, into, other, first_into, first_other, count):
        shape = into.shape
        tall, width = shape[-2:]
        outer = 3 if is_qkv(array) else 1
        step = 32

        def add(flat):
            lead = lax.div(flat, count * 2)
            rest = lax.rem(flat, count * 2)
            high, near = lax.div(rest, 2), lax.rem(rest, 2)
            prefix = (lead,) if is_qkv(array) else ()

            def tile(index):
                span = at(index * step, step)
                into[prefix + (first_into + high, near, span)] += other[prefix + (first_other + high, near, span)]

            loop(0, tall // step, tile)

        loop(0, outer * count * 2, add)

    for array in range(4):
        side_hop(array).start()
        side_load(array).start()
    for copy in loads:
        copy.wait()
    stats = []
    for stream in range(STREAMS):

        def piece(index):
            return rows_in[stream, at(index * chunk, chunk), :].astype(F32)

        centre = sum_rows(piece, depth, chunk, lambda v: v) / depth
        spread = sum_rows(piece, depth, chunk, lambda v: (v - centre) * (v - centre)) / depth
        stats.append((centre, lax.rsqrt(spread + NORM_EPS)))
    for stream in range(STREAMS):
        steps[stream][1](0)
    for array in range(4):
        side_load(array).wait()
        side_hop(array).wait()
        _, side, mine, _, _ = weights[array]
        add_blocks(array, mine, side, 0, 0, n_dp // HIGH)
        high_hop(array, high_bits - 1).start()
    for stream in range(STREAMS):
        steps[stream][2](0)

    for stream in range(STREAMS):
        steps[stream][3](0)
        group = 0 if stream < 3 else 1
        centre, root = stats[stream]

        def parts(index):
            span = at(index * chunk, chunk)
            grad = from_tensor[stream, here.near, span].astype(F32) + from_near[stream, span].astype(F32)
            hat = (rows_in[stream, span, :].astype(F32) - centre) * root
            gain = small[span, MIXH + group : MIXH + group + 1].astype(F32)
            return span, grad, hat, grad * gain

        def sums(index, carry):
            span, grad, hat, scaled = parts(index)
            if stream in (0, 3):
                gains[group, span] = grad * hat
                biases[group, span] = grad
            else:
                gains[group, span] += grad * hat
                biases[group, span] += grad
            return (
                carry[0] + jnp.sum(scaled, axis=0, keepdims=True),
                carry[1] + jnp.sum(scaled * hat, axis=0, keepdims=True),
            )

        zero = jnp.zeros((1, half), F32)
        total, along = lax.fori_loop(0, depth // chunk, sums, (zero, zero))

        def finish(index):
            span, grad, hat, scaled = parts(index)
            value = root * (scaled - total / depth - hat * (along / depth))
            if stream == 3:
                value = value + wide[span, :]
            stream_grad[stream, span] = value.astype(BF16)

        loop(0, depth // chunk, finish)

    def send(step):
        target = lax.rem(me + step, n_dp)
        return remote(
            stream_grad.at[:, at(target * rows, rows), :], arrived.at[step], a2a_s.at[step], a2a_r.at[step], dp=target
        )

    loop(1, n_dp, lambda step: send(step).start())

    def fetch(step, buf):
        source = lax.rem(me - step + n_dp, n_dp)
        return pltpu.make_async_copy(
            hist.at[:, :, at(source * 2 * half + tensor * half, half)], hist_in.at[buf], hist_sem.at[buf]
        )

    fetch(0, 0).start()
    own_block = pltpu.make_async_copy(stream_grad.at[:, at(me * rows, rows), :], arrived.at[0], last_local.at[0])
    own_block.start()

    column = lax.broadcasted_iota(jnp.int32, (chunk, 128), 1)

    def gather_tiny(index):
        span = at(index * chunk, chunk)
        value = mixin_part[span, :]
        for group in range(2):
            gain = jnp.sum(gains[group, span], axis=1, keepdims=True)
            bias = jnp.sum(biases[group, span], axis=1, keepdims=True)
            value = jnp.where(column == MIXH + group, gain, value)
            value = jnp.where(column == MIXH + 2 + group, bias, value)
        tiny[span, :] = value.astype(BF16)

    loop(0, depth // chunk, gather_tiny)

    def tiny_send(step):
        target = lax.rem(me + step, n_dp)
        return remote(tiny.at[at(target * rows, rows), :], tiny_in.at[step], tiny_s.at[step], tiny_r.at[step], dp=target)

    loop(1, n_dp, lambda step: tiny_send(step).start())

    for array in range(4):
        _, _, mine, high, _ = weights[array]
        for phase in reversed(range(high_bits)):
            high_hop(array, phase).wait()
            span = 1 << phase
            add_blocks(array, mine, high, lax.div(here.high, span) * span, span - 1, span)
            if phase:
                high_hop(array, phase - 1).start()

    def peer_hop(array, peer):
        _, _, mine, _, out = weights[array]
        width = mine.shape[-1]
        target, _ = here.peers[peer]
        core = bit(target, CORE)
        return remote(
            mine.at[index_of(array, here.high, bit(target, NEAR), at(core * rows, rows))],
            out.at[index_of(array, slice(None), at(here.quarter * width, width))],
            peer_s.at[array, peer], peer_r.at[array, peer], dp=target,
        )

    def peer_keep(array):
        _, _, mine, _, out = weights[array]
        width = mine.shape[-1]
        return pltpu.make_async_copy(
            mine.at[index_of(array, here.high, here.near, at(here.core * rows, rows))],
            out.at[index_of(array, slice(None), at(here.quarter * width, width))], peer_local.at[array],
        )

    for array in range(4):
        peer_keep(array).start()
        for peer in range(3):
            peer_hop(array, peer).start()
    own_block.wait()

    def keep_lanes(step):
        source = lax.rem(me - step + n_dp, n_dp)
        return at(source * 2 * half + tensor * half, half)

    def keep(step):
        return pltpu.make_async_copy(arrived.at[step], o_stream.at[:, :, keep_lanes(step)], keep_sem.at[step])

    def pass_on(step):
        return remote(
            arrived.at[step], o_stream.at[:, :, keep_lanes(step)], pass_s.at[step], pass_r.at[step], tensor=here.other
        )

    def mix_send(step):
        return remote(
            mix_part.at[step], mix_in.at[step], mix_s.at[step], mix_r.at[step], dp=lax.rem(me - step + n_dp, n_dp)
        )

    def receive(step):
        buf = lax.rem(step, 2)

        @pl.when(step + 1 < n_dp)
        def _():
            fetch(step + 1, 1 - buf).start()

        @pl.when(step > 0)
        def _():
            send(step).wait()

        keep(step).start()
        pass_on(step).start()
        fetch(step, buf).wait()
        for stream in range(STREAMS):
            totals = [jnp.zeros((8, half), F32) for _ in range(HIST)]
            for row in range(0, rows, 16):
                span = pl.ds(row, 16)
                grad = arrived[step, stream, span, :].astype(F32)
                for source in range(HIST):
                    product = grad * hist_in[buf, source, span, :].astype(F32)
                    totals[source] = totals[source] + product[:8] + product[8:]
            for source in range(HIST):
                mix_part[step, pl.ds(stream * HIST + source, 1), :] = jnp.sum(totals[source], axis=0, keepdims=True)

        @pl.when(step > 0)
        def _():
            mix_send(step).start()

    mix_part[0] = jnp.zeros_like(mix_part[0])
    loop(0, n_dp, receive)

    mix_sum[...] = mix_part[0]

    def add_mix(step):
        mix_send(step).wait()
        mix_sum[...] += mix_in[step]

    loop(1, n_dp, add_mix)
    lanes = at(tensor * half, half)
    mix_share = remote(mix_sum, o_mix.at[:, lanes], last_s.at[0], last_r.at[0], tensor=here.other)
    mix_keep = pltpu.make_async_copy(mix_sum, o_mix.at[:, lanes], last_local.at[1])
    mix_share.start()
    mix_keep.start()
    tiny_sum[0] = tiny[at(me * rows, rows), :].astype(F32)

    def add_tiny(step):
        tiny_send(step).wait()
        tiny_sum[0] += tiny_in[step].astype(F32)

    loop(1, n_dp, add_tiny)
    tiny_share = remote(tiny_sum.at[0], tiny_sum.at[1], last_s.at[1], last_r.at[1], tensor=here.other)
    tiny_share.start()
    tiny_share.wait()
    tiny_out[...] = tiny_sum[0] + tiny_sum[1]
    tiny_keep = pltpu.make_async_copy(tiny_out, o_small, last_local.at[2])
    tiny_keep.start()
    for array in range(4):
        peer_keep(array).wait()
        for peer in range(3):
            peer_hop(array, peer).wait()

    def settle(step):
        keep(step).wait()
        pass_on(step).wait()

    loop(0, n_dp, settle)
    mix_share.wait()
    mix_keep.wait()
    tiny_keep.wait()


def scatter(n_dp, attn_grad, mlp_grad, streams, small, wide_grad, mixin_part, hist, g_qkv, g_up, g_down, g_out):
    depth, half = wide_grad.shape
    rows = depth // n_dp
    high = n_dp // HIGH
    high_bits = int(math.log2(high))
    grads = (g_qkv, g_up, g_down, g_out)

    def lead(g):
        return (3,) if g.ndim == 6 else ()

    def halved(g, highs):
        return lead(g) + (highs, 2) + g.shape[-2:]

    outs = [
        ((STREAMS, rows, 2 * half * n_dp), BF16),
        ((MIXH, 2 * half), F32),
        ((rows, 128), F32),
    ] + [(lead(g) + (rows, QUARTERS * g.shape[-1]), BF16) for g in grads]
    return pl.pallas_call(
        functools.partial(scatter_kernel, n_dp),
        out_shape=[jax.ShapeDtypeStruct(*shape) for shape in outs],
        in_specs=[ANY, ANY, ANY, VM, ANY, VM, ANY] + [ANY] * 4,
        out_specs=[ANY] * 7,
        scratch_shapes=[
            pltpu.VMEM((STREAMS, 2, 2, depth, half), BF16),
            pltpu.VMEM((STREAMS, 2, 2, depth, half), BF16),
            pltpu.VMEM((STREAMS, 2, depth, half), BF16),
            pltpu.VMEM((STREAMS, depth, half), BF16),
            pltpu.VMEM((STREAMS, depth, half), BF16),
            pltpu.VMEM((depth, half), F32),
            pltpu.VMEM((STREAMS, depth, half), BF16),
            pltpu.VMEM((2, depth, half), F32),
            pltpu.VMEM((2, depth, half), F32),
            pltpu.VMEM((depth, 128), BF16),
            pltpu.VMEM((n_dp, rows, 128), BF16),
            pltpu.VMEM((rows, 128), F32),
            pltpu.VMEM((2, HIST, rows, half), BF16),
            pltpu.VMEM((n_dp, STREAMS, rows, half), BF16),
            pltpu.VMEM((n_dp, MIXH, half), F32),
            pltpu.VMEM((n_dp, MIXH, half), F32),
            pltpu.VMEM((MIXH, half), F32),
            pltpu.VMEM((2, rows, 128), F32),
        ]
        + [pltpu.VMEM(halved(g, high), BF16) for g in grads]
        + [pltpu.VMEM(halved(g, high), BF16) for g in grads]
        + [pltpu.VMEM(halved(g, high - 1), BF16) for g in grads]
        + [
            DMA((STREAMS, 4)),
            DMA((STREAMS, 4)),
            DMA((STREAMS, 2)),
            DMA((STREAMS, 2)),
            DMA((STREAMS,)),
            DMA((STREAMS,)),
            DMA((STREAMS, 4)),
            DMA((2,)),
            DMA((4,)),
            DMA((4,)),
            DMA((4,)),
            DMA((4, high_bits)),
            DMA((4, high_bits)),
            DMA((4, 3)),
            DMA((4, 3)),
            DMA((4,)),
            DMA((n_dp,)),
            DMA((n_dp,)),
            DMA((n_dp,)),
            DMA((n_dp,)),
            DMA((n_dp,)),
            DMA((n_dp,)),
            DMA((n_dp,)),
            DMA((n_dp,)),
            DMA((n_dp,)),
            DMA((2,)),
            DMA((2,)),
            DMA((2,)),
            DMA((3,)),
        ],
        compiler_params=pltpu.CompilerParams(
            collective_id=3, has_side_effects=True, vmem_limit_bytes=60 * 1024 * 1024
        ),
        name="scatter",
    )(attn_grad, mlp_grad, streams, small, wide_grad, mixin_part, hist, *grads)


def exact_gelu(values):
    return jax.nn.gelu(values, approximate=False)


def rotary_tables(length, rotary, float_type):
    half_rot = rotary // 2
    places = jnp.arange(length).astype(float_type)
    frequency = jnp.exp(
        jnp.arange(half_rot).astype(float_type) * (-2.0 * math.log(10000.0) / rotary)
    )
    angles = places[:, None] * frequency[None, :]
    return (jnp.cos(angles), jnp.sin(angles))


def rotate(values, cos_table, sin_table):
    half_rot = cos_table.shape[-1]
    first_half = values[..., :half_rot]
    second = values[..., half_rot : 2 * half_rot]
    return jnp.concatenate(
        [
            first_half * cos_table - second * sin_table,
            second * cos_table + first_half * sin_table,
            values[..., 2 * half_rot :],
        ],
        axis=-1,
    )


def masked_scores(queries, key_rows):
    length = queries.shape[1]
    score_scale = 1.0 / math.sqrt(queries.shape[2])
    causal = lax.broadcasted_iota(jnp.int32, (length, length), 0) >= lax.broadcasted_iota(
        jnp.int32, (length, length), 1
    )
    scores = (
        jnp.einsum("hqd,hkd->hqk", queries, key_rows, preferred_element_type=jnp.float32)
        * score_scale
    )
    return (jnp.where(causal[None], scores, MASKED), score_scale)


def attend_forward(queries, key_rows, value_rows):
    scores, score_scale = masked_scores(queries, key_rows)
    row_peak = jnp.max(scores, axis=-1, keepdims=True)
    raised = jnp.exp(scores - row_peak)
    row_total = jnp.sum(raised, axis=-1, keepdims=True)
    prob_low = (raised / row_total).astype(jnp.bfloat16)
    context = jnp.einsum("hqk,hkd->hqd", prob_low, value_rows, preferred_element_type=jnp.float32)
    return (context.astype(jnp.bfloat16), row_peak + jnp.log(row_total))


def attend_backward(queries, key_rows, value_rows, log_sum, context_grad):
    scores, score_scale = masked_scores(queries, key_rows)
    attn_prob = jnp.exp(scores - log_sum)
    prob_low = attn_prob.astype(jnp.bfloat16)
    value_grad = jnp.einsum(
        "hqk,hqd->hkd", prob_low, context_grad, preferred_element_type=jnp.float32
    )
    prob_grad = jnp.einsum(
        "hqd,hkd->hqk", context_grad, value_rows, preferred_element_type=jnp.float32
    )
    inner_sum = jnp.sum(attn_prob * prob_grad, axis=-1, keepdims=True)
    score_grad = (attn_prob * (prob_grad - inner_sum)).astype(jnp.bfloat16)
    query_grad = (
        jnp.einsum("hqk,hkd->hqd", score_grad, key_rows, preferred_element_type=jnp.float32)
        * score_scale
    )
    key_grad = (
        jnp.einsum("hqk,hqd->hkd", score_grad, queries, preferred_element_type=jnp.float32)
        * score_scale
    )
    return (query_grad, key_grad, value_grad)


def per_device(
    n_dp, history, mix_weights, w_qkv, w_out, w_up, w_down, norm_gain, norm_bias, mix_in, mix_out, mix_static,
    out_cot, next_cot,
):
    tensor = lax.axis_index("tensor")
    seq_len = mix_weights.shape[0]
    half = seq_len // 2
    depth = mix_in.shape[0] * n_dp

    def own_half(rows):
        return lax.dynamic_slice_in_dim(rows, tensor * half, half, 0)

    mix_rows = jnp.pad(own_half(mix_weights.reshape(seq_len, -1)).T, ((0, MIXH - STREAMS * HIST), (0, 0)))
    small = jnp.concatenate([mix_in, norm_gain.T, norm_bias.T], axis=1)
    small = jnp.pad(small, ((0, 0), (0, 128 - small.shape[1])))
    mix_all, small_all, streams, act, qkv, up, down, out = gather(
        n_dp, history, mix_rows, small, w_qkv, w_up, w_down, w_out
    )
    small_all = small_all.reshape(depth, 128)
    qkv, up, down, out = (
        qkv.reshape(3, depth, -1), up.reshape(depth, -1), down.reshape(depth, -1), out.reshape(depth, -1)
    )
    tokens = act.shape[2]
    seqs = tokens // seq_len
    heads = qkv.shape[2] // HD
    projected = jnp.einsum("sdt,sde->ste", act[:3], qkv, preferred_element_type=F32)
    head_rows = jnp.transpose(projected.reshape(3, seqs, seq_len, heads, HD), (0, 1, 3, 2, 4)).reshape(
        3, seqs * heads, seq_len, HD
    )
    cos_table, sin_table = rotary_tables(seq_len, ROT, F32)
    queries = rotate(head_rows[0], cos_table, sin_table).astype(BF16)
    key_rows = rotate(head_rows[1], cos_table, sin_table).astype(BF16)
    value_rows = head_rows[2].astype(BF16)
    context, log_sum = attend_forward(queries, key_rows, value_rows)

    def join_heads(rows):
        return jnp.transpose(rows.reshape(seqs, heads, seq_len, HD), (0, 2, 1, 3)).reshape(tokens, heads * HD)

    context_rows = join_heads(context)
    up_pre = jnp.einsum("dt,df->tf", act[3], up, preferred_element_type=F32)
    hidden_wide, gelu_back = jax.vjp(exact_gelu, up_pre)
    hidden = hidden_wide.astype(BF16)
    part = (
        jnp.einsum("de,te->dt", out, context_rows, preferred_element_type=F32)
        + jnp.einsum("df,tf->dt", down, hidden, preferred_element_type=F32)
    ).astype(BF16)

    def square(values):
        return jnp.pad(values, ((0, 128 - values.shape[0]), (0, 128 - values.shape[1])))

    next_rows = own_half(next_cot.reshape(seq_len, -1)).T
    next_rows = jnp.pad(next_rows, ((0, 128 - next_rows.shape[0]), (0, 0)))
    mix_in_rows = jnp.pad(small_all[:, :MIXH].T, ((0, 128 - MIXH), (0, 0)))
    static = jnp.pad(mix_static[:, None], ((0, 128 - mix_static.shape[0]), (0, 0)))
    branch_grad, wide_grad, block, next_mix, mixin_part, tiny = join(
        part, streams, own_half(out_cot).T, small_all, mix_in_rows, square(mix_out.T), square(mix_out), static,
        next_rows,
    )
    mixout_total, static_total = lax.psum(
        (tiny[:MIXH, : STREAMS * NEXT], tiny[: STREAMS * NEXT, 128]), ("dp", "tensor")
    )
    hidden_grad = jnp.einsum("dt,df->tf", branch_grad, down, preferred_element_type=F32)
    up_grad_low = gelu_back(hidden_grad)[0].astype(BF16)
    mlp_in_grad = jnp.einsum("df,tf->dt", up, up_grad_low, preferred_element_type=F32).astype(BF16)
    context_grad_rows = jnp.einsum("dt,de->te", branch_grad, out, preferred_element_type=F32).astype(BF16)
    context_grad = jnp.transpose(context_grad_rows.reshape(seqs, seq_len, heads, HD), (0, 2, 1, 3)).reshape(
        seqs * heads, seq_len, HD
    )
    query_grad, key_grad, value_grad = attend_backward(queries, key_rows, value_rows, log_sum, context_grad)
    proj_grad = jnp.stack(
        [
            join_heads(rotate(query_grad, cos_table, -sin_table).astype(BF16)),
            join_heads(rotate(key_grad, cos_table, -sin_table).astype(BF16)),
            join_heads(value_grad.astype(BF16)),
        ]
    )
    attn_in_grad = jnp.einsum("sde,ste->sdt", qkv, proj_grad, preferred_element_type=F32).astype(BF16)
    g_qkv = jnp.einsum("sdt,ste->sde", act[:3], proj_grad, preferred_element_type=F32).astype(BF16)
    g_out = jnp.einsum("dt,te->de", branch_grad, context_rows, preferred_element_type=F32).astype(BF16)
    g_up = jnp.einsum("dt,tf->df", act[3], up_grad_low, preferred_element_type=F32).astype(BF16)
    g_down = jnp.einsum("dt,tf->df", branch_grad, hidden, preferred_element_type=F32).astype(BF16)
    grid = (n_dp // HIGH, 2, 2, 2 * mix_in.shape[0])
    stream_grad, mix_grad, small_total, qkv_total, up_total, down_total, out_total = scatter(
        n_dp, attn_in_grad, mlp_in_grad, streams, small_all, wide_grad, mixin_part, history,
        g_qkv.reshape((3,) + grid + (-1,)), g_up.reshape(grid + (-1,)), g_down.reshape(grid + (-1,)),
        g_out.reshape(grid + (-1,)),
    )
    mix_rows = mix_all.reshape(n_dp, MIXH, 1, half)
    mix_rows = lax.all_gather(mix_rows, "tensor", axis=2, tiled=True)
    mix_rows = jnp.transpose(mix_rows, (1, 0, 2, 3)).reshape(MIXH, n_dp * seq_len)
    history_grad = jnp.stack(
        [
            sum(
                mix_rows[stream * HIST + source][None, :] * stream_grad[stream].astype(F32)
                for stream in range(STREAMS)
            )
            for source in range(HIST)
        ]
    ).astype(BF16)
    return (
        block.T,
        next_mix.T.reshape(seq_len, STREAMS, NEXT),
        history_grad,
        mix_grad[: STREAMS * HIST].T.reshape(seq_len, STREAMS, HIST),
        qkv_total.astype(F32),
        out_total.astype(F32),
        up_total.astype(F32),
        down_total.astype(F32),
        small_total[:, MIXH : MIXH + 2].T,
        small_total[:, MIXH + 2 : MIXH + 4].T,
        small_total[:, :MIXH],
        mixout_total,
        static_total,
    )


def solution(mesh):
    return jax.shard_map(
        functools.partial(per_device, mesh.shape["dp"]),
        mesh=mesh,
        in_specs=(
            P(None, "dp", None),
            P("dp", None, None),
            P(None, "dp", "tensor"),
            P("dp", "tensor"),
            P("dp", "tensor"),
            P("dp", "tensor"),
            P(None, "dp"),
            P(None, "dp"),
            P("dp", None),
            P(),
            P(),
            P("dp", None),
            P("dp", None, None),
        ),
        out_specs=(
            P("dp", None),
            P("dp", None, None),
            P(None, "dp", None),
            P("dp", None, None),
            P(None, "dp", "tensor"),
            P("dp", "tensor"),
            P("dp", "tensor"),
            P("dp", "tensor"),
            P(None, "dp"),
            P(None, "dp"),
            P("dp", None),
            P(),
            P(),
        ),
        check_vma=False,
    )


def lane_block(half, near, core, half_at, count):
    return at(near * 4 * half + core * 2 * half + half_at * half, count * half, half)


def join_kernel(
    part, streams, out_cot, small, mix_raw, next_raw,
    o_grad, o_wide, o_block, o_next, o_mixin, o_tiny,
    mix_out, next_cot, own, from_core, from_first, from_second, residual, wide, normed, block, cot, cot_in, back, low, next_rows, mixin, tiny,
    core_s, core_r, first_s, first_r, second_s, second_r, local, share_s, share_r, own_sem,
):
    here = Place()
    me, tensor = here.me, here.tensor
    depth, half = cot.shape
    spans = core_s.shape[0]
    size = depth // spans
    chunk = 256
    greet([{"dp": flip(me, CORE)}, {"dp": flip(me, NEAR)}, {"tensor": here.other}])

    def piece(span):
        return pl.ds(span * size, size)

    def tensor_first(span):
        return span < spans // 2

    def load(span, near, half_at):
        return pltpu.make_async_copy(
            part.at[piece(span), lane_block(half, near, here.core, half_at, 1)],
            own.at[near, half_at, piece(span)], local.at[span, near * 2 + half_at],
        )

    def to_core(span, near, half_at):
        return remote(
            part.at[piece(span), lane_block(half, near, 1 - here.core, half_at, 1)],
            from_core.at[near, half_at, piece(span)],
            core_s.at[span, near * 2 + half_at], core_r.at[span, near * 2 + half_at], dp=flip(me, CORE),
        )

    across = {"tensor": here.other}
    beside = {"dp": flip(me, NEAR)}

    def first_hop(span, block):
        source = own.at[block, here.other, piece(span)] if tensor_first(span) else own.at[1 - here.near, block, piece(span)]
        return remote(
            source, from_first.at[block, piece(span)], first_s.at[span, block], first_r.at[span, block],
            **(across if tensor_first(span) else beside),
        )

    def kept(span):
        return here.near if tensor_first(span) else tensor

    def second_hop(span):
        return remote(
            from_first.at[1 - kept(span), piece(span)], from_second.at[piece(span)], second_s.at[span], second_r.at[span],
            **(beside if tensor_first(span) else across),
        )

    def start(span):
        for near in range(2):
            for half_at in range(2):
                to_core(span, near, half_at).start()
                load(span, near, half_at).start()

    def after_core(span):
        for near in range(2):
            for half_at in range(2):
                load(span, near, half_at).wait()
                to_core(span, near, half_at).wait()
                own[near, half_at, piece(span)] += from_core[near, half_at, piece(span)]
        for block in range(2):
            first_hop(span, block).start()

    def after_first(span):
        for block in range(2):
            first_hop(span, block).wait()

        def add(block):
            mine = own[block, tensor, piece(span)] if tensor_first(span) else own[here.near, block, piece(span)]
            from_first[block, piece(span)] += mine

        add(1 - kept(span))
        second_hop(span).start()
        add(kept(span))

    mix_out[...] = jnp.zeros_like(mix_out)
    next_cot[...] = jnp.zeros_like(next_cot)
    mix_out[:MIXH, : STREAMS * NEXT] = mix_raw[...]
    next_cot[: STREAMS * NEXT, :] = next_raw[...]
    fetch = pltpu.make_async_copy(streams.at[3], residual, own_sem.at[0])
    fetch.start()
    cot_fetch = pltpu.make_async_copy(out_cot.at[at(tensor * half, half), :], cot_in, own_sem.at[7])
    cot_fetch.start()
    order = [span for pair in zip(range(spans // 2), range(spans // 2, spans)) for span in pair]
    for span in order:
        start(span)
    for span in order:
        after_core(span)
    for span in order:
        after_first(span)
    fetch.wait()
    cot_fetch.wait()

    def turn(index):
        rows = at(index * chunk, chunk)
        cot[rows, :] = cot_in[:, rows].T

    loop(0, depth // chunk, turn)
    squares = jnp.zeros((1, half), F32)
    for span in order:
        second_hop(span).wait()

        def widen(index, total):
            rows = at(span * size + index * chunk, chunk)
            branch = from_first[kept(span), rows, :].astype(F32) + from_second[rows, :].astype(F32)
            value = residual[rows, :].astype(F32) + branch
            wide[rows, :] = value
            block[:, rows] = value.T.astype(BF16)
            return total + jnp.sum(value * value, axis=0, keepdims=True)

        squares = lax.fori_loop(0, size // chunk, widen, squares)
    root = lax.rsqrt(squares / depth + ROOT_EPS)

    def share_block(which):
        mine = o_block.at[at(tensor * half, half), :]
        if which == 0:
            return pltpu.make_async_copy(block, mine, own_sem.at[1])
        return remote(block, mine, share_s.at[0], share_r.at[0], tensor=here.other)

    share_block(0).start()
    share_block(1).start()

    def norm(index):
        rows = at(index * chunk, chunk)
        normed[rows, :] = (wide[rows, :] * root).astype(BF16)

    loop(0, depth // chunk, norm)
    inner, slope = gelu_parts(tn(small[...], normed[...]))
    inner_low = inner.astype(BF16)
    next_rows[...] = tn(mix_out[...], inner_low)[:MIXH]
    next_low = next_cot[...].astype(BF16)

    column = lax.broadcasted_iota(jnp.int32, (128, 128), 1)
    static_grad = jnp.sum(next_cot[...], axis=1, keepdims=True)
    tiny[...] = jnp.where(column == MIXH, static_grad, nt(inner_low, next_low))[:MIXH]
    inner_grad = (nn(mix_out[...], next_low) * slope).astype(BF16)

    def pull(index, total):
        rows = at(index * chunk, chunk)
        value = jnp.dot(small[rows, :], inner_grad, preferred_element_type=F32)
        back[rows, :] = value
        return total + jnp.sum(value * wide[rows, :] * root, axis=0, keepdims=True)

    along = lax.fori_loop(0, depth // chunk, pull, jnp.zeros((1, half), F32)) / depth

    def finish(index):
        rows = at(index * chunk, chunk)
        value = cot[rows, :].astype(F32) + root * (back[rows, :] - wide[rows, :] * root * along)
        back[rows, :] = value
        low[rows, :] = value.astype(BF16)

    loop(0, depth // chunk, finish)

    def share(part_at, kind, index=0):
        rows = pl.ds(part_at * (depth // 2), depth // 2)
        number = 2 + part_at * 5 + kind + index
        if kind < 2:
            source, lanes, where = low.at[rows], lane_block(half, here.near, here.core, tensor, 1), (beside, across)[kind]
        elif kind == 2:
            far, where = (1 - here.near, across) if part_at == 0 else (here.near, beside)
            lanes = lane_block(half, far, here.core, tensor if part_at == 0 else here.other, 1)
            source = o_grad.at[rows, lanes]
        else:
            lanes, where = lane_block(half, index, here.core, 0, 2), {"dp": flip(me, CORE)}
            source = o_grad.at[rows, lanes]
        return remote(source, o_grad.at[rows, lanes], share_s.at[number], share_r.at[number], **where)

    for part_at in range(2):
        share(part_at, 0).start()
        share(part_at, 1).start()
    keep = pltpu.make_async_copy(
        low, o_grad.at[:, lane_block(half, here.near, here.core, tensor, 1)], own_sem.at[2]
    )
    keep.start()

    def mixin_rows(index):
        rows = at(index * chunk, chunk)
        mixin[rows, :] = nt(normed[rows, :], inner_grad)

    loop(0, depth // chunk, mixin_rows)
    for part_at in range(2):
        share(part_at, part_at).wait()
        share(part_at, 2).start()
    lanes = at(tensor * half, half)
    next_share = remote(next_rows, o_next.at[:, lanes], share_s.at[1], share_r.at[1], tensor=here.other)
    next_share.start()
    finals = [
        pltpu.make_async_copy(next_rows, o_next.at[:, lanes], own_sem.at[3]),
        pltpu.make_async_copy(back, o_wide, own_sem.at[4]),
        pltpu.make_async_copy(mixin, o_mixin, own_sem.at[5]),
        pltpu.make_async_copy(tiny, o_tiny, own_sem.at[6]),
    ]
    for copy in finals:
        copy.start()
    keep.wait()
    for part_at in range(2):
        share(part_at, 1 - part_at).wait()
        share(part_at, 2).wait()
        for near in range(2):
            share(part_at, 3, near).start()
    for part_at in range(2):
        for near in range(2):
            share(part_at, 3, near).wait()
    share_block(0).wait()
    share_block(1).wait()
    next_share.wait()
    for copy in finals:
        copy.wait()


def join(part, streams, out_cot, small, mix_out, next_cot):
    depth, half = streams.shape[1:]
    spans = 4
    shapes = [
        ((depth, 8 * half), BF16),
        ((depth, half), F32),
        ((2 * half, depth), BF16),
        ((MIXH, 2 * half), F32),
        ((depth, 128), F32),
        ((MIXH, 128), F32),
    ]
    return pl.pallas_call(
        join_kernel,
        out_shape=[jax.ShapeDtypeStruct(*shape) for shape in shapes],
        in_specs=[ANY] * 3 + [VM] * 3,
        out_specs=[ANY] * 6,
        scratch_shapes=[
            pltpu.VMEM((128, 128), BF16),
            pltpu.VMEM((128, half), F32),
            pltpu.VMEM((2, 2, depth, half), BF16),
            pltpu.VMEM((2, 2, depth, half), BF16),
            pltpu.VMEM((2, depth, half), BF16),
            pltpu.VMEM((depth, half), BF16),
            pltpu.VMEM((depth, half), BF16),
            pltpu.VMEM((depth, half), F32),
            pltpu.VMEM((depth, half), BF16),
            pltpu.VMEM((half, depth), BF16),
            pltpu.VMEM((depth, half), BF16),
            pltpu.VMEM((half, depth), BF16),
            pltpu.VMEM((depth, half), F32),
            pltpu.VMEM((depth, half), BF16),
            pltpu.VMEM((MIXH, half), F32),
            pltpu.VMEM((depth, 128), F32),
            pltpu.VMEM((MIXH, 128), F32),
            DMA((spans, 4)),
            DMA((spans, 4)),
            DMA((spans, 2)),
            DMA((spans, 2)),
            DMA((spans,)),
            DMA((spans,)),
            DMA((spans, 4)),
            DMA((12,)),
            DMA((12,)),
            DMA((8,)),
        ],
        compiler_params=pltpu.CompilerParams(
            collective_id=2, has_side_effects=True, vmem_limit_bytes=56 * 1024 * 1024
        ),
        name="join",
    )(part, streams, out_cot, small, mix_out, next_cot)


def back_kernel(
    grad, w_out, w_up, w_down, slope,
    o_mlp, o_up_grad, o_context,
    grad_in, out_in, up_in, down_in, slope_in,
    up_grad, context_grad, tall, load_sem, tall_sem, save_sem,
):
    depth = grad.shape[0]
    tile = 256
    loads = {}
    pairs = (
        ("grad", grad, grad_in), ("out", w_out, out_in), ("down", w_down, down_in), ("slope", slope, slope_in),
        ("up", w_up, up_in),
    )
    for number, (name, source, target) in enumerate(pairs):
        loads[name] = pltpu.make_async_copy(source, target, load_sem.at[number])
        loads[name].start()

    pending = {}

    def write(turn, out, compute):
        slots = tall.shape[1]
        if turn in pending:
            pending.pop(turn)()

        def copy(index):
            slot = lax.rem(index, slots)
            target = out.at[at(index * tile, tile), :]
            return pltpu.make_async_copy(tall.at[turn, slot], target, tall_sem.at[turn, slot])

        def body(index):
            @pl.when(index >= slots)
            def _():
                copy(index - slots).wait()

            tall[turn, lax.rem(index, slots)] = compute(at(index * tile, tile)).astype(BF16)
            copy(index).start()

        steps = depth // tile
        loop(0, steps, body)
        pending[turn] = lambda: loop(steps - slots, steps, lambda index: copy(index).wait())

    for name in ("grad", "out"):
        loads[name].wait()
    context_grad[...] = tn(out_in[...], grad_in[...]).astype(BF16)
    save_context = pltpu.make_async_copy(context_grad, o_context, save_sem.at[1])
    save_context.start()
    for name in ("down", "slope"):
        loads[name].wait()

    def lift(index):
        span = at(index * tile, tile)
        up_grad[span, :] = (tn(down_in[:, span], grad_in[...]) * slope_in[span, :]).astype(BF16)

    loop(0, up_grad.shape[0] // tile, lift)
    loads["up"].wait()
    save_up = pltpu.make_async_copy(up_grad, o_up_grad, save_sem.at[0])
    save_up.start()
    write(1, o_mlp, lambda span: nn(up_in[span, :], up_grad[...]))
    for drain in pending.values():
        drain()
    save_up.wait()
    save_context.wait()


def back(grad, w_out, w_up, w_down, slope):
    depth, tokens = grad.shape
    operands = (grad, w_out, w_up, w_down, slope)
    shapes = [(depth, tokens), slope.shape, (w_out.shape[1], tokens)]
    return pl.pallas_call(
        back_kernel,
        out_shape=[jax.ShapeDtypeStruct(shape, BF16) for shape in shapes],
        in_specs=[ANY] * 5,
        out_specs=[ANY] * 3,
        scratch_shapes=[pltpu.VMEM(v.shape, v.dtype) for v in operands]
        + [
            pltpu.VMEM(slope.shape, BF16),
            pltpu.VMEM((w_out.shape[1], tokens), BF16),
            pltpu.VMEM((2, 4, 256, tokens), BF16),
            DMA((5,)),
            DMA((2, 4)),
            DMA((2,)),
        ],
        compiler_params=pltpu.CompilerParams(vmem_limit_bytes=56 * 1024 * 1024),
        name="back",
    )(*operands)


ORDER = (3, 0, 1, 2)
SLOT = (1, 0, 1, 0)


def scatter_kernel(
    n_dp, mlp_grad, streams, small, wide_grad, mixin_part, mix_tiny, hist,
    branch_grad, act, hidden, up_grad, context, heads_rows, sums, context_grad, w_qkv, cos, sin,
    o_stream, o_mix, o_small, o_tiny, o_qkv, o_up, o_down, o_out, sent_qkv, sent_up, sent_down, sent_out, attn_grad,
    own, from_core, from_tensor, from_near, rows_in, wide, stream_grad, gains, biases, tiny, tiny_in, tiny_out,
    hist_in, arrived, mix_part, mix_in, mix_sum, tiny_sum, ring, side_in, mine, high_in,
    hidden_in, up_in, context_in, rows_grad_in, heads_in, sums_in, outer_in, qkv_in, tile_in, stage, tile_sem, stage_sem,
    right_sem, qkv_sem,
    core_s, core_r, tensor_s, tensor_r, near_s, near_r, local, in_sem,
    side_s, side_r, high_s, high_r, peer_s, peer_r, peer_local,
    a2a_s, a2a_r, a2a_own, keep_sem, pass_s, pass_r, tiny_s, tiny_r, mix_s, mix_r, hist_sem,
    ring_s, ring_r, last_s, last_r, last_local,
):
    here = Place()
    me, tensor = here.me, here.tensor
    depth, half = wide_grad.shape
    rows = depth // n_dp
    high_bits = int(math.log2(n_dp // HIGH))
    chunk = min(256, depth)
    greet_all(n_dp, me, here.other)

    highs = n_dp // HIGH
    tall = 2 * rows
    arrays = (
        (branch_grad, hidden_in, sent_down, o_down),
        (act.at[3], up_in, sent_up, o_up),
        (branch_grad, context_in, sent_out, o_out),
    ) + tuple((act.at[s], rows_grad_in.at[s], sent_qkv.at[s], o_qkv.at[s]) for s in range(3))
    units, first_unit = [], []
    for _, right, sent, o in arrays:
        first_unit.append(len(units))
        units += [(sent, o, first) for first in range(0, right.shape[0], UNIT)]
    total = len(units)
    rights = [
        pltpu.make_async_copy(source, target, right_sem.at[number])
        for number, (source, target) in enumerate(
            (
                (hidden, hidden_in), (up_grad, up_in), (context, context_in), (heads_rows, heads_in), (sums, sums_in),
                (context_grad, outer_in),
            )
        )
    ]

    def side_hop(unit):
        sent, _, first = units[unit]
        return remote(
            sent.at[:, :, :, pl.ds(first, UNIT)], side_in.at[unit], side_s.at[unit], side_r.at[unit], dp=flip(me, SIDE)
        )

    count = highs * 2

    def tile_load(array, block):
        mine_now = lax.div(block, count)
        side = here.side * mine_now + (1 - here.side) * (1 - mine_now)
        row = (lax.rem(block, count) * 2 + side) * tall
        slot = lax.rem(block, 2)
        return pltpu.make_async_copy(arrays[array][0].at[at(row, tall), :], tile_in.at[slot], tile_sem.at[slot])

    def product(array, block):
        @pl.when(block + 1 < 2 * count)
        def _():
            tile_load(array, block + 1).start()

        tile_load(array, block).wait()
        return nt(tile_in[lax.rem(block, 2)], arrays[array][1][...]).astype(BF16)

    def compute_sent(array):
        _, right, sent, _ = arrays[array]
        width = right.shape[0]

        def put(block):
            slot = lax.rem(block, 2)
            return pltpu.make_async_copy(
                stage.at[slot, :, pl.ds(0, width)], sent.at[lax.div(block, 2), slot], stage_sem.at[slot]
            )

        def body(block):
            value = product(array, block)

            @pl.when(block >= 2)
            def _():
                put(block - 2).wait()

            stage[lax.rem(block, 2), :, :width] = value
            put(block).start()

        tile_load(array, 0).start()
        loop(0, count, body)
        put(count - 2).wait()
        put(count - 1).wait()

    def compute_mine(array):
        width = arrays[array][1].shape[0]

        def body(block):
            value = product(array, block)
            flat = block - count
            for part in range(width // UNIT):
                mine[first_unit[array] + part, lax.div(flat, 2), lax.rem(flat, 2)] = value[
                    :, part * UNIT : (part + 1) * UNIT
                ]

        loop(count, 2 * count, body)

    def high_hop(unit, phase):
        span = 1 << phase
        base = lax.div(here.high, span)
        theirs = base + 1 - 2 * lax.rem(base, 2)
        return remote(
            mine.at[unit, pl.ds(theirs * span, span)], high_in.at[unit, pl.ds(span - 1, span)],
            high_s.at[unit, phase], high_r.at[unit, phase], dp=flip(me, HIGH << phase),
        )

    def peer_hop(unit, peer):
        _, o, first = units[unit]
        target, _ = here.peers[peer]
        return remote(
            mine.at[unit, here.high, bit(target, NEAR), at(bit(target, CORE) * rows, rows)],
            o.at[:, at(here.quarter * (o.shape[-1] // QUARTERS) + first, UNIT)],
            peer_s.at[unit, peer], peer_r.at[unit, peer], dp=target,
        )

    def peer_keep(unit):
        _, o, first = units[unit]
        return pltpu.make_async_copy(
            mine.at[unit, here.high, here.near, at(here.core * rows, rows)],
            o.at[:, at(here.quarter * (o.shape[-1] // QUARTERS) + first, UNIT)], peer_local.at[unit],
        )

    def add_blocks(unit, other, first_mine, first_other, count):
        step = min(64, tall)

        def add(flat):
            high, rest = lax.div(flat, 2 * (tall // step)), lax.rem(flat, 2 * (tall // step))
            near, span = lax.div(rest, tall // step), at(lax.rem(rest, tall // step) * step, step)
            mine[unit, first_mine + high, near, span] += other[unit, first_other + high, near, span]

        loop(0, count * 2 * (tall // step), add)

    def finish_high(unit):
        for phase in reversed(range(high_bits)):
            high_hop(unit, phase).wait()
            span = 1 << phase
            add_blocks(unit, high_in, lax.div(here.high, span) * span, span - 1, span)
            if phase:
                high_hop(unit, phase - 1).start()
        peer_keep(unit).start()
        for peer in range(3):
            peer_hop(unit, peer).start()

    def tick(unit):
        side_hop(unit).wait()
        if unit + 2 < total:
            side_hop(unit + 2).start()
        add_blocks(unit, side_in, 0, 0, n_dp // HIGH)
        if unit:
            finish_high(unit - 1)
        high_hop(unit, high_bits - 1).start()

    done = 0

    def ticks(count):
        nonlocal done
        for unit in range(done, min(done + count, total)):
            tick(unit)
        done = min(done + count, total)

    def load(stream, near, half_at):
        part = attn_grad.at[stream] if stream < 3 else mlp_grad
        return pltpu.make_async_copy(
            part.at[:, lane_block(half, near, here.core, half_at, 1)], own.at[SLOT[stream], near, half_at],
            local.at[stream, near * 2 + half_at],
        )

    def to_core(stream, near, half_at):
        part = attn_grad.at[stream] if stream < 3 else mlp_grad
        return remote(
            part.at[:, lane_block(half, near, 1 - here.core, half_at, 1)], from_core.at[stream, near, half_at],
            core_s.at[stream, near * 2 + half_at], core_r.at[stream, near * 2 + half_at], dp=flip(me, CORE),
        )

    def to_tensor(stream, near):
        return remote(
            own.at[SLOT[stream], near, here.other], from_tensor.at[stream, near],
            tensor_s.at[stream, near], tensor_r.at[stream, near], tensor=here.other,
        )

    def to_near(stream):
        return remote(
            from_tensor.at[stream, 1 - here.near], from_near.at[stream], near_s.at[stream], near_r.at[stream],
            dp=flip(me, NEAR),
        )

    def after_core(stream):
        for near in range(2):
            for half_at in range(2):
                load(stream, near, half_at).wait()
                to_core(stream, near, half_at).wait()

        def add(index):
            span = at(index * chunk, chunk)
            for near in range(2):
                for half_at in range(2):
                    own[SLOT[stream], near, half_at, span] += from_core[stream, near, half_at, span]

        loop(0, depth // chunk, add)

    def after_tensor(stream):
        for near in range(2):
            to_tensor(stream, near).wait()

        def add(index):
            span = at(index * chunk, chunk)
            for near in range(2):
                from_tensor[stream, near, span] += own[SLOT[stream], near, tensor, span]

        loop(0, depth // chunk, add)
        to_near(stream).start()

    stats = []

    def measure(stream):
        def piece(index):
            return rows_in[stream, at(index * chunk, chunk), :].astype(F32)

        centre = sum_rows(piece, depth, chunk, lambda v: v) / depth
        spread = sum_rows(piece, depth, chunk, lambda v: (v - centre) * (v - centre)) / depth
        stats.append((centre, lax.rsqrt(spread + NORM_EPS)))

    def back_norm(stream):
        to_near(stream).wait()
        group = 0 if stream < 3 else 1
        centre, root = stats[stream]

        def parts(index):
            span = at(index * chunk, chunk)
            grad = from_tensor[stream, here.near, span].astype(F32) + from_near[stream, span].astype(F32)
            hat = (rows_in[stream, span, :].astype(F32) - centre) * root
            gain = small[span, MIXH + group : MIXH + group + 1].astype(F32)
            return span, grad, hat, grad * gain

        def sums(index, carry):
            span, grad, hat, scaled = parts(index)
            if stream in (0, 3):
                gains[group, span] = grad * hat
                biases[group, span] = grad
            else:
                gains[group, span] += grad * hat
                biases[group, span] += grad
            return (
                carry[0] + jnp.sum(scaled, axis=0, keepdims=True),
                carry[1] + jnp.sum(scaled * hat, axis=0, keepdims=True),
            )

        zero = jnp.zeros((1, half), F32)
        whole, along = lax.fori_loop(0, depth // chunk, sums, (zero, zero))

        def finish(index):
            span, _, hat, scaled = parts(index)
            value = root * (scaled - whole / depth - hat * (along / depth))
            if stream == 3:
                value = value + wide[span, :]
            stream_grad[stream, span] = value.astype(BF16)

        loop(0, depth // chunk, finish)
        loop(1, n_dp, lambda step: send(stream, step).start())
        send_own(stream).start()

    def send(stream, step):
        target = lax.rem(me + step, n_dp)
        return remote(
            stream_grad.at[stream, at(target * rows, rows), :], arrived.at[stream, step],
            a2a_s.at[stream, step], a2a_r.at[stream, step], dp=target,
        )

    def send_own(stream):
        return pltpu.make_async_copy(
            stream_grad.at[stream, at(me * rows, rows), :], arrived.at[stream, 0], a2a_own.at[stream]
        )

    def source_of(step):
        return lax.rem(me - step + n_dp, n_dp)

    def lanes_of(step):
        return at(source_of(step) * 2 * half + tensor * half, half)

    def fetch(step):
        slot = lax.rem(step, 2)
        return pltpu.make_async_copy(hist.at[:, :, lanes_of(step)], hist_in.at[slot], hist_sem.at[slot])

    def keep(stream, step):
        return pltpu.make_async_copy(
            arrived.at[stream, step], o_stream.at[stream, :, lanes_of(step)], keep_sem.at[stream, step]
        )

    def pass_on(stream, step):
        return remote(
            arrived.at[stream, step], o_stream.at[stream, :, lanes_of(step)],
            pass_s.at[stream, step], pass_r.at[stream, step], tensor=here.other,
        )

    def mix_send(step):
        return remote(mix_part.at[step], mix_in.at[step], mix_s.at[step], mix_r.at[step], dp=source_of(step))

    def receive(stream):
        fetch(0).start()
        send_own(stream).wait()

        def one(step):
            @pl.when(step + 1 < n_dp)
            def _():
                fetch(step + 1).start()

            @pl.when(step > 0)
            def _():
                send(stream, step).wait()

            keep(stream, step).start()
            pass_on(stream, step).start()
            fetch(step).wait()
            totals = [jnp.zeros((8, half), F32) for _ in range(HIST)]
            for row in range(0, rows, 16):
                span = pl.ds(row, 16)
                grad = arrived[stream, step, span, :].astype(F32)
                for source in range(HIST):
                    product = grad * hist_in[lax.rem(step, 2), source, span, :].astype(F32)
                    totals[source] = totals[source] + product[:8] + product[8:]
            for source in range(HIST):
                mix_part[step, pl.ds(stream * HIST + source, 1), :] = jnp.sum(totals[source], axis=0, keepdims=True)
            if stream == ORDER[-1]:

                @pl.when(step > 0)
                def _():
                    mix_send(step).start()

        loop(0, n_dp, one)

    ring_targets = [{"dp": flip(me, value)} for value in (CORE, SIDE, NEAR)]
    ring_targets += [{"dp": flip(me, HIGH << phase)} for phase in range(high_bits)]
    ring_targets.append({"tensor": here.other})
    hops = len(ring_targets)

    def ring_hop(hop):
        return remote(ring.at[hop, 0], ring.at[hop, 1], ring_s.at[hop], ring_r.at[hop], **ring_targets[hop])

    def ring_step(hop):
        ring_hop(hop).wait()
        ring[hop + 1, 0] = ring[hop, 0] + ring[hop, 1]
        if hop + 1 < hops:
            ring_hop(hop + 1).start()

    rights[0].start()
    inputs = [
        pltpu.make_async_copy(streams, rows_in, in_sem.at[0]),
        pltpu.make_async_copy(wide_grad, wide, in_sem.at[1]),
        pltpu.make_async_copy(mix_tiny, ring.at[0, 0], in_sem.at[2]),
    ]

    def load_own(stream):
        for near in range(2):
            for half_at in range(2):
                load(stream, near, half_at).start()

    def tensor_start(stream):
        for near in range(2):
            to_tensor(stream, near).start()

    def core_start(stream):
        for near in range(2):
            for half_at in range(2):
                to_core(stream, near, half_at).start()

    def qkv_load(stream):
        return pltpu.make_async_copy(w_qkv.at[stream], qkv_in.at[stream % 2], qkv_sem.at[stream % 2])

    seq_len = sums_in.shape[1]
    heads = heads_in.shape[1] // HD
    scale = 1.0 / math.sqrt(HD)

    def attend_back(seq):
        span = at(seq * seq_len, seq_len)
        for head in range(heads):
            lane = pl.ds(head * HD, HD)
            queries, keys, values = (heads_in[s, lane, span] for s in range(3))
            prob = jnp.exp(causal_scores(keys, queries) - sums_in[pl.ds(seq * heads + head, 1), :])
            outer = outer_in[lane, span]
            prob_grad = tn(values, outer)
            inner = jnp.sum(prob * prob_grad, axis=0, keepdims=True)
            score_grad = (prob * (prob_grad - inner)).astype(BF16)
            turn_back = (cos[...], -sin[...])
            rows_grad_in[0, lane, span] = turned(nn(keys, score_grad) * scale, *turn_back).astype(BF16)
            rows_grad_in[1, lane, span] = turned(nt(queries, score_grad) * scale, *turn_back).astype(BF16)
            rows_grad_in[2, lane, span] = nt(outer, prob.astype(BF16)).astype(BF16)

    def input_grad(stream):
        def put(block):
            slot = lax.rem(block, 2)
            return pltpu.make_async_copy(
                stage.at[slot, :, pl.ds(0, 8 * half)], attn_grad.at[stream, at(block * tall, tall), :], stage_sem.at[slot]
            )

        def body(block):
            value = nn(qkv_in[stream % 2, at(block * tall, tall), :], rows_grad_in[stream]).astype(BF16)

            @pl.when(block >= 2)
            def _():
                put(block - 2).wait()

            stage[lax.rem(block, 2), :, : 8 * half] = value
            put(block).start()

        qkv_load(stream).wait()
        loop(0, depth // tall, body)
        put(depth // tall - 2).wait()
        put(depth // tall - 1).wait()
        if stream + 2 < 3:
            qkv_load(stream + 2).start()
        core_start(stream)

    core_start(ORDER[0])
    load_own(ORDER[0])
    for copy in rights[1:] + inputs:
        copy.start()
    qkv_load(0).start()
    qkv_load(1).start()
    rights[0].wait()
    compute_sent(0)
    side_hop(0).start()
    side_hop(1).start()
    after_core(ORDER[0])
    tensor_start(ORDER[0])
    compute_mine(0)
    for copy in rights[1:] + inputs:
        copy.wait()
    ring_hop(0).start()
    loop(0, 8 * half // seq_len, attend_back)
    for stream in range(3):
        input_grad(stream)
        if stream == 0:
            ticks(1)
        if stream == ORDER[1]:
            load_own(stream)
    mix_part[...] = jnp.zeros_like(mix_part)
    for stream in range(STREAMS):
        measure(stream)
    after_core(ORDER[1])
    ring_step(0)
    for turn, stream in enumerate(ORDER):
        ticks((1, 3, 2, 2)[turn])
        after_tensor(stream)
        if turn + 1 < STREAMS:
            tensor_start(ORDER[turn + 1])
            if turn + 1 < hops:
                ring_step(turn + 1)
        if turn + 2 < STREAMS:
            load_own(ORDER[turn + 2])
        for array in ((1,), (2, 3), (4, 5), ())[turn]:
            compute_sent(array)
            compute_mine(array)
        if turn + 2 < STREAMS:
            after_core(ORDER[turn + 2])
        if turn > 0:
            back_norm(ORDER[turn - 1])
        if turn > 1:
            receive(ORDER[turn - 2])
    back_norm(ORDER[-1])

    column = lax.broadcasted_iota(jnp.int32, (chunk, 128), 1)
    pltpu.make_async_copy(mixin_part, wide, in_sem.at[0]).start()
    pltpu.make_async_copy(mixin_part, wide, in_sem.at[0]).wait()

    def gather_tiny(index):
        span = at(index * chunk, chunk)
        value = wide[span, :]
        for group in range(2):
            gain = jnp.sum(gains[group, span], axis=1, keepdims=True)
            bias = jnp.sum(biases[group, span], axis=1, keepdims=True)
            value = jnp.where(column == MIXH + group, gain, value)
            value = jnp.where(column == MIXH + 2 + group, bias, value)
        tiny[span, :] = value.astype(BF16)

    loop(0, depth // chunk, gather_tiny)

    def tiny_send(step):
        target = lax.rem(me + step, n_dp)
        return remote(tiny.at[at(target * rows, rows), :], tiny_in.at[step], tiny_s.at[step], tiny_r.at[step], dp=target)

    loop(1, n_dp, lambda step: tiny_send(step).start())
    receive(ORDER[2])
    ticks(2)
    receive(ORDER[3])
    for hop in range(STREAMS, hops):
        ring_step(hop)
    tiny_final = pltpu.make_async_copy(ring.at[hops, 0], o_tiny, last_local.at[0])
    tiny_final.start()
    ticks(total)

    tiny_sum[0] = tiny[at(me * rows, rows), :].astype(F32)

    def add_tiny(step):
        tiny_send(step).wait()
        tiny_sum[0] += tiny_in[step].astype(F32)

    loop(1, n_dp, add_tiny)
    tiny_share = remote(tiny_sum.at[0], tiny_sum.at[1], last_s.at[1], last_r.at[1], tensor=here.other)
    tiny_share.start()
    mix_sum[...] = mix_part[0]

    def add_mix(step):
        mix_send(step).wait()
        mix_sum[...] += mix_in[step]

    loop(1, n_dp, add_mix)
    lanes = at(tensor * half, half)
    mix_share = remote(mix_sum, o_mix.at[:, lanes], last_s.at[0], last_r.at[0], tensor=here.other)
    mix_keep = pltpu.make_async_copy(mix_sum, o_mix.at[:, lanes], last_local.at[1])
    mix_share.start()
    mix_keep.start()
    finish_high(total - 1)
    tiny_share.wait()
    tiny_out[...] = (tiny_sum[0] + tiny_sum[1]).T
    tiny_keep = pltpu.make_async_copy(tiny_out, o_small, last_local.at[2])
    tiny_keep.start()
    for unit in range(total):
        peer_keep(unit).wait()
        for peer in range(3):
            peer_hop(unit, peer).wait()

    def settle(step):
        for stream in range(STREAMS):
            keep(stream, step).wait()
            pass_on(stream, step).wait()

    loop(0, n_dp, settle)
    mix_share.wait()
    mix_keep.wait()
    tiny_keep.wait()
    tiny_final.wait()


def scatter(
    n_dp, mlp_grad, streams, small, wide_grad, mixin_part, mix_tiny, hist, branch_grad, act, hidden, up_grad, context,
    rows_all, sums, context_grad, w_qkv, cos, sin,
):
    depth, half = wide_grad.shape
    rows = depth // n_dp
    high = n_dp // HIGH
    high_bits = int(math.log2(high))
    tokens = act.shape[2]
    narrow, width = context.shape[0], hidden.shape[0]
    widths = ((3,), narrow), ((), width), ((), width), ((), narrow)
    units = (4 * narrow + 2 * width) // UNIT
    hops = high_bits + 4

    outs = [
        ((STREAMS, rows, 2 * half * n_dp), BF16),
        ((MIXH, 2 * half), F32),
        ((128, rows), F32),
        (mix_tiny.shape, F32),
    ]
    outs += [(lead + (rows, QUARTERS * size), BF16) for lead, size in widths]
    outs += [(lead + (high, 2, 2 * rows, size), BF16) for lead, size in widths]
    outs.append(((3, depth, tokens), BF16))
    return pl.pallas_call(
        functools.partial(scatter_kernel, n_dp),
        out_shape=[jax.ShapeDtypeStruct(*shape) for shape in outs],
        in_specs=[ANY, ANY, VM] + [ANY] * 13 + [VM] * 2,
        out_specs=[ANY] * 13,
        scratch_shapes=[
            pltpu.VMEM((2, 2, 2, depth, half), BF16),
            pltpu.VMEM((STREAMS, 2, 2, depth, half), BF16),
            pltpu.VMEM((STREAMS, 2, depth, half), BF16),
            pltpu.VMEM((STREAMS, depth, half), BF16),
            pltpu.VMEM((STREAMS, depth, half), BF16),
            pltpu.VMEM((depth, half), F32),
            pltpu.VMEM((STREAMS, depth, half), BF16),
            pltpu.VMEM((2, depth, half), F32),
            pltpu.VMEM((2, depth, half), F32),
            pltpu.VMEM((depth, 128), BF16),
            pltpu.VMEM((n_dp, rows, 128), BF16),
            pltpu.VMEM((128, rows), F32),
            pltpu.VMEM((2, HIST, rows, half), BF16),
            pltpu.VMEM((STREAMS, n_dp, rows, half), BF16),
            pltpu.VMEM((n_dp, MIXH, half), F32),
            pltpu.VMEM((n_dp, MIXH, half), F32),
            pltpu.VMEM((MIXH, half), F32),
            pltpu.VMEM((2, rows, 128), F32),
            pltpu.VMEM((hops + 1, 2) + mix_tiny.shape, F32),
            pltpu.VMEM((units, high, 2, 2 * rows, UNIT), BF16),
            pltpu.VMEM((units, high, 2, 2 * rows, UNIT), BF16),
            pltpu.VMEM((units, high - 1, 2, 2 * rows, UNIT), BF16),
            pltpu.VMEM(hidden.shape, BF16),
            pltpu.VMEM(up_grad.shape, BF16),
            pltpu.VMEM(context.shape, BF16),
            pltpu.VMEM(rows_all.shape, BF16),
            pltpu.VMEM(rows_all.shape, BF16),
            pltpu.VMEM(sums.shape, F32),
            pltpu.VMEM(context_grad.shape, BF16),
            pltpu.VMEM((2,) + w_qkv.shape[1:], BF16),
            pltpu.VMEM((2, 2 * rows, tokens), BF16),
            pltpu.VMEM((2, 2 * rows, max(width, tokens)), BF16),
            DMA((2,)),
            DMA((2,)),
            DMA((6,)),
            DMA((2,)),
            DMA((STREAMS, 4)),
            DMA((STREAMS, 4)),
            DMA((STREAMS, 2)),
            DMA((STREAMS, 2)),
            DMA((STREAMS,)),
            DMA((STREAMS,)),
            DMA((STREAMS, 4)),
            DMA((3,)),
            DMA((units,)),
            DMA((units,)),
            DMA((units, high_bits)),
            DMA((units, high_bits)),
            DMA((units, 3)),
            DMA((units, 3)),
            DMA((units,)),
            DMA((STREAMS, n_dp)),
            DMA((STREAMS, n_dp)),
            DMA((STREAMS,)),
            DMA((STREAMS, n_dp)),
            DMA((STREAMS, n_dp)),
            DMA((STREAMS, n_dp)),
            DMA((n_dp,)),
            DMA((n_dp,)),
            DMA((n_dp,)),
            DMA((n_dp,)),
            DMA((2,)),
            DMA((hops,)),
            DMA((hops,)),
            DMA((2,)),
            DMA((2,)),
            DMA((3,)),
        ],
        compiler_params=pltpu.CompilerParams(
            collective_id=3, has_side_effects=True, vmem_limit_bytes=62 * 1024 * 1024
        ),
        name="scatter",
    )(
        mlp_grad, streams, small, wide_grad, mixin_part, mix_tiny, hist, branch_grad, act, hidden, up_grad, context,
        rows_all, sums, context_grad, w_qkv, cos, sin,
    )[:8]


def rotary_tables(length, rotary, float_type):
    half_rot = rotary // 2
    places = jnp.arange(length).astype(float_type)
    frequency = jnp.exp(
        jnp.arange(half_rot).astype(float_type) * (-2.0 * math.log(10000.0) / rotary)
    )
    angles = places[:, None] * frequency[None, :]
    return (jnp.cos(angles), jnp.sin(angles))


def finish_kernel(mix_rows, stream_grad, small, tiny, block, *refs):
    narrow, history_grad, wide = refs[:4], refs[4], refs[5:9]
    gain, bias, mix_in_grad, mix_out_grad, block_out = refs[9:]
    rows = stream_grad.shape[1]
    tile, span = min(32, rows), 512

    def body(index):
        row = at(lax.rem(index, rows // tile) * tile, tile)
        lane = at(lax.div(index, rows // tile) * span, span)
        grads = [stream_grad[stream, row, lane].astype(F32) for stream in range(STREAMS)]
        for source in range(HIST):
            total = sum(
                mix_rows[pl.ds(stream * HIST + source, 1), lane] * grads[stream] for stream in range(STREAMS)
            )
            history_grad[source, row, lane] = total.astype(BF16)

    loop(0, rows // tile * (stream_grad.shape[2] // span), body)
    for low, full in zip(narrow, wide):
        full[...] = low[...].astype(F32)
    block_out[...] = block[...]
    gain[...] = small[MIXH : MIXH + 2]
    bias[...] = small[MIXH + 2 : MIXH + 4]
    mix_in_grad[...] = small[:MIXH]
    mix_out_grad[...] = tiny[:, : STREAMS * NEXT]


def finish(mix_rows, stream_grad, small, tiny, block, *grads):
    rows, tokens = stream_grad.shape[1:]
    steps = rows // 16
    lanes = tokens // steps

    def weight(g):
        if g.ndim == 3:
            return pl.BlockSpec((g.shape[0], 16, g.shape[2]), lambda i: (0, i, 0))
        return pl.BlockSpec((16, g.shape[1]), lambda i: (i, 0))

    def along(count):
        return pl.BlockSpec((count, rows, lanes), lambda i: (0, 0, i))

    def whole(shape):
        return pl.BlockSpec(shape, lambda i: (0, 0))

    blocks = pl.BlockSpec((block.shape[0] // steps, block.shape[1]), lambda i: (i, 0))
    smalls = [(2, rows), (2, rows), (MIXH, rows), (MIXH, STREAMS * NEXT)]
    return pl.pallas_call(
        finish_kernel,
        grid=(steps,),
        out_shape=[jax.ShapeDtypeStruct((HIST, rows, tokens), BF16)]
        + [jax.ShapeDtypeStruct(g.shape, F32) for g in grads]
        + [jax.ShapeDtypeStruct(shape, F32) for shape in smalls]
        + [jax.ShapeDtypeStruct(block.shape, BF16)],
        in_specs=[pl.BlockSpec((mix_rows.shape[0], lanes), lambda i: (0, i)), along(STREAMS)]
        + [whole(small.shape), whole(tiny.shape), blocks]
        + [weight(g) for g in grads],
        out_specs=[along(HIST)] + [weight(g) for g in grads] + [whole(shape) for shape in smalls] + [blocks],
        compiler_params=pltpu.CompilerParams(vmem_limit_bytes=60 * 1024 * 1024),
        name="finish",
    )(mix_rows, stream_grad, small, tiny, block, *grads)


def per_device(
    n_dp, history, mix_weights, w_qkv, w_out, w_up, w_down, norm_gain, norm_bias, mix_in, mix_out, mix_static,
    out_cot, next_cot,
):
    tensor = lax.axis_index("tensor")
    seq_len = mix_weights.shape[0]
    half = seq_len // 2
    depth = mix_in.shape[0] * n_dp

    def own_half(rows):
        return lax.dynamic_slice_in_dim(rows, tensor * half, half, 0)

    mix_rows = own_half(mix_weights.reshape(seq_len, -1)).T
    small = jnp.concatenate(
        [mix_in.T, norm_gain, norm_bias, jnp.zeros((128 - MIXH - 4, mix_in.shape[0]), BF16)], axis=0
    )
    cos, sin = (table.T for table in rotary_tables(seq_len, ROT, F32))
    mix_rows, small_all, streams, act, qkv, out, up, down, rows, context, sums, hidden, slope, part = gather(
        n_dp, history, mix_rows, small, w_qkv, w_out, w_up, w_down, cos, sin
    )
    small_all = small_all.reshape(depth, 128)
    qkv, up, down, out = (
        qkv.reshape(3, depth, -1), up.reshape(depth, -1), down.reshape(depth, -1), out.reshape(depth, -1)
    )

    next_rows = own_half(next_cot.reshape(seq_len, -1)).T
    branch_grad, wide_grad, block, next_mix, mixin_part, tiny = join(
        part, streams, out_cot, small_all, mix_out, next_rows
    )
    mlp_in_grad, up_grad, context_grad = back(branch_grad, out, up, down, slope)
    stream_grad, mix_grad, small_total, tiny, qkv_total, up_total, down_total, out_total = scatter(
        n_dp, mlp_in_grad, streams, small_all, wide_grad, mixin_part, tiny, history, branch_grad, act, hidden, up_grad,
        context, rows, sums, context_grad, qkv, cos, sin,
    )
    (
        history_grad, qkv_total, up_total, down_total, out_total, gain_total, bias_total, mixin_total, mixout_total, block,
    ) = finish(
        mix_rows, stream_grad, small_total, tiny, block, qkv_total, up_total, down_total, out_total
    )
    return (
        block,
        (next_mix.T + mix_static).reshape(seq_len, STREAMS, NEXT),
        history_grad,
        mix_grad[: STREAMS * HIST].T.reshape(seq_len, STREAMS, HIST),
        qkv_total,
        out_total,
        up_total,
        down_total,
        gain_total,
        bias_total,
        mixin_total.T,
        mixout_total,
        tiny[: STREAMS * NEXT, MIXH],
    )


def solution(mesh):
    return jax.shard_map(
        functools.partial(per_device, mesh.shape["dp"]),
        mesh=mesh,
        in_specs=(
            P(None, "dp", None),
            P("dp", None, None),
            P(None, "dp", "tensor"),
            P("dp", "tensor"),
            P("dp", "tensor"),
            P("dp", "tensor"),
            P(None, "dp"),
            P(None, "dp"),
            P("dp", None),
            P(),
            P(),
            P("dp", None),
            P("dp", None, None),
        ),
        out_specs=(
            P("dp", None),
            P("dp", None, None),
            P(None, "dp", None),
            P("dp", None, None),
            P(None, "dp", "tensor"),
            P("dp", "tensor"),
            P("dp", "tensor"),
            P("dp", "tensor"),
            P(None, "dp"),
            P(None, "dp"),
            P("dp", None),
            P(),
            P(),
        ),
        check_vma=False,
    )
```

```python
import functools
import math

import jax
import jax.numpy as jnp
from jax import lax
from jax.experimental import pallas as pl
from jax.experimental.pallas import tpu as pltpu
from jax.sharding import PartitionSpec as P

HD = 128
ROT = 32
HIST = 9
STREAMS = 4
NEXT = 10
MIXH = 40

NORM_EPS = 1e-05
ROOT_EPS = 1e-06
MASKED = -1e30

MESH = pl.DeviceIdType.MESH
ANY = pl.BlockSpec(memory_space=pltpu.HBM)
VM = pl.BlockSpec(memory_space=pltpu.VMEM)
DMA = pltpu.SemaphoreType.DMA
F32, BF16 = jnp.float32, jnp.bfloat16
CORE, SIDE, NEAR, HIGH = 1, 2, 4, 8
QUARTERS = 4
UNIT = 256
PLAN = (
    "T", "T", "n0", "T", "T", "n1", "T", "T", "n2", "s0", "T", "n3", "t0", "s1", "w0", "p0", "T", "t1", "s2", "p1",
    "T", "t2", "s3", "p2", "t3", "a0", "u0",
)


def bit(place, value):
    return lax.rem(lax.div(place, value), 2)


def flip(place, value):
    return place + value - 2 * value * bit(place, value)


def at(start, size, multiple=None):
    return pl.ds(pl.multiple_of(start, size if multiple is None else multiple), size)


def remote(src, dst, send, recv, **where):
    return pltpu.make_async_remote_copy(
        src_ref=src, dst_ref=dst, send_sem=send, recv_sem=recv, device_id=where, device_id_type=MESH
    )


def loop(lower, upper, step):
    def body(index, carry):
        step(index)
        return carry

    lax.fori_loop(lower, upper, body, 0)


def greet(targets):
    barrier = pltpu.get_barrier_semaphore()
    for target in targets:
        pl.semaphore_signal(barrier, inc=1, device_id=target, device_id_type=MESH)
    pl.semaphore_wait(barrier, len(targets))


def greet_all(n_dp, me, other_tensor):
    barrier = pltpu.get_barrier_semaphore()
    loop(
        1,
        n_dp,
        lambda step: pl.semaphore_signal(
            barrier, inc=1, device_id={"dp": lax.rem(me + step, n_dp)}, device_id_type=MESH
        ),
    )
    pl.semaphore_signal(barrier, inc=1, device_id={"tensor": other_tensor}, device_id_type=MESH)
    pl.semaphore_wait(barrier, n_dp)


class Place:
    def __init__(self):
        self.me = lax.axis_index("dp")
        self.tensor = lax.axis_index("tensor")
        self.other = 1 - self.tensor
        self.core = bit(self.me, CORE)
        self.side = bit(self.me, SIDE)
        self.near = bit(self.me, NEAR)
        self.high = lax.div(self.me, HIGH)
        self.quarter = self.near * 2 + self.core
        self.peers = (
            (flip(self.me, CORE), self.near * 2 + 1 - self.core),
            (flip(self.me, NEAR), (1 - self.near) * 2 + self.core),
            (flip(flip(self.me, NEAR), CORE), (1 - self.near) * 2 + 1 - self.core),
        )


def sum_rows(ref_at, depth, chunk, of):
    def body(index, total):
        return total + jnp.sum(of(ref_at(index)), axis=0, keepdims=True)

    return lax.fori_loop(0, depth // chunk, body, jnp.zeros((1, 128), F32))


def gelu_parts(values):
    phi = 0.5 * (1.0 + lax.erf(values * (1.0 / math.sqrt(2.0))))
    density = jnp.exp(-0.5 * values * values) * (1.0 / math.sqrt(2.0 * math.pi))
    return values * phi, phi + values * density


def tn(left, right):
    return lax.dot_general(left, right, (((0,), (0,)), ((), ())), preferred_element_type=F32)


def nt(left, right):
    return lax.dot_general(left, right, (((1,), (1,)), ((), ())), preferred_element_type=F32)


def nn(left, right):
    return jnp.dot(left, right, preferred_element_type=F32)


def turned(values, cos, sin):
    pieces = []
    half_rot = ROT // 2
    repeats = values.shape[1] // cos.shape[1]
    cos, sin = (jnp.concatenate([table] * repeats, axis=1) for table in (cos, sin))
    for head in range(values.shape[0] // HD):
        rows = values[head * HD : (head + 1) * HD]
        first, second = rows[:half_rot], rows[half_rot:ROT]
        pieces += [first * cos - second * sin, second * cos + first * sin, rows[ROT:]]
    return jnp.concatenate(pieces, axis=0)


def causal_scores(keys, queries):
    scores = tn(keys, queries) * (1.0 / math.sqrt(HD))
    length = scores.shape[0]
    key = lax.broadcasted_iota(jnp.int32, (length, length), 0)
    query = lax.broadcasted_iota(jnp.int32, (length, length), 1)
    return jnp.where(query >= key, scores, MASKED)


def gather_kernel(
    n_dp, hist, mix, small, w_qkv, w_out, w_up, w_down, cos, sin,
    o_mix, o_small, o_streams, o_act, o_qkv, o_out, o_up, o_down,
    o_rows, o_context, o_sums, o_hidden, o_slope, o_part,
    mix_all, small_all, hist_in, mixed, streams, act,
    early_s, early_r, hist_sem, a2a_s, a2a_r, reshard_s, reshard_r, high_s, high_r, side_s, side_r,
    act_s, act_r, act_local, own_sem, out_sem, share_s, share_r, share_l,
    act_in, qkv_in, out_in, up_in, down_in, rows_out, context, sums, hidden, slope, part, load_sem, save_sem,
):
    here = Place()
    me, tensor = here.me, here.tensor
    rows = small.shape[1]
    depth = rows * n_dp
    half = hist.shape[2] // n_dp // 2
    high_bits = int(math.log2(n_dp // HIGH))
    weights = ((w_qkv, o_qkv), (w_out, o_out), (w_up, o_up), (w_down, o_down))
    greet_all(n_dp, me, here.other)

    def early(which, buf, phase):
        if phase == 0:
            block, target = buf.at[here.high, here.near, here.side, here.core], flip(me, NEAR)
        elif phase <= high_bits:
            span = 1 << (phase - 1)
            block = buf.at[pl.ds(lax.div(here.high, span) * span, span), :, here.side, here.core]
            target = flip(me, HIGH << (phase - 1))
        elif phase == high_bits + 1:
            block, target = buf.at[:, :, here.side, here.core], flip(me, SIDE)
        else:
            block, target = buf.at[:, :, :, here.core], flip(me, CORE)
        return remote(block, block, early_s.at[which, phase], early_r.at[which, phase], dp=target)

    own_mix = pltpu.make_async_copy(mix, mix_all.at[here.high, here.near, here.side, here.core], own_sem.at[0])
    units = []
    for w, o in weights:
        if len(w.shape) == 3:
            units += [(w.at[part], o.at[part], 0) for part in range(w.shape[0])]
        else:
            units += [(w, o, first) for first in range(0, o.shape[-1], UNIT)]

    def cut(unit, quarter):
        w, o, first = units[unit]
        return w.at[:, at(quarter * o.shape[-1] + first, UNIT)]

    def slot(unit):
        _, o, first = units[unit]
        mine = pl.ds(pl.multiple_of(here.core * rows, rows), rows)
        return o.at[here.high, here.near, here.side, mine, pl.ds(first, UNIT)]

    def keep(unit):
        return pltpu.make_async_copy(cut(unit, here.quarter), slot(unit), own_sem.at[2 + unit])

    def reshard(unit, peer):
        target, quarter = here.peers[peer]
        return remote(cut(unit, quarter), slot(unit), reshard_s.at[unit, peer], reshard_r.at[unit, peer], dp=target)

    def high_hop(unit, phase):
        _, o, first = units[unit]
        span = 1 << phase
        block = o.at[pl.ds(lax.div(here.high, span) * span, span), :, here.side, :, pl.ds(first, UNIT)]
        return remote(block, block, high_s.at[unit, phase], high_r.at[unit, phase], dp=flip(me, HIGH << phase))

    def side_hop(unit):
        _, o, first = units[unit]
        block = o.at[:, :, here.side, :, pl.ds(first, UNIT)]
        return remote(block, block, side_s.at[unit], side_r.at[unit], dp=flip(me, SIDE))

    def fetch(step, buf):
        target = lax.rem(me + step, n_dp)
        return pltpu.make_async_copy(
            hist.at[:, :, at(target * 2 * half + tensor * half, half)], hist_in.at[buf], hist_sem.at[buf]
        )

    def send(step):
        target = lax.rem(me + step, n_dp)
        return remote(
            mixed.at[step], streams.at[:, at(me * rows, rows), :], a2a_s.at[step], a2a_r.at[step], dp=target
        )

    fetch(0, 0).start()

    def mix_step(step):
        buf = lax.rem(step, 2)

        @pl.when(step + 1 < n_dp)
        def _():
            fetch(step + 1, 1 - buf).start()

        fetch(step, buf).wait()
        target = lax.rem(me + step, n_dp)
        weight = mix_all[lax.div(target, HIGH), bit(target, NEAR), bit(target, SIDE), bit(target, CORE)]
        for row in range(0, rows, 32):
            part = pl.ds(row, 32)
            sources = [hist_in[buf, source, part, :].astype(F32) for source in range(HIST)]
            for stream in range(STREAMS):
                total = sum(
                    sources[source] * weight[stream * HIST + source][None, :] for source in range(HIST)
                )
                mixed[step, stream, part, :] = total.astype(BF16)

        @pl.when(step > 0)
        def _():
            send(step).start()

    chunk = min(256, depth)

    def lanes(near, core, half_at, count):
        return at(near * 4 * half + core * 2 * half + half_at * half, count * half, half)

    def act_keep(stream):
        return pltpu.make_async_copy(
            act.at[stream], o_act.at[stream, :, lanes(here.near, here.core, tensor, 1)], act_local.at[stream]
        )

    def act_near(stream):
        return remote(
            act.at[stream], o_act.at[stream, :, lanes(here.near, here.core, tensor, 1)],
            act_s.at[0, stream], act_r.at[0, stream], dp=flip(me, NEAR),
        )

    def act_tensor(stream, second):
        span = lanes(1 - here.near if second else here.near, here.core, tensor, 1)
        return remote(
            o_act.at[stream, :, span] if second else act.at[stream], o_act.at[stream, :, span],
            act_s.at[1 + second, stream], act_r.at[1 + second, stream], tensor=here.other,
        )

    def act_core(stream, near):
        span = lanes(near, here.core, 0, 2)
        return remote(
            o_act.at[stream, :, span], o_act.at[stream, :, span],
            act_s.at[3 + near, stream], act_r.at[3 + near, stream], dp=flip(me, CORE),
        )

    def normalise_stream(stream):
        block = 0 if stream < 3 else 1

        def piece(index):
            return streams[stream, at(index * chunk, chunk), :].astype(F32)

        centre = sum_rows(piece, depth, chunk, lambda v: v) / depth
        spread = sum_rows(piece, depth, chunk, lambda v: (v - centre) * (v - centre)) / depth
        root = lax.rsqrt(spread + NORM_EPS)

        def normalise(index):
            span = chunk // rows
            first = index * span
            column = jnp.concatenate(
                [
                    small_all[
                        lax.div(first + k, HIGH), bit(first + k, NEAR), bit(first + k, SIDE), bit(first + k, CORE)
                    ]
                    for k in range(span)
                ],
                axis=0,
            ).astype(F32)
            gain = column[:, MIXH + block : MIXH + block + 1]
            bias = column[:, MIXH + 2 + block : MIXH + 3 + block]
            act[stream, at(index * chunk, chunk), :] = (
                (piece(index) - centre) * root * gain + bias
            ).astype(BF16)

        loop(0, depth // chunk, normalise)
        act_keep(stream).start()

    finals = [
        pltpu.make_async_copy(small_all, o_small, out_sem.at[1]),
        pltpu.make_async_copy(streams, o_streams, out_sem.at[2]),
    ]
    early_pairs = ((0, mix_all), (1, small_all))
    last = high_bits + 2

    def first(array):
        keep(array).start()
        for peer in range(3):
            reshard(array, peer).start()

    def second(array):
        keep(array).wait()
        for peer in range(3):
            reshard(array, peer).wait()
        high_hop(array, 0).start()

    def third(array):
        for phase in range(high_bits):
            high_hop(array, phase).wait()
            if phase + 1 < high_bits:
                high_hop(array, phase + 1).start()
        side_hop(array).start()

    def act_first(stream):
        act_near(stream).wait()
        act_tensor(stream, 1).start()
        if stream + 1 < STREAMS:
            act_near(stream + 1).start()
        if stream and stream + 1 < STREAMS:
            act_tensor(stream + 1, 0).start()

    def act_second(stream):
        act_keep(stream).wait()
        act_tensor(stream, 0).wait()
        act_tensor(stream, 1).wait()
        for near in range(2):
            act_core(stream, near).start()

    own_mix.start()
    small_all[here.high, here.near, here.side, here.core] = small[...].T
    own_mix.wait()
    for which, buf in early_pairs:
        early(which, buf, 0).start()
    total = len(units)

    def tick(unit):
        third(unit)
        if unit + 3 < total:
            first(unit + 3)
        if unit + 1 < total:
            second(unit + 1)

    for unit in range(min(3, total)):
        first(unit)
    for phase in range(1, last + 1):
        for which, buf in early_pairs:
            early(which, buf, phase - 1).wait()
            early(which, buf, phase).start()
        if phase == 1:
            second(0)
    early(0, mix_all, last).wait()
    def mix_lanes(index):
        return mix_all.at[lax.div(index, HIGH), bit(index, NEAR), bit(index, SIDE), bit(index, CORE)], o_mix.at[
            :, at(index * 2 * half + tensor * half, half)
        ]

    def mix_copy(index):
        source, target = mix_lanes(index)
        return pltpu.make_async_copy(source, target, share_l.at[index])

    def mix_share(index):
        source, target = mix_lanes(index)
        return remote(source, target, share_s.at[index], share_r.at[index], tensor=here.other)

    def mix_out(index):
        mix_copy(index).start()
        mix_share(index).start()

    loop(0, n_dp, mix_out)
    loop(0, n_dp, mix_step)
    streams[:, at(me * rows, rows), :] = mixed[0]
    early(1, small_all, last).wait()
    done = 0

    def ticks(count):
        nonlocal done
        for unit in range(done, min(done + count, total)):
            tick(unit)
        done = min(done + count, total)

    ticks(3)
    loop(1, n_dp, lambda step: send(step).wait())
    for stream in range(STREAMS):
        normalise_stream(stream)
        if stream == 0:
            act_near(0).start()
        if stream < 2:
            act_tensor(stream, 0).start()
    for copy in finals:
        copy.start()
    depth, tokens = act_in.shape[1:]
    seq_len = 2 * half
    heads = context.shape[0] // HD
    tile = 256

    def act_load(stream):
        return pltpu.make_async_copy(o_act.at[stream], act_in.at[stream], load_sem.at[stream])

    def act_third(stream):
        for near in range(2):
            act_core(stream, near).wait()
        act_load(stream).start()

    loads = {
        "qkv": pltpu.make_async_copy(o_qkv.reshape(3, depth, qkv_in.shape[2]), qkv_in, load_sem.at[4]),
        "out": pltpu.make_async_copy(o_out.reshape(depth, out_in.shape[1]), out_in, load_sem.at[5]),
        "up": pltpu.make_async_copy(o_up.reshape(depth, up_in.shape[1]), up_in, load_sem.at[6]),
        "down": pltpu.make_async_copy(o_down.reshape(depth, down_in.shape[1]), down_in, load_sem.at[7]),
    }
    held = 0

    def arrive(count):
        nonlocal held
        ticks(max(held + count - done, 0))
        for unit in range(held, held + count):
            side_hop(unit).wait()
        held += count

    def project(stream):
        act_load(stream).wait()
        values = tn(qkv_in[stream], act_in[stream])
        if stream < 2:
            values = turned(values, cos[...], sin[...])
        rows_out[stream] = values.astype(BF16)

    def attend(seq):
        span = at(seq * seq_len, seq_len)
        for head in range(heads):
            lane = pl.ds(head * HD, HD)
            scores = causal_scores(rows_out[1, lane, span], rows_out[0, lane, span])
            peak = jnp.max(scores, axis=0, keepdims=True)
            raised = jnp.exp(scores - peak)
            total_weight = jnp.sum(raised, axis=0, keepdims=True)
            prob = (raised / total_weight).astype(BF16)
            context[lane, span] = nn(rows_out[2, lane, span], prob).astype(BF16)
            sums[pl.ds(seq * heads + head, 1), :] = peak + jnp.log(total_weight)

    def raise_up(index):
        span = at(index * tile, tile)
        value, derivative = gelu_parts(tn(up_in[:, span], act_in[3]))
        hidden[span, :] = value.astype(BF16)
        slope[span, :] = derivative

    def lower(index):
        span = at(index * tile, tile)
        part[span, :] = (nn(out_in[span, :], context[...]) + nn(down_in[span, :], hidden[...])).astype(BF16)

    saves = []

    def save(*pairs):
        for source, target in pairs:
            copy = pltpu.make_async_copy(source, target, save_sem.at[len(saves)])
            copy.start()
            saves.append(copy)

    def rows_arrive(_):
        arrive(4)
        loads["qkv"].start()
        loads["out"].start()
        loads["qkv"].wait()

    def attend_all(_):
        loop(0, tokens // seq_len, attend)
        save((rows_out, o_rows), (context, o_context), (sums, o_sums))

    def raise_all(_):
        arrive(up_in.shape[1] // UNIT)
        loads["up"].start()
        act_load(3).wait()
        loads["up"].wait()
        loop(0, hidden.shape[0] // tile, raise_up)
        save((hidden, o_hidden), (slope, o_slope))

    actions = {
        "n": act_first, "s": act_second, "t": act_third, "w": rows_arrive, "p": project, "a": attend_all, "u": raise_all
    }
    for action in PLAN:
        if action == "T":
            ticks(1)
        else:
            actions[action[0]](int(action[1]))
    arrive(total - held)
    loads["down"].start()
    loads["out"].wait()
    loads["down"].wait()
    loop(0, depth // tile, lower)
    save((part, o_part))
    for copy in finals + saves:
        copy.wait()

    def settle(index):
        mix_copy(index).wait()
        mix_share(index).wait()

    loop(0, n_dp, settle)


def gather(n_dp, hist, mix, small, w_qkv, w_out, w_up, w_down, cos, sin):
    rows = small.shape[1]
    depth = rows * n_dp
    half = hist.shape[2] // n_dp // 2
    high = n_dp // HIGH
    high_bits = int(math.log2(high))
    grid = (high, 2, 2, 2)
    units = sum(w.size // w.shape[-2] for w in (w_qkv, w_out, w_up, w_down)) // QUARTERS // UNIT

    def cut(width):
        return (high, 2, 2, 2 * rows, width // QUARTERS)

    tokens = 8 * half
    narrow, width = w_qkv.shape[2] // QUARTERS, w_up.shape[1] // QUARTERS
    results = [
        ((3, narrow, tokens), BF16),
        ((narrow, tokens), BF16),
        ((tokens // (2 * half) * (narrow // HD), 2 * half), F32),
        ((width, tokens), BF16),
        ((width, tokens), F32),
        ((depth, tokens), BF16),
    ]
    shapes = [
        ((mix.shape[0], n_dp * 2 * half), F32),
        (grid + (rows, 128), BF16),
        ((STREAMS, depth, half), BF16),
        ((STREAMS, depth, tokens), BF16),
        ((3,) + cut(w_qkv.shape[2]), BF16),
        (cut(w_out.shape[1]), BF16),
        (cut(w_up.shape[1]), BF16),
        (cut(w_down.shape[1]), BF16),
    ] + results
    return pl.pallas_call(
        functools.partial(gather_kernel, n_dp),
        out_shape=[jax.ShapeDtypeStruct(*shape) for shape in shapes],
        in_specs=[ANY, ANY, VM] + [ANY] * 4 + [VM] * 2,
        out_specs=[ANY] * 14,
        scratch_shapes=[
            pltpu.VMEM(grid + mix.shape, F32),
            pltpu.VMEM(grid + (rows, 128), BF16),
            pltpu.VMEM((2, HIST, rows, half), BF16),
            pltpu.VMEM((n_dp, STREAMS, rows, half), BF16),
            pltpu.VMEM((STREAMS, depth, half), BF16),
            pltpu.VMEM((STREAMS, depth, half), BF16),
            DMA((2, high_bits + 3)),
            DMA((2, high_bits + 3)),
            DMA((2,)),
            DMA((n_dp,)),
            DMA((n_dp,)),
            DMA((units, 3)),
            DMA((units, 3)),
            DMA((units, high_bits)),
            DMA((units, high_bits)),
            DMA((units,)),
            DMA((units,)),
            DMA((5, STREAMS)),
            DMA((5, STREAMS)),
            DMA((STREAMS,)),
            DMA((2 + units,)),
            DMA((3,)),
            DMA((n_dp,)),
            DMA((n_dp,)),
            DMA((n_dp,)),
            pltpu.VMEM((STREAMS, depth, tokens), BF16),
            pltpu.VMEM((3, depth, narrow), BF16),
            pltpu.VMEM((depth, narrow), BF16),
            pltpu.VMEM((depth, width), BF16),
            pltpu.VMEM((depth, width), BF16),
        ]
        + [pltpu.VMEM(*shape) for shape in results]
        + [DMA((8,)), DMA((6,))],
        compiler_params=pltpu.CompilerParams(
            collective_id=1, has_side_effects=True, vmem_limit_bytes=61 * 1024 * 1024
        ),
        name="gather",
    )(hist, mix, small, w_qkv, w_out, w_up, w_down, cos, sin)


def lane_block(half, near, core, half_at, count):
    return at(near * 4 * half + core * 2 * half + half_at * half, count * half, half)


def gelu_parts(values):
    phi = 0.5 * (1.0 + lax.erf(values * (1.0 / math.sqrt(2.0))))
    density = jnp.exp(-0.5 * values * values) * (1.0 / math.sqrt(2.0 * math.pi))
    return values * phi, phi + values * density


def reduce_group(here, half, part, theirs, own, from_core, from_tensor, from_near, sems, local, pieces, piece):
    core_s, core_r, tensor_s, tensor_r, near_s, near_r = sems

    def load(span, near, half_at):
        return pltpu.make_async_copy(
            part.at[piece(span), lane_block(half, near, here.core, half_at, 1)],
            own.at[near, half_at, piece(span)], local.at[span, near * 2 + half_at],
        )

    def to_core(span, near, half_at):
        return remote(
            part.at[piece(span), lane_block(half, near, 1 - here.core, half_at, 1)],
            from_core.at[near, half_at, piece(span)],
            core_s.at[span, near * 2 + half_at], core_r.at[span, near * 2 + half_at], dp=flip(here.me, CORE),
        )

    def to_tensor(span, near):
        return remote(
            own.at[near, here.other, piece(span)], from_tensor.at[near, piece(span)],
            tensor_s.at[span, near], tensor_r.at[span, near], tensor=here.other,
        )

    def to_near(span):
        return remote(
            from_tensor.at[1 - here.near, piece(span)], from_near.at[piece(span)],
            near_s.at[span], near_r.at[span], dp=flip(here.me, NEAR),
        )

    def start(span):
        for near in range(2):
            for half_at in range(2):
                to_core(span, near, half_at).start()
                load(span, near, half_at).start()

    def after_core(span):
        for near in range(2):
            for half_at in range(2):
                load(span, near, half_at).wait()
                to_core(span, near, half_at).wait()
            own[near, here.other, piece(span)] += from_core[near, here.other, piece(span)]
            to_tensor(span, near).start()
        for near in range(2):
            own[near, here.tensor, piece(span)] += from_core[near, here.tensor, piece(span)]

    def after_tensor(span):
        for near in range(2):
            to_tensor(span, near).wait()
        far = 1 - here.near
        from_tensor[far, piece(span)] += own[far, here.tensor, piece(span)]
        to_near(span).start()
        from_tensor[here.near, piece(span)] += own[here.near, here.tensor, piece(span)]

    def after_near(span):
        to_near(span).wait()

    return start, after_core, after_tensor, after_near


def join_kernel(
    part, streams, cot, small, mix_in, mix_out, mix_back, static, next_cot,
    o_grad, o_wide, o_block, o_next, o_mixin, o_tiny,
    own, from_core, from_tensor, from_near, residual, wide, normed, block, back, low, next_rows, mixin, tiny,
    core_s, core_r, tensor_s, tensor_r, near_s, near_r, local, share_s, share_r, own_sem,
):
    here = Place()
    me, tensor = here.me, here.tensor
    depth, half = cot.shape
    spans = core_s.shape[0]
    size = depth // spans
    chunk = 256
    greet([{"dp": flip(me, CORE)}, {"dp": flip(me, NEAR)}, {"tensor": here.other}])

    def piece(span):
        return pl.ds(span * size, size)

    start, after_core, after_tensor, after_near = reduce_group(
        here, half, part, None, own, from_core, from_tensor, from_near,
        (core_s, core_r, tensor_s, tensor_r, near_s, near_r), local, spans, piece,
    )
    fetch = pltpu.make_async_copy(streams.at[3], residual, own_sem.at[0])
    fetch.start()
    for span in range(spans):
        start(span)
    for span in range(spans):
        after_core(span)
    for span in range(spans):
        after_tensor(span)
    fetch.wait()
    squares = jnp.zeros((1, half), F32)
    for span in range(spans):
        after_near(span)

        def widen(index, total):
            rows = at(span * size + index * chunk, chunk)
            branch = from_tensor[here.near, rows, :].astype(F32) + from_near[rows, :].astype(F32)
            value = residual[rows, :].astype(F32) + branch
            wide[rows, :] = value
            block[rows, :] = value.astype(BF16)
            return total + jnp.sum(value * value, axis=0, keepdims=True)

        squares = lax.fori_loop(0, size // chunk, widen, squares)
    root = lax.rsqrt(squares / depth + ROOT_EPS)

    def share_block(which):
        lanes = at(tensor * half, half)
        if which == 0:
            return pltpu.make_async_copy(block, o_block.at[:, lanes], own_sem.at[1])
        return remote(block, o_block.at[:, lanes], share_s.at[0], share_r.at[0], tensor=here.other)

    share_block(0).start()
    share_block(1).start()

    def norm(index):
        rows = at(index * chunk, chunk)
        normed[rows, :] = (wide[rows, :] * root).astype(BF16)

    loop(0, depth // chunk, norm)
    inner, slope = gelu_parts(jnp.dot(mix_in[...], normed[...], preferred_element_type=F32))
    inner_low = inner.astype(BF16)
    next_rows[...] = (jnp.dot(mix_out[...], inner_low, preferred_element_type=F32) + static[...])[:MIXH]
    next_low = next_cot[...].astype(BF16)

    def nt(left, right):
        return lax.dot_general(left, right, (((1,), (1,)), ((), ())), preferred_element_type=F32)

    tiny[:, :128] = nt(inner_low, next_low)
    tiny[:, 128:] = jnp.broadcast_to(jnp.sum(next_cot[...], axis=1, keepdims=True), (128, 128))
    inner_grad = (jnp.dot(mix_back[...], next_low, preferred_element_type=F32) * slope).astype(BF16)

    def pull(index, total):
        rows = at(index * chunk, chunk)
        value = jnp.dot(small[rows, :], inner_grad, preferred_element_type=F32)
        back[rows, :] = value
        return total + jnp.sum(value * wide[rows, :] * root, axis=0, keepdims=True)

    along = lax.fori_loop(0, depth // chunk, pull, jnp.zeros((1, half), F32)) / depth

    def finish(index):
        rows = at(index * chunk, chunk)
        value = cot[rows, :].astype(F32) + root * (back[rows, :] - wide[rows, :] * root * along)
        back[rows, :] = value
        low[rows, :] = value.astype(BF16)

    loop(0, depth // chunk, finish)

    def share(kind, index):
        if kind == 0:
            source, lanes, where = low, lane_block(half, here.near, here.core, tensor, 1), {"dp": flip(me, NEAR)}
        elif kind == 1:
            lanes = lane_block(half, 1 - here.near if index else here.near, here.core, tensor, 1)
            source, where = (o_grad.at[:, lanes] if index else low), {"tensor": here.other}
        else:
            lanes, where = lane_block(half, index, here.core, 0, 2), {"dp": flip(me, CORE)}
            source = o_grad.at[:, lanes]
        number = 1 + 2 * kind + index
        return remote(source, o_grad.at[:, lanes], share_s.at[number], share_r.at[number], **where)

    share(0, 0).start()
    share(1, 0).start()
    keep = pltpu.make_async_copy(
        low, o_grad.at[:, lane_block(half, here.near, here.core, tensor, 1)], own_sem.at[2]
    )
    keep.start()

    def mixin_rows(index):
        rows = at(index * chunk, chunk)
        mixin[rows, :] = nt(normed[rows, :], inner_grad)

    loop(0, depth // chunk, mixin_rows)
    share(0, 0).wait()
    share(1, 1).start()
    lanes = at(tensor * half, half)
    next_share = remote(next_rows, o_next.at[:, lanes], share_s.at[7], share_r.at[7], tensor=here.other)
    next_share.start()
    finals = [
        pltpu.make_async_copy(next_rows, o_next.at[:, lanes], own_sem.at[3]),
        pltpu.make_async_copy(back, o_wide, own_sem.at[4]),
        pltpu.make_async_copy(mixin, o_mixin, own_sem.at[5]),
        pltpu.make_async_copy(tiny, o_tiny, own_sem.at[6]),
    ]
    for copy in finals:
        copy.start()
    keep.wait()
    share(1, 0).wait()
    share(1, 1).wait()
    for near in range(2):
        share(2, near).start()
    for near in range(2):
        share(2, near).wait()
    share_block(0).wait()
    share_block(1).wait()
    next_share.wait()
    for copy in finals:
        copy.wait()


def join(part, streams, cot, small, mix_in, mix_out, mix_back, static, next_cot):
    depth, half = cot.shape
    spans = 4
    shapes = [
        ((depth, 8 * half), BF16),
        ((depth, half), F32),
        ((depth, 2 * half), BF16),
        ((MIXH, 2 * half), F32),
        ((depth, 128), F32),
        ((128, 256), F32),
    ]
    return pl.pallas_call(
        join_kernel,
        out_shape=[jax.ShapeDtypeStruct(*shape) for shape in shapes],
        in_specs=[ANY, ANY] + [VM] * 7,
        out_specs=[ANY] * 6,
        scratch_shapes=[
            pltpu.VMEM((2, 2, depth, half), BF16),
            pltpu.VMEM((2, 2, depth, half), BF16),
            pltpu.VMEM((2, depth, half), BF16),
            pltpu.VMEM((depth, half), BF16),
            pltpu.VMEM((depth, half), BF16),
            pltpu.VMEM((depth, half), F32),
            pltpu.VMEM((depth, half), BF16),
            pltpu.VMEM((depth, half), BF16),
            pltpu.VMEM((depth, half), F32),
            pltpu.VMEM((depth, half), BF16),
            pltpu.VMEM((MIXH, half), F32),
            pltpu.VMEM((depth, 128), F32),
            pltpu.VMEM((128, 256), F32),
            DMA((spans, 4)),
            DMA((spans, 4)),
            DMA((spans, 2)),
            DMA((spans, 2)),
            DMA((spans,)),
            DMA((spans,)),
            DMA((spans, 4)),
            DMA((8,)),
            DMA((8,)),
            DMA((7,)),
        ],
        compiler_params=pltpu.CompilerParams(
            collective_id=2, has_side_effects=True, vmem_limit_bytes=40 * 1024 * 1024
        ),
        name="join",
    )(part, streams, cot, small, mix_in, mix_out, mix_back, static, next_cot)


def scatter_kernel(
    n_dp, attn_grad, mlp_grad, streams, small, wide_grad, mixin_part, hist, g_qkv, g_up, g_down, g_out,
    o_stream, o_mix, o_small, o_qkv, o_up, o_down, o_out,
    own, from_core, from_tensor, from_near, rows_in, wide, stream_grad, gains, biases, tiny, tiny_in, tiny_out,
    hist_in, arrived, mix_part, mix_in, mix_sum, tiny_sum,
    side_qkv, side_up, side_down, side_out, mine_qkv, mine_up, mine_down, mine_out,
    high_qkv, high_up, high_down, high_out,
    core_s, core_r, tensor_s, tensor_r, near_s, near_r, local, in_sem,
    side_s, side_r, side_local, high_s, high_r, peer_s, peer_r, peer_local,
    a2a_s, a2a_r, keep_sem, pass_s, pass_r, tiny_s, tiny_r, mix_s, mix_r, hist_sem, last_s, last_r, last_local,
):
    here = Place()
    me, tensor = here.me, here.tensor
    depth, half = wide_grad.shape
    rows = depth // n_dp
    high_bits = int(math.log2(n_dp // HIGH))
    chunk = min(256, depth)
    greet_all(n_dp, me, here.other)
    weights = (
        (g_qkv, side_qkv, mine_qkv, high_qkv, o_qkv),
        (g_up, side_up, mine_up, high_up, o_up),
        (g_down, side_down, mine_down, high_down, o_down),
        (g_out, side_out, mine_out, high_out, o_out),
    )

    def pick(ref, *index):
        return ref.at[(slice(None),) + index] if ref.shape[0] == 3 and len(ref.shape) > len(index) + 2 else ref.at[index]

    def everything(_):
        return pl.ds(0, depth)

    steps = []
    for stream in range(STREAMS):
        part = attn_grad.at[stream] if stream < 3 else mlp_grad
        steps.append(
            reduce_group(
                here, half, part, None, own.at[stream], from_core.at[stream], from_tensor.at[stream],
                from_near.at[stream],
                tuple(
                    sem.at[pl.ds(stream, 1)]
                    for sem in (core_s, core_r, tensor_s, tensor_r, near_s, near_r)
                ),
                local.at[pl.ds(stream, 1)], 1, everything,
            )
        )
    for stream in range(STREAMS):
        steps[stream][0](0)
    loads = [
        pltpu.make_async_copy(streams, rows_in, in_sem.at[0]),
        pltpu.make_async_copy(wide_grad, wide, in_sem.at[1]),
    ]
    for copy in loads:
        copy.start()

    def is_qkv(array):
        return array == 0

    def index_of(array, *index):
        return ((slice(None),) if is_qkv(array) else ()) + index

    def side_hop(array):
        g, side, _, _, _ = weights[array]
        return remote(
            g.at[index_of(array, slice(None), slice(None), 1 - here.side)], side, side_s.at[array], side_r.at[array],
            dp=flip(me, SIDE),
        )

    def side_load(array):
        g, _, mine, _, _ = weights[array]
        return pltpu.make_async_copy(
            g.at[index_of(array, slice(None), slice(None), here.side)], mine, side_local.at[array]
        )

    def high_hop(array, phase):
        _, _, mine, high, _ = weights[array]
        span = 1 << phase
        base = lax.div(here.high, span)
        theirs = base + 1 - 2 * lax.rem(base, 2)
        return remote(
            mine.at[index_of(array, pl.ds(theirs * span, span))], high.at[index_of(array, pl.ds(span - 1, span))],
            high_s.at[array, phase], high_r.at[array, phase], dp=flip(me, HIGH << phase),
        )

    def add_blocks(array, into, other, first_into, first_other, count):
        shape = into.shape
        tall, width = shape[-2:]
        outer = 3 if is_qkv(array) else 1
        step = 32

        def add(flat):
            lead = lax.div(flat, count * 2)
            rest = lax.rem(flat, count * 2)
            high, near = lax.div(rest, 2), lax.rem(rest, 2)
            prefix = (lead,) if is_qkv(array) else ()

            def tile(index):
                span = at(index * step, step)
                into[prefix + (first_into + high, near, span)] += other[prefix + (first_other + high, near, span)]

            loop(0, tall // step, tile)

        loop(0, outer * count * 2, add)

    for array in range(4):
        side_hop(array).start()
        side_load(array).start()
    for copy in loads:
        copy.wait()
    stats = []
    for stream in range(STREAMS):

        def piece(index):
            return rows_in[stream, at(index * chunk, chunk), :].astype(F32)

        centre = sum_rows(piece, depth, chunk, lambda v: v) / depth
        spread = sum_rows(piece, depth, chunk, lambda v: (v - centre) * (v - centre)) / depth
        stats.append((centre, lax.rsqrt(spread + NORM_EPS)))
    for stream in range(STREAMS):
        steps[stream][1](0)
    for array in range(4):
        side_load(array).wait()
        side_hop(array).wait()
        _, side, mine, _, _ = weights[array]
        add_blocks(array, mine, side, 0, 0, n_dp // HIGH)
        high_hop(array, high_bits - 1).start()
    for stream in range(STREAMS):
        steps[stream][2](0)

    for stream in range(STREAMS):
        steps[stream][3](0)
        group = 0 if stream < 3 else 1
        centre, root = stats[stream]

        def parts(index):
            span = at(index * chunk, chunk)
            grad = from_tensor[stream, here.near, span].astype(F32) + from_near[stream, span].astype(F32)
            hat = (rows_in[stream, span, :].astype(F32) - centre) * root
            gain = small[span, MIXH + group : MIXH + group + 1].astype(F32)
            return span, grad, hat, grad * gain

        def sums(index, carry):
            span, grad, hat, scaled = parts(index)
            if stream in (0, 3):
                gains[group, span] = grad * hat
                biases[group, span] = grad
            else:
                gains[group, span] += grad * hat
                biases[group, span] += grad
            return (
                carry[0] + jnp.sum(scaled, axis=0, keepdims=True),
                carry[1] + jnp.sum(scaled * hat, axis=0, keepdims=True),
            )

        zero = jnp.zeros((1, half), F32)
        total, along = lax.fori_loop(0, depth // chunk, sums, (zero, zero))

        def finish(index):
            span, grad, hat, scaled = parts(index)
            value = root * (scaled - total / depth - hat * (along / depth))
            if stream == 3:
                value = value + wide[span, :]
            stream_grad[stream, span] = value.astype(BF16)

        loop(0, depth // chunk, finish)

    def send(step):
        target = lax.rem(me + step, n_dp)
        return remote(
            stream_grad.at[:, at(target * rows, rows), :], arrived.at[step], a2a_s.at[step], a2a_r.at[step], dp=target
        )

    loop(1, n_dp, lambda step: send(step).start())

    def fetch(step, buf):
        source = lax.rem(me - step + n_dp, n_dp)
        return pltpu.make_async_copy(
            hist.at[:, :, at(source * 2 * half + tensor * half, half)], hist_in.at[buf], hist_sem.at[buf]
        )

    fetch(0, 0).start()
    own_block = pltpu.make_async_copy(stream_grad.at[:, at(me * rows, rows), :], arrived.at[0], last_local.at[0])
    own_block.start()

    column = lax.broadcasted_iota(jnp.int32, (chunk, 128), 1)

    def gather_tiny(index):
        span = at(index * chunk, chunk)
        value = mixin_part[span, :]
        for group in range(2):
            gain = jnp.sum(gains[group, span], axis=1, keepdims=True)
            bias = jnp.sum(biases[group, span], axis=1, keepdims=True)
            value = jnp.where(column == MIXH + group, gain, value)
            value = jnp.where(column == MIXH + 2 + group, bias, value)
        tiny[span, :] = value.astype(BF16)

    loop(0, depth // chunk, gather_tiny)

    def tiny_send(step):
        target = lax.rem(me + step, n_dp)
        return remote(tiny.at[at(target * rows, rows), :], tiny_in.at[step], tiny_s.at[step], tiny_r.at[step], dp=target)

    loop(1, n_dp, lambda step: tiny_send(step).start())

    for array in range(4):
        _, _, mine, high, _ = weights[array]
        for phase in reversed(range(high_bits)):
            high_hop(array, phase).wait()
            span = 1 << phase
            add_blocks(array, mine, high, lax.div(here.high, span) * span, span - 1, span)
            if phase:
                high_hop(array, phase - 1).start()

    def peer_hop(array, peer):
        _, _, mine, _, out = weights[array]
        width = mine.shape[-1]
        target, _ = here.peers[peer]
        core = bit(target, CORE)
        return remote(
            mine.at[index_of(array, here.high, bit(target, NEAR), at(core * rows, rows))],
            out.at[index_of(array, slice(None), at(here.quarter * width, width))],
            peer_s.at[array, peer], peer_r.at[array, peer], dp=target,
        )

    def peer_keep(array):
        _, _, mine, _, out = weights[array]
        width = mine.shape[-1]
        return pltpu.make_async_copy(
            mine.at[index_of(array, here.high, here.near, at(here.core * rows, rows))],
            out.at[index_of(array, slice(None), at(here.quarter * width, width))], peer_local.at[array],
        )

    for array in range(4):
        peer_keep(array).start()
        for peer in range(3):
            peer_hop(array, peer).start()
    own_block.wait()

    def keep_lanes(step):
        source = lax.rem(me - step + n_dp, n_dp)
        return at(source * 2 * half + tensor * half, half)

    def keep(step):
        return pltpu.make_async_copy(arrived.at[step], o_stream.at[:, :, keep_lanes(step)], keep_sem.at[step])

    def pass_on(step):
        return remote(
            arrived.at[step], o_stream.at[:, :, keep_lanes(step)], pass_s.at[step], pass_r.at[step], tensor=here.other
        )

    def mix_send(step):
        return remote(
            mix_part.at[step], mix_in.at[step], mix_s.at[step], mix_r.at[step], dp=lax.rem(me - step + n_dp, n_dp)
        )

    def receive(step):
        buf = lax.rem(step, 2)

        @pl.when(step + 1 < n_dp)
        def _():
            fetch(step + 1, 1 - buf).start()

        @pl.when(step > 0)
        def _():
            send(step).wait()

        keep(step).start()
        pass_on(step).start()
        fetch(step, buf).wait()
        for stream in range(STREAMS):
            totals = [jnp.zeros((8, half), F32) for _ in range(HIST)]
            for row in range(0, rows, 16):
                span = pl.ds(row, 16)
                grad = arrived[step, stream, span, :].astype(F32)
                for source in range(HIST):
                    product = grad * hist_in[buf, source, span, :].astype(F32)
                    totals[source] = totals[source] + product[:8] + product[8:]
            for source in range(HIST):
                mix_part[step, pl.ds(stream * HIST + source, 1), :] = jnp.sum(totals[source], axis=0, keepdims=True)

        @pl.when(step > 0)
        def _():
            mix_send(step).start()

    mix_part[0] = jnp.zeros_like(mix_part[0])
    loop(0, n_dp, receive)

    mix_sum[...] = mix_part[0]

    def add_mix(step):
        mix_send(step).wait()
        mix_sum[...] += mix_in[step]

    loop(1, n_dp, add_mix)
    lanes = at(tensor * half, half)
    mix_share = remote(mix_sum, o_mix.at[:, lanes], last_s.at[0], last_r.at[0], tensor=here.other)
    mix_keep = pltpu.make_async_copy(mix_sum, o_mix.at[:, lanes], last_local.at[1])
    mix_share.start()
    mix_keep.start()
    tiny_sum[0] = tiny[at(me * rows, rows), :].astype(F32)

    def add_tiny(step):
        tiny_send(step).wait()
        tiny_sum[0] += tiny_in[step].astype(F32)

    loop(1, n_dp, add_tiny)
    tiny_share = remote(tiny_sum.at[0], tiny_sum.at[1], last_s.at[1], last_r.at[1], tensor=here.other)
    tiny_share.start()
    tiny_share.wait()
    tiny_out[...] = tiny_sum[0] + tiny_sum[1]
    tiny_keep = pltpu.make_async_copy(tiny_out, o_small, last_local.at[2])
    tiny_keep.start()
    for array in range(4):
        peer_keep(array).wait()
        for peer in range(3):
            peer_hop(array, peer).wait()

    def settle(step):
        keep(step).wait()
        pass_on(step).wait()

    loop(0, n_dp, settle)
    mix_share.wait()
    mix_keep.wait()
    tiny_keep.wait()


def scatter(n_dp, attn_grad, mlp_grad, streams, small, wide_grad, mixin_part, hist, g_qkv, g_up, g_down, g_out):
    depth, half = wide_grad.shape
    rows = depth // n_dp
    high = n_dp // HIGH
    high_bits = int(math.log2(high))
    grads = (g_qkv, g_up, g_down, g_out)

    def lead(g):
        return (3,) if g.ndim == 6 else ()

    def halved(g, highs):
        return lead(g) + (highs, 2) + g.shape[-2:]

    outs = [
        ((STREAMS, rows, 2 * half * n_dp), BF16),
        ((MIXH, 2 * half), F32),
        ((rows, 128), F32),
    ] + [(lead(g) + (rows, QUARTERS * g.shape[-1]), BF16) for g in grads]
    return pl.pallas_call(
        functools.partial(scatter_kernel, n_dp),
        out_shape=[jax.ShapeDtypeStruct(*shape) for shape in outs],
        in_specs=[ANY, ANY, ANY, VM, ANY, VM, ANY] + [ANY] * 4,
        out_specs=[ANY] * 7,
        scratch_shapes=[
            pltpu.VMEM((STREAMS, 2, 2, depth, half), BF16),
            pltpu.VMEM((STREAMS, 2, 2, depth, half), BF16),
            pltpu.VMEM((STREAMS, 2, depth, half), BF16),
            pltpu.VMEM((STREAMS, depth, half), BF16),
            pltpu.VMEM((STREAMS, depth, half), BF16),
            pltpu.VMEM((depth, half), F32),
            pltpu.VMEM((STREAMS, depth, half), BF16),
            pltpu.VMEM((2, depth, half), F32),
            pltpu.VMEM((2, depth, half), F32),
            pltpu.VMEM((depth, 128), BF16),
            pltpu.VMEM((n_dp, rows, 128), BF16),
            pltpu.VMEM((rows, 128), F32),
            pltpu.VMEM((2, HIST, rows, half), BF16),
            pltpu.VMEM((n_dp, STREAMS, rows, half), BF16),
            pltpu.VMEM((n_dp, MIXH, half), F32),
            pltpu.VMEM((n_dp, MIXH, half), F32),
            pltpu.VMEM((MIXH, half), F32),
            pltpu.VMEM((2, rows, 128), F32),
        ]
        + [pltpu.VMEM(halved(g, high), BF16) for g in grads]
        + [pltpu.VMEM(halved(g, high), BF16) for g in grads]
        + [pltpu.VMEM(halved(g, high - 1), BF16) for g in grads]
        + [
            DMA((STREAMS, 4)),
            DMA((STREAMS, 4)),
            DMA((STREAMS, 2)),
            DMA((STREAMS, 2)),
            DMA((STREAMS,)),
            DMA((STREAMS,)),
            DMA((STREAMS, 4)),
            DMA((2,)),
            DMA((4,)),
            DMA((4,)),
            DMA((4,)),
            DMA((4, high_bits)),
            DMA((4, high_bits)),
            DMA((4, 3)),
            DMA((4, 3)),
            DMA((4,)),
            DMA((n_dp,)),
            DMA((n_dp,)),
            DMA((n_dp,)),
            DMA((n_dp,)),
            DMA((n_dp,)),
            DMA((n_dp,)),
            DMA((n_dp,)),
            DMA((n_dp,)),
            DMA((n_dp,)),
            DMA((2,)),
            DMA((2,)),
            DMA((2,)),
            DMA((3,)),
        ],
        compiler_params=pltpu.CompilerParams(
            collective_id=3, has_side_effects=True, vmem_limit_bytes=60 * 1024 * 1024
        ),
        name="scatter",
    )(attn_grad, mlp_grad, streams, small, wide_grad, mixin_part, hist, *grads)


def exact_gelu(values):
    return jax.nn.gelu(values, approximate=False)


def rotary_tables(length, rotary, float_type):
    half_rot = rotary // 2
    places = jnp.arange(length).astype(float_type)
    frequency = jnp.exp(
        jnp.arange(half_rot).astype(float_type) * (-2.0 * math.log(10000.0) / rotary)
    )
    angles = places[:, None] * frequency[None, :]
    return (jnp.cos(angles), jnp.sin(angles))


def rotate(values, cos_table, sin_table):
    half_rot = cos_table.shape[-1]
    first_half = values[..., :half_rot]
    second = values[..., half_rot : 2 * half_rot]
    return jnp.concatenate(
        [
            first_half * cos_table - second * sin_table,
            second * cos_table + first_half * sin_table,
            values[..., 2 * half_rot :],
        ],
        axis=-1,
    )


def masked_scores(queries, key_rows):
    length = queries.shape[1]
    score_scale = 1.0 / math.sqrt(queries.shape[2])
    causal = lax.broadcasted_iota(jnp.int32, (length, length), 0) >= lax.broadcasted_iota(
        jnp.int32, (length, length), 1
    )
    scores = (
        jnp.einsum("hqd,hkd->hqk", queries, key_rows, preferred_element_type=jnp.float32)
        * score_scale
    )
    return (jnp.where(causal[None], scores, MASKED), score_scale)


def attend_forward(queries, key_rows, value_rows):
    scores, score_scale = masked_scores(queries, key_rows)
    row_peak = jnp.max(scores, axis=-1, keepdims=True)
    raised = jnp.exp(scores - row_peak)
    row_total = jnp.sum(raised, axis=-1, keepdims=True)
    prob_low = (raised / row_total).astype(jnp.bfloat16)
    context = jnp.einsum("hqk,hkd->hqd", prob_low, value_rows, preferred_element_type=jnp.float32)
    return (context.astype(jnp.bfloat16), row_peak + jnp.log(row_total))


def attend_backward(queries, key_rows, value_rows, log_sum, context_grad):
    scores, score_scale = masked_scores(queries, key_rows)
    attn_prob = jnp.exp(scores - log_sum)
    prob_low = attn_prob.astype(jnp.bfloat16)
    value_grad = jnp.einsum(
        "hqk,hqd->hkd", prob_low, context_grad, preferred_element_type=jnp.float32
    )
    prob_grad = jnp.einsum(
        "hqd,hkd->hqk", context_grad, value_rows, preferred_element_type=jnp.float32
    )
    inner_sum = jnp.sum(attn_prob * prob_grad, axis=-1, keepdims=True)
    score_grad = (attn_prob * (prob_grad - inner_sum)).astype(jnp.bfloat16)
    query_grad = (
        jnp.einsum("hqk,hkd->hqd", score_grad, key_rows, preferred_element_type=jnp.float32)
        * score_scale
    )
    key_grad = (
        jnp.einsum("hqk,hqd->hkd", score_grad, queries, preferred_element_type=jnp.float32)
        * score_scale
    )
    return (query_grad, key_grad, value_grad)


def per_device(
    n_dp, history, mix_weights, w_qkv, w_out, w_up, w_down, norm_gain, norm_bias, mix_in, mix_out, mix_static,
    out_cot, next_cot,
):
    tensor = lax.axis_index("tensor")
    seq_len = mix_weights.shape[0]
    half = seq_len // 2
    depth = mix_in.shape[0] * n_dp

    def own_half(rows):
        return lax.dynamic_slice_in_dim(rows, tensor * half, half, 0)

    mix_rows = jnp.pad(own_half(mix_weights.reshape(seq_len, -1)).T, ((0, MIXH - STREAMS * HIST), (0, 0)))
    small = jnp.concatenate([mix_in, norm_gain.T, norm_bias.T], axis=1)
    small = jnp.pad(small, ((0, 0), (0, 128 - small.shape[1])))
    mix_all, small_all, streams, act, qkv, up, down, out = gather(
        n_dp, history, mix_rows, small, w_qkv, w_up, w_down, w_out
    )
    small_all = small_all.reshape(depth, 128)
    qkv, up, down, out = (
        qkv.reshape(3, depth, -1), up.reshape(depth, -1), down.reshape(depth, -1), out.reshape(depth, -1)
    )
    tokens = act.shape[2]
    seqs = tokens // seq_len
    heads = qkv.shape[2] // HD
    projected = jnp.einsum("sdt,sde->ste", act[:3], qkv, preferred_element_type=F32)
    head_rows = jnp.transpose(projected.reshape(3, seqs, seq_len, heads, HD), (0, 1, 3, 2, 4)).reshape(
        3, seqs * heads, seq_len, HD
    )
    cos_table, sin_table = rotary_tables(seq_len, ROT, F32)
    queries = rotate(head_rows[0], cos_table, sin_table).astype(BF16)
    key_rows = rotate(head_rows[1], cos_table, sin_table).astype(BF16)
    value_rows = head_rows[2].astype(BF16)
    context, log_sum = attend_forward(queries, key_rows, value_rows)

    def join_heads(rows):
        return jnp.transpose(rows.reshape(seqs, heads, seq_len, HD), (0, 2, 1, 3)).reshape(tokens, heads * HD)

    context_rows = join_heads(context)
    up_pre = jnp.einsum("dt,df->tf", act[3], up, preferred_element_type=F32)
    hidden_wide, gelu_back = jax.vjp(exact_gelu, up_pre)
    hidden = hidden_wide.astype(BF16)
    part = (
        jnp.einsum("de,te->dt", out, context_rows, preferred_element_type=F32)
        + jnp.einsum("df,tf->dt", down, hidden, preferred_element_type=F32)
    ).astype(BF16)

    def square(values):
        return jnp.pad(values, ((0, 128 - values.shape[0]), (0, 128 - values.shape[1])))

    next_rows = own_half(next_cot.reshape(seq_len, -1)).T
    next_rows = jnp.pad(next_rows, ((0, 128 - next_rows.shape[0]), (0, 0)))
    mix_in_rows = jnp.pad(small_all[:, :MIXH].T, ((0, 128 - MIXH), (0, 0)))
    static = jnp.pad(mix_static[:, None], ((0, 128 - mix_static.shape[0]), (0, 0)))
    branch_grad, wide_grad, block, next_mix, mixin_part, tiny = join(
        part, streams, own_half(out_cot).T, small_all, mix_in_rows, square(mix_out.T), square(mix_out), static,
        next_rows,
    )
    mixout_total, static_total = lax.psum(
        (tiny[:MIXH, : STREAMS * NEXT], tiny[: STREAMS * NEXT, 128]), ("dp", "tensor")
    )
    hidden_grad = jnp.einsum("dt,df->tf", branch_grad, down, preferred_element_type=F32)
    up_grad_low = gelu_back(hidden_grad)[0].astype(BF16)
    mlp_in_grad = jnp.einsum("df,tf->dt", up, up_grad_low, preferred_element_type=F32).astype(BF16)
    context_grad_rows = jnp.einsum("dt,de->te", branch_grad, out, preferred_element_type=F32).astype(BF16)
    context_grad = jnp.transpose(context_grad_rows.reshape(seqs, seq_len, heads, HD), (0, 2, 1, 3)).reshape(
        seqs * heads, seq_len, HD
    )
    query_grad, key_grad, value_grad = attend_backward(queries, key_rows, value_rows, log_sum, context_grad)
    proj_grad = jnp.stack(
        [
            join_heads(rotate(query_grad, cos_table, -sin_table).astype(BF16)),
            join_heads(rotate(key_grad, cos_table, -sin_table).astype(BF16)),
            join_heads(value_grad.astype(BF16)),
        ]
    )
    attn_in_grad = jnp.einsum("sde,ste->sdt", qkv, proj_grad, preferred_element_type=F32).astype(BF16)
    g_qkv = jnp.einsum("sdt,ste->sde", act[:3], proj_grad, preferred_element_type=F32).astype(BF16)
    g_out = jnp.einsum("dt,te->de", branch_grad, context_rows, preferred_element_type=F32).astype(BF16)
    g_up = jnp.einsum("dt,tf->df", act[3], up_grad_low, preferred_element_type=F32).astype(BF16)
    g_down = jnp.einsum("dt,tf->df", branch_grad, hidden, preferred_element_type=F32).astype(BF16)
    grid = (n_dp // HIGH, 2, 2, 2 * mix_in.shape[0])
    stream_grad, mix_grad, small_total, qkv_total, up_total, down_total, out_total = scatter(
        n_dp, attn_in_grad, mlp_in_grad, streams, small_all, wide_grad, mixin_part, history,
        g_qkv.reshape((3,) + grid + (-1,)), g_up.reshape(grid + (-1,)), g_down.reshape(grid + (-1,)),
        g_out.reshape(grid + (-1,)),
    )
    mix_rows = mix_all.reshape(n_dp, MIXH, 1, half)
    mix_rows = lax.all_gather(mix_rows, "tensor", axis=2, tiled=True)
    mix_rows = jnp.transpose(mix_rows, (1, 0, 2, 3)).reshape(MIXH, n_dp * seq_len)
    history_grad = jnp.stack(
        [
            sum(
                mix_rows[stream * HIST + source][None, :] * stream_grad[stream].astype(F32)
                for stream in range(STREAMS)
            )
            for source in range(HIST)
        ]
    ).astype(BF16)
    return (
        block.T,
        next_mix.T.reshape(seq_len, STREAMS, NEXT),
        history_grad,
        mix_grad[: STREAMS * HIST].T.reshape(seq_len, STREAMS, HIST),
        qkv_total.astype(F32),
        out_total.astype(F32),
        up_total.astype(F32),
        down_total.astype(F32),
        small_total[:, MIXH : MIXH + 2].T,
        small_total[:, MIXH + 2 : MIXH + 4].T,
        small_total[:, :MIXH],
        mixout_total,
        static_total,
    )


def solution(mesh):
    return jax.shard_map(
        functools.partial(per_device, mesh.shape["dp"]),
        mesh=mesh,
        in_specs=(
            P(None, "dp", None),
            P("dp", None, None),
            P(None, "dp", "tensor"),
            P("dp", "tensor"),
            P("dp", "tensor"),
            P("dp", "tensor"),
            P(None, "dp"),
            P(None, "dp"),
            P("dp", None),
            P(),
            P(),
            P("dp", None),
            P("dp", None, None),
        ),
        out_specs=(
            P("dp", None),
            P("dp", None, None),
            P(None, "dp", None),
            P("dp", None, None),
            P(None, "dp", "tensor"),
            P("dp", "tensor"),
            P("dp", "tensor"),
            P("dp", "tensor"),
            P(None, "dp"),
            P(None, "dp"),
            P("dp", None),
            P(),
            P(),
        ),
        check_vma=False,
    )


def lane_block(half, near, core, half_at, count):
    return at(near * 4 * half + core * 2 * half + half_at * half, count * half, half)


def join_kernel(
    part, streams, out_cot, small, mix_raw, next_raw,
    o_grad, o_wide, o_block, o_next, o_mixin, o_tiny,
    mix_out, next_cot, own, from_core, from_first, from_second, residual, wide, normed, block, cot, cot_in, back, low, next_rows, mixin, tiny,
    core_s, core_r, first_s, first_r, second_s, second_r, local, share_s, share_r, own_sem,
):
    here = Place()
    me, tensor = here.me, here.tensor
    depth, half = cot.shape
    spans = core_s.shape[0]
    size = depth // spans
    chunk = 256
    greet([{"dp": flip(me, CORE)}, {"dp": flip(me, NEAR)}, {"tensor": here.other}])

    def piece(span):
        return pl.ds(span * size, size)

    def tensor_first(span):
        return span < spans // 2

    def load(span, near, half_at):
        return pltpu.make_async_copy(
            part.at[piece(span), lane_block(half, near, here.core, half_at, 1)],
            own.at[near, half_at, piece(span)], local.at[span, near * 2 + half_at],
        )

    def to_core(span, near, half_at):
        return remote(
            part.at[piece(span), lane_block(half, near, 1 - here.core, half_at, 1)],
            from_core.at[near, half_at, piece(span)],
            core_s.at[span, near * 2 + half_at], core_r.at[span, near * 2 + half_at], dp=flip(me, CORE),
        )

    across = {"tensor": here.other}
    beside = {"dp": flip(me, NEAR)}

    def first_hop(span, block):
        source = own.at[block, here.other, piece(span)] if tensor_first(span) else own.at[1 - here.near, block, piece(span)]
        return remote(
            source, from_first.at[block, piece(span)], first_s.at[span, block], first_r.at[span, block],
            **(across if tensor_first(span) else beside),
        )

    def kept(span):
        return here.near if tensor_first(span) else tensor

    def second_hop(span):
        return remote(
            from_first.at[1 - kept(span), piece(span)], from_second.at[piece(span)], second_s.at[span], second_r.at[span],
            **(beside if tensor_first(span) else across),
        )

    def start(span):
        for near in range(2):
            for half_at in range(2):
                to_core(span, near, half_at).start()
                load(span, near, half_at).start()

    def after_core(span):
        for near in range(2):
            for half_at in range(2):
                load(span, near, half_at).wait()
                to_core(span, near, half_at).wait()
                own[near, half_at, piece(span)] += from_core[near, half_at, piece(span)]
        for block in range(2):
            first_hop(span, block).start()

    def after_first(span):
        for block in range(2):
            first_hop(span, block).wait()

        def add(block):
            mine = own[block, tensor, piece(span)] if tensor_first(span) else own[here.near, block, piece(span)]
            from_first[block, piece(span)] += mine

        add(1 - kept(span))
        second_hop(span).start()
        add(kept(span))

    mix_out[...] = jnp.zeros_like(mix_out)
    next_cot[...] = jnp.zeros_like(next_cot)
    mix_out[:MIXH, : STREAMS * NEXT] = mix_raw[...]
    next_cot[: STREAMS * NEXT, :] = next_raw[...]
    fetch = pltpu.make_async_copy(streams.at[3], residual, own_sem.at[0])
    fetch.start()
    cot_fetch = pltpu.make_async_copy(out_cot.at[at(tensor * half, half), :], cot_in, own_sem.at[7])
    cot_fetch.start()
    order = [span for pair in zip(range(spans // 2), range(spans // 2, spans)) for span in pair]
    for span in order:
        start(span)
    for span in order:
        after_core(span)
    for span in order:
        after_first(span)
    fetch.wait()
    cot_fetch.wait()

    def turn(index):
        rows = at(index * chunk, chunk)
        cot[rows, :] = cot_in[:, rows].T

    loop(0, depth // chunk, turn)
    squares = jnp.zeros((1, half), F32)
    for span in order:
        second_hop(span).wait()

        def widen(index, total):
            rows = at(span * size + index * chunk, chunk)
            branch = from_first[kept(span), rows, :].astype(F32) + from_second[rows, :].astype(F32)
            value = residual[rows, :].astype(F32) + branch
            wide[rows, :] = value
            block[:, rows] = value.T.astype(BF16)
            return total + jnp.sum(value * value, axis=0, keepdims=True)

        squares = lax.fori_loop(0, size // chunk, widen, squares)
    root = lax.rsqrt(squares / depth + ROOT_EPS)

    def share_block(which):
        mine = o_block.at[at(tensor * half, half), :]
        if which == 0:
            return pltpu.make_async_copy(block, mine, own_sem.at[1])
        return remote(block, mine, share_s.at[0], share_r.at[0], tensor=here.other)

    share_block(0).start()
    share_block(1).start()

    def norm(index):
        rows = at(index * chunk, chunk)
        normed[rows, :] = (wide[rows, :] * root).astype(BF16)

    loop(0, depth // chunk, norm)
    inner, slope = gelu_parts(tn(small[...], normed[...]))
    inner_low = inner.astype(BF16)
    next_rows[...] = tn(mix_out[...], inner_low)[:MIXH]
    next_low = next_cot[...].astype(BF16)

    column = lax.broadcasted_iota(jnp.int32, (128, 128), 1)
    static_grad = jnp.sum(next_cot[...], axis=1, keepdims=True)
    tiny[...] = jnp.where(column == MIXH, static_grad, nt(inner_low, next_low))[:MIXH]
    inner_grad = (nn(mix_out[...], next_low) * slope).astype(BF16)

    def pull(index, total):
        rows = at(index * chunk, chunk)
        value = jnp.dot(small[rows, :], inner_grad, preferred_element_type=F32)
        back[rows, :] = value
        return total + jnp.sum(value * wide[rows, :] * root, axis=0, keepdims=True)

    along = lax.fori_loop(0, depth // chunk, pull, jnp.zeros((1, half), F32)) / depth

    def finish(index):
        rows = at(index * chunk, chunk)
        value = cot[rows, :].astype(F32) + root * (back[rows, :] - wide[rows, :] * root * along)
        back[rows, :] = value
        low[rows, :] = value.astype(BF16)

    loop(0, depth // chunk, finish)

    def share(part_at, kind, index=0):
        rows = pl.ds(part_at * (depth // 2), depth // 2)
        number = 2 + part_at * 5 + kind + index
        if kind < 2:
            source, lanes, where = low.at[rows], lane_block(half, here.near, here.core, tensor, 1), (beside, across)[kind]
        elif kind == 2:
            far, where = (1 - here.near, across) if part_at == 0 else (here.near, beside)
            lanes = lane_block(half, far, here.core, tensor if part_at == 0 else here.other, 1)
            source = o_grad.at[rows, lanes]
        else:
            lanes, where = lane_block(half, index, here.core, 0, 2), {"dp": flip(me, CORE)}
            source = o_grad.at[rows, lanes]
        return remote(source, o_grad.at[rows, lanes], share_s.at[number], share_r.at[number], **where)

    for part_at in range(2):
        share(part_at, 0).start()
        share(part_at, 1).start()
    keep = pltpu.make_async_copy(
        low, o_grad.at[:, lane_block(half, here.near, here.core, tensor, 1)], own_sem.at[2]
    )
    keep.start()

    def mixin_rows(index):
        rows = at(index * chunk, chunk)
        mixin[rows, :] = nt(normed[rows, :], inner_grad)

    loop(0, depth // chunk, mixin_rows)
    for part_at in range(2):
        share(part_at, part_at).wait()
        share(part_at, 2).start()
    lanes = at(tensor * half, half)
    next_share = remote(next_rows, o_next.at[:, lanes], share_s.at[1], share_r.at[1], tensor=here.other)
    next_share.start()
    finals = [
        pltpu.make_async_copy(next_rows, o_next.at[:, lanes], own_sem.at[3]),
        pltpu.make_async_copy(back, o_wide, own_sem.at[4]),
        pltpu.make_async_copy(mixin, o_mixin, own_sem.at[5]),
        pltpu.make_async_copy(tiny, o_tiny, own_sem.at[6]),
    ]
    for copy in finals:
        copy.start()
    keep.wait()
    for part_at in range(2):
        share(part_at, 1 - part_at).wait()
        share(part_at, 2).wait()
        for near in range(2):
            share(part_at, 3, near).start()
    for part_at in range(2):
        for near in range(2):
            share(part_at, 3, near).wait()
    share_block(0).wait()
    share_block(1).wait()
    next_share.wait()
    for copy in finals:
        copy.wait()


def join(part, streams, out_cot, small, mix_out, next_cot):
    depth, half = streams.shape[1:]
    spans = 4
    shapes = [
        ((depth, 8 * half), BF16),
        ((depth, half), F32),
        ((2 * half, depth), BF16),
        ((MIXH, 2 * half), F32),
        ((depth, 128), F32),
        ((MIXH, 128), F32),
    ]
    return pl.pallas_call(
        join_kernel,
        out_shape=[jax.ShapeDtypeStruct(*shape) for shape in shapes],
        in_specs=[ANY] * 3 + [VM] * 3,
        out_specs=[ANY] * 6,
        scratch_shapes=[
            pltpu.VMEM((128, 128), BF16),
            pltpu.VMEM((128, half), F32),
            pltpu.VMEM((2, 2, depth, half), BF16),
            pltpu.VMEM((2, 2, depth, half), BF16),
            pltpu.VMEM((2, depth, half), BF16),
            pltpu.VMEM((depth, half), BF16),
            pltpu.VMEM((depth, half), BF16),
            pltpu.VMEM((depth, half), F32),
            pltpu.VMEM((depth, half), BF16),
            pltpu.VMEM((half, depth), BF16),
            pltpu.VMEM((depth, half), BF16),
            pltpu.VMEM((half, depth), BF16),
            pltpu.VMEM((depth, half), F32),
            pltpu.VMEM((depth, half), BF16),
            pltpu.VMEM((MIXH, half), F32),
            pltpu.VMEM((depth, 128), F32),
            pltpu.VMEM((MIXH, 128), F32),
            DMA((spans, 4)),
            DMA((spans, 4)),
            DMA((spans, 2)),
            DMA((spans, 2)),
            DMA((spans,)),
            DMA((spans,)),
            DMA((spans, 4)),
            DMA((12,)),
            DMA((12,)),
            DMA((8,)),
        ],
        compiler_params=pltpu.CompilerParams(
            collective_id=2, has_side_effects=True, vmem_limit_bytes=56 * 1024 * 1024
        ),
        name="join",
    )(part, streams, out_cot, small, mix_out, next_cot)


def back_kernel(
    grad, w_out, w_up, w_down, slope,
    o_mlp, o_up_grad, o_context,
    grad_in, out_in, up_in, down_in, slope_in,
    up_grad, context_grad, tall, load_sem, tall_sem, save_sem,
):
    depth = grad.shape[0]
    tile = 256
    loads = {}
    pairs = (
        [("grad", grad, grad_in), ("out", w_out, out_in)]
        + [
            pair
            for first in range(0, slope.shape[0], tile)
            for pair in (
                (("down", first), w_down.at[:, pl.ds(first, tile)], down_in.at[:, pl.ds(first, tile)]),
                (("slope", first), slope.at[pl.ds(first, tile)], slope_in.at[pl.ds(first, tile)]),
            )
        ]
        + [("up", w_up, up_in)]
    )
    for number, (name, source, target) in enumerate(pairs):
        loads[name] = pltpu.make_async_copy(source, target, load_sem.at[number])
        loads[name].start()

    pending = {}

    def write(turn, out, compute):
        slots = tall.shape[1]
        if turn in pending:
            pending.pop(turn)()

        def copy(index):
            slot = lax.rem(index, slots)
            target = out.at[at(index * tile, tile), :]
            return pltpu.make_async_copy(tall.at[turn, slot], target, tall_sem.at[turn, slot])

        def body(index):
            @pl.when(index >= slots)
            def _():
                copy(index - slots).wait()

            tall[turn, lax.rem(index, slots)] = compute(at(index * tile, tile)).astype(BF16)
            copy(index).start()

        steps = depth // tile
        loop(0, steps, body)
        pending[turn] = lambda: loop(steps - slots, steps, lambda index: copy(index).wait())

    for name in ("grad", "out"):
        loads[name].wait()
    context_grad[...] = tn(out_in[...], grad_in[...]).astype(BF16)
    save_context = pltpu.make_async_copy(context_grad, o_context, save_sem.at[1])
    save_context.start()
    for first in range(0, slope.shape[0], tile):
        loads["down", first].wait()
        loads["slope", first].wait()
        span = pl.ds(first, tile)
        up_grad[span, :] = (tn(down_in[:, span], grad_in[...]) * slope_in[span, :]).astype(BF16)
    loads["up"].wait()
    save_up = pltpu.make_async_copy(up_grad, o_up_grad, save_sem.at[0])
    save_up.start()
    write(1, o_mlp, lambda span: nn(up_in[span, :], up_grad[...]))
    for drain in pending.values():
        drain()
    save_up.wait()
    save_context.wait()


def back(grad, w_out, w_up, w_down, slope):
    depth, tokens = grad.shape
    operands = (grad, w_out, w_up, w_down, slope)
    shapes = [(depth, tokens), slope.shape, (w_out.shape[1], tokens)]
    return pl.pallas_call(
        back_kernel,
        out_shape=[jax.ShapeDtypeStruct(shape, BF16) for shape in shapes],
        in_specs=[ANY] * 5,
        out_specs=[ANY] * 3,
        scratch_shapes=[pltpu.VMEM(v.shape, v.dtype) for v in operands]
        + [
            pltpu.VMEM(slope.shape, BF16),
            pltpu.VMEM((w_out.shape[1], tokens), BF16),
            pltpu.VMEM((2, 4, 256, tokens), BF16),
            DMA((3 + 2 * (slope.shape[0] // 256),)),
            DMA((2, 4)),
            DMA((2,)),
        ],
        compiler_params=pltpu.CompilerParams(vmem_limit_bytes=56 * 1024 * 1024),
        name="back",
    )(*operands)


ORDER = (3, 0, 1, 2)
SLOT = (1, 0, 1, 0)


def scatter_kernel(
    n_dp, mlp_grad, streams, small, wide_grad, mixin_part, mix_tiny, hist,
    branch_grad, act, hidden, up_grad, context, heads_rows, sums, context_grad, w_qkv, cos, sin,
    o_stream, o_mix, o_small, o_tiny, o_qkv, o_up, o_down, o_out, sent_qkv, sent_up, sent_down, sent_out, attn_grad,
    own, from_core, from_tensor, from_near, rows_in, wide, stream_grad, gains, biases, tiny, tiny_in, tiny_out,
    hist_in, arrived, mix_part, mix_in, mix_sum, tiny_sum, ring, side_in, mine, high_in,
    hidden_in, up_in, context_in, rows_grad_in, heads_in, sums_in, outer_in, qkv_in, tile_in, stage, tile_sem, stage_sem,
    right_sem, qkv_sem,
    core_s, core_r, tensor_s, tensor_r, near_s, near_r, local, in_sem,
    side_s, side_r, high_s, high_r, peer_s, peer_r, peer_local,
    a2a_s, a2a_r, a2a_own, keep_sem, pass_s, pass_r, tiny_s, tiny_r, mix_s, mix_r, hist_sem,
    ring_s, ring_r, last_s, last_r, last_local,
):
    here = Place()
    me, tensor = here.me, here.tensor
    depth, half = wide_grad.shape
    rows = depth // n_dp
    high_bits = int(math.log2(n_dp // HIGH))
    chunk = min(256, depth)
    greet_all(n_dp, me, here.other)

    highs = n_dp // HIGH
    tall = 2 * rows
    arrays = (
        (branch_grad, hidden_in, sent_down, o_down),
        (act.at[3], up_in, sent_up, o_up),
        (branch_grad, context_in, sent_out, o_out),
    ) + tuple((act.at[s], rows_grad_in.at[s], sent_qkv.at[s], o_qkv.at[s]) for s in range(3))
    units, first_unit = [], []
    for _, right, sent, o in arrays:
        first_unit.append(len(units))
        units += [(sent, o, first) for first in range(0, right.shape[0], UNIT)]
    total = len(units)
    rights = [
        pltpu.make_async_copy(source, target, right_sem.at[number])
        for number, (source, target) in enumerate(
            (
                (hidden, hidden_in), (up_grad, up_in), (context, context_in), (heads_rows, heads_in), (sums, sums_in),
                (context_grad, outer_in),
            )
        )
    ]

    def side_hop(unit):
        sent, _, first = units[unit]
        return remote(
            sent.at[:, :, :, pl.ds(first, UNIT)], side_in.at[unit], side_s.at[unit], side_r.at[unit], dp=flip(me, SIDE)
        )

    count = highs * 2

    def tile_load(array, block):
        mine_now = lax.div(block, count)
        side = here.side * mine_now + (1 - here.side) * (1 - mine_now)
        row = (lax.rem(block, count) * 2 + side) * tall
        slot = lax.rem(block, 2)
        return pltpu.make_async_copy(arrays[array][0].at[at(row, tall), :], tile_in.at[slot], tile_sem.at[slot])

    def product(array, block):
        @pl.when(block + 1 < 2 * count)
        def _():
            tile_load(array, block + 1).start()

        tile_load(array, block).wait()
        return nt(tile_in[lax.rem(block, 2)], arrays[array][1][...]).astype(BF16)

    def compute_sent(array):
        _, right, sent, _ = arrays[array]
        width = right.shape[0]

        def put(block):
            slot = lax.rem(block, 2)
            return pltpu.make_async_copy(
                stage.at[slot, :, pl.ds(0, width)], sent.at[lax.div(block, 2), slot], stage_sem.at[slot]
            )

        def body(block):
            value = product(array, block)

            @pl.when(block >= 2)
            def _():
                put(block - 2).wait()

            stage[lax.rem(block, 2), :, :width] = value
            put(block).start()

        tile_load(array, 0).start()
        loop(0, count, body)
        put(count - 2).wait()
        put(count - 1).wait()

    def compute_mine(array):
        width = arrays[array][1].shape[0]

        def body(block):
            value = product(array, block)
            flat = block - count
            for part in range(width // UNIT):
                mine[first_unit[array] + part, lax.div(flat, 2), lax.rem(flat, 2)] = value[
                    :, part * UNIT : (part + 1) * UNIT
                ]

        loop(count, 2 * count, body)

    def high_hop(unit, phase):
        span = 1 << phase
        base = lax.div(here.high, span)
        theirs = base + 1 - 2 * lax.rem(base, 2)
        return remote(
            mine.at[unit, pl.ds(theirs * span, span)], high_in.at[unit, pl.ds(span - 1, span)],
            high_s.at[unit, phase], high_r.at[unit, phase], dp=flip(me, HIGH << phase),
        )

    def peer_hop(unit, peer):
        _, o, first = units[unit]
        target, _ = here.peers[peer]
        return remote(
            mine.at[unit, here.high, bit(target, NEAR), at(bit(target, CORE) * rows, rows)],
            o.at[:, at(here.quarter * (o.shape[-1] // QUARTERS) + first, UNIT)],
            peer_s.at[unit, peer], peer_r.at[unit, peer], dp=target,
        )

    def peer_keep(unit):
        _, o, first = units[unit]
        return pltpu.make_async_copy(
            mine.at[unit, here.high, here.near, at(here.core * rows, rows)],
            o.at[:, at(here.quarter * (o.shape[-1] // QUARTERS) + first, UNIT)], peer_local.at[unit],
        )

    def add_blocks(unit, other, first_mine, first_other, count):
        step = min(64, tall)

        def add(flat):
            high, rest = lax.div(flat, 2 * (tall // step)), lax.rem(flat, 2 * (tall // step))
            near, span = lax.div(rest, tall // step), at(lax.rem(rest, tall // step) * step, step)
            mine[unit, first_mine + high, near, span] += other[unit, first_other + high, near, span]

        loop(0, count * 2 * (tall // step), add)

    def finish_high(unit):
        for phase in reversed(range(high_bits)):
            high_hop(unit, phase).wait()
            span = 1 << phase
            add_blocks(unit, high_in, lax.div(here.high, span) * span, span - 1, span)
            if phase:
                high_hop(unit, phase - 1).start()
        peer_keep(unit).start()
        for peer in range(3):
            peer_hop(unit, peer).start()

    def tick(unit):
        side_hop(unit).wait()
        if unit + 2 < total:
            side_hop(unit + 2).start()
        add_blocks(unit, side_in, 0, 0, n_dp // HIGH)
        if unit:
            finish_high(unit - 1)
        high_hop(unit, high_bits - 1).start()

    done = 0

    def ticks(count):
        nonlocal done
        for unit in range(done, min(done + count, total)):
            tick(unit)
        done = min(done + count, total)

    def load(stream, near, half_at):
        part = attn_grad.at[stream] if stream < 3 else mlp_grad
        return pltpu.make_async_copy(
            part.at[:, lane_block(half, near, here.core, half_at, 1)], own.at[SLOT[stream], near, half_at],
            local.at[stream, near * 2 + half_at],
        )

    def to_core(stream, near, half_at):
        part = attn_grad.at[stream] if stream < 3 else mlp_grad
        return remote(
            part.at[:, lane_block(half, near, 1 - here.core, half_at, 1)], from_core.at[stream, near, half_at],
            core_s.at[stream, near * 2 + half_at], core_r.at[stream, near * 2 + half_at], dp=flip(me, CORE),
        )

    def to_tensor(stream, near):
        return remote(
            own.at[SLOT[stream], near, here.other], from_tensor.at[stream, near],
            tensor_s.at[stream, near], tensor_r.at[stream, near], tensor=here.other,
        )

    def to_near(stream):
        return remote(
            from_tensor.at[stream, 1 - here.near], from_near.at[stream], near_s.at[stream], near_r.at[stream],
            dp=flip(me, NEAR),
        )

    def after_core(stream):
        for near in range(2):
            for half_at in range(2):
                load(stream, near, half_at).wait()
                to_core(stream, near, half_at).wait()

        def add(index):
            span = at(index * chunk, chunk)
            for near in range(2):
                for half_at in range(2):
                    own[SLOT[stream], near, half_at, span] += from_core[stream, near, half_at, span]

        loop(0, depth // chunk, add)

    def after_tensor(stream):
        for near in range(2):
            to_tensor(stream, near).wait()

        def add(index):
            span = at(index * chunk, chunk)
            for near in range(2):
                from_tensor[stream, near, span] += own[SLOT[stream], near, tensor, span]

        loop(0, depth // chunk, add)
        to_near(stream).start()

    stats = []

    def measure(stream):
        def piece(index):
            return rows_in[stream, at(index * chunk, chunk), :].astype(F32)

        centre = sum_rows(piece, depth, chunk, lambda v: v) / depth
        spread = sum_rows(piece, depth, chunk, lambda v: (v - centre) * (v - centre)) / depth
        stats.append((centre, lax.rsqrt(spread + NORM_EPS)))

    def back_norm(stream):
        to_near(stream).wait()
        group = 0 if stream < 3 else 1
        centre, root = stats[stream]

        def parts(index):
            span = at(index * chunk, chunk)
            grad = from_tensor[stream, here.near, span].astype(F32) + from_near[stream, span].astype(F32)
            hat = (rows_in[stream, span, :].astype(F32) - centre) * root
            gain = small[span, MIXH + group : MIXH + group + 1].astype(F32)
            return span, grad, hat, grad * gain

        def sums(index, carry):
            span, grad, hat, scaled = parts(index)
            if stream in (0, 3):
                gains[group, span] = grad * hat
                biases[group, span] = grad
            else:
                gains[group, span] += grad * hat
                biases[group, span] += grad
            return (
                carry[0] + jnp.sum(scaled, axis=0, keepdims=True),
                carry[1] + jnp.sum(scaled * hat, axis=0, keepdims=True),
            )

        zero = jnp.zeros((1, half), F32)
        whole, along = lax.fori_loop(0, depth // chunk, sums, (zero, zero))

        def finish(index):
            span, _, hat, scaled = parts(index)
            value = root * (scaled - whole / depth - hat * (along / depth))
            if stream == 3:
                value = value + wide[span, :]
            stream_grad[stream, span] = value.astype(BF16)

        loop(0, depth // chunk, finish)
        loop(1, n_dp, lambda step: send(stream, step).start())
        send_own(stream).start()

    def send(stream, step):
        target = lax.rem(me + step, n_dp)
        return remote(
            stream_grad.at[stream, at(target * rows, rows), :], arrived.at[stream, step],
            a2a_s.at[stream, step], a2a_r.at[stream, step], dp=target,
        )

    def send_own(stream):
        return pltpu.make_async_copy(
            stream_grad.at[stream, at(me * rows, rows), :], arrived.at[stream, 0], a2a_own.at[stream]
        )

    def source_of(step):
        return lax.rem(me - step + n_dp, n_dp)

    def lanes_of(step):
        return at(source_of(step) * 2 * half + tensor * half, half)

    def fetch(step):
        slot = lax.rem(step, 2)
        return pltpu.make_async_copy(hist.at[:, :, lanes_of(step)], hist_in.at[slot], hist_sem.at[slot])

    def keep(stream, step):
        return pltpu.make_async_copy(
            arrived.at[stream, step], o_stream.at[stream, :, lanes_of(step)], keep_sem.at[stream, step]
        )

    def pass_on(stream, step):
        return remote(
            arrived.at[stream, step], o_stream.at[stream, :, lanes_of(step)],
            pass_s.at[stream, step], pass_r.at[stream, step], tensor=here.other,
        )

    def mix_send(step):
        return remote(mix_part.at[step], mix_in.at[step], mix_s.at[step], mix_r.at[step], dp=source_of(step))

    def receive(stream):
        fetch(0).start()
        send_own(stream).wait()

        def one(step):
            @pl.when(step + 1 < n_dp)
            def _():
                fetch(step + 1).start()

            @pl.when(step > 0)
            def _():
                send(stream, step).wait()

            keep(stream, step).start()
            pass_on(stream, step).start()
            fetch(step).wait()
            totals = [jnp.zeros((8, half), F32) for _ in range(HIST)]
            for row in range(0, rows, 16):
                span = pl.ds(row, 16)
                grad = arrived[stream, step, span, :].astype(F32)
                for source in range(HIST):
                    product = grad * hist_in[lax.rem(step, 2), source, span, :].astype(F32)
                    totals[source] = totals[source] + product[:8] + product[8:]
            for source in range(HIST):
                mix_part[step, pl.ds(stream * HIST + source, 1), :] = jnp.sum(totals[source], axis=0, keepdims=True)
            if stream == ORDER[-1]:

                @pl.when(step > 0)
                def _():
                    mix_send(step).start()

        loop(0, n_dp, one)

    ring_targets = [{"dp": flip(me, value)} for value in (CORE, SIDE, NEAR)]
    ring_targets += [{"dp": flip(me, HIGH << phase)} for phase in range(high_bits)]
    ring_targets.append({"tensor": here.other})
    hops = len(ring_targets)

    def ring_hop(hop):
        return remote(ring.at[hop, 0], ring.at[hop, 1], ring_s.at[hop], ring_r.at[hop], **ring_targets[hop])

    def ring_step(hop):
        ring_hop(hop).wait()
        ring[hop + 1, 0] = ring[hop, 0] + ring[hop, 1]
        if hop + 1 < hops:
            ring_hop(hop + 1).start()

    rights[0].start()
    inputs = [
        pltpu.make_async_copy(streams, rows_in, in_sem.at[0]),
        pltpu.make_async_copy(wide_grad, wide, in_sem.at[1]),
        pltpu.make_async_copy(mix_tiny, ring.at[0, 0], in_sem.at[2]),
    ]

    def load_own(stream):
        for near in range(2):
            for half_at in range(2):
                load(stream, near, half_at).start()

    def tensor_start(stream):
        for near in range(2):
            to_tensor(stream, near).start()

    def core_start(stream):
        for near in range(2):
            for half_at in range(2):
                to_core(stream, near, half_at).start()

    def qkv_load(stream):
        return pltpu.make_async_copy(w_qkv.at[stream], qkv_in.at[stream % 2], qkv_sem.at[stream % 2])

    seq_len = sums_in.shape[1]
    heads = heads_in.shape[1] // HD
    scale = 1.0 / math.sqrt(HD)

    def attend_back(seq):
        span = at(seq * seq_len, seq_len)
        for head in range(heads):
            lane = pl.ds(head * HD, HD)
            queries, keys, values = (heads_in[s, lane, span] for s in range(3))
            prob = jnp.exp(causal_scores(keys, queries) - sums_in[pl.ds(seq * heads + head, 1), :])
            outer = outer_in[lane, span]
            prob_grad = tn(values, outer)
            inner = jnp.sum(prob * prob_grad, axis=0, keepdims=True)
            score_grad = (prob * (prob_grad - inner)).astype(BF16)
            turn_back = (cos[...], -sin[...])
            rows_grad_in[0, lane, span] = turned(nn(keys, score_grad) * scale, *turn_back).astype(BF16)
            rows_grad_in[1, lane, span] = turned(nt(queries, score_grad) * scale, *turn_back).astype(BF16)
            rows_grad_in[2, lane, span] = nt(outer, prob.astype(BF16)).astype(BF16)

    def input_grad(stream):
        def put(block):
            slot = lax.rem(block, 2)
            return pltpu.make_async_copy(
                stage.at[slot, :, pl.ds(0, 8 * half)], attn_grad.at[stream, at(block * tall, tall), :], stage_sem.at[slot]
            )

        def body(block):
            value = nn(qkv_in[stream % 2, at(block * tall, tall), :], rows_grad_in[stream]).astype(BF16)

            @pl.when(block >= 2)
            def _():
                put(block - 2).wait()

            stage[lax.rem(block, 2), :, : 8 * half] = value
            put(block).start()

        qkv_load(stream).wait()
        loop(0, depth // tall, body)
        put(depth // tall - 2).wait()
        put(depth // tall - 1).wait()
        if stream + 2 < 3:
            qkv_load(stream + 2).start()
        core_start(stream)

    core_start(ORDER[0])
    load_own(ORDER[0])
    for copy in rights[1:] + inputs:
        copy.start()
    qkv_load(0).start()
    qkv_load(1).start()
    rights[0].wait()
    compute_sent(0)
    side_hop(0).start()
    side_hop(1).start()
    after_core(ORDER[0])
    tensor_start(ORDER[0])
    compute_mine(0)
    for copy in rights[1:] + inputs:
        copy.wait()
    ring_hop(0).start()
    loop(0, 8 * half // seq_len, attend_back)
    for stream in range(3):
        input_grad(stream)
        if stream == 0:
            ticks(1)
        if stream == ORDER[1]:
            load_own(stream)
    mix_part[...] = jnp.zeros_like(mix_part)
    for stream in range(STREAMS):
        measure(stream)
    after_core(ORDER[1])
    ring_step(0)
    for turn, stream in enumerate(ORDER):
        ticks((1, 3, 2, 2)[turn])
        after_tensor(stream)
        if turn + 1 < STREAMS:
            tensor_start(ORDER[turn + 1])
            if turn + 1 < hops:
                ring_step(turn + 1)
        if turn + 2 < STREAMS:
            load_own(ORDER[turn + 2])
        for array in ((1,), (2, 3), (4, 5), ())[turn]:
            compute_sent(array)
            compute_mine(array)
        if turn + 2 < STREAMS:
            after_core(ORDER[turn + 2])
        if turn > 0:
            back_norm(ORDER[turn - 1])
        if turn > 1:
            receive(ORDER[turn - 2])
    back_norm(ORDER[-1])

    column = lax.broadcasted_iota(jnp.int32, (chunk, 128), 1)
    pltpu.make_async_copy(mixin_part, wide, in_sem.at[0]).start()
    pltpu.make_async_copy(mixin_part, wide, in_sem.at[0]).wait()

    def gather_tiny(index):
        span = at(index * chunk, chunk)
        value = wide[span, :]
        for group in range(2):
            gain = jnp.sum(gains[group, span], axis=1, keepdims=True)
            bias = jnp.sum(biases[group, span], axis=1, keepdims=True)
            value = jnp.where(column == MIXH + group, gain, value)
            value = jnp.where(column == MIXH + 2 + group, bias, value)
        tiny[span, :] = value.astype(BF16)

    loop(0, depth // chunk, gather_tiny)

    def tiny_send(step):
        target = lax.rem(me + step, n_dp)
        return remote(tiny.at[at(target * rows, rows), :], tiny_in.at[step], tiny_s.at[step], tiny_r.at[step], dp=target)

    loop(1, n_dp, lambda step: tiny_send(step).start())
    receive(ORDER[2])
    ticks(2)
    receive(ORDER[3])
    for hop in range(STREAMS, hops):
        ring_step(hop)
    tiny_final = pltpu.make_async_copy(ring.at[hops, 0], o_tiny, last_local.at[0])
    tiny_final.start()
    ticks(total)

    tiny_sum[0] = tiny[at(me * rows, rows), :].astype(F32)

    def add_tiny(step):
        tiny_send(step).wait()
        tiny_sum[0] += tiny_in[step].astype(F32)

    loop(1, n_dp, add_tiny)
    tiny_share = remote(tiny_sum.at[0], tiny_sum.at[1], last_s.at[1], last_r.at[1], tensor=here.other)
    tiny_share.start()
    mix_sum[...] = mix_part[0]

    def add_mix(step):
        mix_send(step).wait()
        mix_sum[...] += mix_in[step]

    loop(1, n_dp, add_mix)
    lanes = at(tensor * half, half)
    mix_share = remote(mix_sum, o_mix.at[:, lanes], last_s.at[0], last_r.at[0], tensor=here.other)
    mix_keep = pltpu.make_async_copy(mix_sum, o_mix.at[:, lanes], last_local.at[1])
    mix_share.start()
    mix_keep.start()
    finish_high(total - 1)
    tiny_share.wait()
    tiny_out[...] = (tiny_sum[0] + tiny_sum[1]).T
    tiny_keep = pltpu.make_async_copy(tiny_out, o_small, last_local.at[2])
    tiny_keep.start()
    for unit in range(total):
        peer_keep(unit).wait()
        for peer in range(3):
            peer_hop(unit, peer).wait()

    def settle(step):
        for stream in range(STREAMS):
            keep(stream, step).wait()
            pass_on(stream, step).wait()

    loop(0, n_dp, settle)
    mix_share.wait()
    mix_keep.wait()
    tiny_keep.wait()
    tiny_final.wait()


def scatter(
    n_dp, mlp_grad, streams, small, wide_grad, mixin_part, mix_tiny, hist, branch_grad, act, hidden, up_grad, context,
    rows_all, sums, context_grad, w_qkv, cos, sin,
):
    depth, half = wide_grad.shape
    rows = depth // n_dp
    high = n_dp // HIGH
    high_bits = int(math.log2(high))
    tokens = act.shape[2]
    narrow, width = context.shape[0], hidden.shape[0]
    widths = ((3,), narrow), ((), width), ((), width), ((), narrow)
    units = (4 * narrow + 2 * width) // UNIT
    hops = high_bits + 4

    outs = [
        ((STREAMS, rows, 2 * half * n_dp), BF16),
        ((MIXH, 2 * half), F32),
        ((128, rows), F32),
        (mix_tiny.shape, F32),
    ]
    outs += [(lead + (rows, QUARTERS * size), BF16) for lead, size in widths]
    outs += [(lead + (high, 2, 2 * rows, size), BF16) for lead, size in widths]
    outs.append(((3, depth, tokens), BF16))
    return pl.pallas_call(
        functools.partial(scatter_kernel, n_dp),
        out_shape=[jax.ShapeDtypeStruct(*shape) for shape in outs],
        in_specs=[ANY, ANY, VM] + [ANY] * 13 + [VM] * 2,
        out_specs=[ANY] * 13,
        scratch_shapes=[
            pltpu.VMEM((2, 2, 2, depth, half), BF16),
            pltpu.VMEM((STREAMS, 2, 2, depth, half), BF16),
            pltpu.VMEM((STREAMS, 2, depth, half), BF16),
            pltpu.VMEM((STREAMS, depth, half), BF16),
            pltpu.VMEM((STREAMS, depth, half), BF16),
            pltpu.VMEM((depth, half), F32),
            pltpu.VMEM((STREAMS, depth, half), BF16),
            pltpu.VMEM((2, depth, half), F32),
            pltpu.VMEM((2, depth, half), F32),
            pltpu.VMEM((depth, 128), BF16),
            pltpu.VMEM((n_dp, rows, 128), BF16),
            pltpu.VMEM((128, rows), F32),
            pltpu.VMEM((2, HIST, rows, half), BF16),
            pltpu.VMEM((STREAMS, n_dp, rows, half), BF16),
            pltpu.VMEM((n_dp, MIXH, half), F32),
            pltpu.VMEM((n_dp, MIXH, half), F32),
            pltpu.VMEM((MIXH, half), F32),
            pltpu.VMEM((2, rows, 128), F32),
            pltpu.VMEM((hops + 1, 2) + mix_tiny.shape, F32),
            pltpu.VMEM((units, high, 2, 2 * rows, UNIT), BF16),
            pltpu.VMEM((units, high, 2, 2 * rows, UNIT), BF16),
            pltpu.VMEM((units, high - 1, 2, 2 * rows, UNIT), BF16),
            pltpu.VMEM(hidden.shape, BF16),
            pltpu.VMEM(up_grad.shape, BF16),
            pltpu.VMEM(context.shape, BF16),
            pltpu.VMEM(rows_all.shape, BF16),
            pltpu.VMEM(rows_all.shape, BF16),
            pltpu.VMEM(sums.shape, F32),
            pltpu.VMEM(context_grad.shape, BF16),
            pltpu.VMEM((2,) + w_qkv.shape[1:], BF16),
            pltpu.VMEM((2, 2 * rows, tokens), BF16),
            pltpu.VMEM((2, 2 * rows, max(width, tokens)), BF16),
            DMA((2,)),
            DMA((2,)),
            DMA((6,)),
            DMA((2,)),
            DMA((STREAMS, 4)),
            DMA((STREAMS, 4)),
            DMA((STREAMS, 2)),
            DMA((STREAMS, 2)),
            DMA((STREAMS,)),
            DMA((STREAMS,)),
            DMA((STREAMS, 4)),
            DMA((3,)),
            DMA((units,)),
            DMA((units,)),
            DMA((units, high_bits)),
            DMA((units, high_bits)),
            DMA((units, 3)),
            DMA((units, 3)),
            DMA((units,)),
            DMA((STREAMS, n_dp)),
            DMA((STREAMS, n_dp)),
            DMA((STREAMS,)),
            DMA((STREAMS, n_dp)),
            DMA((STREAMS, n_dp)),
            DMA((STREAMS, n_dp)),
            DMA((n_dp,)),
            DMA((n_dp,)),
            DMA((n_dp,)),
            DMA((n_dp,)),
            DMA((2,)),
            DMA((hops,)),
            DMA((hops,)),
            DMA((2,)),
            DMA((2,)),
            DMA((3,)),
        ],
        compiler_params=pltpu.CompilerParams(
            collective_id=3, has_side_effects=True, vmem_limit_bytes=62 * 1024 * 1024
        ),
        name="scatter",
    )(
        mlp_grad, streams, small, wide_grad, mixin_part, mix_tiny, hist, branch_grad, act, hidden, up_grad, context,
        rows_all, sums, context_grad, w_qkv, cos, sin,
    )[:8]


def rotary_tables(length, rotary, float_type):
    half_rot = rotary // 2
    places = jnp.arange(length).astype(float_type)
    frequency = jnp.exp(
        jnp.arange(half_rot).astype(float_type) * (-2.0 * math.log(10000.0) / rotary)
    )
    angles = places[:, None] * frequency[None, :]
    return (jnp.cos(angles), jnp.sin(angles))


def finish_kernel(mix_rows, stream_grad, small, tiny, block, *refs):
    narrow, history_grad, wide = refs[:4], refs[4], refs[5:9]
    gain, bias, mix_in_grad, mix_out_grad, block_out = refs[9:]
    rows = stream_grad.shape[1]
    tile, span = min(32, rows), 512

    def body(index):
        row = at(lax.rem(index, rows // tile) * tile, tile)
        lane = at(lax.div(index, rows // tile) * span, span)
        grads = [stream_grad[stream, row, lane].astype(F32) for stream in range(STREAMS)]
        for source in range(HIST):
            total = sum(
                mix_rows[pl.ds(stream * HIST + source, 1), lane] * grads[stream] for stream in range(STREAMS)
            )
            history_grad[source, row, lane] = total.astype(BF16)

    loop(0, rows // tile * (stream_grad.shape[2] // span), body)
    for low, full in zip(narrow, wide):
        full[...] = low[...].astype(F32)
    block_out[...] = block[...]
    gain[...] = small[MIXH : MIXH + 2]
    bias[...] = small[MIXH + 2 : MIXH + 4]
    mix_in_grad[...] = small[:MIXH]
    mix_out_grad[...] = tiny[:, : STREAMS * NEXT]


def finish(mix_rows, stream_grad, small, tiny, block, *grads):
    rows, tokens = stream_grad.shape[1:]
    steps = rows // 16
    lanes = tokens // steps

    def weight(g):
        if g.ndim == 3:
            return pl.BlockSpec((g.shape[0], 16, g.shape[2]), lambda i: (0, i, 0))
        return pl.BlockSpec((16, g.shape[1]), lambda i: (i, 0))

    def along(count):
        return pl.BlockSpec((count, rows, lanes), lambda i: (0, 0, i))

    def whole(shape):
        return pl.BlockSpec(shape, lambda i: (0, 0))

    blocks = pl.BlockSpec((block.shape[0] // steps, block.shape[1]), lambda i: (i, 0))
    smalls = [(2, rows), (2, rows), (MIXH, rows), (MIXH, STREAMS * NEXT)]
    return pl.pallas_call(
        finish_kernel,
        grid=(steps,),
        out_shape=[jax.ShapeDtypeStruct((HIST, rows, tokens), BF16)]
        + [jax.ShapeDtypeStruct(g.shape, F32) for g in grads]
        + [jax.ShapeDtypeStruct(shape, F32) for shape in smalls]
        + [jax.ShapeDtypeStruct(block.shape, BF16)],
        in_specs=[pl.BlockSpec((mix_rows.shape[0], lanes), lambda i: (0, i)), along(STREAMS)]
        + [whole(small.shape), whole(tiny.shape), blocks]
        + [weight(g) for g in grads],
        out_specs=[along(HIST)] + [weight(g) for g in grads] + [whole(shape) for shape in smalls] + [blocks],
        compiler_params=pltpu.CompilerParams(vmem_limit_bytes=60 * 1024 * 1024),
        name="finish",
    )(mix_rows, stream_grad, small, tiny, block, *grads)


def per_device(
    n_dp, history, mix_weights, w_qkv, w_out, w_up, w_down, norm_gain, norm_bias, mix_in, mix_out, mix_static,
    out_cot, next_cot,
):
    tensor = lax.axis_index("tensor")
    seq_len = mix_weights.shape[0]
    half = seq_len // 2
    depth = mix_in.shape[0] * n_dp

    def own_half(rows):
        return lax.dynamic_slice_in_dim(rows, tensor * half, half, 0)

    mix_rows = own_half(mix_weights.reshape(seq_len, -1)).T
    small = jnp.concatenate(
        [mix_in.T, norm_gain, norm_bias, jnp.zeros((128 - MIXH - 4, mix_in.shape[0]), BF16)], axis=0
    )
    cos, sin = (table.T for table in rotary_tables(seq_len, ROT, F32))
    mix_rows, small_all, streams, act, qkv, out, up, down, rows, context, sums, hidden, slope, part = gather(
        n_dp, history, mix_rows, small, w_qkv, w_out, w_up, w_down, cos, sin
    )
    small_all = small_all.reshape(depth, 128)
    qkv, up, down, out = (
        qkv.reshape(3, depth, -1), up.reshape(depth, -1), down.reshape(depth, -1), out.reshape(depth, -1)
    )

    next_rows = own_half(next_cot.reshape(seq_len, -1)).T
    branch_grad, wide_grad, block, next_mix, mixin_part, tiny = join(
        part, streams, out_cot, small_all, mix_out, next_rows
    )
    mlp_in_grad, up_grad, context_grad = back(branch_grad, out, up, down, slope)
    stream_grad, mix_grad, small_total, tiny, qkv_total, up_total, down_total, out_total = scatter(
        n_dp, mlp_in_grad, streams, small_all, wide_grad, mixin_part, tiny, history, branch_grad, act, hidden, up_grad,
        context, rows, sums, context_grad, qkv, cos, sin,
    )
    (
        history_grad, qkv_total, up_total, down_total, out_total, gain_total, bias_total, mixin_total, mixout_total, block,
    ) = finish(
        mix_rows, stream_grad, small_total, tiny, block, qkv_total, up_total, down_total, out_total
    )
    return (
        block,
        (next_mix.T + mix_static).reshape(seq_len, STREAMS, NEXT),
        history_grad,
        mix_grad[: STREAMS * HIST].T.reshape(seq_len, STREAMS, HIST),
        qkv_total,
        out_total,
        up_total,
        down_total,
        gain_total,
        bias_total,
        mixin_total.T,
        mixout_total,
        tiny[: STREAMS * NEXT, MIXH],
    )


def solution(mesh):
    return jax.shard_map(
        functools.partial(per_device, mesh.shape["dp"]),
        mesh=mesh,
        in_specs=(
            P(None, "dp", None),
            P("dp", None, None),
            P(None, "dp", "tensor"),
            P("dp", "tensor"),
            P("dp", "tensor"),
            P("dp", "tensor"),
            P(None, "dp"),
            P(None, "dp"),
            P("dp", None),
            P(),
            P(),
            P("dp", None),
            P("dp", None, None),
        ),
        out_specs=(
            P("dp", None),
            P("dp", None, None),
            P(None, "dp", None),
            P("dp", None, None),
            P(None, "dp", "tensor"),
            P("dp", "tensor"),
            P("dp", "tensor"),
            P("dp", "tensor"),
            P(None, "dp"),
            P(None, "dp"),
            P("dp", None),
            P(),
            P(),
        ),
        check_vma=False,
    )
```
